32 devices in a mesh: seq: 16 (over z, x, core), tp: 2 (over y).
Axes of the slice: x: 2, y: 2, z: 4, core: 2. Of those that a mesh axis runs over, the one named last changes fastest.
Arguments:
- tokens: bfloat16 [4096, 3200], P('seq'), may hold values from -8 to 8
- norm_gain: float32 [3200], replicated, may hold values from 0.5 to 1.5
- qkv_weight: bfloat16 [3200, 3, 2048], P('seq', None, 'tp'), may hold values from -1 to 1
- q_gain: float32 [2048], P('tp'), may hold values from 0.5 to 5, as said below
- k_gain: float32 [2048], P('tp'), may hold values from 0.5 to 5, as said below
- out_weight: bfloat16 [2048, 3200], P('tp', 'seq'), may hold values from -0.125 to 0.125
- layer_scale: float32 [3200], P('tp'), may hold values from 0.5 to 2
- segment_ids: int32 [4096], replicated, may hold values from 0 to 15, never falling along the last dimension, each value on 1 to 512 neighbouring positions
Outputs:
- mixed: bfloat16 [4096, 3200], P('seq', 'tp')
The draws below stay inside these ranges and needn't reach their ends.
Inputs may be any that keep to these rules, and one draw needn't show every extreme that they name: `segment_ids`: image numbers never fall along the row; each image has 1 to 512 patches, one exactly 512. `q_gain`: positive gains. `k_gain`: positive gains.
All inputs are finite; a program needn't handle non-finite values.
Results may differ from the reference program's by a relative error of at most 0.0078.
Values may be sent and summed in bfloat16 or wider, within the bound.
No kernel may reach another device: no remote copies, remote signals or barrier semaphores. Data moves between devices by JAX's collectives and lax.ppermute only.
A program may use at most 64 MiB of HBM per device.

```python
import math
import jax
import jax.numpy as jnp
import numpy as np
from jax import lax

D = 3200
HEAD_DIM = 128
HEADS = 16
TOK_DEV = 256
TOKENS = 4096
IMAGES = 16
N_SEQ = 16


def draw_tokens(key, part):
    parts = jax.random.split(jax.random.fold_in(key, 11), 1)
    base = jax.random.normal(parts[0], (TOKENS, D), jnp.float32)
    return jnp.clip(base, -6.0, 6.0).astype(jnp.bfloat16)


def draw_qkv_weight(key, part):
    width = HEADS * HEAD_DIM
    parts = jax.random.split(jax.random.fold_in(key, 23), 1)
    base = jax.random.normal(parts[0], (D, 3, width), jnp.float32)
    head = (jnp.arange(width) // HEAD_DIM).astype(jnp.float32)
    growth = 3.0
    scale = jnp.power(growth, head / (HEADS - 1)) / math.sqrt(D)
    return jnp.clip(base * scale[None, None, :], -1.0, 1.0).astype(jnp.bfloat16)


def gain_draw(key, salt):
    upper = 2.0
    level = jax.random.uniform(jax.random.fold_in(key, salt), (HEADS * HEAD_DIM,), jnp.float32, math.log(0.5), math.log(upper))
    return jnp.exp(level)


def draw_q_gain(key, part):
    return gain_draw(key, 37)


def draw_k_gain(key, part):
    return gain_draw(key, 41)


def shard_levels(key, extent, cuts, low, high):
    loudness = 1.0
    for dim, blocks in cuts:
        steps = jax.random.uniform(jax.random.fold_in(jax.random.fold_in(key, 6), dim), (blocks,), jnp.float32, low / len(cuts), high / len(cuts))
        loudness = loudness * jnp.repeat(jnp.exp(steps), extent[dim] // blocks).reshape((-1,) + (1,) * (len(extent) - 1 - dim))
    return loudness


def profile(count, total, limit, slope):
    weights = [(1 << 20) // math.isqrt(rank ** slope) + 1 for rank in range(2, count + 1)]
    rest, given = total - limit - (count - 1), [1] * (count - 1)
    while rest > 0:
        candidates = [i for i in range(count - 1) if given[i] < limit]
        whole, remaining = sum([weights[i] for i in candidates]), rest
        for i in candidates:
            extra = min(limit - given[i], max(1, remaining * weights[i] // whole), rest)
            given[i] = given[i] + extra
            rest = rest - extra
    return np.array([limit] + given)


def ragged(key, amount, total, reach, skew):
    if amount == 2:
        one = jax.random.randint(key, (), max(1, total - reach), min(reach, total - 1) + 1)
        return jnp.stack([one, total - one])
    sizes = jnp.asarray(profile(amount, total, reach, skew), jnp.int32)
    twos = (amount - 1) // 2
    source_of, sink = sizes[1:1 + 2 * twos:2], sizes[2:2 + 2 * twos:2]
    room = jnp.minimum(source_of - 1, reach - sink)
    shifted = jax.random.randint(jax.random.fold_in(key, 1), (twos,), 0, 1 << 20) % (room + 1)
    sizes = sizes.at[1:1 + 2 * twos:2].set(source_of - shifted).at[2:2 + 2 * twos:2].set(sink + shifted)
    return sizes[jax.random.permutation(jax.random.fold_in(key, 2), amount)]


def bell_draw(key, dims, scale, reach, cuts=(), held_as=jnp.bfloat16):
    array = scale * jax.random.normal(key, dims, jnp.float32)
    if cuts:
        array = array * shard_levels(key, dims, cuts, -0.22, 0.18)
    return jnp.clip(array, -reach, reach).astype(held_as)


def setup_inputs(seed: int = 0) -> dict:
    splits = jax.random.split(jax.random.key(seed), 9)
    tokens = draw_tokens(jax.random.fold_in(splits[8], 71), 0)
    norm_gain = jnp.clip(jax.random.uniform(splits[1], (D,), jnp.float32, 0.5, 1.5), 0.5, 1.5)
    qkv_weight = draw_qkv_weight(jax.random.fold_in(splits[8], 71), 0)
    q_gain = draw_q_gain(jax.random.fold_in(splits[8], 71), 0)
    k_gain = draw_k_gain(jax.random.fold_in(splits[8], 71), 0)
    out_weight = bell_draw(splits[5], (HEADS * HEAD_DIM, D), (HEADS * HEAD_DIM) ** -0.5, 0.125, ((0, 2), (1, 16)))
    layer_scale = jnp.clip(jnp.exp(math.log(2.0) - 1.3862944 * jax.random.uniform(splits[6], (D,), jnp.float32) ** shard_levels(splits[6], (D,), ((0, 2),), -0.2, 0.2)), 0.5, 2.0)
    segment_ids = jnp.searchsorted(jnp.cumsum(ragged(splits[7], IMAGES, TOKENS, 2 * TOK_DEV, 2)), jnp.arange(TOKENS), side="right").astype(jnp.int32)
    return dict(tokens=tokens, norm_gain=norm_gain, qkv_weight=qkv_weight, q_gain=q_gain, k_gain=k_gain, out_weight=out_weight, layer_scale=layer_scale, segment_ids=segment_ids)


eps = 1e-06
floor_score = -1e+30

def attend(query, keys, values, query_seg, key_seg):
    count = query.shape[0]
    width = query.shape[1]
    heads = width // HEAD_DIM
    query_f = query.astype(jnp.float32).reshape(count, heads, HEAD_DIM)
    keys_f = keys.astype(jnp.float32).reshape(keys.shape[0], heads, HEAD_DIM)
    values_f = values.astype(jnp.float32).reshape(values.shape[0], heads, HEAD_DIM)
    scores = jnp.einsum('qhd,khd->hqk', query_f, keys_f) * HEAD_DIM ** (-0.5)
    mask = (query_seg[:, None] == key_seg[None, :])[None]
    scores = jnp.where(mask, scores, floor_score)
    peak = lax.optimization_barrier(jnp.max(scores, axis=-1, keepdims=True))
    weights = jnp.where(mask, jnp.exp(scores - peak), 0.0)
    total = lax.optimization_barrier(jnp.sum(weights, axis=-1))
    probs = weights.astype(jnp.bfloat16).astype(jnp.float32)
    context = jnp.einsum('hqk,khd->qhd', probs, values_f)
    context = context / jnp.transpose(total)[:, :, None]
    return context.reshape(count, width).astype(jnp.bfloat16)

def reference(tokens, norm_gain, qkv_weight, q_gain, k_gain, out_weight, layer_scale, segment_ids):
    source = tokens.astype(jnp.float32)
    normed = (source * lax.rsqrt(lax.optimization_barrier(jnp.mean(source * source, axis=-1, keepdims=True)) + eps) * norm_gain).astype(jnp.bfloat16)
    width = HEADS * HEAD_DIM
    flat = qkv_weight.reshape(D, 3 * width)
    joined = jnp.dot(normed, flat, preferred_element_type=jnp.float32).reshape(TOKENS, 3, width)
    query = joined[:, 0]
    keys = joined[:, 1]
    values = joined[:, 2]
    query_normed = (query * lax.rsqrt(lax.optimization_barrier(jnp.mean(query * query, axis=-1, keepdims=True)) + eps) * q_gain).astype(jnp.bfloat16)
    key_normed = (keys * lax.rsqrt(lax.optimization_barrier(jnp.mean(keys * keys, axis=-1, keepdims=True)) + eps) * k_gain).astype(jnp.bfloat16)
    values_low = values.astype(jnp.bfloat16)
    blank = jnp.zeros((2 * TOK_DEV, width), jnp.bfloat16)
    keys_pad = jnp.concatenate([blank, key_normed, blank], axis=0)
    values_pad = jnp.concatenate([blank, values_low, blank], axis=0)
    outside = jnp.full((2 * TOK_DEV,), -1, jnp.int32)
    seg_pad = jnp.concatenate([outside, segment_ids.astype(jnp.int32), outside], axis=0)

    def one_block(block):
        start = (block * TOK_DEV).astype(jnp.int32)
        query_block = lax.dynamic_slice_in_dim(query_normed, start, TOK_DEV, 0)
        query_seg = lax.dynamic_slice_in_dim(segment_ids.astype(jnp.int32), start, TOK_DEV, 0)
        key_block = lax.dynamic_slice_in_dim(keys_pad, start, 5 * TOK_DEV, 0)
        value_block = lax.dynamic_slice_in_dim(values_pad, start, 5 * TOK_DEV, 0)
        key_seg = lax.dynamic_slice_in_dim(seg_pad, start, 5 * TOK_DEV, 0)
        return attend(query_block, key_block, value_block, query_seg, key_seg)
    context = lax.map(one_block, jnp.arange(N_SEQ, dtype=jnp.int32)).reshape(TOKENS, width)
    projected = jnp.dot(context, out_weight, preferred_element_type=jnp.float32)
    return (source + layer_scale * projected).astype(jnp.bfloat16)
```

```python
import functools

import jax
import jax.numpy as jnp
from jax import lax
from jax.experimental import pallas as pl
from jax.experimental.pallas import tpu as pltpu
from jax.sharding import PartitionSpec as P

HEAD_DIM = 128
SLAB = 4

eps = 1e-06
floor_score = -1e30


def passed_along(x, axis, by):
    size = lax.axis_size(axis)
    pairs = [(i, i + by) for i in range(size) if 0 <= i + by < size]
    return lax.ppermute(x, axis, pairs)


def masked_scores(query, keys, query_seg, key_seg):
    scores = jnp.einsum(
        "qhd,khd->hqk", query, keys, preferred_element_type=jnp.float32
    ) * HEAD_DIM ** (-0.5)
    mask = (query_seg[:, None] == key_seg[None, :])[None]
    return (jnp.where(mask, scores, floor_score), mask)


def row_plan(tokens, norm_gain, qkv_weight, q_gain, k_gain, out_weight, layer_scale, segment_ids):
    count = tokens.shape[0]
    source = tokens.astype(jnp.float32)
    normed = (
        source * lax.rsqrt(jnp.mean(source * source, axis=-1, keepdims=True) + eps) * norm_gain
    ).astype(jnp.bfloat16)
    local_width = qkv_weight.shape[2]
    heads = local_width // HEAD_DIM
    joined = jnp.einsum(
        "td,dch->tch",
        normed,
        lax.all_gather(qkv_weight, "seq", axis=0, tiled=True),
        preferred_element_type=jnp.float32,
    )
    query = joined[:, 0]
    keys = joined[:, 1]
    values = joined[:, 2]
    query_sq, key_sq = lax.psum(
        (jnp.sum(query * query, axis=-1), jnp.sum(keys * keys, axis=-1)), "tp"
    )
    full_width = local_width * lax.axis_size("tp")
    query_normed = (query * lax.rsqrt(query_sq / full_width + eps)[:, None] * q_gain).astype(
        jnp.bfloat16
    )
    key_normed = (keys * lax.rsqrt(key_sq / full_width + eps)[:, None] * k_gain).astype(
        jnp.bfloat16
    )
    paired = jnp.stack([key_normed, values.astype(jnp.bfloat16)], axis=1)
    pieces = []
    for offset in (2, 1, 0, -1, -2):
        if offset == 0:
            pieces.append(paired)
        else:
            pieces.append(passed_along(paired, "seq", offset))
    widened = jnp.concatenate(pieces, axis=0)
    position = lax.axis_index("seq")
    outside = jnp.full((2 * count,), -1, jnp.int32)
    seg_pad = jnp.concatenate([outside, segment_ids, outside], axis=0)
    key_seg = lax.dynamic_slice_in_dim(seg_pad, position * count, 5 * count, 0)
    query_seg = lax.dynamic_slice_in_dim(segment_ids, position * count, count, 0)
    query_heads = query_normed.reshape(count, heads, HEAD_DIM)
    key_heads = widened[:, 0].reshape(5 * count, heads, HEAD_DIM)
    value_heads = widened[:, 1].reshape(5 * count, heads, HEAD_DIM)
    scores, mask = masked_scores(query_heads, key_heads, query_seg, key_seg)
    peak = jnp.max(scores, axis=-1, keepdims=True)
    weights = jnp.where(mask, jnp.exp(scores - peak), 0.0)
    total = jnp.sum(weights, axis=-1)
    probs = weights.astype(jnp.bfloat16)
    summed = jnp.einsum("hqk,khd->qhd", probs, value_heads, preferred_element_type=jnp.float32)
    context = (
        (summed / jnp.transpose(total)[:, :, None]).reshape(count, local_width).astype(jnp.bfloat16)
    )
    terms = jnp.dot(
        context,
        lax.all_gather(out_weight, "seq", axis=1, tiled=True),
        preferred_element_type=jnp.float32,
    )
    projected = lax.psum_scatter(terms, "tp", scatter_dimension=1, tiled=True)
    share = layer_scale.shape[0]
    residual = lax.dynamic_slice_in_dim(source, lax.axis_index("tp") * share, share, 1)
    return (residual + layer_scale * projected).astype(jnp.bfloat16)


ANY = pl.BlockSpec(memory_space=pl.ANY)
VMEM = pl.BlockSpec(memory_space=pltpu.VMEM)
SMEM = pl.BlockSpec(memory_space=pltpu.SMEM)


def in_slab(x, flip):
    size = lax.axis_size("seq")
    return lax.ppermute(x, "seq", [(i, i ^ flip) for i in range(size)])


def across(x):
    return lax.ppermute(x, "tp", [(0, 1), (1, 0)])


def along_z(x, by):
    return passed_along(x, "seq", SLAB * by)


def as_row(column):
    wide = jnp.broadcast_to(column, (column.shape[0], 128))
    return jnp.transpose(wide)[:8]


def as_column(row):
    return jnp.transpose(jnp.broadcast_to(row, (128, row.shape[1])))


def project_kernel(
    slabs, place, x0, x1, x2, x3, own, above, below, q_gain, k_gain,
    query, keys, values, squares, x_all, w_all, x_sem, w_sem, up_sem, down_sem,
):
    z, q = place[0], place[1]
    rows = own.shape[1]
    w_copies = []

    def weight_copy(src, at, sem):
        at = pl.multiple_of(at * rows, 32)
        return pltpu.make_async_copy(src, w_all.at[:, pl.ds(at, rows), :], sem)

    mine = weight_copy(own, z, w_sem)
    mine.start()
    for r in range(1, slabs):
        @pl.when(z + r < slabs)
        def _():
            weight_copy(above[r - 1], z + r, up_sem.at[r - 1]).start()

        @pl.when(z - r >= 0)
        def _():
            weight_copy(below[r - 1], z - r, down_sem.at[r - 1]).start()

    x_copies = []
    for r, x in enumerate((x0, x1, x2, x3)):
        copy = pltpu.make_async_copy(x, x_all.at[r], x_sem.at[r])
        copy.start()
        x_copies.append(copy)
    mine.wait()
    for r in range(1, slabs):
        @pl.when(z + r < slabs)
        def _():
            weight_copy(above[r - 1], z + r, up_sem.at[r - 1]).wait()

        @pl.when(z - r >= 0)
        def _():
            weight_copy(below[r - 1], z - r, down_sem.at[r - 1]).wait()

    for r in range(SLAB):
        x_copies[r].wait()
        block = q ^ r
        source = x_all[r]
        part = jnp.dot(source, w_all[0], preferred_element_type=jnp.float32)
        squares[block, 0] = as_row(jnp.sum(part * part, axis=1, keepdims=True))
        query[block] = part * q_gain[...]
        part = jnp.dot(source, w_all[1], preferred_element_type=jnp.float32)
        squares[block, 1] = as_row(jnp.sum(part * part, axis=1, keepdims=True))
        keys[block] = (part * k_gain[...]).astype(jnp.bfloat16)
        part = jnp.dot(source, w_all[2], preferred_element_type=jnp.float32)
        values[block] = part.astype(jnp.bfloat16)


def project(place, xs, own, above, below, q_gain, k_gain):
    slabs = len(above) + 1
    count, depth = xs[0].shape
    width = own.shape[2]
    f32, bf16 = jnp.float32, jnp.bfloat16
    body = functools.partial(project_body, slabs)
    return pl.pallas_call(
        body,
        out_shape=(
            jax.ShapeDtypeStruct((SLAB, count, width), f32),
            jax.ShapeDtypeStruct((SLAB, count, width), bf16),
            jax.ShapeDtypeStruct((SLAB, count, width), bf16),
            jax.ShapeDtypeStruct((SLAB, 2, 8, count), f32),
        ),
        in_specs=[SMEM] + [ANY] * (4 + 2 * slabs - 1) + [VMEM, VMEM],
        out_specs=(VMEM, VMEM, VMEM, VMEM),
        scratch_shapes=[
            pltpu.VMEM((SLAB, count, depth), bf16),
            pltpu.VMEM((3, depth, width), bf16),
            pltpu.SemaphoreType.DMA((SLAB,)),
            pltpu.SemaphoreType.DMA,
            pltpu.SemaphoreType.DMA((slabs,)),
            pltpu.SemaphoreType.DMA((slabs,)),
        ],
        compiler_params=pltpu.CompilerParams(vmem_limit_bytes=40 * 1024 * 1024),
        cost_estimate=pl.CostEstimate(
            flops=2 * SLAB * count * depth * 3 * width,
            bytes_accessed=2 * depth * (SLAB * count + 3 * width),
            transcendentals=0,
        ),
        name="project",
    )(place, *xs, own, *above, *below, q_gain, k_gain)


def project_body(slabs, *refs):
    place, x0, x1, x2, x3, own = refs[:6]
    above = refs[6:6 + slabs - 1]
    below = refs[6 + slabs - 1:6 + 2 * (slabs - 1)]
    rest = refs[6 + 2 * (slabs - 1):]
    project_kernel(slabs, place, x0, x1, x2, x3, own, above, below, *rest)


def attend_kernel(
    full_width, place, query, keys, k_low, k_high, values, v_low, v_high, sums, seg,
    o0, o1, o2, o3, k_all, v_all, sems,
):
    q = place[1]
    count = query.shape[1]
    half = k_low.shape[0]
    own = SLAB * count
    copies = []
    for i, (src, dst, at, n) in enumerate((
        (k_low, k_all, 0, half), (keys, k_all, half, own), (k_high, k_all, half + own, half),
        (v_low, v_all, 0, half), (values, v_all, half, own), (v_high, v_all, half + own, half),
    )):
        copy = pltpu.make_async_copy(src, dst.at[pl.ds(at, n), :], sems.at[i])
        copy.start()
        copies.append(copy)
    for copy in copies:
        copy.wait()
    window = count + 2 * half
    heads = query.shape[2] // HEAD_DIM
    for r, out in ((1, o1), (2, o2), (3, o3), (0, o0)):
        block = q ^ r
        start = pl.multiple_of(block * count, count)
        at_query = pl.multiple_of(block * count + half, count)
        key_seg = seg[:, pl.ds(start, window)]
        query_seg = as_column(seg[:, pl.ds(at_query, count)])
        k_scale = lax.rsqrt(sums[1:2, pl.ds(start, window)] / full_width + eps)
        q_scale = lax.rsqrt(as_column(sums[0:1, pl.ds(at_query, count)]) / full_width + eps)
        mask = jnp.tile(query_seg, (1, window // 128)) == key_seg
        for h in range(heads):
            cols = slice(h * HEAD_DIM, (h + 1) * HEAD_DIM)
            q_low = (query[block, :, cols] * (q_scale * HEAD_DIM ** (-0.5))).astype(jnp.bfloat16)
            scores = lax.dot_general(
                q_low, k_all[pl.ds(start, window), cols], (((1,), (1,)), ((), ())),
                preferred_element_type=jnp.float32,
            )
            scores = jnp.where(mask, scores * k_scale, floor_score)
            peak = jnp.max(scores, axis=1, keepdims=True)
            weights = jnp.exp(scores - peak)
            total = jnp.sum(weights, axis=1, keepdims=True)
            summed = jnp.dot(
                weights.astype(jnp.bfloat16), v_all[pl.ds(start, window), cols],
                preferred_element_type=jnp.float32,
            )
            out[:, cols] = (summed / total).astype(jnp.bfloat16)


def attend(full_width, place, query, keys, k_low, k_high, values, v_low, v_high, sums, seg):
    count, width = query.shape[1:]
    half = k_low.shape[0]
    ext = SLAB * count + 2 * half
    bf16 = jnp.bfloat16
    block = jax.ShapeDtypeStruct((count, width), bf16)
    window = count + 2 * half
    return pl.pallas_call(
        functools.partial(attend_kernel, full_width),
        out_shape=(block,) * 4,
        in_specs=[SMEM, VMEM] + [ANY] * 6 + [VMEM, VMEM],
        out_specs=(VMEM,) * 4,
        scratch_shapes=[
            pltpu.VMEM((ext, width), bf16),
            pltpu.VMEM((ext, width), bf16),
            pltpu.SemaphoreType.DMA((6,)),
        ],
        compiler_params=pltpu.CompilerParams(vmem_limit_bytes=40 * 1024 * 1024),
        cost_estimate=pl.CostEstimate(
            flops=4 * SLAB * count * window * width,
            bytes_accessed=4 * ext * width + 4 * SLAB * count * width,
            transcendentals=SLAB * count * window * width // HEAD_DIM,
        ),
        name="attend",
    )(place, query, keys, k_low, k_high, values, v_low, v_high, sums, seg)


def gather_blocks(place, blocks, c_all):
    for r, c in enumerate(blocks):
        c_all[place[1] ^ r] = c[...]


def away_kernel(place, c0, c1, c2, c3, w, out, c_all, w_vmem, sem):
    share = w_vmem.shape[0]
    at = pl.multiple_of((1 - place[2]) * share, 32)
    copy = pltpu.make_async_copy(w.at[pl.ds(at, share), :], w_vmem, sem)
    copy.start()
    gather_blocks(place, (c0, c1, c2, c3), c_all)
    copy.wait()
    out[...] = out_terms(c_all, w_vmem).astype(jnp.bfloat16)


def out_terms(c_all, w_vmem):
    width = c_all.shape[2]
    total = None
    for b in range(SLAB):
        term = lax.dot_general(
            w_vmem[:, b * width:(b + 1) * width], c_all[b], (((1,), (1,)), ((), ())),
            preferred_element_type=jnp.float32,
        )
        total = term if total is None else total + term
    return total


def home_kernel(place, c0, c1, c2, c3, w, sent, residual, scale, out, c_all, w_vmem, sem):
    share = w_vmem.shape[0]
    at = pl.multiple_of(place[2] * share, 32)
    copy = pltpu.make_async_copy(w.at[pl.ds(at, share), :], w_vmem, sem)
    copy.start()
    gather_blocks(place, (c0, c1, c2, c3), c_all)
    copy.wait()
    total = out_terms(c_all, w_vmem) + sent[...].astype(jnp.float32)
    out[...] = (residual[...].astype(jnp.float32) + scale[...] * total).astype(jnp.bfloat16)


def out_call(kernel, place, blocks, w, share, extra):
    count, width = blocks[0].shape
    return pl.pallas_call(
        kernel,
        out_shape=jax.ShapeDtypeStruct((share, count), jnp.bfloat16),
        in_specs=[SMEM] + [VMEM] * 4 + [ANY] + [VMEM] * len(extra),
        out_specs=VMEM,
        scratch_shapes=[
            pltpu.VMEM((SLAB, count, width), jnp.bfloat16),
            pltpu.VMEM((share, SLAB * width), jnp.bfloat16),
            pltpu.SemaphoreType.DMA,
        ],
        compiler_params=pltpu.CompilerParams(vmem_limit_bytes=40 * 1024 * 1024),
        cost_estimate=pl.CostEstimate(
            flops=2 * share * count * SLAB * width,
            bytes_accessed=2 * share * SLAB * width,
            transcendentals=0,
        ),
        name=kernel.__name__,
    )(place, *blocks, w, *extra)


def slab_plan(tokens, norm_gain, qkv_weight, q_gain, k_gain, out_weight, layer_scale, segment_ids):
    count = tokens.shape[0]
    seq, tp = lax.axis_index("seq"), lax.axis_index("tp")
    slabs = lax.axis_size("seq") // SLAB
    z, q = seq // SLAB, seq % SLAB
    place = jnp.stack([z, q, tp]).astype(jnp.int32)
    width = qkv_weight.shape[2] // SLAB
    full_width = qkv_weight.shape[2] * lax.axis_size("tp")

    by_kind = jnp.transpose(qkv_weight, (1, 0, 2))
    cut = [lax.dynamic_slice_in_dim(by_kind, (q ^ r) * width, width, 2) for r in range(SLAB)]
    got = [cut[0]] + [in_slab(cut[r], r) for r in range(1, SLAB)]
    placed = []
    for b in range(SLAB):
        piece = got[b]
        for other in range(1, SLAB):
            piece = jnp.where(q == other, got[b ^ other], piece)
        placed.append(piece)
    own = jnp.concatenate(placed, axis=1)

    source = tokens.astype(jnp.float32)
    normed = (
        source * lax.rsqrt(jnp.mean(source * source, axis=-1, keepdims=True) + eps) * norm_gain
    ).astype(jnp.bfloat16)

    above, below = [], []
    down, up = own, own
    xs = None
    for r in range(1, slabs):
        down, up = along_z(down, -1), along_z(up, 1)
        above.append(down)
        below.append(up)
        if r == 1:
            x2 = in_slab(normed, 2)
            xs = (normed, in_slab(normed, 1), x2, in_slab(x2, 1))

    gains = [lax.dynamic_slice_in_dim(g, q * width, width, 0)[None] for g in (q_gain, k_gain)]
    query, keys, values, squares = project(place, xs, own, above, below, *gains)

    tied = lax.optimization_barrier((out_weight, above[-1], below[-1]))[0]
    all_out = jnp.transpose(lax.all_gather(tied, "seq", axis=1, tiled=True))

    half = 2 * count
    flat_keys, flat_values = keys.reshape(-1, width), values.reshape(-1, width)
    k_low, v_low = along_z(flat_keys[-half:], 1), along_z(flat_values[-half:], 1)
    k_high, v_high = along_z(flat_keys[:half], -1), along_z(flat_values[:half], -1)
    sums = jnp.transpose(squares[:, :, 0], (1, 0, 2)).reshape(2, SLAB * count)
    sums = sums + in_slab(sums, 1)
    sums = sums + in_slab(sums, 2)
    sums = sums + across(sums)
    sums_low, sums_high = along_z(sums[:, -half:], 1), along_z(sums[:, :half], -1)
    sums = jnp.concatenate([sums_low, sums, sums_high], axis=1)
    outside = jnp.full((half,), -1, jnp.int32)
    seg = jnp.concatenate([outside, segment_ids, outside], axis=0)
    seg = lax.dynamic_slice_in_dim(seg, z * SLAB * count, SLAB * count + 2 * half, 0)
    seg = seg.astype(jnp.float32)[None]
    blocks = attend(
        full_width, place, query, flat_keys, k_low, k_high, flat_values, v_low, v_high, sums, seg
    )
    blocks = [blocks[0]] + [in_slab(blocks[r], r) for r in range(1, SLAB)]

    share = layer_scale.shape[0]
    residual = jnp.transpose(lax.dynamic_slice_in_dim(tokens, tp * share, share, 1))
    sent = across(out_call(away_kernel, place, blocks, all_out, share, ()))
    mixed = out_call(
        home_kernel, place, blocks, all_out, share, (sent, residual, layer_scale[:, None])
    )
    return jnp.transpose(mixed)


def solution(mesh):
    def shards(*args):
        heads = args[2].shape[2] // HEAD_DIM
        slab = mesh.shape["seq"] == 16 and mesh.shape["tp"] == 2 and heads % SLAB == 0
        return (slab_plan if slab else row_plan)(*args)

    return jax.shard_map(
        shards,
        mesh=mesh,
        in_specs=(
            P("seq", None),
            P(),
            P("seq", None, "tp"),
            P("tp"),
            P("tp"),
            P("tp", "seq"),
            P("tp"),
            P(),
        ),
        out_specs=P("seq", "tp"),
        check_vma=False,
    )
```

```python
import functools

import jax
import jax.numpy as jnp
from jax import lax
from jax.experimental import pallas as pl
from jax.experimental.pallas import tpu as pltpu
from jax.sharding import PartitionSpec as P

HEAD_DIM = 128
SLAB = 4

eps = 1e-06
floor_score = -1e30


def passed_along(x, axis, by):
    size = lax.axis_size(axis)
    pairs = [(i, i + by) for i in range(size) if 0 <= i + by < size]
    return lax.ppermute(x, axis, pairs)


def masked_scores(query, keys, query_seg, key_seg):
    scores = jnp.einsum(
        "qhd,khd->hqk", query, keys, preferred_element_type=jnp.float32
    ) * HEAD_DIM ** (-0.5)
    mask = (query_seg[:, None] == key_seg[None, :])[None]
    return (jnp.where(mask, scores, floor_score), mask)


def row_plan(tokens, norm_gain, qkv_weight, q_gain, k_gain, out_weight, layer_scale, segment_ids):
    count = tokens.shape[0]
    source = tokens.astype(jnp.float32)
    normed = (
        source * lax.rsqrt(jnp.mean(source * source, axis=-1, keepdims=True) + eps) * norm_gain
    ).astype(jnp.bfloat16)
    local_width = qkv_weight.shape[2]
    heads = local_width // HEAD_DIM
    joined = jnp.einsum(
        "td,dch->tch",
        normed,
        lax.all_gather(qkv_weight, "seq", axis=0, tiled=True),
        preferred_element_type=jnp.float32,
    )
    query = joined[:, 0]
    keys = joined[:, 1]
    values = joined[:, 2]
    query_sq, key_sq = lax.psum(
        (jnp.sum(query * query, axis=-1), jnp.sum(keys * keys, axis=-1)), "tp"
    )
    full_width = local_width * lax.axis_size("tp")
    query_normed = (query * lax.rsqrt(query_sq / full_width + eps)[:, None] * q_gain).astype(
        jnp.bfloat16
    )
    key_normed = (keys * lax.rsqrt(key_sq / full_width + eps)[:, None] * k_gain).astype(
        jnp.bfloat16
    )
    paired = jnp.stack([key_normed, values.astype(jnp.bfloat16)], axis=1)
    pieces = []
    for offset in (2, 1, 0, -1, -2):
        if offset == 0:
            pieces.append(paired)
        else:
            pieces.append(passed_along(paired, "seq", offset))
    widened = jnp.concatenate(pieces, axis=0)
    position = lax.axis_index("seq")
    outside = jnp.full((2 * count,), -1, jnp.int32)
    seg_pad = jnp.concatenate([outside, segment_ids, outside], axis=0)
    key_seg = lax.dynamic_slice_in_dim(seg_pad, position * count, 5 * count, 0)
    query_seg = lax.dynamic_slice_in_dim(segment_ids, position * count, count, 0)
    query_heads = query_normed.reshape(count, heads, HEAD_DIM)
    key_heads = widened[:, 0].reshape(5 * count, heads, HEAD_DIM)
    value_heads = widened[:, 1].reshape(5 * count, heads, HEAD_DIM)
    scores, mask = masked_scores(query_heads, key_heads, query_seg, key_seg)
    peak = jnp.max(scores, axis=-1, keepdims=True)
    weights = jnp.where(mask, jnp.exp(scores - peak), 0.0)
    total = jnp.sum(weights, axis=-1)
    probs = weights.astype(jnp.bfloat16)
    summed = jnp.einsum("hqk,khd->qhd", probs, value_heads, preferred_element_type=jnp.float32)
    context = (
        (summed / jnp.transpose(total)[:, :, None]).reshape(count, local_width).astype(jnp.bfloat16)
    )
    terms = jnp.dot(
        context,
        lax.all_gather(out_weight, "seq", axis=1, tiled=True),
        preferred_element_type=jnp.float32,
    )
    projected = lax.psum_scatter(terms, "tp", scatter_dimension=1, tiled=True)
    share = layer_scale.shape[0]
    residual = lax.dynamic_slice_in_dim(source, lax.axis_index("tp") * share, share, 1)
    return (residual + layer_scale * projected).astype(jnp.bfloat16)


ANY = pl.BlockSpec(memory_space=pl.ANY)
VMEM = pl.BlockSpec(memory_space=pltpu.VMEM)
SMEM = pl.BlockSpec(memory_space=pltpu.SMEM)
MIB = 1024 * 1024


def permuted(x, to):
    slabs, tps = lax.axis_size("seq") // SLAB, lax.axis_size("tp")
    pairs = []
    for i in range(slabs * SLAB * tps):
        z, q, y = to(i // (SLAB * tps), i // tps % SLAB, i % tps)
        pairs.append((i, (z * SLAB + q) * tps + y))
    return lax.ppermute(x, ("seq", "tp"), pairs)


def in_slab(x, flip):
    return permuted(x, lambda z, q, y: (z, q ^ flip, y))


def across(x):
    return permuted(x, lambda z, q, y: (z, q, 1 - y))


def even_of(z):
    return z ^ 1


def odd_of(z):
    return 3 - z if z in (1, 2) else z


def even_pair(x, flip=0):
    return permuted(x, lambda z, q, y: (even_of(z), q, y ^ flip))


def odd_pair(x, flip=0):
    return permuted(x, lambda z, q, y: (odd_of(z), q, y ^ flip))


def tied(*arrays):
    return lax.optimization_barrier(arrays)


def as_row(column):
    wide = jnp.broadcast_to(column, (column.shape[0], 128))
    return jnp.transpose(wide)[:8]


def as_column(row):
    return jnp.transpose(jnp.broadcast_to(row, (128, row.shape[1])))


def norm_kernel(place, tokens, gain, first, pair):
    half, part = pair.shape[2], pair.shape[3]
    for i in range(2):
        at = pl.multiple_of((place[2] ^ i) * half, half)
        source = tokens[pl.ds(at, half), :].astype(jnp.float32)
        mean = jnp.mean(source * source, axis=1, keepdims=True)
        normed = source * lax.rsqrt(mean + eps) * gain[...]
        for j in range(pair.shape[1]):
            chunk = normed[:, j * part:(j + 1) * part].astype(jnp.bfloat16)
            pair[i, j] = chunk
            if i == 0:
                first[j] = chunk


def norm(place, tokens, gain, slabs):
    count, depth = tokens.shape
    shape = (slabs, count // 2, depth // slabs)
    return pl.pallas_call(
        norm_kernel,
        out_shape=(
            jax.ShapeDtypeStruct(shape, jnp.bfloat16),
            jax.ShapeDtypeStruct((2,) + shape, jnp.bfloat16),
        ),
        in_specs=[SMEM, VMEM, VMEM],
        out_specs=(VMEM, VMEM),
        compiler_params=pltpu.CompilerParams(vmem_limit_bytes=16 * MIB),
        name="norm",
    )(place, tokens, gain[None])


def far_slabs(z):
    return jnp.where(z < 2, 2, 1), jnp.where(z < 2, 3, 0)


def pick(z, middle, end, out):
    inner = (z == 1) | (z == 2)

    @pl.when(inner)
    def _():
        out[...] = middle[...]

    @pl.when(jnp.logical_not(inner))
    def _():
        out[...] = end[...]


def token_chunk(xs, r, at):
    if r < 2:
        return jnp.concatenate([xs[r][0, at], xs[r][1, at]], axis=0)
    return jnp.concatenate([xs[2 * r - 2][at], xs[2 * r - 1][at]], axis=0)


def early_kernel(place, xa, xb, xc, xd, xe, xf, own, near, middle, end, acc, far):
    z = place[0]
    pick(z, middle, end, far)
    xs = (xa, xb, xc, xd, xe, xf)
    for r in range(SLAB):
        lhs = [token_chunk(xs, r, at) for at in (z, z ^ 1, far_slabs(z)[0])]
        for kind in range(3):
            total = None
            for x, w in zip(lhs, (own, near, far)):
                term = jnp.dot(x, w[kind], preferred_element_type=jnp.float32)
                total = term if total is None else total + term
            acc[kind, r] = total


def early(place, xs, own, near, middle, end):
    kinds, rows, width = own.shape
    count = 2 * xs[0].shape[2]
    return pl.pallas_call(
        early_kernel,
        out_shape=jax.ShapeDtypeStruct((kinds, SLAB, count, width), jnp.float32),
        in_specs=[SMEM] + [VMEM] * 10,
        out_specs=VMEM,
        scratch_shapes=[pltpu.VMEM((kinds, rows, width), jnp.bfloat16)],
        compiler_params=pltpu.CompilerParams(vmem_limit_bytes=24 * MIB),
        cost_estimate=pl.CostEstimate(
            flops=6 * kinds * SLAB * count * rows * width,
            bytes_accessed=8 * kinds * rows * width + 6 * SLAB * count * rows,
            transcendentals=0,
        ),
        name="early",
    )(place, *xs, own, near, middle, end)


def late_kernel(
    place, xa, xb, xc, xd, xe, xf, acc, middle, end, q_gain, k_gain,
    query, keys, values, squares, even, odd, far,
):
    z, q, y = place[0], place[1], place[2]
    pick(z, middle, end, far)
    xs = (xa, xb, xc, xd, xe, xf)
    count = acc.shape[2]
    half = count // 2
    for r in range(SLAB):
        x = token_chunk(xs, r, far_slabs(z)[1])
        for kind in range(3):
            part = acc[kind, r] + jnp.dot(x, far[kind], preferred_element_type=jnp.float32)
            if kind < 2:
                summed = as_row(jnp.sum(part * part, axis=1, keepdims=True))
                part = part * (q_gain, k_gain)[kind][...]
            for i in range(2):
                at = pl.multiple_of((q ^ r) * count + (y ^ i) * half, half)
                rows = slice(i * half, (i + 1) * half)
                if kind == 0:
                    query[pl.ds(at, half), :] = part[rows]
                else:
                    low = part[rows].astype(jnp.bfloat16)
                    (keys, values)[kind - 1][pl.ds(at, half), :] = low
                if kind < 2:
                    squares[kind:kind + 1, pl.ds(at, half)] = summed[:1, rows]
    reach = even.shape[1]
    for out, at in ((even, 1 - z % 2), (odd, z % 2)):
        rows = pl.ds(pl.multiple_of(at * reach, reach), reach)
        out[0] = keys[rows, :]
        out[1] = values[rows, :]


def late(place, xs, acc, middle, end, q_gain, k_gain):
    kinds, rows, width = middle.shape
    count = acc.shape[2]
    slab = SLAB * count
    f32, bf16 = jnp.float32, jnp.bfloat16
    return pl.pallas_call(
        late_kernel,
        out_shape=(
            jax.ShapeDtypeStruct((slab, width), f32),
            jax.ShapeDtypeStruct((slab, width), bf16),
            jax.ShapeDtypeStruct((slab, width), bf16),
            jax.ShapeDtypeStruct((2, slab), f32),
            jax.ShapeDtypeStruct((2, 2 * count, width), bf16),
            jax.ShapeDtypeStruct((2, 2 * count, width), bf16),
        ),
        in_specs=[SMEM] + [VMEM] * 11,
        out_specs=(VMEM,) * 6,
        scratch_shapes=[pltpu.VMEM((kinds, rows, width), bf16)],
        compiler_params=pltpu.CompilerParams(vmem_limit_bytes=24 * MIB),
        cost_estimate=pl.CostEstimate(
            flops=2 * kinds * slab * rows * width,
            bytes_accessed=2 * kinds * rows * width + 2 * slab * rows,
            transcendentals=0,
        ),
        name="late",
    )(place, *xs, acc, middle, end, q_gain, k_gain)


def attend_kernel(
    full_width, place, query, keys, values, even, odd, mine, mine_y, e, e_y, o, o_y, seg,
    o0, o1, o2, o3, k_all, v_all, scale_all,
):
    z, q = place[0], place[1]
    slab = query.shape[0]
    count = slab // SLAB
    half = even.shape[1]
    sums = mine[...] + mine_y[...]
    scale_all[:, pl.ds(half, slab)] = lax.rsqrt(sums / full_width + eps)
    k_all[pl.ds(half, slab), :] = keys[...]
    v_all[pl.ds(half, slab), :] = values[...]
    upper = half + slab

    def put(kv, a, b, high):
        at = upper if high else 0
        part = slice(0, half) if high else slice(slab - half, slab)
        k_all[pl.ds(at, half), :] = kv[0]
        v_all[pl.ds(at, half), :] = kv[1]
        scale_all[:, pl.ds(at, half)] = lax.rsqrt((a[:, part] + b[:, part]) / full_width + eps)

    @pl.when(z % 2 == 0)
    def _():
        put(even, e, e_y, True)
        put(odd, o, o_y, False)

    @pl.when(z % 2 == 1)
    def _():
        put(even, e, e_y, False)
        put(odd, o, o_y, True)

    window = count + 2 * half
    heads = query.shape[1] // HEAD_DIM
    for r, out in ((1, o1), (2, o2), (3, o3), (0, o0)):
        start = pl.multiple_of((q ^ r) * count, count)
        at_query = pl.multiple_of((q ^ r) * count + half, count)
        key_seg = seg[:, pl.ds(start, window)]
        query_seg = as_column(seg[:, pl.ds(at_query, count)])
        k_scale = scale_all[1:2, pl.ds(start, window)]
        q_scale = as_column(scale_all[0:1, pl.ds(at_query, count)])
        mask = jnp.tile(query_seg, (1, window // 128)) == key_seg
        for h in range(heads):
            cols = slice(h * HEAD_DIM, (h + 1) * HEAD_DIM)
            q_low = query[pl.ds(start, count), cols] * (q_scale * HEAD_DIM ** (-0.5))
            scores = lax.dot_general(
                q_low.astype(jnp.bfloat16), k_all[pl.ds(start, window), cols],
                (((1,), (1,)), ((), ())), preferred_element_type=jnp.float32,
            )
            scores = jnp.where(mask, scores * k_scale, floor_score)
            peak = jnp.max(scores, axis=1, keepdims=True)
            weights = jnp.exp(scores - peak)
            total = jnp.sum(weights, axis=1, keepdims=True)
            summed = jnp.dot(
                weights.astype(jnp.bfloat16), v_all[pl.ds(start, window), cols],
                preferred_element_type=jnp.float32,
            )
            out[:, cols] = (summed / total).astype(jnp.bfloat16)


def attend(full_width, place, query, keys, values, even, odd, sums, seg):
    slab, width = query.shape
    half = even.shape[1]
    count = slab // SLAB
    ext = slab + 2 * half
    bf16 = jnp.bfloat16
    block = jax.ShapeDtypeStruct((count, width), bf16)
    window = count + 2 * half
    return pl.pallas_call(
        functools.partial(attend_kernel, full_width),
        out_shape=(block,) * 4,
        in_specs=[SMEM] + [VMEM] * 12,
        out_specs=(VMEM,) * 4,
        scratch_shapes=[
            pltpu.VMEM((ext, width), bf16),
            pltpu.VMEM((ext, width), bf16),
            pltpu.VMEM((2, ext), jnp.float32),
        ],
        compiler_params=pltpu.CompilerParams(vmem_limit_bytes=24 * MIB),
        cost_estimate=pl.CostEstimate(
            flops=4 * slab * window * width,
            bytes_accessed=4 * ext * width + 4 * slab * width,
            transcendentals=slab * window * width // HEAD_DIM,
        ),
        name="attend",
    )(place, query, keys, values, even, odd, *sums, seg)


def gather_blocks(place, blocks, c_all):
    for r, c in enumerate(blocks):
        c_all[place[1] ^ r] = c[...]


def away_kernel(place, c0, c1, c2, c3, w, out, c_all, w_vmem, sem):
    share = w_vmem.shape[0]
    at = pl.multiple_of((1 - place[2]) * share, 32)
    copy = pltpu.make_async_copy(w.at[pl.ds(at, share), :], w_vmem, sem)
    copy.start()
    gather_blocks(place, (c0, c1, c2, c3), c_all)
    copy.wait()
    out[...] = out_terms(c_all, w_vmem).astype(jnp.bfloat16)


def out_terms(c_all, w_vmem):
    width = c_all.shape[2]
    total = None
    for b in range(SLAB):
        term = lax.dot_general(
            w_vmem[:, b * width:(b + 1) * width], c_all[b], (((1,), (1,)), ((), ())),
            preferred_element_type=jnp.float32,
        )
        total = term if total is None else total + term
    return total


def home_kernel(place, c0, c1, c2, c3, w, sent, residual, scale, out, c_all, w_vmem, sem):
    share = w_vmem.shape[0]
    at = pl.multiple_of(place[2] * share, 32)
    copy = pltpu.make_async_copy(w.at[pl.ds(at, share), :], w_vmem, sem)
    copy.start()
    gather_blocks(place, (c0, c1, c2, c3), c_all)
    copy.wait()
    total = out_terms(c_all, w_vmem) + sent[...].astype(jnp.float32)
    out[...] = (residual[...].astype(jnp.float32) + scale[...] * total).astype(jnp.bfloat16)


def out_call(kernel, place, blocks, w, share, extra):
    count, width = blocks[0].shape
    return pl.pallas_call(
        kernel,
        out_shape=jax.ShapeDtypeStruct((share, count), jnp.bfloat16),
        in_specs=[SMEM] + [VMEM] * 4 + [ANY] + [VMEM] * len(extra),
        out_specs=VMEM,
        scratch_shapes=[
            pltpu.VMEM((SLAB, count, width), jnp.bfloat16),
            pltpu.VMEM((share, SLAB * width), jnp.bfloat16),
            pltpu.SemaphoreType.DMA,
        ],
        compiler_params=pltpu.CompilerParams(vmem_limit_bytes=24 * MIB),
        cost_estimate=pl.CostEstimate(
            flops=2 * share * count * SLAB * width,
            bytes_accessed=2 * share * SLAB * width,
            transcendentals=0,
        ),
        name=kernel.__name__,
    )(place, *blocks, w, *extra)


def slab_plan(tokens, norm_gain, qkv_weight, q_gain, k_gain, out_weight, layer_scale, segment_ids):
    count = tokens.shape[0]
    seq, tp = lax.axis_index("seq"), lax.axis_index("tp")
    slabs = lax.axis_size("seq") // SLAB
    z, q = seq // SLAB, seq % SLAB
    place = jnp.stack([z, q, tp]).astype(jnp.int32)
    width = qkv_weight.shape[2] // SLAB
    full_width = qkv_weight.shape[2] * lax.axis_size("tp")

    by_kind = jnp.transpose(qkv_weight, (1, 0, 2))
    cut = [lax.dynamic_slice_in_dim(by_kind, (q ^ r) * width, width, 2) for r in range(SLAB)]
    got = [cut[0]] + [in_slab(cut[r], r) for r in range(1, SLAB)]
    placed = []
    for b in range(SLAB):
        piece = got[b]
        for other in range(1, SLAB):
            piece = jnp.where(q == other, got[b ^ other], piece)
        placed.append(piece)
    own = jnp.concatenate(placed, axis=1)
    first, pair = norm(place, tokens, norm_gain, slabs)

    own, first, pair = tied(own, first, pair)
    near, middle1 = even_pair(own), odd_pair(own)
    x2a = in_slab(first, 2)
    near, middle1, x2a, pair = tied(near, middle1, x2a, pair)
    end1, middle2 = even_pair(middle1), odd_pair(near)
    x2b = across(x2a)
    x1, x3a = in_slab(pair, 1), in_slab(x2a, 1)
    end1, middle2, x2b, x1, x3a, out_weight = tied(end1, middle2, x2b, x1, x3a, out_weight)
    end2 = even_pair(middle2)
    x3b = in_slab(x2b, 1)
    xs = (pair, x1, x2a, x2b, x3a, x3b)
    acc = early(place, xs, own, near, middle1, end1)
    all_out = jnp.transpose(lax.all_gather(out_weight, "seq", axis=1, tiled=True))

    gains = [lax.dynamic_slice_in_dim(g, q * width, width, 0)[None] for g in (q_gain, k_gain)]
    query, keys, values, squares, even, odd = late(place, xs, acc, middle2, end2, *gains)
    even, odd = even_pair(even), odd_pair(odd)
    slab_sum = squares
    for r in range(1, SLAB):
        slab_sum = slab_sum + in_slab(squares, r)
    sums = (
        slab_sum, across(slab_sum), even_pair(slab_sum), even_pair(slab_sum, 1),
        odd_pair(slab_sum), odd_pair(slab_sum, 1),
    )
    half = 2 * count
    outside = jnp.full((half,), -1, jnp.int32)
    seg = jnp.concatenate([outside, segment_ids, outside], axis=0)
    seg = lax.dynamic_slice_in_dim(seg, z * SLAB * count, SLAB * count + 2 * half, 0)
    seg = seg.astype(jnp.float32)[None]
    blocks = attend(full_width, place, query, keys, values, even, odd, sums, seg)
    blocks = [blocks[0]] + [in_slab(blocks[r], r) for r in range(1, SLAB)]

    share = layer_scale.shape[0]
    residual = jnp.transpose(lax.dynamic_slice_in_dim(tokens, tp * share, share, 1))
    sent = across(out_call(away_kernel, place, blocks, all_out, share, ()))
    mixed = out_call(
        home_kernel, place, blocks, all_out, share, (sent, residual, layer_scale[:, None])
    )
    return jnp.transpose(mixed)


def solution(mesh):
    def shards(*args):
        heads = args[2].shape[2] // HEAD_DIM
        slab = mesh.shape["seq"] == 16 and mesh.shape["tp"] == 2 and heads % SLAB == 0
        return (slab_plan if slab else row_plan)(*args)

    return jax.shard_map(
        shards,
        mesh=mesh,
        in_specs=(
            P("seq", None),
            P(),
            P("seq", None, "tp"),
            P("tp"),
            P("tp"),
            P("tp", "seq"),
            P("tp"),
            P(),
        ),
        out_specs=P("seq", "tp"),
        check_vma=False,
    )
```

```python
import functools

import jax
import jax.numpy as jnp
from jax import lax
from jax.experimental import pallas as pl
from jax.experimental.pallas import tpu as pltpu
from jax.sharding import PartitionSpec as P

HEAD_DIM = 128
SLAB = 4

eps = 1e-06
floor_score = -1e30


def passed_along(x, axis, by):
    size = lax.axis_size(axis)
    pairs = [(i, i + by) for i in range(size) if 0 <= i + by < size]
    return lax.ppermute(x, axis, pairs)


def masked_scores(query, keys, query_seg, key_seg):
    scores = jnp.einsum(
        "qhd,khd->hqk", query, keys, preferred_element_type=jnp.float32
    ) * HEAD_DIM ** (-0.5)
    mask = (query_seg[:, None] == key_seg[None, :])[None]
    return (jnp.where(mask, scores, floor_score), mask)


def row_plan(tokens, norm_gain, qkv_weight, q_gain, k_gain, out_weight, layer_scale, segment_ids):
    count = tokens.shape[0]
    source = tokens.astype(jnp.float32)
    normed = (
        source * lax.rsqrt(jnp.mean(source * source, axis=-1, keepdims=True) + eps) * norm_gain
    ).astype(jnp.bfloat16)
    local_width = qkv_weight.shape[2]
    heads = local_width // HEAD_DIM
    joined = jnp.einsum(
        "td,dch->tch",
        normed,
        lax.all_gather(qkv_weight, "seq", axis=0, tiled=True),
        preferred_element_type=jnp.float32,
    )
    query = joined[:, 0]
    keys = joined[:, 1]
    values = joined[:, 2]
    query_sq, key_sq = lax.psum(
        (jnp.sum(query * query, axis=-1), jnp.sum(keys * keys, axis=-1)), "tp"
    )
    full_width = local_width * lax.axis_size("tp")
    query_normed = (query * lax.rsqrt(query_sq / full_width + eps)[:, None] * q_gain).astype(
        jnp.bfloat16
    )
    key_normed = (keys * lax.rsqrt(key_sq / full_width + eps)[:, None] * k_gain).astype(
        jnp.bfloat16
    )
    paired = jnp.stack([key_normed, values.astype(jnp.bfloat16)], axis=1)
    pieces = []
    for offset in (2, 1, 0, -1, -2):
        if offset == 0:
            pieces.append(paired)
        else:
            pieces.append(passed_along(paired, "seq", offset))
    widened = jnp.concatenate(pieces, axis=0)
    position = lax.axis_index("seq")
    outside = jnp.full((2 * count,), -1, jnp.int32)
    seg_pad = jnp.concatenate([outside, segment_ids, outside], axis=0)
    key_seg = lax.dynamic_slice_in_dim(seg_pad, position * count, 5 * count, 0)
    query_seg = lax.dynamic_slice_in_dim(segment_ids, position * count, count, 0)
    query_heads = query_normed.reshape(count, heads, HEAD_DIM)
    key_heads = widened[:, 0].reshape(5 * count, heads, HEAD_DIM)
    value_heads = widened[:, 1].reshape(5 * count, heads, HEAD_DIM)
    scores, mask = masked_scores(query_heads, key_heads, query_seg, key_seg)
    peak = jnp.max(scores, axis=-1, keepdims=True)
    weights = jnp.where(mask, jnp.exp(scores - peak), 0.0)
    total = jnp.sum(weights, axis=-1)
    probs = weights.astype(jnp.bfloat16)
    summed = jnp.einsum("hqk,khd->qhd", probs, value_heads, preferred_element_type=jnp.float32)
    context = (
        (summed / jnp.transpose(total)[:, :, None]).reshape(count, local_width).astype(jnp.bfloat16)
    )
    terms = jnp.dot(
        context,
        lax.all_gather(out_weight, "seq", axis=1, tiled=True),
        preferred_element_type=jnp.float32,
    )
    projected = lax.psum_scatter(terms, "tp", scatter_dimension=1, tiled=True)
    share = layer_scale.shape[0]
    residual = lax.dynamic_slice_in_dim(source, lax.axis_index("tp") * share, share, 1)
    return (residual + layer_scale * projected).astype(jnp.bfloat16)


ANY = pl.BlockSpec(memory_space=pl.ANY)
VMEM = pl.BlockSpec(memory_space=pltpu.VMEM)
SMEM = pl.BlockSpec(memory_space=pltpu.SMEM)
HBM = pl.BlockSpec(memory_space=pltpu.HBM)
MIB = 1024 * 1024


def permuted(x, to):
    slabs, tps = lax.axis_size("seq") // SLAB, lax.axis_size("tp")
    pairs = []
    for i in range(slabs * SLAB * tps):
        z, q, y = to(i // (SLAB * tps), i // tps % SLAB, i % tps)
        pairs.append((i, (z * SLAB + q) * tps + y))
    return lax.ppermute(x, ("seq", "tp"), pairs)


def in_slab(x, flip):
    return permuted(x, lambda z, q, y: (z, q ^ flip, y))


def across(x):
    return permuted(x, lambda z, q, y: (z, q, 1 - y))


def even_of(z):
    return z ^ 1


def odd_of(z):
    return 3 - z if z in (1, 2) else z


def even_pair(x, flip=0):
    return permuted(x, lambda z, q, y: (even_of(z), q, y ^ flip))


def odd_pair(x, flip=0):
    return permuted(x, lambda z, q, y: (odd_of(z), q, y ^ flip))


def tied(*arrays):
    return lax.optimization_barrier(arrays)


def as_row(column):
    wide = jnp.broadcast_to(column, (column.shape[0], 128))
    return jnp.transpose(wide)[:8]


def as_column(row):
    return jnp.transpose(jnp.broadcast_to(row, (128, row.shape[1])))


def norm_kernel(place, tokens, gain, first, pair):
    half = pair.shape[2]
    part = tokens.shape[1] // pair.shape[1]
    blank = jnp.zeros((half, pair.shape[3] - part), jnp.bfloat16)
    for i in range(2):
        at = pl.multiple_of((place[2] ^ i) * half, half)
        source = tokens[pl.ds(at, half), :].astype(jnp.float32)
        mean = jnp.mean(source * source, axis=1, keepdims=True)
        normed = source * lax.rsqrt(mean + eps) * gain[...]
        for j in range(pair.shape[1]):
            chunk = normed[:, j * part:(j + 1) * part].astype(jnp.bfloat16)
            for out in (pair.at[i, j],) + ((first.at[j],) if i == 0 else ()):
                out[:, :part] = chunk
                out[:, part:] = blank


def norm(place, tokens, gain, slabs):
    count, depth = tokens.shape
    shape = (slabs, count // 2, pl.cdiv(depth // slabs, 128) * 128)
    return pl.pallas_call(
        norm_kernel,
        out_shape=(
            jax.ShapeDtypeStruct(shape, jnp.bfloat16),
            jax.ShapeDtypeStruct((2,) + shape, jnp.bfloat16),
        ),
        in_specs=[SMEM, VMEM, VMEM],
        out_specs=(VMEM, VMEM),
        compiler_params=pltpu.CompilerParams(vmem_limit_bytes=16 * MIB),
        name="norm",
    )(place, tokens, gain[None])


def far_slabs(z):
    return jnp.where(z < 2, 2, 1), jnp.where(z < 2, 3, 0)


def token_copies(xs, at, out, sems):
    copies = []
    for r in range(SLAB):
        for i in range(2):
            src = xs[r].at[i, at] if r < 2 else xs[2 * r - 2 + i].at[at]
            copies.append(pltpu.make_async_copy(src, out.at[r, i], sems.at[r, i]))
    for copy in copies:
        copy.start()
    return copies


def picked_copy(z, middle, end, out, sem, wait):
    inner = (z == 1) | (z == 2)

    @pl.when(inner)
    def _():
        copy = pltpu.make_async_copy(middle, out, sem)
        copy.wait() if wait else copy.start()

    @pl.when(jnp.logical_not(inner))
    def _():
        copy = pltpu.make_async_copy(end, out, sem)
        copy.wait() if wait else copy.start()


def chunk_of(x_all, r, rows):
    return x_all[r].reshape(-1, x_all.shape[-1])[:, :rows]


def early_kernel(place, xa, xb, xc, xd, xe, xf, own, near, middle, end, acc, x_all, w_all, x_sem, w_sem):
    z = place[0]
    xs = (xa, xb, xc, xd, xe, xf)
    near_copy = pltpu.make_async_copy(near, w_all.at[1], w_sem.at[1])
    own_copy = pltpu.make_async_copy(own, w_all.at[0], w_sem.at[0])
    own_copy.start()
    steps = (z, z ^ 1, far_slabs(z)[0])
    x_copies = [token_copies(xs, steps[0], x_all.at[0], x_sem.at[0])]
    near_copy.start()
    x_copies.append(token_copies(xs, steps[1], x_all.at[1], x_sem.at[1]))
    picked_copy(z, middle, end, w_all.at[2], w_sem.at[2], False)
    x_copies.append(token_copies(xs, steps[2], x_all.at[2], x_sem.at[2]))
    rows = own.shape[1]
    for step in range(3):
        if step < 2:
            (own_copy, near_copy)[step].wait()
        else:
            picked_copy(z, middle, end, w_all.at[2], w_sem.at[2], True)
        for copy in x_copies[step]:
            copy.wait()
        for r in range(SLAB):
            x = chunk_of(x_all.at[step], r, rows)
            for kind in range(own.shape[0]):
                term = jnp.dot(x, w_all[step, kind], preferred_element_type=jnp.float32)
                acc[kind, r] = term if step == 0 else acc[kind, r] + term


def early(place, xs, own, near, middle, end):
    kinds, rows, width = own.shape
    half, wide = xs[0].shape[2:]
    return pl.pallas_call(
        early_kernel,
        out_shape=jax.ShapeDtypeStruct((kinds, SLAB, 2 * half, width), jnp.float32),
        in_specs=[SMEM] + [HBM] * 10,
        out_specs=VMEM,
        scratch_shapes=[
            pltpu.VMEM((3, SLAB, 2, half, wide), jnp.bfloat16),
            pltpu.VMEM((3, kinds, rows, width), jnp.bfloat16),
            pltpu.SemaphoreType.DMA((3, SLAB, 2)),
            pltpu.SemaphoreType.DMA((3,)),
        ],
        compiler_params=pltpu.CompilerParams(vmem_limit_bytes=24 * MIB),
        cost_estimate=pl.CostEstimate(
            flops=12 * kinds * SLAB * half * rows * width,
            bytes_accessed=6 * kinds * rows * width + 12 * SLAB * half * rows,
            transcendentals=0,
        ),
        name="early",
    )(place, *xs, own, near, middle, end)


def late_kernel(
    place, xa, xb, xc, xd, xe, xf, acc, middle, end, q_gain, k_gain,
    query, keys, values, squares, even, odd, x_all, far, x_sem, w_sem,
):
    z, q, y = place[0], place[1], place[2]
    picked_copy(z, middle, end, far, w_sem, False)
    copies = token_copies((xa, xb, xc, xd, xe, xf), far_slabs(z)[1], x_all, x_sem)
    count = acc.shape[2]
    half = count // 2
    picked_copy(z, middle, end, far, w_sem, True)
    for r in range(SLAB):
        copies[2 * r].wait()
        copies[2 * r + 1].wait()
        x = chunk_of(x_all, r, far.shape[1])
        for kind in range(3):
            part = acc[kind, r] + jnp.dot(x, far[kind], preferred_element_type=jnp.float32)
            if kind < 2:
                summed = as_row(jnp.sum(part * part, axis=1, keepdims=True))
                part = part * (q_gain, k_gain)[kind][...]
            for i in range(2):
                at = pl.multiple_of((q ^ r) * count + (y ^ i) * half, half)
                rows = slice(i * half, (i + 1) * half)
                if kind == 0:
                    query[pl.ds(at, half), :] = part[rows]
                else:
                    low = part[rows].astype(jnp.bfloat16)
                    (keys, values)[kind - 1][pl.ds(at, half), :] = low
                if kind < 2:
                    squares[kind:kind + 1, pl.ds(at, half)] = summed[:1, rows]
    reach = even.shape[1]
    for out, at in ((even, 1 - z % 2), (odd, z % 2)):
        rows = pl.ds(pl.multiple_of(at * reach, reach), reach)
        out[0] = keys[rows, :]
        out[1] = values[rows, :]


def late(place, xs, acc, middle, end, q_gain, k_gain):
    kinds, rows, width = middle.shape
    count = acc.shape[2]
    slab = SLAB * count
    f32, bf16 = jnp.float32, jnp.bfloat16
    return pl.pallas_call(
        late_kernel,
        out_shape=(
            jax.ShapeDtypeStruct((slab, width), f32),
            jax.ShapeDtypeStruct((slab, width), bf16),
            jax.ShapeDtypeStruct((slab, width), bf16),
            jax.ShapeDtypeStruct((2, slab), f32),
            jax.ShapeDtypeStruct((2, 2 * count, width), bf16),
            jax.ShapeDtypeStruct((2, 2 * count, width), bf16),
        ),
        in_specs=[SMEM] + [HBM] * 6 + [VMEM] + [HBM] * 2 + [VMEM] * 2,
        out_specs=(VMEM,) * 6,
        scratch_shapes=[
            pltpu.VMEM((SLAB,) + xs[0].shape[:1] + xs[0].shape[2:], bf16),
            pltpu.VMEM((kinds, rows, width), bf16),
            pltpu.SemaphoreType.DMA((SLAB, 2)),
            pltpu.SemaphoreType.DMA,
        ],
        compiler_params=pltpu.CompilerParams(vmem_limit_bytes=24 * MIB),
        cost_estimate=pl.CostEstimate(
            flops=2 * kinds * slab * rows * width,
            bytes_accessed=2 * kinds * rows * width + 2 * slab * rows,
            transcendentals=0,
        ),
        name="late",
    )(place, *xs, acc, middle, end, q_gain, k_gain)


def attend_kernel(
    full_width, place, query, keys, values, even, odd, mine, mine_y, e, e_y, o, o_y, seg,
    o0, o1, o2, o3, k_all, v_all, scale_all,
):
    z, q = place[0], place[1]
    slab = query.shape[0]
    count = slab // SLAB
    half = even.shape[1]
    sums = mine[...] + mine_y[...]
    scale_all[:, pl.ds(half, slab)] = lax.rsqrt(sums / full_width + eps)
    k_all[pl.ds(half, slab), :] = keys[...]
    v_all[pl.ds(half, slab), :] = values[...]
    upper = half + slab

    def put(kv, a, b, high):
        at = upper if high else 0
        part = slice(0, half) if high else slice(slab - half, slab)
        k_all[pl.ds(at, half), :] = kv[0]
        v_all[pl.ds(at, half), :] = kv[1]
        scale_all[:, pl.ds(at, half)] = lax.rsqrt((a[:, part] + b[:, part]) / full_width + eps)

    @pl.when(z % 2 == 0)
    def _():
        put(even, e, e_y, True)
        put(odd, o, o_y, False)

    @pl.when(z % 2 == 1)
    def _():
        put(even, e, e_y, False)
        put(odd, o, o_y, True)

    window = count + 2 * half
    heads = query.shape[1] // HEAD_DIM
    for r, out in ((1, o1), (2, o2), (3, o3), (0, o0)):
        start = pl.multiple_of((q ^ r) * count, count)
        at_query = pl.multiple_of((q ^ r) * count + half, count)
        key_seg = seg[:, pl.ds(start, window)]
        query_seg = as_column(seg[:, pl.ds(at_query, count)])
        k_scale = scale_all[1:2, pl.ds(start, window)]
        q_scale = as_column(scale_all[0:1, pl.ds(at_query, count)])
        mask = jnp.tile(query_seg, (1, window // 128)) == key_seg
        for h in range(heads):
            cols = slice(h * HEAD_DIM, (h + 1) * HEAD_DIM)
            q_low = query[pl.ds(start, count), cols] * (q_scale * HEAD_DIM ** (-0.5))
            scores = lax.dot_general(
                q_low.astype(jnp.bfloat16), k_all[pl.ds(start, window), cols],
                (((1,), (1,)), ((), ())), preferred_element_type=jnp.float32,
            )
            scores = jnp.where(mask, scores * k_scale, floor_score)
            peak = jnp.max(scores, axis=1, keepdims=True)
            weights = jnp.exp(scores - peak)
            total = jnp.sum(weights, axis=1, keepdims=True)
            summed = jnp.dot(
                weights.astype(jnp.bfloat16), v_all[pl.ds(start, window), cols],
                preferred_element_type=jnp.float32,
            )
            out[:, cols] = (summed / total).astype(jnp.bfloat16)


def attend(full_width, place, query, keys, values, even, odd, sums, seg):
    slab, width = query.shape
    half = even.shape[1]
    count = slab // SLAB
    ext = slab + 2 * half
    bf16 = jnp.bfloat16
    block = jax.ShapeDtypeStruct((count, width), bf16)
    window = count + 2 * half
    return pl.pallas_call(
        functools.partial(attend_kernel, full_width),
        out_shape=(block,) * 4,
        in_specs=[SMEM] + [VMEM] * 12,
        out_specs=(VMEM,) * 4,
        scratch_shapes=[
            pltpu.VMEM((ext, width), bf16),
            pltpu.VMEM((ext, width), bf16),
            pltpu.VMEM((2, ext), jnp.float32),
        ],
        compiler_params=pltpu.CompilerParams(vmem_limit_bytes=24 * MIB),
        cost_estimate=pl.CostEstimate(
            flops=4 * slab * window * width,
            bytes_accessed=4 * ext * width + 4 * slab * width,
            transcendentals=slab * window * width // HEAD_DIM,
        ),
        name="attend",
    )(place, query, keys, values, even, odd, *sums, seg)


def out_kernel(
    place, c00, c01, c10, c11, c20, c21, c30, c31, wa0, wa1, wb0, wb1, wc0, wc1, wd0, wd1,
    residual, scale, out, c_all, w_all, total, sems,
):
    z, q, y = place[0], place[1], place[2]
    copies = []
    for r, pair in enumerate(((wa0, wa1), (wb0, wb1), (wc0, wc1), (wd0, wd1))):
        for j in range(2):
            copy = pltpu.make_async_copy(pair[j], w_all.at[r, j], sems.at[r, j])
            copy.start()
            copies.append(copy)
    width = c00.shape[1]
    for r, pair in enumerate(((c00, c01), (c10, c11), (c20, c21), (c30, c31))):
        at = pl.multiple_of((q ^ r) * width, width)
        for i in range(2):
            c_all[i, :, pl.ds(at, width)] = pair[i][...]
    rows = wa0.shape[1]
    home = z // 2 == y
    for r in range(SLAB):
        for j in range(2):
            copies[2 * r + j].wait()
            slab = jnp.where(home, z ^ j, far_slabs(z)[j]) % 2
            at = pl.multiple_of((slab * SLAB + (q ^ r)) * rows, 8)
            term = None
            for i in range(2):
                part = lax.dot_general(
                    w_all[r, j, i], c_all[i], (((1,), (1,)), ((), ())),
                    preferred_element_type=jnp.float32,
                )
                term = part if term is None else term + part
            total[pl.ds(at, rows), :] = term
    out[...] = (residual[...].astype(jnp.float32) + scale[...] * total[...]).astype(jnp.bfloat16)


def output(place, blocks, pieces, residual, scale):
    count, width = blocks[0].shape
    rows, depth = pieces[0].shape[1:]
    share = residual.shape[0]
    return pl.pallas_call(
        out_kernel,
        out_shape=jax.ShapeDtypeStruct((share, count), jnp.bfloat16),
        in_specs=[SMEM] + [VMEM] * 8 + [HBM] * 8 + [VMEM] * 2,
        out_specs=VMEM,
        scratch_shapes=[
            pltpu.VMEM((2, count, depth), jnp.bfloat16),
            pltpu.VMEM((SLAB, 2, 2, rows, depth), jnp.bfloat16),
            pltpu.VMEM((share, count), jnp.float32),
            pltpu.SemaphoreType.DMA((SLAB, 2)),
        ],
        compiler_params=pltpu.CompilerParams(vmem_limit_bytes=24 * MIB),
        cost_estimate=pl.CostEstimate(
            flops=4 * share * count * depth,
            bytes_accessed=4 * share * depth,
            transcendentals=0,
        ),
        name="output",
    )(place, *blocks, *pieces, residual, scale)


def slab_plan(tokens, norm_gain, qkv_weight, q_gain, k_gain, out_weight, layer_scale, segment_ids):
    count = tokens.shape[0]
    seq, tp = lax.axis_index("seq"), lax.axis_index("tp")
    slabs = lax.axis_size("seq") // SLAB
    z, q = seq // SLAB, seq % SLAB
    place = jnp.stack([z, q, tp]).astype(jnp.int32)
    width = qkv_weight.shape[2] // SLAB
    full_width = qkv_weight.shape[2] * lax.axis_size("tp")

    by_kind = jnp.transpose(qkv_weight, (1, 0, 2))
    cut = [lax.dynamic_slice_in_dim(by_kind, (q ^ r) * width, width, 2) for r in range(SLAB)]
    got = [cut[0]] + [in_slab(cut[r], r) for r in range(1, SLAB)]
    placed = []
    for b in range(SLAB):
        piece = got[b]
        for other in range(1, SLAB):
            piece = jnp.where(q == other, got[b ^ other], piece)
        placed.append(piece)
    own = jnp.concatenate(placed, axis=1)
    first, pair = norm(place, tokens, norm_gain, slabs)

    out_own = jnp.transpose(out_weight)
    out_near, out_mid1 = even_pair(out_own), odd_pair(out_own)
    out_end1, out_mid2 = even_pair(out_mid1), odd_pair(out_near)
    inner, home = (z == 1) | (z == 2), z // 2 == tp

    def over_tp(close, far):
        keep, give = jnp.where(home, close, far), jnp.where(home, far, close)
        return keep, across(give)

    own, first, pair, out_end1, out_mid2 = tied(own, first, pair, out_end1, out_mid2)
    near, middle1 = even_pair(own), odd_pair(own)
    x2a = in_slab(first, 2)
    out_end2 = even_pair(out_mid2)
    keep0, got0 = over_tp(out_own, jnp.where(inner, out_mid1, out_end1))
    near, middle1, x2a, pair, out_end2, keep0, got0 = tied(
        near, middle1, x2a, pair, out_end2, keep0, got0
    )
    end1, middle2 = even_pair(middle1), odd_pair(near)
    x2b = across(x2a)
    x1, x3a = in_slab(pair, 1), in_slab(x2a, 1)
    wa0 = jnp.stack([keep0, got0])
    wc0 = in_slab(wa0, 2)
    keep1, got1 = over_tp(out_near, jnp.where(inner, out_mid2, out_end2))
    end1, middle2, x2b, x1, x3a, wa0, wc0, keep1, got1 = tied(
        end1, middle2, x2b, x1, x3a, wa0, wc0, keep1, got1
    )
    end2 = even_pair(middle2)
    x3b = in_slab(x2b, 1)
    wa1 = jnp.stack([keep1, got1])
    wc1 = in_slab(wa1, 2)
    wb0, wd0 = in_slab(wa0, 1), in_slab(wc0, 1)
    xs = (pair, x1, x2a, x2b, x3a, x3b)
    acc = early(place, xs, own, near, middle1, end1)
    end2, acc, wc1 = tied(end2, acc, wc1)

    gains = [lax.dynamic_slice_in_dim(g, q * width, width, 0)[None] for g in (q_gain, k_gain)]
    query, keys, values, squares, even, odd = late(place, xs, acc, middle2, end2, *gains)
    slab_sum = squares
    for r in range(1, SLAB):
        slab_sum = slab_sum + in_slab(squares, r)
    sums = (
        slab_sum, across(slab_sum), even_pair(slab_sum), even_pair(slab_sum, 1),
        odd_pair(slab_sum), odd_pair(slab_sum, 1),
    )
    even, odd = even_pair(even), odd_pair(odd)
    wb1, wd1 = in_slab(wa1, 1), in_slab(wc1, 1)
    half = 2 * count
    outside = jnp.full((half,), -1, jnp.int32)
    seg = jnp.concatenate([outside, segment_ids, outside], axis=0)
    seg = lax.dynamic_slice_in_dim(seg, z * SLAB * count, SLAB * count + 2 * half, 0)
    seg = seg.astype(jnp.float32)[None]
    blocks = attend(full_width, place, query, keys, values, even, odd, sums, seg)
    spread = []
    for r in range(SLAB):
        for i in range(2):
            to = functools.partial(lambda r, i, z, q, y: (z, q ^ r, y ^ i), r, i)
            spread.append(permuted(blocks[r], to) if r or i else blocks[r])
    pieces = (wa0, wa1, wb0, wb1, wc0, wc1, wd0, wd1)

    share = layer_scale.shape[0]
    residual = jnp.transpose(lax.dynamic_slice_in_dim(tokens, tp * share, share, 1))
    return jnp.transpose(output(place, spread, pieces, residual, layer_scale[:, None]))


def solution(mesh):
    def shards(*args):
        heads = args[2].shape[2] // HEAD_DIM
        slab = mesh.shape["seq"] == 16 and mesh.shape["tp"] == 2 and heads % SLAB == 0
        return (slab_plan if slab else row_plan)(*args)

    return jax.shard_map(
        shards,
        mesh=mesh,
        in_specs=(
            P("seq", None),
            P(),
            P("seq", None, "tp"),
            P("tp"),
            P("tp"),
            P("tp", "seq"),
            P("tp"),
            P(),
        ),
        out_specs=P("seq", "tp"),
        check_vma=False,
    )
```

```python
import functools
import math

import jax
import jax.numpy as jnp
from jax import lax
from jax.experimental import pallas as pl
from jax.experimental.pallas import tpu as pltpu
from jax.sharding import PartitionSpec as P

HEAD_DIM = 128
SLAB = 4

eps = 1e-06
floor_score = -1e30


def passed_along(x, axis, by):
    size = lax.axis_size(axis)
    pairs = [(i, i + by) for i in range(size) if 0 <= i + by < size]
    return lax.ppermute(x, axis, pairs)


def masked_scores(query, keys, query_seg, key_seg):
    scores = jnp.einsum(
        "qhd,khd->hqk", query, keys, preferred_element_type=jnp.float32
    ) * HEAD_DIM ** (-0.5)
    mask = (query_seg[:, None] == key_seg[None, :])[None]
    return (jnp.where(mask, scores, floor_score), mask)


def row_plan(tokens, norm_gain, qkv_weight, q_gain, k_gain, out_weight, layer_scale, segment_ids):
    count = tokens.shape[0]
    source = tokens.astype(jnp.float32)
    normed = (
        source * lax.rsqrt(jnp.mean(source * source, axis=-1, keepdims=True) + eps) * norm_gain
    ).astype(jnp.bfloat16)
    local_width = qkv_weight.shape[2]
    heads = local_width // HEAD_DIM
    joined = jnp.einsum(
        "td,dch->tch",
        normed,
        lax.all_gather(qkv_weight, "seq", axis=0, tiled=True),
        preferred_element_type=jnp.float32,
    )
    query = joined[:, 0]
    keys = joined[:, 1]
    values = joined[:, 2]
    query_sq, key_sq = lax.psum(
        (jnp.sum(query * query, axis=-1), jnp.sum(keys * keys, axis=-1)), "tp"
    )
    full_width = local_width * lax.axis_size("tp")
    query_normed = (query * lax.rsqrt(query_sq / full_width + eps)[:, None] * q_gain).astype(
        jnp.bfloat16
    )
    key_normed = (keys * lax.rsqrt(key_sq / full_width + eps)[:, None] * k_gain).astype(
        jnp.bfloat16
    )
    paired = jnp.stack([key_normed, values.astype(jnp.bfloat16)], axis=1)
    pieces = []
    for offset in (2, 1, 0, -1, -2):
        if offset == 0:
            pieces.append(paired)
        else:
            pieces.append(passed_along(paired, "seq", offset))
    widened = jnp.concatenate(pieces, axis=0)
    position = lax.axis_index("seq")
    outside = jnp.full((2 * count,), -1, jnp.int32)
    seg_pad = jnp.concatenate([outside, segment_ids, outside], axis=0)
    key_seg = lax.dynamic_slice_in_dim(seg_pad, position * count, 5 * count, 0)
    query_seg = lax.dynamic_slice_in_dim(segment_ids, position * count, count, 0)
    query_heads = query_normed.reshape(count, heads, HEAD_DIM)
    key_heads = widened[:, 0].reshape(5 * count, heads, HEAD_DIM)
    value_heads = widened[:, 1].reshape(5 * count, heads, HEAD_DIM)
    scores, mask = masked_scores(query_heads, key_heads, query_seg, key_seg)
    peak = jnp.max(scores, axis=-1, keepdims=True)
    weights = jnp.where(mask, jnp.exp(scores - peak), 0.0)
    total = jnp.sum(weights, axis=-1)
    probs = weights.astype(jnp.bfloat16)
    summed = jnp.einsum("hqk,khd->qhd", probs, value_heads, preferred_element_type=jnp.float32)
    context = (
        (summed / jnp.transpose(total)[:, :, None]).reshape(count, local_width).astype(jnp.bfloat16)
    )
    terms = jnp.dot(
        context,
        lax.all_gather(out_weight, "seq", axis=1, tiled=True),
        preferred_element_type=jnp.float32,
    )
    projected = lax.psum_scatter(terms, "tp", scatter_dimension=1, tiled=True)
    share = layer_scale.shape[0]
    residual = lax.dynamic_slice_in_dim(source, lax.axis_index("tp") * share, share, 1)
    return (residual + layer_scale * projected).astype(jnp.bfloat16)


ANY = pl.BlockSpec(memory_space=pl.ANY)
VMEM = pl.BlockSpec(memory_space=pltpu.VMEM)
SMEM = pl.BlockSpec(memory_space=pltpu.SMEM)
HBM = pl.BlockSpec(memory_space=pltpu.HBM)
MIB = 1024 * 1024


def permuted(x, to):
    slabs, tps = lax.axis_size("seq") // SLAB, lax.axis_size("tp")
    pairs = []
    for i in range(slabs * SLAB * tps):
        z, q, y = to(i // (SLAB * tps), i // tps % SLAB, i % tps)
        pairs.append((i, (z * SLAB + q) * tps + y))
    return lax.ppermute(x, ("seq", "tp"), pairs)


def in_slab(x, flip):
    return permuted(x, lambda z, q, y: (z, q ^ flip, y))


def across(x):
    return permuted(x, lambda z, q, y: (z, q, 1 - y))


def even_pair(x):
    return permuted(x, lambda z, q, y: (z ^ 1, q, y))


def odd_pair(x):
    return permuted(x, lambda z, q, y: (3 - z if z in (1, 2) else z, q, y))


def z_line(x):
    size = lax.axis_size("seq")
    groups = [list(range(i, size, SLAB)) for i in range(SLAB)]
    return lax.all_gather(x, "seq", axis_index_groups=groups)


def tied(*arrays):
    return lax.optimization_barrier(arrays)


def as_row(column):
    wide = jnp.broadcast_to(column, (column.shape[0], 128))
    return jnp.transpose(wide)[:8]


def as_column(row):
    return jnp.transpose(jnp.broadcast_to(row, (128, row.shape[1])))


def norm_kernel(place, tokens, gain, first, pair):
    half = pair.shape[2]
    part = tokens.shape[1] // pair.shape[1]
    blank = jnp.zeros((half, pair.shape[3] - part), jnp.bfloat16)
    for i in range(2):
        at = pl.multiple_of((place[2] ^ i) * half, half)
        source = tokens[pl.ds(at, half), :].astype(jnp.float32)
        mean = jnp.mean(source * source, axis=1, keepdims=True)
        normed = source * lax.rsqrt(mean + eps) * gain[...]
        for j in range(pair.shape[1]):
            chunk = normed[:, j * part:(j + 1) * part].astype(jnp.bfloat16)
            for out in (pair.at[i, j],) + ((first.at[j],) if i == 0 else ()):
                out[:, :part] = chunk
                out[:, part:] = blank


def norm(place, tokens, gain, slabs):
    count, depth = tokens.shape
    shape = (slabs, count // 2, pl.cdiv(depth // slabs, 128) * 128)
    return pl.pallas_call(
        norm_kernel,
        out_shape=(
            jax.ShapeDtypeStruct(shape, jnp.bfloat16),
            jax.ShapeDtypeStruct((2,) + shape, jnp.bfloat16),
        ),
        in_specs=[SMEM, VMEM, VMEM],
        out_specs=(VMEM, VMEM),
        compiler_params=pltpu.CompilerParams(vmem_limit_bytes=16 * MIB),
        name="norm",
    )(place, tokens, gain[None])


def token_copies(xs, at, out, sems):
    copies = []
    for r in range(SLAB):
        for i in range(2):
            src = xs[r].at[i, at] if r < 2 else xs[2 * r - 2 + i].at[at]
            copies.append(pltpu.make_async_copy(src, out.at[r, i], sems.at[r, i]))
    return copies


def start(copies):
    for copy in copies:
        copy.start()


def wait(copies):
    for copy in copies:
        copy.wait()


def add_products(xs, w, x_all, w_all, acc, x_sem, w_sem):
    slabs, kinds, rows = w.shape[:3]
    steps = []
    for j in range(slabs):
        copies = [pltpu.make_async_copy(w.at[j], w_all.at[j], w_sem.at[j])]
        copies += token_copies(xs, j, x_all.at[j], x_sem.at[j])
        start(copies)
        steps.append(copies)
    for j in range(slabs):
        wait(steps[j])
        for r in range(SLAB):
            x = x_all[j, r].reshape(-1, x_all.shape[-1])[:, :rows]
            for kind in range(kinds):
                term = jnp.dot(x, w_all[j, kind], preferred_element_type=jnp.float32)
                acc[kind, r] = term if j == 0 else acc[kind, r] + term


def block_rows(place, r, i, count):
    half = count // 2
    at = (place[1] ^ r) * count + (place[2] ^ i) * half
    return pl.ds(pl.multiple_of(at, half), half), slice(i * half, (i + 1) * half)


def pair_rows(place, reach):
    z = place[0]
    return [pl.ds(pl.multiple_of(at * reach, reach), reach) for at in (1 - z % 2, z % 2)]


def query_key_kernel(
    place, xa, xb, xc, xd, xe, xf, w, both, squares, x_all, w_all, acc, both_all, x_sem, w_sem, sem,
):
    add_products((xa, xb, xc, xd, xe, xf), w, x_all, w_all, acc, x_sem, w_sem)
    for kind in range(2):
        for r in range(SLAB):
            part = acc[kind, r]
            summed = as_row(jnp.sum(part * part, axis=1, keepdims=True))
            for i in range(2):
                rows, cut = block_rows(place, r, i, part.shape[0])
                both_all[kind, rows, :] = part[cut]
                squares[kind:kind + 1, rows] = summed[:1, cut]
    copy = pltpu.make_async_copy(both_all, both, sem)
    copy.start()
    copy.wait()


def value_kernel(
    place, xa, xb, xc, xd, xe, xf, w, values, even, odd, x_all, w_all, acc, v_all, x_sem, w_sem, sem,
):
    add_products((xa, xb, xc, xd, xe, xf), w, x_all, w_all, acc, x_sem, w_sem)
    for r in range(SLAB):
        low = acc[0, r].astype(jnp.bfloat16)
        for i in range(2):
            rows, cut = block_rows(place, r, i, low.shape[0])
            v_all[rows, :] = low[cut]
    copy = pltpu.make_async_copy(v_all, values, sem)
    copy.start()
    for out, rows in zip((even, odd), pair_rows(place, even.shape[0])):
        out[...] = v_all[rows, :]
    copy.wait()


def project(kernel, out_shape, out_specs, held, place, xs, w):
    slabs, kinds, rows, width = w.shape
    half, wide = xs[0].shape[2:]
    slab = 2 * SLAB * half
    return pl.pallas_call(
        kernel,
        out_shape=out_shape,
        in_specs=[SMEM] + [HBM] * 7,
        out_specs=out_specs,
        scratch_shapes=[
            pltpu.VMEM((slabs, SLAB, 2, half, wide), jnp.bfloat16),
            pltpu.VMEM((slabs, kinds, rows, width), jnp.bfloat16),
            pltpu.VMEM((kinds, SLAB, 2 * half, width), jnp.float32),
            held,
            pltpu.SemaphoreType.DMA((slabs, SLAB, 2)),
            pltpu.SemaphoreType.DMA((slabs,)),
            pltpu.SemaphoreType.DMA,
        ],
        compiler_params=pltpu.CompilerParams(vmem_limit_bytes=28 * MIB),
        cost_estimate=pl.CostEstimate(
            flops=2 * kinds * slab * slabs * rows * width,
            bytes_accessed=2 * slabs * rows * (kinds * width + slab),
            transcendentals=0,
        ),
        name=kernel.__name__,
    )(place, *xs, w)


def norm_heads_kernel(
    full_width, place, both, mine, other, q_gain, k_gain, query, keys, even, odd,
    held, q_all, k_all, sems,
):
    load = pltpu.make_async_copy(both, held, sems.at[0])
    load.start()
    scale = lax.rsqrt((mine[...] + other[...]) / full_width + eps)
    count = 2 * 128
    load.wait()
    for kind, gain, out in ((1, k_gain, k_all), (0, q_gain, q_all)):
        for at in range(0, held.shape[1], count):
            column = as_column(scale[kind:kind + 1, at:at + count])
            column = jnp.tile(column, (1, held.shape[2] // 128))
            out[at:at + count, :] = (held[kind, at:at + count, :] * column * gain[...]).astype(
                jnp.bfloat16
            )
    stores = [
        pltpu.make_async_copy(k_all, keys, sems.at[1]),
        pltpu.make_async_copy(q_all, query, sems.at[2]),
    ]
    start(stores)
    for out, rows in zip((even, odd), pair_rows(place, even.shape[0])):
        out[...] = k_all[rows, :]
    wait(stores)


def norm_heads(full_width, place, both, mine, other, q_gain, k_gain, reach):
    slab, width = both.shape[1:]
    bf16 = jnp.bfloat16
    whole, part = jax.ShapeDtypeStruct((slab, width), bf16), jax.ShapeDtypeStruct((reach, width), bf16)
    return pl.pallas_call(
        functools.partial(norm_heads_kernel, full_width),
        out_shape=(whole, whole, part, part),
        in_specs=[SMEM, HBM] + [VMEM] * 4,
        out_specs=(HBM, HBM, VMEM, VMEM),
        scratch_shapes=[
            pltpu.VMEM((2, slab, width), jnp.float32),
            pltpu.VMEM((slab, width), bf16),
            pltpu.VMEM((slab, width), bf16),
            pltpu.SemaphoreType.DMA((3,)),
        ],
        compiler_params=pltpu.CompilerParams(vmem_limit_bytes=16 * MIB),
        name="norm_heads",
    )(place, both, mine, other, q_gain, k_gain)


def attend_kernel(
    place, query, keys, k_even, k_odd, values, v_even, v_odd, seg, o0, o1, o2, o3,
    q_all, k_all, v_all, sems,
):
    z, q = place[0], place[1]
    slab = query.shape[0]
    count = slab // SLAB
    half = k_even.shape[0]
    upper = half + slab
    even_at = pl.multiple_of(jnp.where(z % 2 == 0, upper, 0), half)
    odd_at = pl.multiple_of(jnp.where(z % 2 == 0, 0, upper), half)
    copies = [pltpu.make_async_copy(query, q_all, sems.at[0])]
    for k, (whole, even, odd, out) in enumerate(
        ((keys, k_even, k_odd, k_all), (values, v_even, v_odd, v_all))
    ):
        for n, (src, at) in enumerate(((whole, half), (even, even_at), (odd, odd_at))):
            dst = out.at[pl.ds(at, src.shape[0]), :]
            copies.append(pltpu.make_async_copy(src, dst, sems.at[1 + 3 * k + n]))
    start(copies)
    wait(copies)
    window = count + 2 * half
    heads = query.shape[1] // HEAD_DIM
    factor = HEAD_DIM ** (-0.5) * math.log2(math.e)
    for r, out in ((1, o1), (2, o2), (3, o3), (0, o0)):
        begin = pl.multiple_of((q ^ r) * count, count)
        at_query = pl.multiple_of((q ^ r) * count + half, count)
        key_seg = seg[:, pl.ds(begin, window)]
        query_seg = as_column(seg[:, pl.ds(at_query, count)])
        mask = jnp.tile(query_seg, (1, window // 128)) == key_seg
        for h in range(heads):
            cols = slice(h * HEAD_DIM, (h + 1) * HEAD_DIM)
            scores = lax.dot_general(
                q_all[pl.ds(begin, count), cols], k_all[pl.ds(begin, window), cols],
                (((1,), (1,)), ((), ())), preferred_element_type=jnp.float32,
            )
            scores = jnp.where(mask, scores, floor_score)
            peak = jnp.max(scores, axis=1, keepdims=True)
            weights = jnp.exp2((scores - peak) * factor)
            total = jnp.sum(weights, axis=1, keepdims=True)
            summed = jnp.dot(
                weights.astype(jnp.bfloat16), v_all[pl.ds(begin, window), cols],
                preferred_element_type=jnp.float32,
            )
            out[:, cols] = (summed / total).astype(jnp.bfloat16)


def attend(place, query, keys, k_even, k_odd, values, v_even, v_odd, seg):
    slab, width = query.shape
    half = k_even.shape[0]
    count = slab // SLAB
    ext = slab + 2 * half
    bf16 = jnp.bfloat16
    window = count + 2 * half
    return pl.pallas_call(
        attend_kernel,
        out_shape=(jax.ShapeDtypeStruct((count, width), bf16),) * 4,
        in_specs=[SMEM] + [HBM] * 7 + [VMEM],
        out_specs=(VMEM,) * 4,
        scratch_shapes=[
            pltpu.VMEM((slab, width), bf16),
            pltpu.VMEM((ext, width), bf16),
            pltpu.VMEM((ext, width), bf16),
            pltpu.SemaphoreType.DMA((7,)),
        ],
        compiler_params=pltpu.CompilerParams(vmem_limit_bytes=24 * MIB),
        cost_estimate=pl.CostEstimate(
            flops=4 * slab * window * width,
            bytes_accessed=4 * ext * width + 4 * slab * width,
            transcendentals=slab * window * width // HEAD_DIM,
        ),
        name="attend",
    )(place, query, keys, k_even, k_odd, values, v_even, v_odd, seg)


def out_kernel(
    place, c00, c01, c10, c11, c20, c21, c30, c31, wa, wb, wc, wd, residual, scale,
    out, c_all, w_all, total, sems,
):
    q = place[1]
    copies = []
    for r, w in enumerate((wa, wb, wc, wd)):
        copy = pltpu.make_async_copy(w, w_all.at[r], sems.at[r])
        copy.start()
        copies.append(copy)
    width = c00.shape[1]
    for r, pair in enumerate(((c00, c01), (c10, c11), (c20, c21), (c30, c31))):
        at = pl.multiple_of((q ^ r) * width, width)
        for i in range(2):
            c_all[i, :, pl.ds(at, width)] = pair[i][...]
    rows = wa.shape[2]
    for r in range(SLAB):
        copies[r].wait()
        for j in range(2):
            at = pl.multiple_of((j * SLAB + (q ^ r)) * rows, 8)
            term = None
            for i in range(2):
                part = lax.dot_general(
                    w_all[r, i, j], c_all[i], (((1,), (1,)), ((), ())),
                    preferred_element_type=jnp.float32,
                )
                term = part if term is None else term + part
            total[pl.ds(at, rows), :] = term
    out[...] = (residual[...].astype(jnp.float32) + scale[...] * total[...]).astype(jnp.bfloat16)


def output(place, blocks, pieces, residual, scale):
    count, width = blocks[0].shape
    rows, depth = pieces[0].shape[2:]
    share = residual.shape[0]
    return pl.pallas_call(
        out_kernel,
        out_shape=jax.ShapeDtypeStruct((share, count), jnp.bfloat16),
        in_specs=[SMEM] + [VMEM] * 8 + [HBM] * 4 + [VMEM] * 2,
        out_specs=VMEM,
        scratch_shapes=[
            pltpu.VMEM((2, count, depth), jnp.bfloat16),
            pltpu.VMEM((SLAB, 2, 2, rows, depth), jnp.bfloat16),
            pltpu.VMEM((share, count), jnp.float32),
            pltpu.SemaphoreType.DMA((SLAB,)),
        ],
        compiler_params=pltpu.CompilerParams(vmem_limit_bytes=24 * MIB),
        cost_estimate=pl.CostEstimate(
            flops=4 * share * count * depth,
            bytes_accessed=4 * share * depth,
            transcendentals=0,
        ),
        name="output",
    )(place, *blocks, *pieces, residual, scale)


def rows_of_slab(q, cut):
    got = [cut[0]] + [in_slab(cut[r], r) for r in range(1, SLAB)]
    placed = []
    for b in range(SLAB):
        piece = got[b]
        for other in range(1, SLAB):
            piece = jnp.where(q == other, got[b ^ other], piece)
        placed.append(piece)
    return jnp.concatenate(placed, axis=1)


def slab_plan(tokens, norm_gain, qkv_weight, q_gain, k_gain, out_weight, layer_scale, segment_ids):
    count = tokens.shape[0]
    seq, tp = lax.axis_index("seq"), lax.axis_index("tp")
    slabs = lax.axis_size("seq") // SLAB
    z, q = seq // SLAB, seq % SLAB
    place = jnp.stack([z, q, tp]).astype(jnp.int32)
    width = qkv_weight.shape[2] // SLAB
    full_width = qkv_weight.shape[2] * lax.axis_size("tp")
    slab, half = SLAB * count, 2 * count
    f32, bf16 = jnp.float32, jnp.bfloat16

    out_all = z_line(jnp.transpose(out_weight))

    by_kind = jnp.transpose(qkv_weight, (1, 0, 2))
    cut = [lax.dynamic_slice_in_dim(by_kind, (q ^ r) * width, width, 2) for r in range(SLAB)]
    own_qk = rows_of_slab(q, [c[:2] for c in cut])
    w_qk = z_line(own_qk)
    first, pair = norm(place, tokens, norm_gain, slabs)

    tied_cut = tied(own_qk, first, pair, *[c[2:] for c in cut])
    _, first, pair = tied_cut[:3]
    own_v = rows_of_slab(q, tied_cut[3:])
    w_v = z_line(tied(own_v, w_qk)[0])
    x2a = in_slab(first, 2)
    x1 = in_slab(pair, 1)
    own_v, x2a, x1 = tied(own_v, x2a, x1)
    x2b, x3a = across(x2a), in_slab(x2a, 1)
    x3b = in_slab(x2b, 1)
    xs = (pair, x1, x2a, x2b, x3a, x3b)

    close, far = out_all[:2], out_all[2:]
    close, far, x2b, x3a = tied(close, far, x2b, x3a)
    wa = jnp.stack(
        [jnp.where(tp == 0, close, far), across(jnp.where(tp == 0, far, close))]
    )
    wc = in_slab(wa, 2)
    pieces = (wa, in_slab(wa, 1), wc, in_slab(wc, 1))

    both, squares = project(
        query_key_kernel,
        (jax.ShapeDtypeStruct((2, slab, width), f32), jax.ShapeDtypeStruct((2, slab), f32)),
        (HBM, VMEM), pltpu.VMEM((2, slab, width), f32), place, xs, w_qk,
    )
    mine = squares
    for r in range(1, SLAB):
        mine = mine + in_slab(squares, r)
    gains = [lax.dynamic_slice_in_dim(g, q * width, width, 0)[None] for g in (q_gain, k_gain)]
    query, keys, k_even, k_odd = norm_heads(
        full_width, place, both, mine, across(mine), *gains, half
    )
    k_even, k_odd = even_pair(k_even), odd_pair(k_odd)

    values, v_even, v_odd = project(
        value_kernel,
        (
            jax.ShapeDtypeStruct((slab, width), bf16),
            jax.ShapeDtypeStruct((half, width), bf16),
            jax.ShapeDtypeStruct((half, width), bf16),
        ),
        (HBM, VMEM, VMEM), pltpu.VMEM((slab, width), bf16), place, xs, w_v,
    )
    v_even, v_odd = even_pair(v_even), odd_pair(v_odd)
    outside = jnp.full((half,), -1, jnp.int32)
    seg = jnp.concatenate([outside, segment_ids, outside], axis=0)
    seg = lax.dynamic_slice_in_dim(seg, z * slab, slab + 2 * half, 0).astype(f32)[None]
    blocks = attend(place, query, keys, k_even, k_odd, values, v_even, v_odd, seg)
    spread = []
    for r in range(SLAB):
        for i in range(2):
            to = functools.partial(lambda r, i, z, q, y: (z, q ^ r, y ^ i), r, i)
            spread.append(permuted(blocks[r], to) if r or i else blocks[r])

    share = layer_scale.shape[0]
    residual = jnp.transpose(lax.dynamic_slice_in_dim(tokens, tp * share, share, 1))
    return jnp.transpose(output(place, spread, pieces, residual, layer_scale[:, None]))


def solution(mesh):
    def shards(*args):
        heads = args[2].shape[2] // HEAD_DIM
        slab = mesh.shape["seq"] == 16 and mesh.shape["tp"] == 2 and heads % SLAB == 0
        return (slab_plan if slab else row_plan)(*args)

    return jax.shard_map(
        shards,
        mesh=mesh,
        in_specs=(
            P("seq", None),
            P(),
            P("seq", None, "tp"),
            P("tp"),
            P("tp"),
            P("tp", "seq"),
            P("tp"),
            P(),
        ),
        out_specs=P("seq", "tp"),
        check_vma=False,
    )
```

```python
import functools
import math

import jax
import jax.numpy as jnp
from jax import lax
from jax.experimental import pallas as pl
from jax.experimental.pallas import tpu as pltpu
from jax.sharding import PartitionSpec as P

HEAD_DIM = 128
SLAB = 4

eps = 1e-06
floor_score = -1e30


def passed_along(x, axis, by):
    size = lax.axis_size(axis)
    pairs = [(i, i + by) for i in range(size) if 0 <= i + by < size]
    return lax.ppermute(x, axis, pairs)


def masked_scores(query, keys, query_seg, key_seg):
    scores = jnp.einsum(
        "qhd,khd->hqk", query, keys, preferred_element_type=jnp.float32
    ) * HEAD_DIM ** (-0.5)
    mask = (query_seg[:, None] == key_seg[None, :])[None]
    return (jnp.where(mask, scores, floor_score), mask)


def row_plan(tokens, norm_gain, qkv_weight, q_gain, k_gain, out_weight, layer_scale, segment_ids):
    count = tokens.shape[0]
    source = tokens.astype(jnp.float32)
    normed = (
        source * lax.rsqrt(jnp.mean(source * source, axis=-1, keepdims=True) + eps) * norm_gain
    ).astype(jnp.bfloat16)
    local_width = qkv_weight.shape[2]
    heads = local_width // HEAD_DIM
    joined = jnp.einsum(
        "td,dch->tch",
        normed,
        lax.all_gather(qkv_weight, "seq", axis=0, tiled=True),
        preferred_element_type=jnp.float32,
    )
    query = joined[:, 0]
    keys = joined[:, 1]
    values = joined[:, 2]
    query_sq, key_sq = lax.psum(
        (jnp.sum(query * query, axis=-1), jnp.sum(keys * keys, axis=-1)), "tp"
    )
    full_width = local_width * lax.axis_size("tp")
    query_normed = (query * lax.rsqrt(query_sq / full_width + eps)[:, None] * q_gain).astype(
        jnp.bfloat16
    )
    key_normed = (keys * lax.rsqrt(key_sq / full_width + eps)[:, None] * k_gain).astype(
        jnp.bfloat16
    )
    paired = jnp.stack([key_normed, values.astype(jnp.bfloat16)], axis=1)
    pieces = []
    for offset in (2, 1, 0, -1, -2):
        if offset == 0:
            pieces.append(paired)
        else:
            pieces.append(passed_along(paired, "seq", offset))
    widened = jnp.concatenate(pieces, axis=0)
    position = lax.axis_index("seq")
    outside = jnp.full((2 * count,), -1, jnp.int32)
    seg_pad = jnp.concatenate([outside, segment_ids, outside], axis=0)
    key_seg = lax.dynamic_slice_in_dim(seg_pad, position * count, 5 * count, 0)
    query_seg = lax.dynamic_slice_in_dim(segment_ids, position * count, count, 0)
    query_heads = query_normed.reshape(count, heads, HEAD_DIM)
    key_heads = widened[:, 0].reshape(5 * count, heads, HEAD_DIM)
    value_heads = widened[:, 1].reshape(5 * count, heads, HEAD_DIM)
    scores, mask = masked_scores(query_heads, key_heads, query_seg, key_seg)
    peak = jnp.max(scores, axis=-1, keepdims=True)
    weights = jnp.where(mask, jnp.exp(scores - peak), 0.0)
    total = jnp.sum(weights, axis=-1)
    probs = weights.astype(jnp.bfloat16)
    summed = jnp.einsum("hqk,khd->qhd", probs, value_heads, preferred_element_type=jnp.float32)
    context = (
        (summed / jnp.transpose(total)[:, :, None]).reshape(count, local_width).astype(jnp.bfloat16)
    )
    terms = jnp.dot(
        context,
        lax.all_gather(out_weight, "seq", axis=1, tiled=True),
        preferred_element_type=jnp.float32,
    )
    projected = lax.psum_scatter(terms, "tp", scatter_dimension=1, tiled=True)
    share = layer_scale.shape[0]
    residual = lax.dynamic_slice_in_dim(source, lax.axis_index("tp") * share, share, 1)
    return (residual + layer_scale * projected).astype(jnp.bfloat16)


ANY = pl.BlockSpec(memory_space=pl.ANY)
VMEM = pl.BlockSpec(memory_space=pltpu.VMEM)
SMEM = pl.BlockSpec(memory_space=pltpu.SMEM)
HBM = pl.BlockSpec(memory_space=pltpu.HBM)
KERNEL_VMEM = 60 * 1024 * 1024


def permuted(x, to):
    slabs, tps = lax.axis_size("seq") // SLAB, lax.axis_size("tp")
    pairs = []
    for i in range(slabs * SLAB * tps):
        z, q, y = to(i // (SLAB * tps), i // tps % SLAB, i % tps)
        pairs.append((i, (z * SLAB + q) * tps + y))
    return lax.ppermute(x, ("seq", "tp"), pairs)


def in_slab(x, flip):
    return permuted(x, lambda z, q, y: (z, q ^ flip, y))


def across(x):
    return permuted(x, lambda z, q, y: (z, q, 1 - y))


def even_pair(x):
    return permuted(x, lambda z, q, y: (z ^ 1, q, y))


def odd_pair(x):
    return permuted(x, lambda z, q, y: (3 - z if z in (1, 2) else z, q, y))


def z_line(x):
    size = lax.axis_size("seq")
    groups = [list(range(i, size, SLAB)) for i in range(SLAB)]
    return lax.all_gather(x, "seq", axis_index_groups=groups)


def tied(*arrays):
    return lax.optimization_barrier(arrays)


def as_row(column):
    wide = jnp.broadcast_to(column, (column.shape[0], 128))
    return jnp.transpose(wide)[:8]


def as_column(row):
    return jnp.transpose(jnp.broadcast_to(row, (128, row.shape[1])))


def norm_kernel(place, tokens, gain, first, pair):
    half = pair.shape[2]
    part = tokens.shape[1] // pair.shape[1]
    blank = jnp.zeros((half, pair.shape[3] - part), jnp.bfloat16)
    for i in range(2):
        at = pl.multiple_of((place[2] ^ i) * half, half)
        source = tokens[pl.ds(at, half), :].astype(jnp.float32)
        mean = jnp.mean(source * source, axis=1, keepdims=True)
        normed = source * lax.rsqrt(mean + eps) * gain[...]
        for j in range(pair.shape[1]):
            chunk = normed[:, j * part:(j + 1) * part].astype(jnp.bfloat16)
            for out in (pair.at[i, j],) + ((first.at[j],) if i == 0 else ()):
                out[:, :part] = chunk
                out[:, part:] = blank


def norm(place, tokens, gain, slabs):
    count, depth = tokens.shape
    shape = (slabs, count // 2, pl.cdiv(depth // slabs, 128) * 128)
    return pl.pallas_call(
        norm_kernel,
        out_shape=(
            jax.ShapeDtypeStruct(shape, jnp.bfloat16),
            jax.ShapeDtypeStruct((2,) + shape, jnp.bfloat16),
        ),
        in_specs=[SMEM, VMEM, VMEM],
        out_specs=(VMEM, VMEM),
        compiler_params=pltpu.CompilerParams(vmem_limit_bytes=KERNEL_VMEM),
        name="norm",
    )(place, tokens, gain[None])


def token_copies(xs, at, out, sems):
    copies = []
    for r in range(SLAB):
        for i in range(2):
            src = xs[r].at[i, at] if r < 2 else xs[2 * r - 2 + i].at[at]
            copies.append(pltpu.make_async_copy(src, out.at[r, i], sems.at[r, i]))
    return copies


def start(copies):
    for copy in copies:
        copy.start()


def wait(copies):
    for copy in copies:
        copy.wait()


def add_products(xs, w, x_all, w_all, acc, x_sem, w_sem):
    slabs, kinds, rows = w.shape[:3]
    steps = []
    for j in range(slabs):
        copies = [pltpu.make_async_copy(w.at[j], w_all.at[j], w_sem.at[j])]
        copies += token_copies(xs, j, x_all.at[j], x_sem.at[j])
        start(copies)
        steps.append(copies)
    for j in range(slabs):
        wait(steps[j])
        for r in range(SLAB):
            x = x_all[j, r].reshape(-1, x_all.shape[-1])[:, :rows]
            for kind in range(kinds):
                term = jnp.dot(x, w_all[j, kind], preferred_element_type=jnp.float32)
                acc[kind, r] = term if j == 0 else acc[kind, r] + term


def block_rows(place, r, i, count):
    half = count // 2
    at = (place[1] ^ r) * count + (place[2] ^ i) * half
    return pl.ds(pl.multiple_of(at, half), half), slice(i * half, (i + 1) * half)


def pair_rows(place, reach):
    z = place[0]
    return [pl.ds(pl.multiple_of(at * reach, reach), reach) for at in (1 - z % 2, z % 2)]


def query_key_kernel(
    place, xa, xb, xc, xd, xe, xf, w, both, squares, x_all, w_all, acc, both_all, x_sem, w_sem, sem,
):
    add_products((xa, xb, xc, xd, xe, xf), w, x_all, w_all, acc, x_sem, w_sem)
    for kind in range(2):
        for r in range(SLAB):
            part = acc[kind, r]
            summed = as_row(jnp.sum(part * part, axis=1, keepdims=True))
            for i in range(2):
                rows, cut = block_rows(place, r, i, part.shape[0])
                both_all[kind, rows, :] = part[cut]
                squares[kind:kind + 1, rows] = summed[:1, cut]
    copy = pltpu.make_async_copy(both_all, both, sem)
    copy.start()
    copy.wait()


def value_kernel(
    place, xa, xb, xc, xd, xe, xf, w, values, even, odd, x_all, w_all, acc, v_all, x_sem, w_sem, sem,
):
    add_products((xa, xb, xc, xd, xe, xf), w, x_all, w_all, acc, x_sem, w_sem)
    for r in range(SLAB):
        low = acc[0, r].astype(jnp.bfloat16)
        for i in range(2):
            rows, cut = block_rows(place, r, i, low.shape[0])
            v_all[rows, :] = low[cut]
    copy = pltpu.make_async_copy(v_all, values, sem)
    copy.start()
    for out, rows in zip((even, odd), pair_rows(place, even.shape[0])):
        out[...] = v_all[rows, :]
    copy.wait()


def project(kernel, out_shape, out_specs, held, place, xs, w):
    slabs, kinds, rows, width = w.shape
    half, wide = xs[0].shape[2:]
    slab = 2 * SLAB * half
    return pl.pallas_call(
        kernel,
        out_shape=out_shape,
        in_specs=[SMEM] + [HBM] * 7,
        out_specs=out_specs,
        scratch_shapes=[
            pltpu.VMEM((slabs, SLAB, 2, half, wide), jnp.bfloat16),
            pltpu.VMEM((slabs, kinds, rows, width), jnp.bfloat16),
            pltpu.VMEM((kinds, SLAB, 2 * half, width), jnp.float32),
            held,
            pltpu.SemaphoreType.DMA((slabs, SLAB, 2)),
            pltpu.SemaphoreType.DMA((slabs,)),
            pltpu.SemaphoreType.DMA,
        ],
        compiler_params=pltpu.CompilerParams(vmem_limit_bytes=KERNEL_VMEM),
        cost_estimate=pl.CostEstimate(
            flops=2 * kinds * slab * slabs * rows * width,
            bytes_accessed=2 * slabs * rows * (kinds * width + slab),
            transcendentals=0,
        ),
        name=kernel.__name__,
    )(place, *xs, w)


def norm_heads_kernel(
    full_width, place, both, mine, other, q_gain, k_gain, query, keys, even, odd,
    held, q_all, k_all, sems,
):
    load = pltpu.make_async_copy(both, held, sems.at[0])
    load.start()
    scale = lax.rsqrt((mine[...] + other[...]) / full_width + eps)
    count = 2 * 128
    load.wait()
    for kind, gain, out in ((1, k_gain, k_all), (0, q_gain, q_all)):
        for at in range(0, held.shape[1], count):
            column = as_column(scale[kind:kind + 1, at:at + count])
            column = jnp.tile(column, (1, held.shape[2] // 128))
            out[at:at + count, :] = (held[kind, at:at + count, :] * column * gain[...]).astype(
                jnp.bfloat16
            )
    stores = [
        pltpu.make_async_copy(k_all, keys, sems.at[1]),
        pltpu.make_async_copy(q_all, query, sems.at[2]),
    ]
    start(stores)
    for out, rows in zip((even, odd), pair_rows(place, even.shape[0])):
        out[...] = k_all[rows, :]
    wait(stores)


def norm_heads(full_width, place, both, mine, other, q_gain, k_gain, reach):
    slab, width = both.shape[1:]
    bf16 = jnp.bfloat16
    whole, part = jax.ShapeDtypeStruct((slab, width), bf16), jax.ShapeDtypeStruct((reach, width), bf16)
    return pl.pallas_call(
        functools.partial(norm_heads_kernel, full_width),
        out_shape=(whole, whole, part, part),
        in_specs=[SMEM, HBM] + [VMEM] * 4,
        out_specs=(HBM, HBM, VMEM, VMEM),
        scratch_shapes=[
            pltpu.VMEM((2, slab, width), jnp.float32),
            pltpu.VMEM((slab, width), bf16),
            pltpu.VMEM((slab, width), bf16),
            pltpu.SemaphoreType.DMA((3,)),
        ],
        compiler_params=pltpu.CompilerParams(vmem_limit_bytes=KERNEL_VMEM),
        name="norm_heads",
    )(place, both, mine, other, q_gain, k_gain)


def attend_kernel(
    place, query, keys, k_even, k_odd, values, v_even, v_odd, seg, o0, o1, o2, o3,
    q_all, k_all, v_all, sems,
):
    z, q = place[0], place[1]
    slab = query.shape[0]
    count = slab // SLAB
    half = k_even.shape[0]
    upper = half + slab
    even_at = pl.multiple_of(jnp.where(z % 2 == 0, upper, 0), half)
    odd_at = pl.multiple_of(jnp.where(z % 2 == 0, 0, upper), half)
    copies = [pltpu.make_async_copy(query, q_all, sems.at[0])]
    for k, (whole, even, odd, out) in enumerate(
        ((keys, k_even, k_odd, k_all), (values, v_even, v_odd, v_all))
    ):
        for n, (src, at) in enumerate(((whole, half), (even, even_at), (odd, odd_at))):
            dst = out.at[pl.ds(at, src.shape[0]), :]
            copies.append(pltpu.make_async_copy(src, dst, sems.at[1 + 3 * k + n]))
    start(copies)
    wait(copies)
    window = count + 2 * half
    heads = query.shape[1] // HEAD_DIM
    factor = HEAD_DIM ** (-0.5) * math.log2(math.e)
    for r, out in ((1, o1), (2, o2), (3, o3), (0, o0)):
        begin = pl.multiple_of((q ^ r) * count, count)
        at_query = pl.multiple_of((q ^ r) * count + half, count)
        key_seg = seg[:, pl.ds(begin, window)]
        query_seg = as_column(seg[:, pl.ds(at_query, count)])
        mask = jnp.tile(query_seg, (1, window // 128)) == key_seg
        for h in range(heads):
            cols = slice(h * HEAD_DIM, (h + 1) * HEAD_DIM)
            scores = lax.dot_general(
                q_all[pl.ds(begin, count), cols], k_all[pl.ds(begin, window), cols],
                (((1,), (1,)), ((), ())), preferred_element_type=jnp.float32,
            )
            scores = jnp.where(mask, scores, floor_score)
            peak = jnp.max(scores, axis=1, keepdims=True)
            weights = jnp.exp2((scores - peak) * factor)
            total = jnp.sum(weights, axis=1, keepdims=True)
            summed = jnp.dot(
                weights.astype(jnp.bfloat16), v_all[pl.ds(begin, window), cols],
                preferred_element_type=jnp.float32,
            )
            out[:, cols] = (summed / total).astype(jnp.bfloat16)


def attend(place, query, keys, k_even, k_odd, values, v_even, v_odd, seg):
    slab, width = query.shape
    half = k_even.shape[0]
    count = slab // SLAB
    ext = slab + 2 * half
    bf16 = jnp.bfloat16
    window = count + 2 * half
    return pl.pallas_call(
        attend_kernel,
        out_shape=(jax.ShapeDtypeStruct((count, width), bf16),) * 4,
        in_specs=[SMEM] + [HBM] * 7 + [VMEM],
        out_specs=(VMEM,) * 4,
        scratch_shapes=[
            pltpu.VMEM((slab, width), bf16),
            pltpu.VMEM((ext, width), bf16),
            pltpu.VMEM((ext, width), bf16),
            pltpu.SemaphoreType.DMA((7,)),
        ],
        compiler_params=pltpu.CompilerParams(vmem_limit_bytes=KERNEL_VMEM),
        cost_estimate=pl.CostEstimate(
            flops=4 * slab * window * width,
            bytes_accessed=4 * ext * width + 4 * slab * width,
            transcendentals=slab * window * width // HEAD_DIM,
        ),
        name="attend",
    )(place, query, keys, k_even, k_odd, values, v_even, v_odd, seg)


def out_kernel(
    place, c00, c01, c10, c11, c20, c21, c30, c31, wa, wb, wc, wd, residual, scale,
    out, c_all, w_all, total, c_sem, w_sem,
):
    z, q, y = place[0], place[1], place[2]
    width = c00.shape[1]
    c_copies = []
    for r, pair in enumerate(((c00, c01), (c10, c11), (c20, c21), (c30, c31))):
        at = pl.multiple_of((q ^ r) * width, width)
        for i in range(2):
            dst = c_all.at[i, :, pl.ds(at, width)]
            c_copies.append(pltpu.make_async_copy(pair[i], dst, c_sem.at[r, i]))
    start(c_copies)
    w_copies = [
        pltpu.make_async_copy(w, w_all.at[r], w_sem.at[r]) for r, w in enumerate((wa, wb, wc, wd))
    ]
    start(w_copies)
    column = as_column(scale[...])[:out.shape[0]]
    column = jnp.tile(column, (1, out.shape[1] // 128))
    wait(c_copies)
    rows = wa.shape[2]
    for r in range(SLAB):
        w_copies[r].wait()
        for j in range(2):
            slab = jnp.where(z // 2 == y, (z % 2) ^ j, jnp.where(z < 2, j, 1 - j))
            at = pl.multiple_of((slab * SLAB + (q ^ r)) * rows, 8)
            term = None
            for i in range(2):
                part = lax.dot_general(
                    w_all[r, i, j], c_all[i], (((1,), (1,)), ((), ())),
                    preferred_element_type=jnp.float32,
                )
                term = part if term is None else term + part
            total[pl.ds(at, rows), :] = term
    out[...] = (residual[...].astype(jnp.float32) + column * total[...]).astype(jnp.bfloat16)


def output(place, blocks, pieces, residual, scale):
    count, width = blocks[0].shape
    rows, depth = pieces[0].shape[2:]
    share = residual.shape[0]
    scale = jnp.pad(scale, (0, -share % 128))[None]
    return pl.pallas_call(
        out_kernel,
        out_shape=jax.ShapeDtypeStruct((share, count), jnp.bfloat16),
        in_specs=[SMEM] + [HBM] * 12 + [VMEM] * 2,
        out_specs=VMEM,
        scratch_shapes=[
            pltpu.VMEM((2, count, depth), jnp.bfloat16),
            pltpu.VMEM((SLAB, 2, 2, rows, depth), jnp.bfloat16),
            pltpu.VMEM((share, count), jnp.float32),
            pltpu.SemaphoreType.DMA((SLAB, 2)),
            pltpu.SemaphoreType.DMA((SLAB,)),
        ],
        compiler_params=pltpu.CompilerParams(vmem_limit_bytes=KERNEL_VMEM),
        cost_estimate=pl.CostEstimate(
            flops=4 * share * count * depth,
            bytes_accessed=4 * share * depth,
            transcendentals=0,
        ),
        name="output",
    )(place, *blocks, *pieces, residual, scale)


def rows_of_slab(q, cut):
    got = [cut[0]] + [in_slab(cut[r], r) for r in range(1, SLAB)]
    placed = []
    for b in range(SLAB):
        piece = got[b]
        for other in range(1, SLAB):
            piece = jnp.where(q == other, got[b ^ other], piece)
        placed.append(piece)
    return jnp.concatenate(placed, axis=1)


def slab_plan(tokens, norm_gain, qkv_weight, q_gain, k_gain, out_weight, layer_scale, segment_ids):
    count = tokens.shape[0]
    seq, tp = lax.axis_index("seq"), lax.axis_index("tp")
    slabs = lax.axis_size("seq") // SLAB
    z, q = seq // SLAB, seq % SLAB
    place = jnp.stack([z, q, tp]).astype(jnp.int32)
    width = qkv_weight.shape[2] // SLAB
    full_width = qkv_weight.shape[2] * lax.axis_size("tp")
    slab, half = SLAB * count, 2 * count
    f32, bf16 = jnp.float32, jnp.bfloat16

    out_own = jnp.transpose(out_weight)
    out_near, out_mid1 = even_pair(out_own), odd_pair(out_own)
    out_end1, out_mid2 = even_pair(out_mid1), odd_pair(out_near)
    out_end2 = even_pair(out_mid2)
    inner, home = (z == 1) | (z == 2), z // 2 == tp
    close = jnp.stack([out_own, out_near])
    far = jnp.stack(
        [jnp.where(inner, out_mid1, out_end1), jnp.where(inner, out_mid2, out_end2)]
    )

    by_kind = jnp.transpose(qkv_weight, (1, 0, 2))
    cut = [lax.dynamic_slice_in_dim(by_kind, (q ^ r) * width, width, 2) for r in range(SLAB)]
    own_qk = rows_of_slab(q, [c[:2] for c in cut])
    w_qk = z_line(own_qk)
    first, pair = norm(place, tokens, norm_gain, slabs)

    tied_cut = tied(own_qk, first, pair, *[c[2:] for c in cut])
    _, first, pair = tied_cut[:3]
    own_v = rows_of_slab(q, tied_cut[3:])
    w_v = z_line(own_v)
    x2a = in_slab(first, 2)
    x1 = in_slab(pair, 1)
    own_v, x2a, x1 = tied(own_v, x2a, x1)
    x2b, x3a = across(x2a), in_slab(x2a, 1)
    x3b = in_slab(x2b, 1)

    wa = jnp.stack([jnp.where(home, close, far), across(jnp.where(home, far, close))])
    wc = in_slab(wa, 2)
    pieces = (wa, in_slab(wa, 1), wc, in_slab(wc, 1))

    w_qk, x3b, *pieces = tied(w_qk, x3b, *pieces)
    xs = (pair, x1, x2a, x2b, x3a, x3b)
    both, squares = project(
        query_key_kernel,
        (jax.ShapeDtypeStruct((2, slab, width), f32), jax.ShapeDtypeStruct((2, slab), f32)),
        (HBM, VMEM), pltpu.VMEM((2, slab, width), f32), place, xs, w_qk,
    )
    mine = squares
    for r in range(1, SLAB):
        mine = mine + in_slab(squares, r)
    gains = [lax.dynamic_slice_in_dim(g, q * width, width, 0)[None] for g in (q_gain, k_gain)]
    query, keys, k_even, k_odd = norm_heads(
        full_width, place, both, mine, across(mine), *gains, half
    )
    k_even, k_odd = even_pair(k_even), odd_pair(k_odd)

    values, v_even, v_odd = project(
        value_kernel,
        (
            jax.ShapeDtypeStruct((slab, width), bf16),
            jax.ShapeDtypeStruct((half, width), bf16),
            jax.ShapeDtypeStruct((half, width), bf16),
        ),
        (HBM, VMEM, VMEM), pltpu.VMEM((slab, width), bf16), place, xs, w_v,
    )
    v_even, v_odd = even_pair(v_even), odd_pair(v_odd)
    outside = jnp.full((half,), -1, jnp.int32)
    seg = jnp.concatenate([outside, segment_ids, outside], axis=0)
    seg = lax.dynamic_slice_in_dim(seg, z * slab, slab + 2 * half, 0).astype(f32)[None]
    blocks = attend(place, query, keys, k_even, k_odd, values, v_even, v_odd, seg)
    spread = []
    for r in range(SLAB):
        for i in range(2):
            to = functools.partial(lambda r, i, z, q, y: (z, q ^ r, y ^ i), r, i)
            spread.append(permuted(blocks[r], to) if r or i else blocks[r])

    share = layer_scale.shape[0]
    residual = jnp.transpose(lax.dynamic_slice_in_dim(tokens, tp * share, share, 1))
    return jnp.transpose(output(place, spread, pieces, residual, layer_scale))


def solution(mesh):
    def shards(*args):
        heads = args[2].shape[2] // HEAD_DIM
        slab = mesh.shape["seq"] == 16 and mesh.shape["tp"] == 2 and heads % SLAB == 0
        return (slab_plan if slab else row_plan)(*args)

    return jax.shard_map(
        shards,
        mesh=mesh,
        in_specs=(
            P("seq", None),
            P(),
            P("seq", None, "tp"),
            P("tp"),
            P("tp"),
            P("tp", "seq"),
            P("tp"),
            P(),
        ),
        out_specs=P("seq", "tp"),
        check_vma=False,
    )
```

```python
import functools
import math

import jax
import jax.numpy as jnp
from jax import lax
from jax.experimental import pallas as pl
from jax.experimental.pallas import tpu as pltpu
from jax.sharding import PartitionSpec as P

HEAD_DIM = 128
SLAB = 4

eps = 1e-06
floor_score = -1e30


def passed_along(x, axis, by):
    size = lax.axis_size(axis)
    pairs = [(i, i + by) for i in range(size) if 0 <= i + by < size]
    return lax.ppermute(x, axis, pairs)


def masked_scores(query, keys, query_seg, key_seg):
    scores = jnp.einsum(
        "qhd,khd->hqk", query, keys, preferred_element_type=jnp.float32
    ) * HEAD_DIM ** (-0.5)
    mask = (query_seg[:, None] == key_seg[None, :])[None]
    return (jnp.where(mask, scores, floor_score), mask)


def row_plan(tokens, norm_gain, qkv_weight, q_gain, k_gain, out_weight, layer_scale, segment_ids):
    count = tokens.shape[0]
    source = tokens.astype(jnp.float32)
    normed = (
        source * lax.rsqrt(jnp.mean(source * source, axis=-1, keepdims=True) + eps) * norm_gain
    ).astype(jnp.bfloat16)
    local_width = qkv_weight.shape[2]
    heads = local_width // HEAD_DIM
    joined = jnp.einsum(
        "td,dch->tch",
        normed,
        lax.all_gather(qkv_weight, "seq", axis=0, tiled=True),
        preferred_element_type=jnp.float32,
    )
    query = joined[:, 0]
    keys = joined[:, 1]
    values = joined[:, 2]
    query_sq, key_sq = lax.psum(
        (jnp.sum(query * query, axis=-1), jnp.sum(keys * keys, axis=-1)), "tp"
    )
    full_width = local_width * lax.axis_size("tp")
    query_normed = (query * lax.rsqrt(query_sq / full_width + eps)[:, None] * q_gain).astype(
        jnp.bfloat16
    )
    key_normed = (keys * lax.rsqrt(key_sq / full_width + eps)[:, None] * k_gain).astype(
        jnp.bfloat16
    )
    paired = jnp.stack([key_normed, values.astype(jnp.bfloat16)], axis=1)
    pieces = []
    for offset in (2, 1, 0, -1, -2):
        if offset == 0:
            pieces.append(paired)
        else:
            pieces.append(passed_along(paired, "seq", offset))
    widened = jnp.concatenate(pieces, axis=0)
    position = lax.axis_index("seq")
    outside = jnp.full((2 * count,), -1, jnp.int32)
    seg_pad = jnp.concatenate([outside, segment_ids, outside], axis=0)
    key_seg = lax.dynamic_slice_in_dim(seg_pad, position * count, 5 * count, 0)
    query_seg = lax.dynamic_slice_in_dim(segment_ids, position * count, count, 0)
    query_heads = query_normed.reshape(count, heads, HEAD_DIM)
    key_heads = widened[:, 0].reshape(5 * count, heads, HEAD_DIM)
    value_heads = widened[:, 1].reshape(5 * count, heads, HEAD_DIM)
    scores, mask = masked_scores(query_heads, key_heads, query_seg, key_seg)
    peak = jnp.max(scores, axis=-1, keepdims=True)
    weights = jnp.where(mask, jnp.exp(scores - peak), 0.0)
    total = jnp.sum(weights, axis=-1)
    probs = weights.astype(jnp.bfloat16)
    summed = jnp.einsum("hqk,khd->qhd", probs, value_heads, preferred_element_type=jnp.float32)
    context = (
        (summed / jnp.transpose(total)[:, :, None]).reshape(count, local_width).astype(jnp.bfloat16)
    )
    terms = jnp.dot(
        context,
        lax.all_gather(out_weight, "seq", axis=1, tiled=True),
        preferred_element_type=jnp.float32,
    )
    projected = lax.psum_scatter(terms, "tp", scatter_dimension=1, tiled=True)
    share = layer_scale.shape[0]
    residual = lax.dynamic_slice_in_dim(source, lax.axis_index("tp") * share, share, 1)
    return (residual + layer_scale * projected).astype(jnp.bfloat16)


ANY = pl.BlockSpec(memory_space=pl.ANY)
VMEM = pl.BlockSpec(memory_space=pltpu.VMEM)
SMEM = pl.BlockSpec(memory_space=pltpu.SMEM)
HBM = pl.BlockSpec(memory_space=pltpu.HBM)
KERNEL_VMEM = 60 * 1024 * 1024


def permuted(x, to):
    slabs, tps = lax.axis_size("seq") // SLAB, lax.axis_size("tp")
    pairs = []
    for i in range(slabs * SLAB * tps):
        z, q, y = to(i // (SLAB * tps), i // tps % SLAB, i % tps)
        pairs.append((i, (z * SLAB + q) * tps + y))
    return lax.ppermute(x, ("seq", "tp"), pairs)


def in_slab(x, flip):
    return permuted(x, lambda z, q, y: (z, q ^ flip, y))


def across(x):
    return permuted(x, lambda z, q, y: (z, q, 1 - y))


def even_pair(x):
    return permuted(x, lambda z, q, y: (z ^ 1, q, y))


def odd_pair(x):
    return permuted(x, lambda z, q, y: (3 - z if z in (1, 2) else z, q, y))


def tied(*arrays):
    return lax.optimization_barrier(arrays)


def as_row(column):
    wide = jnp.broadcast_to(column, (column.shape[0], 128))
    return jnp.transpose(wide)[:8]


def as_column(row):
    return jnp.transpose(jnp.broadcast_to(row, (128, row.shape[1])))


def start(copies):
    for copy in copies:
        copy.start()


def wait(copies):
    for copy in copies:
        copy.wait()


def norm_kernel(tokens, gain, out):
    part = tokens.shape[1] // out.shape[0]
    source = tokens[...].astype(jnp.float32)
    mean = jnp.mean(source * source, axis=1, keepdims=True)
    normed = source * lax.rsqrt(mean + eps) * gain[...]
    for j in range(out.shape[0]):
        out[j, :, :part] = normed[:, j * part:(j + 1) * part].astype(jnp.bfloat16)
        out[j, :, part:] = jnp.zeros((out.shape[1], out.shape[2] - part), jnp.bfloat16)


def norm(tokens, gain, slabs):
    count, depth = tokens.shape
    shape = (slabs, count, pl.cdiv(depth // slabs, 128) * 128)
    return pl.pallas_call(
        norm_kernel,
        out_shape=jax.ShapeDtypeStruct(shape, jnp.bfloat16),
        in_specs=[VMEM, VMEM],
        out_specs=VMEM,
        compiler_params=pltpu.CompilerParams(vmem_limit_bytes=KERNEL_VMEM),
        name="norm",
    )(tokens, gain[None])


def far_slabs(z):
    return jnp.where(z < 2, 2, 1), jnp.where(z < 2, 3, 0)


def token_copies(xs, at, out, sems):
    return [
        pltpu.make_async_copy(x.at[at], out.at[r], sems.at[r]) for r, x in enumerate(xs)
    ]


def picked_copy(z, middle, end, out, sem, wait):
    inner = (z == 1) | (z == 2)

    @pl.when(inner)
    def _():
        copy = pltpu.make_async_copy(middle, out, sem)
        copy.wait() if wait else copy.start()

    @pl.when(jnp.logical_not(inner))
    def _():
        copy = pltpu.make_async_copy(end, out, sem)
        copy.wait() if wait else copy.start()


def early_kernel(
    place, xa, xb, xc, xd, own, near, middle, end, acc, x_all, w_all, held, x_sem, w_sem, sems,
):
    z = place[0]
    xs = (xa, xb, xc, xd)
    near_copy = pltpu.make_async_copy(near, w_all.at[1], w_sem.at[1])
    own_copy = pltpu.make_async_copy(own, w_all.at[0], w_sem.at[0])
    x_copies = [
        token_copies(xs, at, x_all.at[i], x_sem.at[i])
        for i, at in enumerate((z, z ^ 1, far_slabs(z)[0]))
    ]
    own_copy.start()
    start(x_copies[0])
    near_copy.start()
    start(x_copies[1])
    picked_copy(z, middle, end, w_all.at[2], w_sem.at[2], False)
    start(x_copies[2])
    kinds, rows = own.shape[:2]
    stores = []
    for step in range(3):
        if step < 2:
            (own_copy, near_copy)[step].wait()
        else:
            picked_copy(z, middle, end, w_all.at[2], w_sem.at[2], True)
        wait(x_copies[step])
        for r in range(SLAB):
            x = x_all[step, r][:, :rows]
            for kind in range(kinds):
                term = jnp.dot(x, w_all[step, kind], preferred_element_type=jnp.float32)
                held[r, kind] = term if step == 0 else held[r, kind] + term
            if step == 2:
                stores.append(pltpu.make_async_copy(held.at[r], acc.at[r], sems.at[r]))
                stores[-1].start()
    wait(stores)


def early(place, xs, own, near, middle, end):
    kinds, rows, width = own.shape
    slabs, count, wide = xs[0].shape
    return pl.pallas_call(
        early_kernel,
        out_shape=jax.ShapeDtypeStruct((SLAB, kinds, count, width), jnp.float32),
        in_specs=[SMEM] + [HBM] * 8,
        out_specs=HBM,
        scratch_shapes=[
            pltpu.VMEM((3, SLAB, count, wide), jnp.bfloat16),
            pltpu.VMEM((3, kinds, rows, width), jnp.bfloat16),
            pltpu.VMEM((SLAB, kinds, count, width), jnp.float32),
            pltpu.SemaphoreType.DMA((3, SLAB)),
            pltpu.SemaphoreType.DMA((3,)),
            pltpu.SemaphoreType.DMA((SLAB,)),
        ],
        compiler_params=pltpu.CompilerParams(vmem_limit_bytes=KERNEL_VMEM),
        cost_estimate=pl.CostEstimate(
            flops=6 * kinds * SLAB * count * rows * width,
            bytes_accessed=6 * kinds * rows * width + 6 * SLAB * count * rows,
            transcendentals=0,
        ),
        name="early",
    )(place, *xs, own, near, middle, end)


def late_kernel(
    place, xa, xb, xc, xd, acc, middle, end, q_gain, k_gain,
    query, keys, values, squares, even, odd,
    x_all, far, held, q_all, k_all, v_all, x_sem, w_sem, acc_sem, sems,
):
    z, q = place[0], place[1]
    picked_copy(z, middle, end, far, w_sem, False)
    copies = token_copies((xa, xb, xc, xd), far_slabs(z)[1], x_all, x_sem)
    loads = [pltpu.make_async_copy(acc.at[r], held.at[r], acc_sem.at[r]) for r in range(SLAB)]
    for r in range(SLAB):
        copies[r].start()
        loads[r].start()
    count = held.shape[2]
    picked_copy(z, middle, end, far, w_sem, True)
    for r in range(SLAB):
        copies[r].wait()
        loads[r].wait()
        x = x_all[r][:, :far.shape[1]]
        rows = pl.ds(pl.multiple_of((q ^ r) * count, count), count)
        for kind in range(3):
            part = held[r, kind] + jnp.dot(x, far[kind], preferred_element_type=jnp.float32)
            if kind < 2:
                summed = as_row(jnp.sum(part * part, axis=1, keepdims=True))
                squares[kind:kind + 1, rows] = summed[:1]
                part = part * (q_gain, k_gain)[kind][...]
            (q_all, k_all, v_all)[kind][rows, :] = part.astype((q_all, k_all, v_all)[kind].dtype)
    reach = even.shape[1]
    stores = []
    for n, (out, at) in enumerate(((even, 1 - z % 2), (odd, z % 2))):
        rows = pl.ds(pl.multiple_of(at * reach, reach), reach)
        stores.append(pltpu.make_async_copy(k_all.at[rows, :], out.at[0], sems.at[2 * n]))
        stores.append(pltpu.make_async_copy(v_all.at[rows, :], out.at[1], sems.at[2 * n + 1]))
    for n, (src, out) in enumerate(((q_all, query), (k_all, keys), (v_all, values))):
        stores.append(pltpu.make_async_copy(src, out, sems.at[4 + n]))
    start(stores)
    wait(stores)


def late(place, xs, acc, middle, end, q_gain, k_gain):
    kinds, rows, width = middle.shape
    count, wide = xs[0].shape[1:]
    slab = SLAB * count
    f32, bf16 = jnp.float32, jnp.bfloat16
    return pl.pallas_call(
        late_kernel,
        out_shape=(
            jax.ShapeDtypeStruct((slab, width), f32),
            jax.ShapeDtypeStruct((slab, width), bf16),
            jax.ShapeDtypeStruct((slab, width), bf16),
            jax.ShapeDtypeStruct((2, slab), f32),
            jax.ShapeDtypeStruct((2, 2 * count, width), bf16),
            jax.ShapeDtypeStruct((2, 2 * count, width), bf16),
        ),
        in_specs=[SMEM] + [HBM] * 7 + [VMEM] * 2,
        out_specs=(HBM, HBM, HBM, VMEM, HBM, HBM),
        scratch_shapes=[
            pltpu.VMEM((SLAB, count, wide), bf16),
            pltpu.VMEM((kinds, rows, width), bf16),
            pltpu.VMEM((SLAB, kinds, count, width), f32),
            pltpu.VMEM((slab, width), f32),
            pltpu.VMEM((slab, width), bf16),
            pltpu.VMEM((slab, width), bf16),
            pltpu.SemaphoreType.DMA((SLAB,)),
            pltpu.SemaphoreType.DMA,
            pltpu.SemaphoreType.DMA((SLAB,)),
            pltpu.SemaphoreType.DMA((7,)),
        ],
        compiler_params=pltpu.CompilerParams(vmem_limit_bytes=KERNEL_VMEM),
        cost_estimate=pl.CostEstimate(
            flops=2 * kinds * slab * rows * width,
            bytes_accessed=2 * kinds * rows * width + 2 * slab * rows,
            transcendentals=0,
        ),
        name="late",
    )(place, *xs, acc, middle, end, q_gain, k_gain)


def attend_kernel(
    full_width, flips, place, query, keys, values, even, odd, mine, other, seg, *rest,
):
    outs, (q_all, k_all, v_all, scale_all, sems) = rest[:len(flips)], rest[len(flips):]
    z, q = place[0], place[1]
    slab = query.shape[0]
    count = slab // SLAB
    half = even.shape[1]
    upper = half + slab
    is_even = z % 2 == 0
    even_at = pl.multiple_of(jnp.where(is_even, upper, 0), half)
    odd_at = pl.multiple_of(jnp.where(is_even, 0, upper), half)
    copies = [pltpu.make_async_copy(query, q_all, sems.at[0])]
    for k, (whole, out) in enumerate(((keys, k_all), (values, v_all))):
        for n, (src, at) in enumerate(((whole, half), (even.at[k], even_at), (odd.at[k], odd_at))):
            dst = out.at[pl.ds(at, src.shape[0]), :]
            copies.append(pltpu.make_async_copy(src, dst, sems.at[1 + 3 * k + n]))
    start(copies)
    scale = [lax.rsqrt((mine[n] + other[n]) / full_width + eps) for n in range(3)]
    scale_all[:, half:upper] = scale[0]
    scale_all[:, :half] = jnp.where(is_even, scale[2], scale[1])[:, slab - half:]
    scale_all[:, upper:] = jnp.where(is_even, scale[1], scale[2])[:, :half]
    wait(copies)
    window = count + 2 * half
    heads = query.shape[1] // HEAD_DIM
    factor = HEAD_DIM ** (-0.5) * math.log2(math.e)
    for r, out in zip(flips, outs):
        begin = pl.multiple_of((q ^ r) * count, count)
        at_query = pl.multiple_of((q ^ r) * count + half, count)
        key_seg = seg[:, pl.ds(begin, window)]
        query_seg = as_column(seg[:, pl.ds(at_query, count)])
        k_scale = scale_all[1:2, pl.ds(begin, window)] * factor
        q_scale = as_column(scale_all[0:1, pl.ds(at_query, count)])
        mask = jnp.tile(query_seg, (1, window // 128)) == key_seg
        for h in range(heads):
            cols = slice(h * HEAD_DIM, (h + 1) * HEAD_DIM)
            q_low = (q_all[pl.ds(begin, count), cols] * q_scale).astype(jnp.bfloat16)
            scores = lax.dot_general(
                q_low, k_all[pl.ds(begin, window), cols],
                (((1,), (1,)), ((), ())), preferred_element_type=jnp.float32,
            )
            scores = jnp.where(mask, scores * k_scale, floor_score)
            peak = jnp.max(scores, axis=1, keepdims=True)
            weights = jnp.exp2(scores - peak)
            total = jnp.sum(weights, axis=1, keepdims=True)
            summed = jnp.dot(
                weights.astype(jnp.bfloat16), v_all[pl.ds(begin, window), cols],
                preferred_element_type=jnp.float32,
            )
            out[:, cols] = (summed / total).astype(jnp.bfloat16)


def attend(full_width, flips, place, query, keys, values, even, odd, mine, other, seg):
    slab, width = query.shape
    half = even.shape[1]
    count = slab // SLAB
    ext = slab + 2 * half
    bf16 = jnp.bfloat16
    window = count + 2 * half
    return pl.pallas_call(
        functools.partial(attend_kernel, full_width, flips),
        out_shape=(jax.ShapeDtypeStruct((count, width), bf16),) * len(flips),
        in_specs=[SMEM] + [HBM] * 5 + [VMEM] * 3,
        out_specs=(VMEM,) * len(flips),
        scratch_shapes=[
            pltpu.VMEM((slab, width), jnp.float32),
            pltpu.VMEM((ext, width), bf16),
            pltpu.VMEM((ext, width), bf16),
            pltpu.VMEM((2, ext), jnp.float32),
            pltpu.SemaphoreType.DMA((7,)),
        ],
        compiler_params=pltpu.CompilerParams(vmem_limit_bytes=KERNEL_VMEM),
        cost_estimate=pl.CostEstimate(
            flops=len(flips) * 4 * count * window * width,
            bytes_accessed=4 * ext * width + 4 * slab * width,
            transcendentals=len(flips) * count * window * width // HEAD_DIM,
        ),
        name="attend",
    )(place, query, keys, values, even, odd, mine, other, seg)


def out_kernel(
    place, c00, c01, c10, c11, c20, c21, c30, c31, wa0, wa1, wb0, wb1, wc0, wc1, wd0, wd1,
    residual, scale, out, c_all, w_all, total, c_sem, w_sem,
):
    z, q, y = place[0], place[1], place[2]
    width = c00.shape[1]
    c_copies = []
    for r, pair in enumerate(((c00, c01), (c10, c11), (c20, c21), (c30, c31))):
        at = pl.multiple_of((q ^ r) * width, width)
        for i in range(2):
            dst = c_all.at[i, :, pl.ds(at, width)]
            c_copies.append(pltpu.make_async_copy(pair[i], dst, c_sem.at[r, i]))
    start(c_copies)
    w_copies = [
        pltpu.make_async_copy(w, w_all.at[r, j], w_sem.at[r, j])
        for r, pair in enumerate(((wa0, wa1), (wb0, wb1), (wc0, wc1), (wd0, wd1)))
        for j, w in enumerate(pair)
    ]
    start(w_copies)
    column = as_column(scale[...])[:out.shape[0]]
    column = jnp.tile(column, (1, out.shape[1] // 128))
    wait(c_copies)
    rows = wa0.shape[1]
    for r in range(SLAB):
        for j in range(2):
            w_copies[2 * r + j].wait()
            slab = jnp.where(z // 2 == y, (z % 2) ^ j, jnp.where(z < 2, j, 1 - j))
            at = pl.multiple_of((slab * SLAB + (q ^ r)) * rows, 8)
            term = None
            for i in range(2):
                part = lax.dot_general(
                    w_all[r, j, i], c_all[i], (((1,), (1,)), ((), ())),
                    preferred_element_type=jnp.float32,
                )
                term = part if term is None else term + part
            total[pl.ds(at, rows), :] = term
    out[...] = (residual[...].astype(jnp.float32) + column * total[...]).astype(jnp.bfloat16)


def output(place, blocks, pieces, residual, scale):
    count, width = blocks[0].shape
    rows, depth = pieces[0].shape[1:]
    share = residual.shape[0]
    scale = jnp.pad(scale, (0, -share % 128))[None]
    return pl.pallas_call(
        out_kernel,
        out_shape=jax.ShapeDtypeStruct((share, count), jnp.bfloat16),
        in_specs=[SMEM] + [HBM] * 16 + [VMEM] * 2,
        out_specs=VMEM,
        scratch_shapes=[
            pltpu.VMEM((2, count, depth), jnp.bfloat16),
            pltpu.VMEM((SLAB, 2, 2, rows, depth), jnp.bfloat16),
            pltpu.VMEM((share, count), jnp.float32),
            pltpu.SemaphoreType.DMA((SLAB, 2)),
            pltpu.SemaphoreType.DMA((SLAB, 2)),
        ],
        compiler_params=pltpu.CompilerParams(vmem_limit_bytes=KERNEL_VMEM),
        cost_estimate=pl.CostEstimate(
            flops=4 * share * count * depth,
            bytes_accessed=4 * share * depth,
            transcendentals=0,
        ),
        name="output",
    )(place, *blocks, *pieces, residual, scale)


def rows_of_slab(q, cut):
    got = [cut[0]] + [in_slab(cut[r], r) for r in range(1, SLAB)]
    placed = []
    for b in range(SLAB):
        piece = got[b]
        for other in range(1, SLAB):
            piece = jnp.where(q == other, got[b ^ other], piece)
        placed.append(piece)
    return jnp.concatenate(placed, axis=1)


def slab_plan(tokens, norm_gain, qkv_weight, q_gain, k_gain, out_weight, layer_scale, segment_ids):
    count = tokens.shape[0]
    seq, tp = lax.axis_index("seq"), lax.axis_index("tp")
    slabs = lax.axis_size("seq") // SLAB
    z, q = seq // SLAB, seq % SLAB
    place = jnp.stack([z, q, tp]).astype(jnp.int32)
    width = qkv_weight.shape[2] // SLAB
    full_width = qkv_weight.shape[2] * lax.axis_size("tp")
    slab, half = SLAB * count, 2 * count
    inner, home = (z == 1) | (z == 2), z // 2 == tp

    by_kind = jnp.transpose(qkv_weight, (1, 0, 2))
    cut = [lax.dynamic_slice_in_dim(by_kind, (q ^ r) * width, width, 2) for r in range(SLAB)]
    *cut, out_own = tied(*cut, jnp.transpose(out_weight))
    own = rows_of_slab(q, cut)
    out_near, out_mid1 = even_pair(out_own), odd_pair(out_own)
    x0 = norm(tokens, norm_gain, slabs)
    out_end1, out_mid2 = even_pair(out_mid1), odd_pair(out_near)

    def over_tp(close, far):
        keep, give = jnp.where(home, close, far), jnp.where(home, far, close)
        return keep, across(give)

    own, x0, out_end1, out_mid2 = tied(own, x0, out_end1, out_mid2)
    near, middle1 = even_pair(own), odd_pair(own)
    x2 = in_slab(x0, 2)
    out_end2 = even_pair(out_mid2)
    keep0, got0 = over_tp(out_own, jnp.where(inner, out_mid1, out_end1))
    near, middle1 = tied(near, middle1)
    end1, middle2 = even_pair(middle1), odd_pair(near)
    x2, x0, out_end2, keep0, got0, _ = tied(x2, x0, out_end2, keep0, got0, near)
    wa0 = jnp.stack([keep0, got0])
    wc0 = in_slab(wa0, 2)
    x1 = in_slab(x0, 1)
    keep1, got1 = over_tp(out_near, jnp.where(inner, out_mid2, out_end2))
    end1, middle2, x1, x2, wa0, wc0, keep1, got1 = tied(
        end1, middle2, x1, x2, wa0, wc0, keep1, got1
    )
    end2 = even_pair(middle2)
    x3 = in_slab(x2, 1)
    wa1 = jnp.stack([keep1, got1])
    wc1 = in_slab(wa1, 2)
    xs = (x0, x1, x2, x3)
    acc = early(place, xs, own, near, middle1, end1)
    wb0, wd0 = in_slab(wa0, 1), in_slab(wc0, 1)
    end2, acc, wc1, wb0, wd0 = tied(end2, acc, wc1, wb0, wd0)

    gains = [lax.dynamic_slice_in_dim(g, q * width, width, 0)[None] for g in (q_gain, k_gain)]
    query, keys, values, squares, even, odd = late(place, xs, acc, middle2, end2, *gains)
    sums = jnp.stack([squares, even_pair(squares), odd_pair(squares)])
    sums, even, odd = tied(sums, even, odd)
    even, odd = even_pair(even), odd_pair(odd)
    mine = sums
    for r in range(1, SLAB):
        mine = mine + in_slab(sums, r)
    other = across(mine)
    wb1, wd1 = in_slab(wa1, 1), in_slab(wc1, 1)
    even, odd, other, wb1, wd1 = tied(even, odd, other, wb1, wd1)
    pieces = (wa0, wa1, wb0, wb1, wc0, wc1, wd0, wd1)

    outside = jnp.full((half,), -1, jnp.int32)
    seg = jnp.concatenate([outside, segment_ids, outside], axis=0)
    seg = lax.dynamic_slice_in_dim(seg, z * slab, slab + 2 * half, 0)
    seg = seg.astype(jnp.float32)[None]
    blocks, spread = {}, {}
    for flips in ((2, 3), (1, 0)):
        found = attend(
            full_width, flips, place, query, keys, values, even, odd, mine, other, seg
        )
        blocks.update(zip(flips, found))
    for r in (2, 3, 1, 0):
        for i in range(2):
            to = functools.partial(lambda r, i, z, q, y: (z, q ^ r, y ^ i), r, i)
            spread[r, i] = permuted(blocks[r], to) if r or i else blocks[r]
    spread = [spread[r, i] for r in range(SLAB) for i in range(2)]

    share = layer_scale.shape[0]
    residual = jnp.transpose(lax.dynamic_slice_in_dim(tokens, tp * share, share, 1))
    return jnp.transpose(output(place, spread, pieces, residual, layer_scale))


def solution(mesh):
    def shards(*args):
        heads = args[2].shape[2] // HEAD_DIM
        slab = mesh.shape["seq"] == 16 and mesh.shape["tp"] == 2 and heads % SLAB == 0
        return (slab_plan if slab else row_plan)(*args)

    return jax.shard_map(
        shards,
        mesh=mesh,
        in_specs=(
            P("seq", None),
            P(),
            P("seq", None, "tp"),
            P("tp"),
            P("tp"),
            P("tp", "seq"),
            P("tp"),
            P(),
        ),
        out_specs=P("seq", "tp"),
        check_vma=False,
    )
```

```python
import functools
import math

import jax
import jax.numpy as jnp
from jax import lax
from jax.experimental import pallas as pl
from jax.experimental.pallas import tpu as pltpu
from jax.sharding import PartitionSpec as P

HEAD_DIM = 128
SLAB = 4

eps = 1e-06
floor_score = -1e30


def passed_along(x, axis, by):
    size = lax.axis_size(axis)
    pairs = [(i, i + by) for i in range(size) if 0 <= i + by < size]
    return lax.ppermute(x, axis, pairs)


def masked_scores(query, keys, query_seg, key_seg):
    scores = jnp.einsum(
        "qhd,khd->hqk", query, keys, preferred_element_type=jnp.float32
    ) * HEAD_DIM ** (-0.5)
    mask = (query_seg[:, None] == key_seg[None, :])[None]
    return (jnp.where(mask, scores, floor_score), mask)


def row_plan(tokens, norm_gain, qkv_weight, q_gain, k_gain, out_weight, layer_scale, segment_ids):
    count = tokens.shape[0]
    source = tokens.astype(jnp.float32)
    normed = (
        source * lax.rsqrt(jnp.mean(source * source, axis=-1, keepdims=True) + eps) * norm_gain
    ).astype(jnp.bfloat16)
    local_width = qkv_weight.shape[2]
    heads = local_width // HEAD_DIM
    joined = jnp.einsum(
        "td,dch->tch",
        normed,
        lax.all_gather(qkv_weight, "seq", axis=0, tiled=True),
        preferred_element_type=jnp.float32,
    )
    query = joined[:, 0]
    keys = joined[:, 1]
    values = joined[:, 2]
    query_sq, key_sq = lax.psum(
        (jnp.sum(query * query, axis=-1), jnp.sum(keys * keys, axis=-1)), "tp"
    )
    full_width = local_width * lax.axis_size("tp")
    query_normed = (query * lax.rsqrt(query_sq / full_width + eps)[:, None] * q_gain).astype(
        jnp.bfloat16
    )
    key_normed = (keys * lax.rsqrt(key_sq / full_width + eps)[:, None] * k_gain).astype(
        jnp.bfloat16
    )
    paired = jnp.stack([key_normed, values.astype(jnp.bfloat16)], axis=1)
    pieces = []
    for offset in (2, 1, 0, -1, -2):
        if offset == 0:
            pieces.append(paired)
        else:
            pieces.append(passed_along(paired, "seq", offset))
    widened = jnp.concatenate(pieces, axis=0)
    position = lax.axis_index("seq")
    outside = jnp.full((2 * count,), -1, jnp.int32)
    seg_pad = jnp.concatenate([outside, segment_ids, outside], axis=0)
    key_seg = lax.dynamic_slice_in_dim(seg_pad, position * count, 5 * count, 0)
    query_seg = lax.dynamic_slice_in_dim(segment_ids, position * count, count, 0)
    query_heads = query_normed.reshape(count, heads, HEAD_DIM)
    key_heads = widened[:, 0].reshape(5 * count, heads, HEAD_DIM)
    value_heads = widened[:, 1].reshape(5 * count, heads, HEAD_DIM)
    scores, mask = masked_scores(query_heads, key_heads, query_seg, key_seg)
    peak = jnp.max(scores, axis=-1, keepdims=True)
    weights = jnp.where(mask, jnp.exp(scores - peak), 0.0)
    total = jnp.sum(weights, axis=-1)
    probs = weights.astype(jnp.bfloat16)
    summed = jnp.einsum("hqk,khd->qhd", probs, value_heads, preferred_element_type=jnp.float32)
    context = (
        (summed / jnp.transpose(total)[:, :, None]).reshape(count, local_width).astype(jnp.bfloat16)
    )
    terms = jnp.dot(
        context,
        lax.all_gather(out_weight, "seq", axis=1, tiled=True),
        preferred_element_type=jnp.float32,
    )
    projected = lax.psum_scatter(terms, "tp", scatter_dimension=1, tiled=True)
    share = layer_scale.shape[0]
    residual = lax.dynamic_slice_in_dim(source, lax.axis_index("tp") * share, share, 1)
    return (residual + layer_scale * projected).astype(jnp.bfloat16)


ANY = pl.BlockSpec(memory_space=pl.ANY)
VMEM = pl.BlockSpec(memory_space=pltpu.VMEM)
SMEM = pl.BlockSpec(memory_space=pltpu.SMEM)
HBM = pl.BlockSpec(memory_space=pltpu.HBM)
KERNEL_VMEM = 60 * 1024 * 1024


def permuted(x, to):
    slabs, tps = lax.axis_size("seq") // SLAB, lax.axis_size("tp")
    pairs = []
    for i in range(slabs * SLAB * tps):
        z, q, y = to(i // (SLAB * tps), i // tps % SLAB, i % tps)
        pairs.append((i, (z * SLAB + q) * tps + y))
    return lax.ppermute(x, ("seq", "tp"), pairs)


def in_slab(x, flip):
    return permuted(x, lambda z, q, y: (z, q ^ flip, y))


def across(x):
    return permuted(x, lambda z, q, y: (z, q, 1 - y))


def even_pair(x):
    return permuted(x, lambda z, q, y: (z ^ 1, q, y))


def odd_pair(x):
    return permuted(x, lambda z, q, y: (3 - z if z in (1, 2) else z, q, y))


def tied(*arrays):
    return lax.optimization_barrier(arrays)


def as_row(column):
    wide = jnp.broadcast_to(column, (column.shape[0], 128))
    return jnp.transpose(wide)[:8]


def as_column(row):
    return jnp.transpose(jnp.broadcast_to(row, (128, row.shape[1])))


def start(copies):
    for copy in copies:
        copy.start()


def wait(copies):
    for copy in copies:
        copy.wait()


def norm_kernel(tokens, gain, out):
    part = tokens.shape[1] // out.shape[0]
    source = tokens[...].astype(jnp.float32)
    mean = jnp.mean(source * source, axis=1, keepdims=True)
    normed = source * lax.rsqrt(mean + eps) * gain[...]
    for j in range(out.shape[0]):
        out[j, :, :part] = normed[:, j * part:(j + 1) * part].astype(jnp.bfloat16)
        out[j, :, part:] = jnp.zeros((out.shape[1], out.shape[2] - part), jnp.bfloat16)


def norm(tokens, gain, slabs):
    count, depth = tokens.shape
    shape = (slabs, count, pl.cdiv(depth // slabs, 128) * 128)
    return pl.pallas_call(
        norm_kernel,
        out_shape=jax.ShapeDtypeStruct(shape, jnp.bfloat16),
        in_specs=[VMEM, VMEM],
        out_specs=VMEM,
        compiler_params=pltpu.CompilerParams(vmem_limit_bytes=KERNEL_VMEM),
        name="norm",
    )(tokens, gain[None])


def far_slabs(z):
    return jnp.where(z < 2, 2, 1), jnp.where(z < 2, 3, 0)


def token_copies(xs, at, out, sems):
    return [
        pltpu.make_async_copy(x.at[at], out.at[r], sems.at[r]) for r, x in enumerate(xs)
    ]


def picked_copy(z, middle, end, out, sem, wait):
    inner = (z == 1) | (z == 2)

    @pl.when(inner)
    def _():
        copy = pltpu.make_async_copy(middle, out, sem)
        copy.wait() if wait else copy.start()

    @pl.when(jnp.logical_not(inner))
    def _():
        copy = pltpu.make_async_copy(end, out, sem)
        copy.wait() if wait else copy.start()


def early_kernel(
    place, xa, xb, xc, xd, own, near, middle, end, acc, x_all, w_all, held, x_sem, w_sem, sems,
):
    z = place[0]
    xs = (xa, xb, xc, xd)
    near_copy = pltpu.make_async_copy(near, w_all.at[1], w_sem.at[1])
    own_copy = pltpu.make_async_copy(own, w_all.at[0], w_sem.at[0])
    x_copies = [
        token_copies(xs, at, x_all.at[i], x_sem.at[i])
        for i, at in enumerate((z, z ^ 1, far_slabs(z)[0]))
    ]
    own_copy.start()
    start(x_copies[0])
    near_copy.start()
    start(x_copies[1])
    picked_copy(z, middle, end, w_all.at[2], w_sem.at[2], False)
    start(x_copies[2])
    kinds, rows = own.shape[:2]
    stores = []
    for step in range(3):
        if step < 2:
            (own_copy, near_copy)[step].wait()
        else:
            picked_copy(z, middle, end, w_all.at[2], w_sem.at[2], True)
        wait(x_copies[step])
        for r in range(SLAB):
            x = x_all[step, r][:, :rows]
            for kind in range(kinds):
                term = jnp.dot(x, w_all[step, kind], preferred_element_type=jnp.float32)
                held[r, kind] = term if step == 0 else held[r, kind] + term
            if step == 2:
                stores.append(pltpu.make_async_copy(held.at[r], acc.at[r], sems.at[r]))
                stores[-1].start()
    wait(stores)


def early(place, xs, own, near, middle, end):
    kinds, rows, width = own.shape
    slabs, count, wide = xs[0].shape
    return pl.pallas_call(
        early_kernel,
        out_shape=jax.ShapeDtypeStruct((SLAB, kinds, count, width), jnp.float32),
        in_specs=[SMEM] + [HBM] * 8,
        out_specs=HBM,
        scratch_shapes=[
            pltpu.VMEM((3, SLAB, count, wide), jnp.bfloat16),
            pltpu.VMEM((3, kinds, rows, width), jnp.bfloat16),
            pltpu.VMEM((SLAB, kinds, count, width), jnp.float32),
            pltpu.SemaphoreType.DMA((3, SLAB)),
            pltpu.SemaphoreType.DMA((3,)),
            pltpu.SemaphoreType.DMA((SLAB,)),
        ],
        compiler_params=pltpu.CompilerParams(vmem_limit_bytes=KERNEL_VMEM),
        cost_estimate=pl.CostEstimate(
            flops=6 * kinds * SLAB * count * rows * width,
            bytes_accessed=6 * kinds * rows * width + 6 * SLAB * count * rows,
            transcendentals=0,
        ),
        name="early",
    )(place, *xs, own, near, middle, end)


def late_kernel(
    place, xa, xb, xc, xd, acc, middle, end, q_gain, k_gain,
    query, keys, values, squares, even, odd,
    x_all, far, held, q_all, k_all, v_all, x_sem, w_sem, acc_sem, sems,
):
    z, q = place[0], place[1]
    picked_copy(z, middle, end, far, w_sem, False)
    copies = token_copies((xa, xb, xc, xd), far_slabs(z)[1], x_all, x_sem)
    loads = [pltpu.make_async_copy(acc.at[r], held.at[r], acc_sem.at[r]) for r in range(SLAB)]
    for r in range(SLAB):
        copies[r].start()
        loads[r].start()
    count = held.shape[2]
    stores = []
    picked_copy(z, middle, end, far, w_sem, True)
    for r in range(SLAB):
        copies[r].wait()
        loads[r].wait()
        x = x_all[r][:, :far.shape[1]]
        rows = pl.ds(pl.multiple_of((q ^ r) * count, count), count)
        for kind in range(3):
            part = held[r, kind] + jnp.dot(x, far[kind], preferred_element_type=jnp.float32)
            if kind < 2:
                summed = as_row(jnp.sum(part * part, axis=1, keepdims=True))
                squares[kind:kind + 1, rows] = summed[:1]
                part = part * (q_gain, k_gain)[kind][...]
            held_out, out = ((q_all, query), (k_all, keys), (v_all, values))[kind]
            held_out[rows, :] = part.astype(held_out.dtype)
            store = pltpu.make_async_copy(held_out.at[rows, :], out.at[rows, :], sems.at[3 * r + kind])
            store.start()
            stores.append(store)
    reach = even.shape[1]
    for n, (out, at) in enumerate(((even, 1 - z % 2), (odd, z % 2))):
        rows = pl.ds(pl.multiple_of(at * reach, reach), reach)
        for k, src in enumerate((k_all, v_all)):
            sem = sems.at[3 * SLAB + 2 * n + k]
            stores.append(pltpu.make_async_copy(src.at[rows, :], out.at[k], sem))
            stores[-1].start()
    wait(stores)


def late(place, xs, acc, middle, end, q_gain, k_gain):
    kinds, rows, width = middle.shape
    count, wide = xs[0].shape[1:]
    slab = SLAB * count
    f32, bf16 = jnp.float32, jnp.bfloat16
    return pl.pallas_call(
        late_kernel,
        out_shape=(
            jax.ShapeDtypeStruct((slab, width), f32),
            jax.ShapeDtypeStruct((slab, width), bf16),
            jax.ShapeDtypeStruct((slab, width), bf16),
            jax.ShapeDtypeStruct((2, slab), f32),
            jax.ShapeDtypeStruct((2, 2 * count, width), bf16),
            jax.ShapeDtypeStruct((2, 2 * count, width), bf16),
        ),
        in_specs=[SMEM] + [HBM] * 7 + [VMEM] * 2,
        out_specs=(HBM, HBM, HBM, VMEM, HBM, HBM),
        scratch_shapes=[
            pltpu.VMEM((SLAB, count, wide), bf16),
            pltpu.VMEM((kinds, rows, width), bf16),
            pltpu.VMEM((SLAB, kinds, count, width), f32),
            pltpu.VMEM((slab, width), f32),
            pltpu.VMEM((slab, width), bf16),
            pltpu.VMEM((slab, width), bf16),
            pltpu.SemaphoreType.DMA((SLAB,)),
            pltpu.SemaphoreType.DMA,
            pltpu.SemaphoreType.DMA((SLAB,)),
            pltpu.SemaphoreType.DMA((3 * SLAB + 4,)),
        ],
        compiler_params=pltpu.CompilerParams(vmem_limit_bytes=KERNEL_VMEM),
        cost_estimate=pl.CostEstimate(
            flops=2 * kinds * slab * rows * width,
            bytes_accessed=2 * kinds * rows * width + 2 * slab * rows,
            transcendentals=0,
        ),
        name="late",
    )(place, *xs, acc, middle, end, q_gain, k_gain)


def attend_kernel(
    full_width, place, query, keys, values, even, odd, mine, other, seg, o0, o1, o2, o3,
    q_all, k_all, v_all, k_turned, scale_all, sems,
):
    z, q = place[0], place[1]
    slab = query.shape[0]
    count = slab // SLAB
    half = even.shape[1]
    upper = half + slab
    is_even = z % 2 == 0
    even_at = pl.multiple_of(jnp.where(is_even, upper, 0), half)
    odd_at = pl.multiple_of(jnp.where(is_even, 0, upper), half)
    copies = [pltpu.make_async_copy(query, q_all, sems.at[0])]
    for k, (whole, out) in enumerate(((keys, k_all), (values, v_all))):
        for n, (src, at) in enumerate(((whole, half), (even.at[k], even_at), (odd.at[k], odd_at))):
            dst = out.at[pl.ds(at, src.shape[0]), :]
            copies.append(pltpu.make_async_copy(src, dst, sems.at[1 + 3 * k + n]))
    start(copies)
    scale = [lax.rsqrt((mine[n] + other[n]) / full_width + eps) for n in range(3)]
    scale_all[:, half:upper] = scale[0]
    scale_all[:, :half] = jnp.where(is_even, scale[2], scale[1])[:, slab - half:]
    scale_all[:, upper:] = jnp.where(is_even, scale[1], scale[2])[:, :half]
    wait(copies)
    for at in range(0, k_all.shape[0], count):
        k_turned[:, at:at + count] = jnp.transpose(k_all[at:at + count, :])
    window = count + 2 * half
    heads = query.shape[1] // HEAD_DIM
    factor = HEAD_DIM ** (-0.5) * math.log2(math.e)
    for r, out in ((2, o2), (3, o3), (1, o1), (0, o0)):
        begin = pl.multiple_of((q ^ r) * count, count)
        at_query = pl.multiple_of((q ^ r) * count + half, count)
        key_seg = seg[:, pl.ds(begin, window)]
        query_seg = as_column(seg[:, pl.ds(at_query, count)])
        k_scale = scale_all[1:2, pl.ds(begin, window)] * factor
        q_scale = as_column(scale_all[0:1, pl.ds(at_query, count)])
        mask = jnp.tile(query_seg, (1, window // 128)) == key_seg
        for h in range(heads):
            cols = slice(h * HEAD_DIM, (h + 1) * HEAD_DIM)
            q_low = (q_all[pl.ds(begin, count), cols] * q_scale).astype(jnp.bfloat16)
            scores = jnp.dot(
                q_low, k_turned[cols, pl.ds(begin, window)], preferred_element_type=jnp.float32
            )
            scores = jnp.where(mask, scores * k_scale, floor_score)
            peak = jnp.max(scores, axis=1, keepdims=True)
            weights = jnp.exp2(scores - peak)
            total = jnp.sum(weights, axis=1, keepdims=True)
            summed = jnp.dot(
                weights.astype(jnp.bfloat16), v_all[pl.ds(begin, window), cols],
                preferred_element_type=jnp.float32,
            )
            out[cols, :] = jnp.transpose(summed / total).astype(jnp.bfloat16)


def attend(full_width, place, query, keys, values, even, odd, mine, other, seg):
    slab, width = query.shape
    half = even.shape[1]
    count = slab // SLAB
    ext = slab + 2 * half
    bf16 = jnp.bfloat16
    window = count + 2 * half
    return pl.pallas_call(
        functools.partial(attend_kernel, full_width),
        out_shape=(jax.ShapeDtypeStruct((width, count), bf16),) * SLAB,
        in_specs=[SMEM] + [HBM] * 5 + [VMEM] * 3,
        out_specs=(VMEM,) * SLAB,
        scratch_shapes=[
            pltpu.VMEM((slab, width), jnp.float32),
            pltpu.VMEM((ext, width), bf16),
            pltpu.VMEM((ext, width), bf16),
            pltpu.VMEM((width, ext), bf16),
            pltpu.VMEM((2, ext), jnp.float32),
            pltpu.SemaphoreType.DMA((7,)),
        ],
        compiler_params=pltpu.CompilerParams(vmem_limit_bytes=KERNEL_VMEM),
        cost_estimate=pl.CostEstimate(
            flops=SLAB * 4 * count * window * width,
            bytes_accessed=4 * ext * width + 4 * slab * width,
            transcendentals=SLAB * count * window * width // HEAD_DIM,
        ),
        name="attend",
    )(place, query, keys, values, even, odd, mine, other, seg)


def out_kernel(
    place, c00, c01, c10, c11, c20, c21, c30, c31, wa0, wa1, wb0, wb1, wc0, wc1, wd0, wd1,
    residual, scale, out, c_all, w_all, total, c_sem, w_sem,
):
    z, q, y = place[0], place[1], place[2]
    width = c00.shape[0]
    c_copies = []
    for r, pair in enumerate(((c00, c01), (c10, c11), (c20, c21), (c30, c31))):
        at = pl.multiple_of((q ^ r) * width, width)
        for i in range(2):
            dst = c_all.at[i, pl.ds(at, width), :]
            c_copies.append(pltpu.make_async_copy(pair[i], dst, c_sem.at[r, i]))
    start(c_copies)
    w_copies = [
        pltpu.make_async_copy(w, w_all.at[r, j], w_sem.at[r, j])
        for r, pair in enumerate(((wa0, wa1), (wb0, wb1), (wc0, wc1), (wd0, wd1)))
        for j, w in enumerate(pair)
    ]
    start(w_copies)
    column = as_column(scale[...])[:out.shape[0]]
    column = jnp.tile(column, (1, out.shape[1] // 128))
    wait(c_copies)
    rows = wa0.shape[1]
    for r in range(SLAB):
        for j in range(2):
            w_copies[2 * r + j].wait()
            slab = jnp.where(z // 2 == y, (z % 2) ^ j, jnp.where(z < 2, j, 1 - j))
            at = pl.multiple_of((slab * SLAB + (q ^ r)) * rows, 8)
            term = None
            for i in range(2):
                part = jnp.dot(w_all[r, j, i], c_all[i], preferred_element_type=jnp.float32)
                term = part if term is None else term + part
            total[pl.ds(at, rows), :] = term
    out[...] = (residual[...].astype(jnp.float32) + column * total[...]).astype(jnp.bfloat16)


def output(place, blocks, pieces, residual, scale):
    count = blocks[0].shape[1]
    rows, depth = pieces[0].shape[1:]
    share = residual.shape[0]
    scale = jnp.pad(scale, (0, -share % 128))[None]
    return pl.pallas_call(
        out_kernel,
        out_shape=jax.ShapeDtypeStruct((share, count), jnp.bfloat16),
        in_specs=[SMEM] + [HBM] * 16 + [VMEM] * 2,
        out_specs=VMEM,
        scratch_shapes=[
            pltpu.VMEM((2, depth, count), jnp.bfloat16),
            pltpu.VMEM((SLAB, 2, 2, rows, depth), jnp.bfloat16),
            pltpu.VMEM((share, count), jnp.float32),
            pltpu.SemaphoreType.DMA((SLAB, 2)),
            pltpu.SemaphoreType.DMA((SLAB, 2)),
        ],
        compiler_params=pltpu.CompilerParams(vmem_limit_bytes=KERNEL_VMEM),
        cost_estimate=pl.CostEstimate(
            flops=4 * share * count * depth,
            bytes_accessed=4 * share * depth,
            transcendentals=0,
        ),
        name="output",
    )(place, *blocks, *pieces, residual, scale)


def rows_of_slab(q, got):
    placed = []
    for b in range(SLAB):
        piece = got[b]
        for other in range(1, SLAB):
            piece = jnp.where(q == other, got[b ^ other], piece)
        placed.append(piece)
    return jnp.concatenate(placed, axis=1)


def slab_plan(tokens, norm_gain, qkv_weight, q_gain, k_gain, out_weight, layer_scale, segment_ids):
    count = tokens.shape[0]
    seq, tp = lax.axis_index("seq"), lax.axis_index("tp")
    slabs = lax.axis_size("seq") // SLAB
    z, q = seq // SLAB, seq % SLAB
    place = jnp.stack([z, q, tp]).astype(jnp.int32)
    width = qkv_weight.shape[2] // SLAB
    full_width = qkv_weight.shape[2] * lax.axis_size("tp")
    slab, half = SLAB * count, 2 * count
    inner, home = (z == 1) | (z == 2), z // 2 == tp

    by_kind = jnp.transpose(qkv_weight, (1, 0, 2))
    cut = [lax.dynamic_slice_in_dim(by_kind, (q ^ r) * width, width, 2) for r in range(SLAB)]
    got = [cut[0]] + [in_slab(cut[r], r) for r in range(1, SLAB)]
    x0, out_own = norm(tokens, norm_gain, slabs), jnp.transpose(out_weight)
    own = rows_of_slab(q, got)
    out_near, out_mid1 = even_pair(out_own), odd_pair(out_own)
    gains = [lax.dynamic_slice_in_dim(g, q * width, width, 0)[None] for g in (q_gain, k_gain)]

    def over_tp(close, far):
        keep, give = jnp.where(home, close, far), jnp.where(home, far, close)
        return keep, across(give)

    own, x0, out_near, out_mid1, *gains = tied(own, x0, out_near, out_mid1, *gains)
    near, middle1 = even_pair(own), odd_pair(own)
    out_end1, out_mid2 = even_pair(out_mid1), odd_pair(out_near)
    x2 = in_slab(x0, 2)
    out_end2 = even_pair(out_mid2)
    keep0, got0 = over_tp(out_own, jnp.where(inner, out_mid1, out_end1))
    near, middle1, x0, x2, keep0, got0, out_end2 = tied(
        near, middle1, x0, x2, keep0, got0, out_end2
    )
    end1, middle2 = even_pair(middle1), odd_pair(near)
    x1, x3 = in_slab(x0, 1), in_slab(x2, 1)
    x1, out_end2, keep0, got0 = tied(x1, out_end2, keep0, got0)
    wa0 = jnp.stack([keep0, got0])
    wc0 = in_slab(wa0, 2)
    keep1, got1 = over_tp(out_near, jnp.where(inner, out_mid2, out_end2))
    end1, middle2, x1, x3, wa0, wc0, keep1, got1 = tied(
        end1, middle2, x1, x3, wa0, wc0, keep1, got1
    )
    end2 = even_pair(middle2)
    wa1 = jnp.stack([keep1, got1])
    wc1 = in_slab(wa1, 2)
    wb0, wd0 = in_slab(wa0, 1), in_slab(wc0, 1)
    xs = (x0, x1, x2, x3)
    acc = early(place, xs, own, near, middle1, end1)
    wb1, wd1 = in_slab(wa1, 1), in_slab(wc1, 1)
    end2, acc, wb0, wd0, wb1, wd1 = tied(end2, acc, wb0, wd0, wb1, wd1)
    pieces = (wa0, wa1, wb0, wb1, wc0, wc1, wd0, wd1)

    query, keys, values, squares, even, odd = late(place, xs, acc, middle2, end2, *gains)
    sums = jnp.stack([squares, even_pair(squares), odd_pair(squares)])
    sums, even, odd = tied(sums, even, odd)
    even, odd = even_pair(even), odd_pair(odd)
    mine = sums
    for r in range(1, SLAB):
        mine = mine + in_slab(sums, r)
    other = across(mine)

    outside = jnp.full((half,), -1, jnp.int32)
    seg = jnp.concatenate([outside, segment_ids, outside], axis=0)
    seg = lax.dynamic_slice_in_dim(seg, z * slab, slab + 2 * half, 0)
    seg = seg.astype(jnp.float32)[None]
    blocks = attend(full_width, place, query, keys, values, even, odd, mine, other, seg)
    spread = []
    for r in range(SLAB):
        for i in range(2):
            to = functools.partial(lambda r, i, z, q, y: (z, q ^ r, y ^ i), r, i)
            spread.append(permuted(blocks[r], to) if r or i else blocks[r])

    share = layer_scale.shape[0]
    residual = jnp.transpose(lax.dynamic_slice_in_dim(tokens, tp * share, share, 1))
    return jnp.transpose(output(place, spread, pieces, residual, layer_scale))


def solution(mesh):
    def shards(*args):
        heads = args[2].shape[2] // HEAD_DIM
        slab = mesh.shape["seq"] == 16 and mesh.shape["tp"] == 2 and heads % SLAB == 0
        return (slab_plan if slab else row_plan)(*args)

    return jax.shard_map(
        shards,
        mesh=mesh,
        in_specs=(
            P("seq", None),
            P(),
            P("seq", None, "tp"),
            P("tp"),
            P("tp"),
            P("tp", "seq"),
            P("tp"),
            P(),
        ),
        out_specs=P("seq", "tp"),
        check_vma=False,
    )
```

```python
import functools
import math

import jax
import jax.numpy as jnp
from jax import lax
from jax.experimental import pallas as pl
from jax.experimental.pallas import tpu as pltpu
from jax.sharding import PartitionSpec as P

HEAD_DIM = 128
SLAB = 4

eps = 1e-06
floor_score = -1e30


def passed_along(x, axis, by):
    size = lax.axis_size(axis)
    pairs = [(i, i + by) for i in range(size) if 0 <= i + by < size]
    return lax.ppermute(x, axis, pairs)


def masked_scores(query, keys, query_seg, key_seg):
    scores = jnp.einsum(
        "qhd,khd->hqk", query, keys, preferred_element_type=jnp.float32
    ) * HEAD_DIM ** (-0.5)
    mask = (query_seg[:, None] == key_seg[None, :])[None]
    return (jnp.where(mask, scores, floor_score), mask)


def row_plan(tokens, norm_gain, qkv_weight, q_gain, k_gain, out_weight, layer_scale, segment_ids):
    count = tokens.shape[0]
    source = tokens.astype(jnp.float32)
    normed = (
        source * lax.rsqrt(jnp.mean(source * source, axis=-1, keepdims=True) + eps) * norm_gain
    ).astype(jnp.bfloat16)
    local_width = qkv_weight.shape[2]
    heads = local_width // HEAD_DIM
    joined = jnp.einsum(
        "td,dch->tch",
        normed,
        lax.all_gather(qkv_weight, "seq", axis=0, tiled=True),
        preferred_element_type=jnp.float32,
    )
    query = joined[:, 0]
    keys = joined[:, 1]
    values = joined[:, 2]
    query_sq, key_sq = lax.psum(
        (jnp.sum(query * query, axis=-1), jnp.sum(keys * keys, axis=-1)), "tp"
    )
    full_width = local_width * lax.axis_size("tp")
    query_normed = (query * lax.rsqrt(query_sq / full_width + eps)[:, None] * q_gain).astype(
        jnp.bfloat16
    )
    key_normed = (keys * lax.rsqrt(key_sq / full_width + eps)[:, None] * k_gain).astype(
        jnp.bfloat16
    )
    paired = jnp.stack([key_normed, values.astype(jnp.bfloat16)], axis=1)
    pieces = []
    for offset in (2, 1, 0, -1, -2):
        if offset == 0:
            pieces.append(paired)
        else:
            pieces.append(passed_along(paired, "seq", offset))
    widened = jnp.concatenate(pieces, axis=0)
    position = lax.axis_index("seq")
    outside = jnp.full((2 * count,), -1, jnp.int32)
    seg_pad = jnp.concatenate([outside, segment_ids, outside], axis=0)
    key_seg = lax.dynamic_slice_in_dim(seg_pad, position * count, 5 * count, 0)
    query_seg = lax.dynamic_slice_in_dim(segment_ids, position * count, count, 0)
    query_heads = query_normed.reshape(count, heads, HEAD_DIM)
    key_heads = widened[:, 0].reshape(5 * count, heads, HEAD_DIM)
    value_heads = widened[:, 1].reshape(5 * count, heads, HEAD_DIM)
    scores, mask = masked_scores(query_heads, key_heads, query_seg, key_seg)
    peak = jnp.max(scores, axis=-1, keepdims=True)
    weights = jnp.where(mask, jnp.exp(scores - peak), 0.0)
    total = jnp.sum(weights, axis=-1)
    probs = weights.astype(jnp.bfloat16)
    summed = jnp.einsum("hqk,khd->qhd", probs, value_heads, preferred_element_type=jnp.float32)
    context = (
        (summed / jnp.transpose(total)[:, :, None]).reshape(count, local_width).astype(jnp.bfloat16)
    )
    terms = jnp.dot(
        context,
        lax.all_gather(out_weight, "seq", axis=1, tiled=True),
        preferred_element_type=jnp.float32,
    )
    projected = lax.psum_scatter(terms, "tp", scatter_dimension=1, tiled=True)
    share = layer_scale.shape[0]
    residual = lax.dynamic_slice_in_dim(source, lax.axis_index("tp") * share, share, 1)
    return (residual + layer_scale * projected).astype(jnp.bfloat16)


ANY = pl.BlockSpec(memory_space=pl.ANY)
VMEM = pl.BlockSpec(memory_space=pltpu.VMEM)
SMEM = pl.BlockSpec(memory_space=pltpu.SMEM)
HBM = pl.BlockSpec(memory_space=pltpu.HBM)
KERNEL_VMEM = 60 * 1024 * 1024


def permuted(x, to):
    slabs, tps = lax.axis_size("seq") // SLAB, lax.axis_size("tp")
    pairs = []
    for i in range(slabs * SLAB * tps):
        z, q, y = to(i // (SLAB * tps), i // tps % SLAB, i % tps)
        pairs.append((i, (z * SLAB + q) * tps + y))
    return lax.ppermute(x, ("seq", "tp"), pairs)


def in_slab(x, flip):
    return permuted(x, lambda z, q, y: (z, q ^ flip, y))


def across(x):
    return permuted(x, lambda z, q, y: (z, q, 1 - y))


def even_pair(x):
    return permuted(x, lambda z, q, y: (z ^ 1, q, y))


def odd_pair(x):
    return permuted(x, lambda z, q, y: (3 - z, q, y) if z in (1, 2) else (z, q ^ 1, y))


def tied(*arrays):
    return lax.optimization_barrier(arrays)


def as_row(column):
    wide = jnp.broadcast_to(column, (column.shape[0], 128))
    return jnp.transpose(wide)[:8]


def as_column(row):
    return jnp.transpose(jnp.broadcast_to(row, (128, row.shape[1])))


def start(copies):
    for copy in copies:
        copy.start()


def wait(copies):
    for copy in copies:
        copy.wait()


def norm_kernel(tokens, gain, out):
    part = tokens.shape[1] // out.shape[0]
    source = tokens[...].astype(jnp.float32)
    mean = jnp.mean(source * source, axis=1, keepdims=True)
    normed = source * lax.rsqrt(mean + eps) * gain[...]
    for j in range(out.shape[0]):
        out[j, :, :part] = normed[:, j * part:(j + 1) * part].astype(jnp.bfloat16)
        out[j, :, part:] = jnp.zeros((out.shape[1], out.shape[2] - part), jnp.bfloat16)


def norm(tokens, gain, slabs):
    count, depth = tokens.shape
    shape = (slabs, count, pl.cdiv(depth // slabs, 128) * 128)
    return pl.pallas_call(
        norm_kernel,
        out_shape=jax.ShapeDtypeStruct(shape, jnp.bfloat16),
        in_specs=[VMEM, VMEM],
        out_specs=VMEM,
        compiler_params=pltpu.CompilerParams(vmem_limit_bytes=KERNEL_VMEM),
        name="norm",
    )(tokens, gain[None])


def far_slabs(z):
    return jnp.where(z < 2, 2, 1), jnp.where(z < 2, 3, 0)


def token_copies(xs, at, out, sems):
    return [
        pltpu.make_async_copy(x.at[at], out.at[r], sems.at[r]) for r, x in enumerate(xs)
    ]


def picked_copy(z, middle, end, out, sem, wait):
    inner = (z == 1) | (z == 2)

    @pl.when(inner)
    def _():
        copy = pltpu.make_async_copy(middle, out, sem)
        copy.wait() if wait else copy.start()

    @pl.when(jnp.logical_not(inner))
    def _():
        copy = pltpu.make_async_copy(end, out, sem)
        copy.wait() if wait else copy.start()


def early_kernel(
    place, xa, xb, xc, xd, own, near, middle, end, acc, x_all, w_all, held, x_sem, w_sem, sems,
):
    z = place[0]
    xs = (xa, xb, xc, xd)
    near_copy = pltpu.make_async_copy(near, w_all.at[1], w_sem.at[1])
    own_copy = pltpu.make_async_copy(own, w_all.at[0], w_sem.at[0])
    x_copies = [
        token_copies(xs, at, x_all.at[i], x_sem.at[i])
        for i, at in enumerate((z, z ^ 1, far_slabs(z)[0]))
    ]
    own_copy.start()
    start(x_copies[0])
    near_copy.start()
    start(x_copies[1])
    picked_copy(z, middle, end, w_all.at[2], w_sem.at[2], False)
    start(x_copies[2])
    kinds, rows = own.shape[:2]
    stores = []
    for step in range(3):
        if step < 2:
            (own_copy, near_copy)[step].wait()
        else:
            picked_copy(z, middle, end, w_all.at[2], w_sem.at[2], True)
        wait(x_copies[step])
        for r in range(SLAB):
            x = x_all[step, r][:, :rows]
            for kind in range(kinds):
                term = jnp.dot(x, w_all[step, kind], preferred_element_type=jnp.float32)
                held[r, kind] = term if step == 0 else held[r, kind] + term
            if step == 2:
                stores.append(pltpu.make_async_copy(held.at[r], acc.at[r], sems.at[r]))
                stores[-1].start()
    wait(stores)


def early(place, xs, own, near, middle, end):
    kinds, rows, width = own.shape
    slabs, count, wide = xs[0].shape
    return pl.pallas_call(
        early_kernel,
        out_shape=jax.ShapeDtypeStruct((SLAB, kinds, count, width), jnp.float32),
        in_specs=[SMEM] + [HBM] * 8,
        out_specs=HBM,
        scratch_shapes=[
            pltpu.VMEM((3, SLAB, count, wide), jnp.bfloat16),
            pltpu.VMEM((3, kinds, rows, width), jnp.bfloat16),
            pltpu.VMEM((SLAB, kinds, count, width), jnp.float32),
            pltpu.SemaphoreType.DMA((3, SLAB)),
            pltpu.SemaphoreType.DMA((3,)),
            pltpu.SemaphoreType.DMA((SLAB,)),
        ],
        compiler_params=pltpu.CompilerParams(vmem_limit_bytes=KERNEL_VMEM),
        cost_estimate=pl.CostEstimate(
            flops=6 * kinds * SLAB * count * rows * width,
            bytes_accessed=6 * kinds * rows * width + 6 * SLAB * count * rows,
            transcendentals=0,
        ),
        name="early",
    )(place, *xs, own, near, middle, end)


def late_kernel(
    place, xa, xb, xc, xd, acc, middle, end, q_gain, k_gain,
    query, keys, values, squares, even, odd,
    x_all, far, held, q_all, k_all, v_all, x_sem, w_sem, acc_sem, sems,
):
    z, q = place[0], place[1]
    picked_copy(z, middle, end, far, w_sem, False)
    copies = token_copies((xa, xb, xc, xd), far_slabs(z)[1], x_all, x_sem)
    loads = [pltpu.make_async_copy(acc.at[r], held.at[r], acc_sem.at[r]) for r in range(SLAB)]
    for r in range(SLAB):
        copies[r].start()
        loads[r].start()
    count = held.shape[2]
    stores = []
    picked_copy(z, middle, end, far, w_sem, True)
    for r in range(SLAB):
        copies[r].wait()
        loads[r].wait()
        x = x_all[r][:, :far.shape[1]]
        rows = pl.ds(pl.multiple_of((q ^ r) * count, count), count)
        for kind in range(3):
            part = held[r, kind] + jnp.dot(x, far[kind], preferred_element_type=jnp.float32)
            if kind < 2:
                summed = as_row(jnp.sum(part * part, axis=1, keepdims=True))
                squares[kind:kind + 1, rows] = summed[:1]
                part = part * (q_gain, k_gain)[kind][...]
            held_out, out = ((q_all, query), (k_all, keys), (v_all, values))[kind]
            held_out[rows, :] = part.astype(held_out.dtype)
            store = pltpu.make_async_copy(held_out.at[rows, :], out.at[rows, :], sems.at[3 * r + kind])
            store.start()
            stores.append(store)
    reach = even.shape[1]
    for n, (out, at) in enumerate(((even, 1 - z % 2), (odd, z % 2))):
        rows = pl.ds(pl.multiple_of(at * reach, reach), reach)
        for k, src in enumerate((k_all, v_all)):
            sem = sems.at[3 * SLAB + 2 * n + k]
            stores.append(pltpu.make_async_copy(src.at[rows, :], out.at[k], sem))
            stores[-1].start()
    wait(stores)


def late(place, xs, acc, middle, end, q_gain, k_gain):
    kinds, rows, width = middle.shape
    count, wide = xs[0].shape[1:]
    slab = SLAB * count
    f32, bf16 = jnp.float32, jnp.bfloat16
    return pl.pallas_call(
        late_kernel,
        out_shape=(
            jax.ShapeDtypeStruct((slab, width), f32),
            jax.ShapeDtypeStruct((slab, width), bf16),
            jax.ShapeDtypeStruct((slab, width), bf16),
            jax.ShapeDtypeStruct((2, slab), f32),
            jax.ShapeDtypeStruct((2, 2 * count, width), bf16),
            jax.ShapeDtypeStruct((2, 2 * count, width), bf16),
        ),
        in_specs=[SMEM] + [HBM] * 7 + [VMEM] * 2,
        out_specs=(HBM, HBM, HBM, VMEM, HBM, HBM),
        scratch_shapes=[
            pltpu.VMEM((SLAB, count, wide), bf16),
            pltpu.VMEM((kinds, rows, width), bf16),
            pltpu.VMEM((SLAB, kinds, count, width), f32),
            pltpu.VMEM((slab, width), f32),
            pltpu.VMEM((slab, width), bf16),
            pltpu.VMEM((slab, width), bf16),
            pltpu.SemaphoreType.DMA((SLAB,)),
            pltpu.SemaphoreType.DMA,
            pltpu.SemaphoreType.DMA((SLAB,)),
            pltpu.SemaphoreType.DMA((3 * SLAB + 4,)),
        ],
        compiler_params=pltpu.CompilerParams(vmem_limit_bytes=KERNEL_VMEM),
        cost_estimate=pl.CostEstimate(
            flops=2 * kinds * slab * rows * width,
            bytes_accessed=2 * kinds * rows * width + 2 * slab * rows,
            transcendentals=0,
        ),
        name="late",
    )(place, *xs, acc, middle, end, q_gain, k_gain)


def attend_kernel(
    full_width, place, query, keys, values, even, odd, mine, other, seg, o0, o1, o2, o3,
    q_all, k_all, v_all, k_turned, scale_all, sems,
):
    z, q = place[0], place[1]
    slab = query.shape[0]
    count = slab // SLAB
    half = even.shape[1]
    upper = half + slab
    is_even = z % 2 == 0
    even_at = pl.multiple_of(jnp.where(is_even, upper, 0), half)
    odd_at = pl.multiple_of(jnp.where(is_even, 0, upper), half)
    copies = [pltpu.make_async_copy(query, q_all, sems.at[0])]
    for k, (whole, out) in enumerate(((keys, k_all), (values, v_all))):
        for n, (src, at) in enumerate(((whole, half), (even.at[k], even_at), (odd.at[k], odd_at))):
            dst = out.at[pl.ds(at, src.shape[0]), :]
            copies.append(pltpu.make_async_copy(src, dst, sems.at[1 + 3 * k + n]))
    start(copies)
    scale = [lax.rsqrt((mine[n] + other[n]) / full_width + eps) for n in range(3)]
    scale_all[:, half:upper] = scale[0]
    scale_all[:, :half] = jnp.where(is_even, scale[2], scale[1])[:, slab - half:]
    scale_all[:, upper:] = jnp.where(is_even, scale[1], scale[2])[:, :half]
    wait(copies)
    for at in range(0, k_all.shape[0], count):
        k_turned[:, at:at + count] = jnp.transpose(k_all[at:at + count, :])
    window = count + 2 * half
    heads = query.shape[1] // HEAD_DIM
    factor = HEAD_DIM ** (-0.5) * math.log2(math.e)
    for r, out in ((2, o2), (3, o3), (1, o1), (0, o0)):
        begin = pl.multiple_of((q ^ r) * count, count)
        at_query = pl.multiple_of((q ^ r) * count + half, count)
        key_seg = seg[:, pl.ds(begin, window)]
        query_seg = as_column(seg[:, pl.ds(at_query, count)])
        k_scale = scale_all[1:2, pl.ds(begin, window)] * factor
        q_scale = as_column(scale_all[0:1, pl.ds(at_query, count)])
        mask = jnp.tile(query_seg, (1, window // 128)) == key_seg
        for h in range(heads):
            cols = slice(h * HEAD_DIM, (h + 1) * HEAD_DIM)
            q_low = (q_all[pl.ds(begin, count), cols] * q_scale).astype(jnp.bfloat16)
            scores = jnp.dot(
                q_low, k_turned[cols, pl.ds(begin, window)], preferred_element_type=jnp.float32
            )
            scores = jnp.where(mask, scores * k_scale, floor_score)
            peak = jnp.max(scores, axis=1, keepdims=True)
            weights = jnp.exp2(scores - peak)
            total = jnp.sum(weights, axis=1, keepdims=True)
            summed = jnp.dot(
                weights.astype(jnp.bfloat16), v_all[pl.ds(begin, window), cols],
                preferred_element_type=jnp.float32,
            )
            out[cols, :] = jnp.transpose(summed / total).astype(jnp.bfloat16)


def attend(full_width, place, query, keys, values, even, odd, mine, other, seg):
    slab, width = query.shape
    half = even.shape[1]
    count = slab // SLAB
    ext = slab + 2 * half
    bf16 = jnp.bfloat16
    window = count + 2 * half
    return pl.pallas_call(
        functools.partial(attend_kernel, full_width),
        out_shape=(jax.ShapeDtypeStruct((width, count), bf16),) * SLAB,
        in_specs=[SMEM] + [HBM] * 5 + [VMEM] * 3,
        out_specs=(VMEM,) * SLAB,
        scratch_shapes=[
            pltpu.VMEM((slab, width), jnp.float32),
            pltpu.VMEM((ext, width), bf16),
            pltpu.VMEM((ext, width), bf16),
            pltpu.VMEM((width, ext), bf16),
            pltpu.VMEM((2, ext), jnp.float32),
            pltpu.SemaphoreType.DMA((7,)),
        ],
        compiler_params=pltpu.CompilerParams(vmem_limit_bytes=KERNEL_VMEM),
        cost_estimate=pl.CostEstimate(
            flops=SLAB * 4 * count * window * width,
            bytes_accessed=4 * ext * width + 4 * slab * width,
            transcendentals=SLAB * count * window * width // HEAD_DIM,
        ),
        name="attend",
    )(place, query, keys, values, even, odd, mine, other, seg)


def out_kernel(
    place, c00, c01, c10, c11, c20, c21, c30, c31, wa0, wa1, wb0, wb1, wc0, wc1, wd0, wd1,
    residual, scale, out, c_all, w_all, total, placed, c_sem, w_sem,
):
    z, q, y = place[0], place[1], place[2]
    width = c00.shape[0]
    c_copies = []
    for r, pair in enumerate(((c00, c01), (c10, c11), (c20, c21), (c30, c31))):
        at = pl.multiple_of((q ^ r) * width, width)
        for i in range(2):
            dst = c_all.at[i, pl.ds(at, width), :]
            c_copies.append(pltpu.make_async_copy(pair[i], dst, c_sem.at[r, i]))
    start(c_copies)
    rows = wa0.shape[1]
    w_copies = []
    for r, pair in enumerate(((wa0, wa1), (wb0, wb1), (wc0, wc1), (wd0, wd1))):
        for j in range(2):
            for i in range(2):
                dst = w_all.at[i, pl.ds((2 * r + j) * rows, rows), :]
                w_copies.append(pltpu.make_async_copy(pair[j].at[i], dst, w_sem.at[r, j, i]))
    start(w_copies)
    column = as_column(scale[...])[:out.shape[0]]
    column = jnp.tile(column, (1, out.shape[1] // 128))
    wait(c_copies)
    wait(w_copies)
    total[...] = jnp.dot(w_all[0], c_all[0], preferred_element_type=jnp.float32)
    total[...] += jnp.dot(w_all[1], c_all[1], preferred_element_type=jnp.float32)
    kept = out.shape[0] // (2 * SLAB)
    for r in range(SLAB):
        for j in range(2):
            slab = jnp.where(z // 2 == y, (z % 2) ^ j, jnp.where(z < 2, j, 1 - j))
            at = pl.multiple_of((slab * SLAB + (q ^ r)) * kept, 8)
            begin = (2 * r + j) * rows
            placed[pl.ds(at, kept), :] = total[begin:begin + kept, :]
    out[...] = (residual[...].astype(jnp.float32) + column * placed[...]).astype(jnp.bfloat16)


def output(place, blocks, pieces, residual, scale):
    count = blocks[0].shape[1]
    rows, depth = pieces[0].shape[1:]
    share = residual.shape[0]
    scale = jnp.pad(scale, (0, -share % 128))[None]
    return pl.pallas_call(
        out_kernel,
        out_shape=jax.ShapeDtypeStruct((share, count), jnp.bfloat16),
        in_specs=[SMEM] + [HBM] * 16 + [VMEM] * 2,
        out_specs=VMEM,
        scratch_shapes=[
            pltpu.VMEM((2, depth, count), jnp.bfloat16),
            pltpu.VMEM((2, 2 * SLAB * rows, depth), jnp.bfloat16),
            pltpu.VMEM((2 * SLAB * rows, count), jnp.float32),
            pltpu.VMEM((share, count), jnp.float32),
            pltpu.SemaphoreType.DMA((SLAB, 2)),
            pltpu.SemaphoreType.DMA((SLAB, 2, 2)),
        ],
        compiler_params=pltpu.CompilerParams(vmem_limit_bytes=KERNEL_VMEM),
        cost_estimate=pl.CostEstimate(
            flops=4 * share * count * depth,
            bytes_accessed=4 * share * depth,
            transcendentals=0,
        ),
        name="output",
    )(place, *blocks, *pieces, residual, scale)


def rows_of_slab(q, got):
    placed = []
    for b in range(SLAB):
        piece = got[b]
        for other in range(1, SLAB):
            piece = jnp.where(q == other, got[b ^ other], piece)
        placed.append(piece)
    return jnp.concatenate(placed, axis=1)


def slab_plan(tokens, norm_gain, qkv_weight, q_gain, k_gain, out_weight, layer_scale, segment_ids):
    count = tokens.shape[0]
    seq, tp = lax.axis_index("seq"), lax.axis_index("tp")
    slabs = lax.axis_size("seq") // SLAB
    z, q = seq // SLAB, seq % SLAB
    place = jnp.stack([z, q, tp]).astype(jnp.int32)
    width = qkv_weight.shape[2] // SLAB
    full_width = qkv_weight.shape[2] * lax.axis_size("tp")
    slab, half = SLAB * count, 2 * count
    inner, home = (z == 1) | (z == 2), z // 2 == tp

    by_kind = jnp.transpose(qkv_weight, (1, 0, 2))
    cut = [lax.dynamic_slice_in_dim(by_kind, (q ^ r) * width, width, 2) for r in range(SLAB)]
    got = [cut[0]] + [in_slab(cut[r], r) for r in range(1, SLAB)]
    x0 = norm(tokens, norm_gain, slabs)
    out_own = jnp.pad(jnp.transpose(out_weight), ((0, -out_weight.shape[1] % 16), (0, 0)))
    own = rows_of_slab(q, got)
    out_near, out_mid1 = even_pair(out_own), odd_pair(out_own)
    out_end1, out_mid2 = even_pair(out_mid1), odd_pair(out_near)
    gains = [lax.dynamic_slice_in_dim(g, q * width, width, 0)[None] for g in (q_gain, k_gain)]

    def over_tp(close, far):
        keep, give = jnp.where(home, close, far), jnp.where(home, far, close)
        return keep, across(give)

    own, x0, out_end1, out_mid2, *gains = tied(own, x0, out_end1, out_mid2, *gains)
    near, middle1 = even_pair(own), odd_pair(own)
    x2 = in_slab(x0, 2)
    out_end2 = even_pair(out_mid2)
    keep0, got0 = over_tp(out_own, jnp.where(inner, out_mid1, out_end1))
    near, middle1, x0, x2, keep0, got0, out_end2 = tied(
        near, middle1, x0, x2, keep0, got0, out_end2
    )
    end1, middle2 = even_pair(middle1), odd_pair(near)
    x1, x3 = in_slab(x0, 1), in_slab(x2, 1)
    x1, out_end2, keep0, got0 = tied(x1, out_end2, keep0, got0)
    wa0 = jnp.stack([keep0, got0])
    wc0 = in_slab(wa0, 2)
    keep1, got1 = over_tp(out_near, jnp.where(inner, out_mid2, out_end2))
    end1, middle2, x1, x3, wa0, wc0, keep1, got1 = tied(
        end1, middle2, x1, x3, wa0, wc0, keep1, got1
    )
    end2 = even_pair(middle2)
    wa1 = jnp.stack([keep1, got1])
    wc1 = in_slab(wa1, 2)
    wb0, wd0 = in_slab(wa0, 1), in_slab(wc0, 1)
    xs = (x0, x1, x2, x3)
    acc = early(place, xs, own, near, middle1, end1)
    wb1, wd1 = in_slab(wa1, 1), in_slab(wc1, 1)
    end2, acc, wb0, wd0, wb1, wd1 = tied(end2, acc, wb0, wd0, wb1, wd1)
    pieces = (wa0, wa1, wb0, wb1, wc0, wc1, wd0, wd1)

    query, keys, values, squares, even, odd = late(place, xs, acc, middle2, end2, *gains)
    sums = jnp.stack([squares, even_pair(squares), odd_pair(squares)])
    sums, even, odd = tied(sums, even, odd)
    even, odd = even_pair(even), odd_pair(odd)
    mine = sums
    for r in range(1, SLAB):
        mine = mine + in_slab(sums, r)
    other = across(mine)

    outside = jnp.full((half,), -1, jnp.int32)
    seg = jnp.concatenate([outside, segment_ids, outside], axis=0)
    seg = lax.dynamic_slice_in_dim(seg, z * slab, slab + 2 * half, 0)
    seg = seg.astype(jnp.float32)[None]
    blocks = attend(full_width, place, query, keys, values, even, odd, mine, other, seg)
    spread = []
    for r in range(SLAB):
        for i in range(2):
            to = functools.partial(lambda r, i, z, q, y: (z, q ^ r, y ^ i), r, i)
            spread.append(permuted(blocks[r], to) if r or i else blocks[r])

    share = layer_scale.shape[0]
    residual = jnp.transpose(lax.dynamic_slice_in_dim(tokens, tp * share, share, 1))
    return jnp.transpose(output(place, spread, pieces, residual, layer_scale))


def solution(mesh):
    def shards(*args):
        heads = args[2].shape[2] // HEAD_DIM
        slab = mesh.shape["seq"] == 16 and mesh.shape["tp"] == 2 and heads % SLAB == 0
        return (slab_plan if slab else row_plan)(*args)

    return jax.shard_map(
        shards,
        mesh=mesh,
        in_specs=(
            P("seq", None),
            P(),
            P("seq", None, "tp"),
            P("tp"),
            P("tp"),
            P("tp", "seq"),
            P("tp"),
            P(),
        ),
        out_specs=P("seq", "tp"),
        check_vma=False,
    )
```

```python
import functools
import math

import jax
import jax.numpy as jnp
from jax import lax
from jax.experimental import pallas as pl
from jax.experimental.pallas import tpu as pltpu
from jax.sharding import PartitionSpec as P

HEAD_DIM = 128
SLAB = 4

eps = 1e-06
floor_score = -1e30


def passed_along(x, axis, by):
    size = lax.axis_size(axis)
    pairs = [(i, i + by) for i in range(size) if 0 <= i + by < size]
    return lax.ppermute(x, axis, pairs)


def masked_scores(query, keys, query_seg, key_seg):
    scores = jnp.einsum(
        "qhd,khd->hqk", query, keys, preferred_element_type=jnp.float32
    ) * HEAD_DIM ** (-0.5)
    mask = (query_seg[:, None] == key_seg[None, :])[None]
    return (jnp.where(mask, scores, floor_score), mask)


def row_plan(tokens, norm_gain, qkv_weight, q_gain, k_gain, out_weight, layer_scale, segment_ids):
    count = tokens.shape[0]
    source = tokens.astype(jnp.float32)
    normed = (
        source * lax.rsqrt(jnp.mean(source * source, axis=-1, keepdims=True) + eps) * norm_gain
    ).astype(jnp.bfloat16)
    local_width = qkv_weight.shape[2]
    heads = local_width // HEAD_DIM
    joined = jnp.einsum(
        "td,dch->tch",
        normed,
        lax.all_gather(qkv_weight, "seq", axis=0, tiled=True),
        preferred_element_type=jnp.float32,
    )
    query = joined[:, 0]
    keys = joined[:, 1]
    values = joined[:, 2]
    query_sq, key_sq = lax.psum(
        (jnp.sum(query * query, axis=-1), jnp.sum(keys * keys, axis=-1)), "tp"
    )
    full_width = local_width * lax.axis_size("tp")
    query_normed = (query * lax.rsqrt(query_sq / full_width + eps)[:, None] * q_gain).astype(
        jnp.bfloat16
    )
    key_normed = (keys * lax.rsqrt(key_sq / full_width + eps)[:, None] * k_gain).astype(
        jnp.bfloat16
    )
    paired = jnp.stack([key_normed, values.astype(jnp.bfloat16)], axis=1)
    pieces = []
    for offset in (2, 1, 0, -1, -2):
        if offset == 0:
            pieces.append(paired)
        else:
            pieces.append(passed_along(paired, "seq", offset))
    widened = jnp.concatenate(pieces, axis=0)
    position = lax.axis_index("seq")
    outside = jnp.full((2 * count,), -1, jnp.int32)
    seg_pad = jnp.concatenate([outside, segment_ids, outside], axis=0)
    key_seg = lax.dynamic_slice_in_dim(seg_pad, position * count, 5 * count, 0)
    query_seg = lax.dynamic_slice_in_dim(segment_ids, position * count, count, 0)
    query_heads = query_normed.reshape(count, heads, HEAD_DIM)
    key_heads = widened[:, 0].reshape(5 * count, heads, HEAD_DIM)
    value_heads = widened[:, 1].reshape(5 * count, heads, HEAD_DIM)
    scores, mask = masked_scores(query_heads, key_heads, query_seg, key_seg)
    peak = jnp.max(scores, axis=-1, keepdims=True)
    weights = jnp.where(mask, jnp.exp(scores - peak), 0.0)
    total = jnp.sum(weights, axis=-1)
    probs = weights.astype(jnp.bfloat16)
    summed = jnp.einsum("hqk,khd->qhd", probs, value_heads, preferred_element_type=jnp.float32)
    context = (
        (summed / jnp.transpose(total)[:, :, None]).reshape(count, local_width).astype(jnp.bfloat16)
    )
    terms = jnp.dot(
        context,
        lax.all_gather(out_weight, "seq", axis=1, tiled=True),
        preferred_element_type=jnp.float32,
    )
    projected = lax.psum_scatter(terms, "tp", scatter_dimension=1, tiled=True)
    share = layer_scale.shape[0]
    residual = lax.dynamic_slice_in_dim(source, lax.axis_index("tp") * share, share, 1)
    return (residual + layer_scale * projected).astype(jnp.bfloat16)


ANY = pl.BlockSpec(memory_space=pl.ANY)
VMEM = pl.BlockSpec(memory_space=pltpu.VMEM)
SMEM = pl.BlockSpec(memory_space=pltpu.SMEM)
HBM = pl.BlockSpec(memory_space=pltpu.HBM)
KERNEL_VMEM = 60 * 1024 * 1024


def permuted(x, to):
    slabs, tps = lax.axis_size("seq") // SLAB, lax.axis_size("tp")
    pairs = []
    for i in range(slabs * SLAB * tps):
        z, q, y = to(i // (SLAB * tps), i // tps % SLAB, i % tps)
        pairs.append((i, (z * SLAB + q) * tps + y))
    return lax.ppermute(x, ("seq", "tp"), pairs)


def in_slab(x, flip):
    return permuted(x, lambda z, q, y: (z, q ^ flip, y))


def across(x):
    return permuted(x, lambda z, q, y: (z, q, 1 - y))


def even_pair(x):
    return permuted(x, lambda z, q, y: (z ^ 1, q, y))


def odd_pair(x):
    return permuted(x, lambda z, q, y: (3 - z, q, y) if z in (1, 2) else (z, q ^ 1, y))


def tied(*arrays):
    return lax.optimization_barrier(arrays)


def as_row(column):
    wide = jnp.broadcast_to(column, (column.shape[0], 128))
    return jnp.transpose(wide)[:8]


def as_column(row):
    return jnp.transpose(jnp.broadcast_to(row, (128, row.shape[1])))


def start(copies):
    for copy in copies:
        copy.start()


def wait(copies):
    for copy in copies:
        copy.wait()


def norm_kernel(tokens, gain, out):
    part = tokens.shape[1] // out.shape[0]
    source = tokens[...].astype(jnp.float32)
    mean = jnp.mean(source * source, axis=1, keepdims=True)
    normed = source * lax.rsqrt(mean + eps) * gain[...]
    for j in range(out.shape[0]):
        out[j, :, :part] = normed[:, j * part:(j + 1) * part].astype(jnp.bfloat16)
        out[j, :, part:] = jnp.zeros((out.shape[1], out.shape[2] - part), jnp.bfloat16)


def norm(tokens, gain, slabs):
    count, depth = tokens.shape
    shape = (slabs, count, pl.cdiv(depth // slabs, 128) * 128)
    return pl.pallas_call(
        norm_kernel,
        out_shape=jax.ShapeDtypeStruct(shape, jnp.bfloat16),
        in_specs=[VMEM, VMEM],
        out_specs=VMEM,
        compiler_params=pltpu.CompilerParams(vmem_limit_bytes=KERNEL_VMEM),
        name="norm",
    )(tokens, gain[None])


def far_slabs(z):
    return jnp.where(z < 2, 2, 1), jnp.where(z < 2, 3, 0)


def token_copies(xs, at, out, sems):
    return [
        pltpu.make_async_copy(x.at[at], out.at[r], sems.at[r]) for r, x in enumerate(xs)
    ]


def picked_copy(z, middle, end, out, sem, wait):
    inner = (z == 1) | (z == 2)

    @pl.when(inner)
    def _():
        copy = pltpu.make_async_copy(middle, out, sem)
        copy.wait() if wait else copy.start()

    @pl.when(jnp.logical_not(inner))
    def _():
        copy = pltpu.make_async_copy(end, out, sem)
        copy.wait() if wait else copy.start()


def early_kernel(
    place, xa, xb, xc, xd, own, near, middle, end, acc, x_all, w_all, held, x_sem, w_sem, sems,
):
    z = place[0]
    xs = (xa, xb, xc, xd)
    near_copy = pltpu.make_async_copy(near, w_all.at[1], w_sem.at[1])
    own_copy = pltpu.make_async_copy(own, w_all.at[0], w_sem.at[0])
    x_copies = [
        token_copies(xs, at, x_all.at[i], x_sem.at[i])
        for i, at in enumerate((z, z ^ 1, far_slabs(z)[0]))
    ]
    own_copy.start()
    start(x_copies[0])
    near_copy.start()
    start(x_copies[1])
    picked_copy(z, middle, end, w_all.at[2], w_sem.at[2], False)
    start(x_copies[2])
    kinds, rows = own.shape[:2]
    stores = []
    for step in range(3):
        if step < 2:
            (own_copy, near_copy)[step].wait()
        else:
            picked_copy(z, middle, end, w_all.at[2], w_sem.at[2], True)
        wait(x_copies[step])
        for r in range(SLAB):
            x = x_all[step, r][:, :rows]
            for kind in range(kinds):
                term = jnp.dot(x, w_all[step, kind], preferred_element_type=jnp.float32)
                held[r, kind] = term if step == 0 else held[r, kind] + term
            if step == 2:
                stores.append(pltpu.make_async_copy(held.at[r], acc.at[r], sems.at[r]))
                stores[-1].start()
    wait(stores)


def early(place, xs, own, near, middle, end):
    kinds, rows, width = own.shape
    slabs, count, wide = xs[0].shape
    return pl.pallas_call(
        early_kernel,
        out_shape=jax.ShapeDtypeStruct((SLAB, kinds, count, width), jnp.float32),
        in_specs=[SMEM] + [HBM] * 8,
        out_specs=HBM,
        scratch_shapes=[
            pltpu.VMEM((3, SLAB, count, wide), jnp.bfloat16),
            pltpu.VMEM((3, kinds, rows, width), jnp.bfloat16),
            pltpu.VMEM((SLAB, kinds, count, width), jnp.float32),
            pltpu.SemaphoreType.DMA((3, SLAB)),
            pltpu.SemaphoreType.DMA((3,)),
            pltpu.SemaphoreType.DMA((SLAB,)),
        ],
        compiler_params=pltpu.CompilerParams(vmem_limit_bytes=KERNEL_VMEM),
        cost_estimate=pl.CostEstimate(
            flops=6 * kinds * SLAB * count * rows * width,
            bytes_accessed=6 * kinds * rows * width + 6 * SLAB * count * rows,
            transcendentals=0,
        ),
        name="early",
    )(place, *xs, own, near, middle, end)


def last_step(place, xs, acc, middle, end, kinds, x_all, far, held, x_sem, w_sem, acc_sem, use):
    z = place[0]
    picked_copy(z, middle, end, far, w_sem, False)
    copies = token_copies(xs, far_slabs(z)[1], x_all, x_sem)
    loads = [
        pltpu.make_async_copy(acc.at[r, pl.ds(kinds[0], len(kinds))], held.at[r], acc_sem.at[r])
        for r in range(SLAB)
    ]
    for r in range(SLAB):
        copies[r].start()
        loads[r].start()
    picked_copy(z, middle, end, far, w_sem, True)
    for r in range(SLAB):
        copies[r].wait()
        loads[r].wait()
        x = x_all[r][:, :far.shape[1]]
        for n, kind in enumerate(kinds):
            use(r, kind, held[r, n] + jnp.dot(x, far[n], preferred_element_type=jnp.float32))


def block_rows(place, r, count):
    return pl.ds(pl.multiple_of((place[1] ^ r) * count, count), count)


def halo_copies(place, src, even, odd, sems):
    z, reach = place[0], even.shape[0]
    return [
        pltpu.make_async_copy(
            src.at[pl.ds(pl.multiple_of(at * reach, reach), reach), :], out, sems.at[n]
        )
        for n, (out, at) in enumerate(((even, 1 - z % 2), (odd, z % 2)))
    ]


def late_qk_kernel(
    place, xa, xb, xc, xd, acc, middle, end, q_gain, k_gain, query, keys, even, odd, squares,
    x_all, far, held, q_all, k_all, x_sem, w_sem, acc_sem, sems, halo_sems,
):
    count = held.shape[2]
    stores = []

    def use(r, kind, part):
        rows = block_rows(place, r, count)
        squares[kind:kind + 1, rows] = as_row(jnp.sum(part * part, axis=1, keepdims=True))[:1]
        gain, whole, out = ((q_gain, q_all, query), (k_gain, k_all, keys))[kind]
        whole[rows, :] = (part * gain[...]).astype(whole.dtype)
        sem = sems.at[r, kind]
        stores.append(pltpu.make_async_copy(whole.at[rows, :], out.at[rows, :], sem))
        stores[-1].start()

    last_step(
        place, (xa, xb, xc, xd), acc, middle, end, (0, 1), x_all, far, held, x_sem, w_sem, acc_sem, use
    )
    halo = halo_copies(place, k_all, even, odd, halo_sems)
    start(halo)
    wait(stores + halo)


def late_v_kernel(
    place, xa, xb, xc, xd, acc, middle, end, values, even, odd,
    x_all, far, held, v_all, x_sem, w_sem, acc_sem, sems, halo_sems,
):
    count = held.shape[2]
    stores = []

    def use(r, kind, part):
        rows = block_rows(place, r, count)
        v_all[rows, :] = part.astype(v_all.dtype)
        stores.append(pltpu.make_async_copy(v_all.at[rows, :], values.at[rows, :], sems.at[r, 0]))
        stores[-1].start()

    last_step(
        place, (xa, xb, xc, xd), acc, middle, end, (2,), x_all, far, held, x_sem, w_sem, acc_sem, use
    )
    halo = halo_copies(place, v_all, even, odd, halo_sems)
    start(halo)
    wait(stores + halo)


def late(kernel, place, xs, acc, middle, end, gains):
    kinds, rows, width = middle.shape
    count, wide = xs[0].shape[1:]
    slab, reach = SLAB * count, 2 * count
    f32, bf16 = jnp.float32, jnp.bfloat16
    types = (f32, bf16) if gains else (bf16,)
    return pl.pallas_call(
        kernel,
        out_shape=tuple(jax.ShapeDtypeStruct((slab, width), t) for t in types)
        + (jax.ShapeDtypeStruct((reach, width), bf16),) * 2
        + ((jax.ShapeDtypeStruct((2, slab), f32),) if gains else ()),
        in_specs=[SMEM] + [HBM] * 7 + [VMEM] * len(gains),
        out_specs=(HBM,) * (len(types) + 2) + ((VMEM,) if gains else ()),
        scratch_shapes=[
            pltpu.VMEM((SLAB, count, wide), bf16),
            pltpu.VMEM((kinds, rows, width), bf16),
            pltpu.VMEM((SLAB, kinds, count, width), f32),
            *[pltpu.VMEM((slab, width), t) for t in types],
            pltpu.SemaphoreType.DMA((SLAB,)),
            pltpu.SemaphoreType.DMA,
            pltpu.SemaphoreType.DMA((SLAB,)),
            pltpu.SemaphoreType.DMA((SLAB, len(types))),
            pltpu.SemaphoreType.DMA((2,)),
        ],
        compiler_params=pltpu.CompilerParams(vmem_limit_bytes=KERNEL_VMEM),
        cost_estimate=pl.CostEstimate(
            flops=2 * kinds * slab * rows * width,
            bytes_accessed=2 * kinds * rows * width + 2 * slab * rows,
            transcendentals=0,
        ),
        name=kernel.__name__,
    )(place, *xs, acc, middle, end, *gains)


def attend_kernel(
    full_width, place, query, keys, k_even, k_odd, values, v_even, v_odd, mine, near, mid, seg,
    o0, o1, o2, o3,
    q_all, k_all, v_all, k_turned, scale_all, sems,
):
    z, q = place[0], place[1]
    slab = query.shape[0]
    count = slab // SLAB
    half = k_even.shape[0]
    upper = half + slab
    is_even = z % 2 == 0
    even_at = pl.multiple_of(jnp.where(is_even, upper, 0), half)
    odd_at = pl.multiple_of(jnp.where(is_even, 0, upper), half)
    copies = [pltpu.make_async_copy(query, q_all, sems.at[0])]
    for k, (whole, even, odd, out) in enumerate(
        ((keys, k_even, k_odd, k_all), (values, v_even, v_odd, v_all))
    ):
        for n, (src, at) in enumerate(((whole, half), (even, even_at), (odd, odd_at))):
            dst = out.at[pl.ds(at, src.shape[0]), :]
            copies.append(pltpu.make_async_copy(src, dst, sems.at[1 + 3 * k + n]))
    start(copies)
    scale = [lax.rsqrt(sums[...] / full_width + eps) for sums in (mine, near, mid)]
    scale_all[:, half:upper] = scale[0]
    scale_all[:, :half] = jnp.where(is_even, scale[2], scale[1])[:, slab - half:]
    scale_all[:, upper:] = jnp.where(is_even, scale[1], scale[2])[:, :half]
    wait(copies)
    for at in range(0, k_all.shape[0], count):
        k_turned[:, at:at + count] = jnp.transpose(k_all[at:at + count, :])
    window = count + 2 * half
    heads = query.shape[1] // HEAD_DIM
    factor = HEAD_DIM ** (-0.5) * math.log2(math.e)
    for r, out in ((2, o2), (3, o3), (1, o1), (0, o0)):
        begin = pl.multiple_of((q ^ r) * count, count)
        at_query = pl.multiple_of((q ^ r) * count + half, count)
        key_seg = seg[:, pl.ds(begin, window)]
        query_seg = as_column(seg[:, pl.ds(at_query, count)])
        k_scale = scale_all[1:2, pl.ds(begin, window)] * factor
        q_scale = as_column(scale_all[0:1, pl.ds(at_query, count)])
        mask = jnp.tile(query_seg, (1, window // 128)) == key_seg
        for h in range(heads):
            cols = slice(h * HEAD_DIM, (h + 1) * HEAD_DIM)
            q_low = (q_all[pl.ds(begin, count), cols] * q_scale).astype(jnp.bfloat16)
            scores = jnp.dot(
                q_low, k_turned[cols, pl.ds(begin, window)], preferred_element_type=jnp.float32
            )
            scores = jnp.where(mask, scores * k_scale, floor_score)
            peak = jnp.max(scores, axis=1, keepdims=True)
            weights = jnp.exp2(scores - peak)
            total = jnp.sum(weights, axis=1, keepdims=True)
            summed = jnp.dot(
                weights.astype(jnp.bfloat16), v_all[pl.ds(begin, window), cols],
                preferred_element_type=jnp.float32,
            )
            out[cols, :] = jnp.transpose(summed / total).astype(jnp.bfloat16)


def attend(full_width, place, query, keys, k_even, k_odd, values, v_even, v_odd, sums, seg):
    slab, width = query.shape
    half = k_even.shape[0]
    count = slab // SLAB
    ext = slab + 2 * half
    bf16 = jnp.bfloat16
    window = count + 2 * half
    return pl.pallas_call(
        functools.partial(attend_kernel, full_width),
        out_shape=(jax.ShapeDtypeStruct((width, count), bf16),) * SLAB,
        in_specs=[SMEM] + [HBM] * 7 + [VMEM] * 4,
        out_specs=(VMEM,) * SLAB,
        scratch_shapes=[
            pltpu.VMEM((slab, width), jnp.float32),
            pltpu.VMEM((ext, width), bf16),
            pltpu.VMEM((ext, width), bf16),
            pltpu.VMEM((width, ext), bf16),
            pltpu.VMEM((2, ext), jnp.float32),
            pltpu.SemaphoreType.DMA((7,)),
        ],
        compiler_params=pltpu.CompilerParams(vmem_limit_bytes=KERNEL_VMEM),
        cost_estimate=pl.CostEstimate(
            flops=SLAB * 4 * count * window * width,
            bytes_accessed=4 * ext * width + 4 * slab * width,
            transcendentals=SLAB * count * window * width // HEAD_DIM,
        ),
        name="attend",
    )(place, query, keys, k_even, k_odd, values, v_even, v_odd, *sums, seg)


def out_kernel(
    place, c00, c01, c10, c11, c20, c21, c30, c31, wa0, wa1, wb0, wb1, wc0, wc1, wd0, wd1,
    residual, scale, out, c_all, w_all, total, placed, c_sem, w_sem,
):
    z, q, y = place[0], place[1], place[2]
    width = c00.shape[0]
    c_copies = []
    for r, pair in enumerate(((c00, c01), (c10, c11), (c20, c21), (c30, c31))):
        at = pl.multiple_of((q ^ r) * width, width)
        for i in range(2):
            dst = c_all.at[i, pl.ds(at, width), :]
            c_copies.append(pltpu.make_async_copy(pair[i], dst, c_sem.at[r, i]))
    start(c_copies)
    rows = wa0.shape[1]
    w_copies = []
    for r, pair in enumerate(((wa0, wa1), (wb0, wb1), (wc0, wc1), (wd0, wd1))):
        for j in range(2):
            for i in range(2):
                dst = w_all.at[i, pl.ds((2 * r + j) * rows, rows), :]
                w_copies.append(pltpu.make_async_copy(pair[j].at[i], dst, w_sem.at[r, j, i]))
    start(w_copies)
    column = as_column(scale[...])[:out.shape[0]]
    column = jnp.tile(column, (1, out.shape[1] // 128))
    wait(c_copies)
    wait(w_copies)
    total[...] = jnp.dot(w_all[0], c_all[0], preferred_element_type=jnp.float32)
    total[...] += jnp.dot(w_all[1], c_all[1], preferred_element_type=jnp.float32)
    kept = out.shape[0] // (2 * SLAB)
    for r in range(SLAB):
        for j in range(2):
            slab = jnp.where(z // 2 == y, (z % 2) ^ j, jnp.where(z < 2, j, 1 - j))
            at = pl.multiple_of((slab * SLAB + (q ^ r)) * kept, 8)
            begin = (2 * r + j) * rows
            placed[pl.ds(at, kept), :] = total[begin:begin + kept, :]
    out[...] = (residual[...].astype(jnp.float32) + column * placed[...]).astype(jnp.bfloat16)


def output(place, blocks, pieces, residual, scale):
    count = blocks[0].shape[1]
    rows, depth = pieces[0].shape[1:]
    share = residual.shape[0]
    scale = jnp.pad(scale, (0, -share % 128))[None]
    return pl.pallas_call(
        out_kernel,
        out_shape=jax.ShapeDtypeStruct((share, count), jnp.bfloat16),
        in_specs=[SMEM] + [HBM] * 16 + [VMEM] * 2,
        out_specs=VMEM,
        scratch_shapes=[
            pltpu.VMEM((2, depth, count), jnp.bfloat16),
            pltpu.VMEM((2, 2 * SLAB * rows, depth), jnp.bfloat16),
            pltpu.VMEM((2 * SLAB * rows, count), jnp.float32),
            pltpu.VMEM((share, count), jnp.float32),
            pltpu.SemaphoreType.DMA((SLAB, 2)),
            pltpu.SemaphoreType.DMA((SLAB, 2, 2)),
        ],
        compiler_params=pltpu.CompilerParams(vmem_limit_bytes=KERNEL_VMEM),
        cost_estimate=pl.CostEstimate(
            flops=4 * share * count * depth,
            bytes_accessed=4 * share * depth,
            transcendentals=0,
        ),
        name="output",
    )(place, *blocks, *pieces, residual, scale)


def rows_of_slab(q, got):
    placed = []
    for b in range(SLAB):
        piece = got[b]
        for other in range(1, SLAB):
            piece = jnp.where(q == other, got[b ^ other], piece)
        placed.append(piece)
    return jnp.concatenate(placed, axis=1)


def slab_plan(tokens, norm_gain, qkv_weight, q_gain, k_gain, out_weight, layer_scale, segment_ids):
    count = tokens.shape[0]
    seq, tp = lax.axis_index("seq"), lax.axis_index("tp")
    slabs = lax.axis_size("seq") // SLAB
    z, q = seq // SLAB, seq % SLAB
    place = jnp.stack([z, q, tp]).astype(jnp.int32)
    width = qkv_weight.shape[2] // SLAB
    full_width = qkv_weight.shape[2] * lax.axis_size("tp")
    slab, half = SLAB * count, 2 * count
    inner, home = (z == 1) | (z == 2), z // 2 == tp

    by_kind = jnp.transpose(qkv_weight, (1, 0, 2))
    cut = [lax.dynamic_slice_in_dim(by_kind, (q ^ r) * width, width, 2) for r in range(SLAB)]
    got = [cut[0]] + [in_slab(cut[r], r) for r in range(1, SLAB)]
    x0 = norm(tokens, norm_gain, slabs)
    out_own = jnp.pad(jnp.transpose(out_weight), ((0, -out_weight.shape[1] % 16), (0, 0)))
    own = rows_of_slab(q, got)
    out_near, out_mid1 = even_pair(out_own), odd_pair(out_own)
    out_end1, out_mid2 = even_pair(out_mid1), odd_pair(out_near)
    gains = [lax.dynamic_slice_in_dim(g, q * width, width, 0)[None] for g in (q_gain, k_gain)]

    def over_tp(close, far):
        keep, give = jnp.where(home, close, far), jnp.where(home, far, close)
        return keep, across(give)

    own, x0, out_end1, out_mid2, *gains = tied(own, x0, out_end1, out_mid2, *gains)
    near, middle1 = even_pair(own), odd_pair(own)
    x2 = in_slab(x0, 2)
    out_end2 = even_pair(out_mid2)
    keep0, got0 = over_tp(out_own, jnp.where(inner, out_mid1, out_end1))
    near, middle1, x0, x2, keep0, got0, out_end2 = tied(
        near, middle1, x0, x2, keep0, got0, out_end2
    )
    end1, middle2 = even_pair(middle1), odd_pair(near)
    x1, x3 = in_slab(x0, 1), in_slab(x2, 1)
    x1, out_end2, keep0, got0 = tied(x1, out_end2, keep0, got0)
    wa0 = jnp.stack([keep0, got0])
    wc0 = in_slab(wa0, 2)
    keep1, got1 = over_tp(out_near, jnp.where(inner, out_mid2, out_end2))
    end1, middle2, x1, x3, wa0, wc0, keep1, got1 = tied(
        end1, middle2, x1, x3, wa0, wc0, keep1, got1
    )
    middle2 = middle2[:2], middle2[2:]
    end2_qk, end2_v = even_pair(middle2[0]), even_pair(middle2[1])
    wa1 = jnp.stack([keep1, got1])
    wc1 = in_slab(wa1, 2)
    wb0, wd0 = in_slab(wa0, 1), in_slab(wc0, 1)
    xs = (x0, x1, x2, x3)
    acc = early(place, xs, own, near, middle1, end1)
    acc, wc1, wa1 = tied(acc, wc1, wa1)
    wb1, wd1 = in_slab(wa1, 1), in_slab(wc1, 1)
    end2_qk, acc, wb0, wd0, wb1, wd1 = tied(end2_qk, acc, wb0, wd0, wb1, wd1)
    pieces = (wa0, wa1, wb0, wb1, wc0, wc1, wd0, wd1)

    query, keys, k_even, k_odd, squares = late(
        late_qk_kernel, place, xs, acc, middle2[0], end2_qk, gains
    )
    sums = squares
    for r in range(1, SLAB):
        sums = sums + in_slab(squares, r)
    sums = sums + across(sums)
    sums, k_even, k_odd, end2_v, acc = tied(sums, k_even, k_odd, end2_v, acc)
    k_even, k_odd = even_pair(k_even), odd_pair(k_odd)
    values, v_even, v_odd = late(late_v_kernel, place, xs, acc, middle2[1], end2_v, ())
    v_even, v_odd = even_pair(v_even), odd_pair(v_odd)
    sums = (sums, even_pair(sums), odd_pair(sums))

    outside = jnp.full((half,), -1, jnp.int32)
    seg = jnp.concatenate([outside, segment_ids, outside], axis=0)
    seg = lax.dynamic_slice_in_dim(seg, z * slab, slab + 2 * half, 0)
    seg = seg.astype(jnp.float32)[None]
    blocks = attend(
        full_width, place, query, keys, k_even, k_odd, values, v_even, v_odd, sums, seg
    )
    spread = []
    for r in range(SLAB):
        for i in range(2):
            to = functools.partial(lambda r, i, z, q, y: (z, q ^ r, y ^ i), r, i)
            spread.append(permuted(blocks[r], to) if r or i else blocks[r])

    share = layer_scale.shape[0]
    residual = jnp.transpose(lax.dynamic_slice_in_dim(tokens, tp * share, share, 1))
    return jnp.transpose(output(place, spread, pieces, residual, layer_scale))


def solution(mesh):
    def shards(*args):
        heads = args[2].shape[2] // HEAD_DIM
        slab = mesh.shape["seq"] == 16 and mesh.shape["tp"] == 2 and heads % SLAB == 0
        return (slab_plan if slab else row_plan)(*args)

    return jax.shard_map(
        shards,
        mesh=mesh,
        in_specs=(
            P("seq", None),
            P(),
            P("seq", None, "tp"),
            P("tp"),
            P("tp"),
            P("tp", "seq"),
            P("tp"),
            P(),
        ),
        out_specs=P("seq", "tp"),
        check_vma=False,
    )
```

```python
import functools
import math

import jax
import jax.numpy as jnp
from jax import lax
from jax.experimental import pallas as pl
from jax.experimental.pallas import tpu as pltpu
from jax.sharding import PartitionSpec as P

HEAD_DIM = 128
SLAB = 4

eps = 1e-06
floor_score = -1e30


def passed_along(x, axis, by):
    size = lax.axis_size(axis)
    pairs = [(i, i + by) for i in range(size) if 0 <= i + by < size]
    return lax.ppermute(x, axis, pairs)


def masked_scores(query, keys, query_seg, key_seg):
    scores = jnp.einsum(
        "qhd,khd->hqk", query, keys, preferred_element_type=jnp.float32
    ) * HEAD_DIM ** (-0.5)
    mask = (query_seg[:, None] == key_seg[None, :])[None]
    return (jnp.where(mask, scores, floor_score), mask)


def row_plan(tokens, norm_gain, qkv_weight, q_gain, k_gain, out_weight, layer_scale, segment_ids):
    count = tokens.shape[0]
    source = tokens.astype(jnp.float32)
    normed = (
        source * lax.rsqrt(jnp.mean(source * source, axis=-1, keepdims=True) + eps) * norm_gain
    ).astype(jnp.bfloat16)
    local_width = qkv_weight.shape[2]
    heads = local_width // HEAD_DIM
    joined = jnp.einsum(
        "td,dch->tch",
        normed,
        lax.all_gather(qkv_weight, "seq", axis=0, tiled=True),
        preferred_element_type=jnp.float32,
    )
    query = joined[:, 0]
    keys = joined[:, 1]
    values = joined[:, 2]
    query_sq, key_sq = lax.psum(
        (jnp.sum(query * query, axis=-1), jnp.sum(keys * keys, axis=-1)), "tp"
    )
    full_width = local_width * lax.axis_size("tp")
    query_normed = (query * lax.rsqrt(query_sq / full_width + eps)[:, None] * q_gain).astype(
        jnp.bfloat16
    )
    key_normed = (keys * lax.rsqrt(key_sq / full_width + eps)[:, None] * k_gain).astype(
        jnp.bfloat16
    )
    paired = jnp.stack([key_normed, values.astype(jnp.bfloat16)], axis=1)
    pieces = []
    for offset in (2, 1, 0, -1, -2):
        if offset == 0:
            pieces.append(paired)
        else:
            pieces.append(passed_along(paired, "seq", offset))
    widened = jnp.concatenate(pieces, axis=0)
    position = lax.axis_index("seq")
    outside = jnp.full((2 * count,), -1, jnp.int32)
    seg_pad = jnp.concatenate([outside, segment_ids, outside], axis=0)
    key_seg = lax.dynamic_slice_in_dim(seg_pad, position * count, 5 * count, 0)
    query_seg = lax.dynamic_slice_in_dim(segment_ids, position * count, count, 0)
    query_heads = query_normed.reshape(count, heads, HEAD_DIM)
    key_heads = widened[:, 0].reshape(5 * count, heads, HEAD_DIM)
    value_heads = widened[:, 1].reshape(5 * count, heads, HEAD_DIM)
    scores, mask = masked_scores(query_heads, key_heads, query_seg, key_seg)
    peak = jnp.max(scores, axis=-1, keepdims=True)
    weights = jnp.where(mask, jnp.exp(scores - peak), 0.0)
    total = jnp.sum(weights, axis=-1)
    probs = weights.astype(jnp.bfloat16)
    summed = jnp.einsum("hqk,khd->qhd", probs, value_heads, preferred_element_type=jnp.float32)
    context = (
        (summed / jnp.transpose(total)[:, :, None]).reshape(count, local_width).astype(jnp.bfloat16)
    )
    terms = jnp.dot(
        context,
        lax.all_gather(out_weight, "seq", axis=1, tiled=True),
        preferred_element_type=jnp.float32,
    )
    projected = lax.psum_scatter(terms, "tp", scatter_dimension=1, tiled=True)
    share = layer_scale.shape[0]
    residual = lax.dynamic_slice_in_dim(source, lax.axis_index("tp") * share, share, 1)
    return (residual + layer_scale * projected).astype(jnp.bfloat16)


ANY = pl.BlockSpec(memory_space=pl.ANY)
VMEM = pl.BlockSpec(memory_space=pltpu.VMEM)
SMEM = pl.BlockSpec(memory_space=pltpu.SMEM)
HBM = pl.BlockSpec(memory_space=pltpu.HBM)
KERNEL_VMEM = 60 * 1024 * 1024


def permuted(x, to):
    slabs, tps = lax.axis_size("seq") // SLAB, lax.axis_size("tp")
    pairs = []
    for i in range(slabs * SLAB * tps):
        z, q, y = to(i // (SLAB * tps), i // tps % SLAB, i % tps)
        pairs.append((i, (z * SLAB + q) * tps + y))
    return lax.ppermute(x, ("seq", "tp"), pairs)


def in_slab(x, flip):
    return permuted(x, lambda z, q, y: (z, q ^ flip, y))


def across(x):
    return permuted(x, lambda z, q, y: (z, q, 1 - y))


def even_pair(x):
    return permuted(x, lambda z, q, y: (z ^ 1, q, y))


def odd_pair(x):
    return permuted(x, lambda z, q, y: (3 - z, q, y) if z in (1, 2) else (z, q ^ 1, y))


def tied(*arrays):
    return lax.optimization_barrier(arrays)


def as_row(column):
    wide = jnp.broadcast_to(column, (column.shape[0], 128))
    return jnp.transpose(wide)[:8]


def as_column(row):
    return jnp.transpose(jnp.broadcast_to(row, (128, row.shape[1])))


def start(copies):
    for copy in copies:
        copy.start()


def wait(copies):
    for copy in copies:
        copy.wait()


def norm_kernel(tokens, gain, out):
    part = tokens.shape[1] // out.shape[0]
    source = tokens[...].astype(jnp.float32)
    mean = jnp.mean(source * source, axis=1, keepdims=True)
    normed = source * lax.rsqrt(mean + eps) * gain[...]
    for j in range(out.shape[0]):
        out[j, :, :part] = normed[:, j * part:(j + 1) * part].astype(jnp.bfloat16)
        out[j, :, part:] = jnp.zeros((out.shape[1], out.shape[2] - part), jnp.bfloat16)


def norm(tokens, gain, slabs):
    count, depth = tokens.shape
    shape = (slabs, count, pl.cdiv(depth // slabs, 128) * 128)
    return pl.pallas_call(
        norm_kernel,
        out_shape=jax.ShapeDtypeStruct(shape, jnp.bfloat16),
        in_specs=[VMEM, VMEM],
        out_specs=VMEM,
        compiler_params=pltpu.CompilerParams(vmem_limit_bytes=KERNEL_VMEM),
        name="norm",
    )(tokens, gain[None])


def far_slabs(z):
    return jnp.where(z < 2, 2, 1), jnp.where(z < 2, 3, 0)


def token_copies(xs, at, out, sems):
    return [
        pltpu.make_async_copy(x.at[at], out.at[r], sems.at[r]) for r, x in enumerate(xs)
    ]


def picked_copy(z, middle, end, out, sem, wait):
    inner = (z == 1) | (z == 2)

    @pl.when(inner)
    def _():
        copy = pltpu.make_async_copy(middle, out, sem)
        copy.wait() if wait else copy.start()

    @pl.when(jnp.logical_not(inner))
    def _():
        copy = pltpu.make_async_copy(end, out, sem)
        copy.wait() if wait else copy.start()


def blank_tail(w, rows):
    tail = w.shape[-2] - rows
    w[..., rows:, :] = jnp.zeros(w.shape[:-2] + (tail, w.shape[-1]), w.dtype)


def early_kernel(
    place, xa, xb, xc, xd, own, near, middle, end, acc, x_all, w_all, held, x_sem, w_sem, sems,
):
    z = place[0]
    xs = (xa, xb, xc, xd)
    kinds, rows = own.shape[:2]
    taken = pl.ds(0, rows)
    near_copy = pltpu.make_async_copy(near, w_all.at[1, :, taken, :], w_sem.at[1])
    own_copy = pltpu.make_async_copy(own, w_all.at[0, :, taken, :], w_sem.at[0])
    x_copies = [
        token_copies(xs, at, x_all.at[i], x_sem.at[i])
        for i, at in enumerate((z, z ^ 1, far_slabs(z)[0]))
    ]
    own_copy.start()
    start(x_copies[0])
    near_copy.start()
    start(x_copies[1])
    picked_copy(z, middle, end, w_all.at[2, :, taken, :], w_sem.at[2], False)
    start(x_copies[2])
    blank_tail(w_all, rows)
    stores = []
    for step in range(3):
        if step < 2:
            (own_copy, near_copy)[step].wait()
        else:
            picked_copy(z, middle, end, w_all.at[2, :, taken, :], w_sem.at[2], True)
        wait(x_copies[step])
        for r in range(SLAB):
            x = x_all[step, r]
            for kind in range(kinds):
                term = jnp.dot(x, w_all[step, kind], preferred_element_type=jnp.float32)
                held[r, kind] = term if step == 0 else held[r, kind] + term
            if step == 2:
                stores.append(pltpu.make_async_copy(held.at[r], acc.at[r], sems.at[r]))
                stores[-1].start()
    wait(stores)


def early(place, xs, own, near, middle, end):
    kinds, rows, width = own.shape
    slabs, count, wide = xs[0].shape
    return pl.pallas_call(
        early_kernel,
        out_shape=jax.ShapeDtypeStruct((SLAB, kinds, count, width), jnp.float32),
        in_specs=[SMEM] + [HBM] * 8,
        out_specs=HBM,
        scratch_shapes=[
            pltpu.VMEM((3, SLAB, count, wide), jnp.bfloat16),
            pltpu.VMEM((3, kinds, wide, width), jnp.bfloat16),
            pltpu.VMEM((SLAB, kinds, count, width), jnp.float32),
            pltpu.SemaphoreType.DMA((3, SLAB)),
            pltpu.SemaphoreType.DMA((3,)),
            pltpu.SemaphoreType.DMA((SLAB,)),
        ],
        compiler_params=pltpu.CompilerParams(vmem_limit_bytes=KERNEL_VMEM),
        cost_estimate=pl.CostEstimate(
            flops=6 * kinds * SLAB * count * rows * width,
            bytes_accessed=6 * kinds * rows * width + 6 * SLAB * count * rows,
            transcendentals=0,
        ),
        name="early",
    )(place, *xs, own, near, middle, end)


def late_kernel(
    place, xa, xb, xc, xd, acc, middle, end, q_gain, k_gain,
    query, keys, values, squares, even, odd,
    x_all, far, held, q_all, k_all, v_all, x_sem, w_sem, acc_sem, sems,
):
    z, q = place[0], place[1]
    taken = far.at[:, pl.ds(0, middle.shape[1]), :]
    picked_copy(z, middle, end, taken, w_sem, False)
    copies = token_copies((xa, xb, xc, xd), far_slabs(z)[1], x_all, x_sem)
    loads = [pltpu.make_async_copy(acc.at[r], held.at[r], acc_sem.at[r]) for r in range(SLAB)]
    for r in range(SLAB):
        copies[r].start()
        loads[r].start()
    count = held.shape[2]
    stores = []
    blank_tail(far, middle.shape[1])
    picked_copy(z, middle, end, taken, w_sem, True)
    for r in range(SLAB):
        copies[r].wait()
        loads[r].wait()
        x = x_all[r]
        rows = pl.ds(pl.multiple_of((q ^ r) * count, count), count)
        for kind in range(3):
            part = held[r, kind] + jnp.dot(x, far[kind], preferred_element_type=jnp.float32)
            if kind < 2:
                summed = as_row(jnp.sum(part * part, axis=1, keepdims=True))
                squares[kind:kind + 1, rows] = summed[:1]
                part = part * (q_gain, k_gain)[kind][...]
            held_out, out = ((q_all, query), (k_all, keys), (v_all, values))[kind]
            held_out[rows, :] = part.astype(held_out.dtype)
            store = pltpu.make_async_copy(held_out.at[rows, :], out.at[rows, :], sems.at[3 * r + kind])
            store.start()
            stores.append(store)
    reach = even.shape[1]
    for n, (out, at) in enumerate(((even, 1 - z % 2), (odd, z % 2))):
        rows = pl.ds(pl.multiple_of(at * reach, reach), reach)
        for k, src in enumerate((k_all, v_all)):
            sem = sems.at[3 * SLAB + 2 * n + k]
            stores.append(pltpu.make_async_copy(src.at[rows, :], out.at[k], sem))
            stores[-1].start()
    wait(stores)


def late(place, xs, acc, middle, end, q_gain, k_gain):
    kinds, rows, width = middle.shape
    count, wide = xs[0].shape[1:]
    slab = SLAB * count
    f32, bf16 = jnp.float32, jnp.bfloat16
    return pl.pallas_call(
        late_kernel,
        out_shape=(
            jax.ShapeDtypeStruct((slab, width), f32),
            jax.ShapeDtypeStruct((slab, width), bf16),
            jax.ShapeDtypeStruct((slab, width), bf16),
            jax.ShapeDtypeStruct((2, slab), f32),
            jax.ShapeDtypeStruct((2, 2 * count, width), bf16),
            jax.ShapeDtypeStruct((2, 2 * count, width), bf16),
        ),
        in_specs=[SMEM] + [HBM] * 7 + [VMEM] * 2,
        out_specs=(HBM, HBM, HBM, VMEM, HBM, HBM),
        scratch_shapes=[
            pltpu.VMEM((SLAB, count, wide), bf16),
            pltpu.VMEM((kinds, wide, width), bf16),
            pltpu.VMEM((SLAB, kinds, count, width), f32),
            pltpu.VMEM((slab, width), f32),
            pltpu.VMEM((slab, width), bf16),
            pltpu.VMEM((slab, width), bf16),
            pltpu.SemaphoreType.DMA((SLAB,)),
            pltpu.SemaphoreType.DMA,
            pltpu.SemaphoreType.DMA((SLAB,)),
            pltpu.SemaphoreType.DMA((3 * SLAB + 4,)),
        ],
        compiler_params=pltpu.CompilerParams(vmem_limit_bytes=KERNEL_VMEM),
        cost_estimate=pl.CostEstimate(
            flops=2 * kinds * slab * rows * width,
            bytes_accessed=2 * kinds * rows * width + 2 * slab * rows,
            transcendentals=0,
        ),
        name="late",
    )(place, *xs, acc, middle, end, q_gain, k_gain)


def attend_kernel(
    full_width, place, query, keys, values, even, odd, mine, near, mid, seg, o0, o1, o2, o3,
    q_all, k_all, v_all, k_turned, scale_all, sems,
):
    z, q = place[0], place[1]
    slab = query.shape[0]
    count = slab // SLAB
    half = even.shape[1]
    upper = half + slab
    is_even = z % 2 == 0
    even_at = pl.multiple_of(jnp.where(is_even, upper, 0), half)
    odd_at = pl.multiple_of(jnp.where(is_even, 0, upper), half)
    copies = [pltpu.make_async_copy(query, q_all, sems.at[0])]
    for k, (whole, out) in enumerate(((keys, k_all), (values, v_all))):
        for n, (src, at) in enumerate(((whole, half), (even.at[k], even_at), (odd.at[k], odd_at))):
            dst = out.at[pl.ds(at, src.shape[0]), :]
            copies.append(pltpu.make_async_copy(src, dst, sems.at[1 + 3 * k + n]))
    start(copies)
    scale = [lax.rsqrt(sums[...] / full_width + eps) for sums in (mine, near, mid)]
    scale_all[:, half:upper] = scale[0]
    scale_all[:, :half] = jnp.where(is_even, scale[2], scale[1])[:, slab - half:]
    scale_all[:, upper:] = jnp.where(is_even, scale[1], scale[2])[:, :half]
    wait(copies)
    for at in range(0, k_all.shape[0], count):
        k_turned[:, at:at + count] = jnp.transpose(k_all[at:at + count, :])
    window = count + 2 * half
    heads = query.shape[1] // HEAD_DIM
    factor = HEAD_DIM ** (-0.5) * math.log2(math.e)
    for r, out in ((2, o2), (3, o3), (1, o1), (0, o0)):
        begin = pl.multiple_of((q ^ r) * count, count)
        at_query = pl.multiple_of((q ^ r) * count + half, count)
        key_seg = seg[:, pl.ds(begin, window)]
        query_seg = as_column(seg[:, pl.ds(at_query, count)])
        k_scale = scale_all[1:2, pl.ds(begin, window)] * factor
        q_scale = as_column(scale_all[0:1, pl.ds(at_query, count)])
        mask = jnp.tile(query_seg, (1, window // 128)) == key_seg
        for h in range(heads):
            cols = slice(h * HEAD_DIM, (h + 1) * HEAD_DIM)
            q_low = (q_all[pl.ds(begin, count), cols] * q_scale).astype(jnp.bfloat16)
            scores = jnp.dot(
                q_low, k_turned[cols, pl.ds(begin, window)], preferred_element_type=jnp.float32
            )
            scores = jnp.where(mask, scores * k_scale, floor_score)
            peak = jnp.max(scores, axis=1, keepdims=True)
            weights = jnp.exp2(scores - peak)
            total = jnp.sum(weights, axis=1, keepdims=True)
            summed = jnp.dot(
                weights.astype(jnp.bfloat16), v_all[pl.ds(begin, window), cols],
                preferred_element_type=jnp.float32,
            )
            out[cols, :] = jnp.transpose(summed / total).astype(jnp.bfloat16)


def attend(full_width, place, query, keys, values, even, odd, sums, seg):
    slab, width = query.shape
    half = even.shape[1]
    count = slab // SLAB
    ext = slab + 2 * half
    bf16 = jnp.bfloat16
    window = count + 2 * half
    return pl.pallas_call(
        functools.partial(attend_kernel, full_width),
        out_shape=(jax.ShapeDtypeStruct((width, count), bf16),) * SLAB,
        in_specs=[SMEM] + [HBM] * 5 + [VMEM] * 4,
        out_specs=(VMEM,) * SLAB,
        scratch_shapes=[
            pltpu.VMEM((slab, width), jnp.float32),
            pltpu.VMEM((ext, width), bf16),
            pltpu.VMEM((ext, width), bf16),
            pltpu.VMEM((width, ext), bf16),
            pltpu.VMEM((2, ext), jnp.float32),
            pltpu.SemaphoreType.DMA((7,)),
        ],
        compiler_params=pltpu.CompilerParams(vmem_limit_bytes=KERNEL_VMEM),
        cost_estimate=pl.CostEstimate(
            flops=SLAB * 4 * count * window * width,
            bytes_accessed=4 * ext * width + 4 * slab * width,
            transcendentals=SLAB * count * window * width // HEAD_DIM,
        ),
        name="attend",
    )(place, query, keys, values, even, odd, *sums, seg)


def out_kernel(
    place, c20, c01, c31, c30, c11, c21, c10, c00, wa0, wa1, wb0, wb1, wc0, wc1, wd0, wd1,
    residual, scale, out, c_all, w_all, total, placed, c_sem, w_sem,
):
    z, q, y = place[0], place[1], place[2]
    width = c00.shape[0]
    c_copies = []
    for i in range(2):
        for r, pair in enumerate(((c00, c01), (c10, c11), (c20, c21), (c30, c31))):
            at = pl.multiple_of((q ^ r) * width, width)
            dst = c_all.at[i, pl.ds(at, width), :]
            c_copies.append(pltpu.make_async_copy(pair[i], dst, c_sem.at[r, i]))
    start(c_copies)
    rows = wa0.shape[1]
    w_copies = []
    for i in range(2):
        for r, pair in enumerate(((wa0, wa1), (wb0, wb1), (wc0, wc1), (wd0, wd1))):
            for j in range(2):
                dst = w_all.at[i, pl.ds((2 * r + j) * rows, rows), :]
                w_copies.append(pltpu.make_async_copy(pair[j].at[i], dst, w_sem.at[r, j, i]))
    start(w_copies)
    column = as_column(scale[...])[:out.shape[0]]
    column = jnp.tile(column, (1, out.shape[1] // 128))
    wait(c_copies[:SLAB] + w_copies[:2 * SLAB])
    total[...] = jnp.dot(w_all[0], c_all[0], preferred_element_type=jnp.float32)
    wait(c_copies[SLAB:] + w_copies[2 * SLAB:])
    total[...] += jnp.dot(w_all[1], c_all[1], preferred_element_type=jnp.float32)
    kept = out.shape[0] // (2 * SLAB)
    for r in range(SLAB):
        for j in range(2):
            slab = jnp.where(z // 2 == y, (z % 2) ^ j, jnp.where(z < 2, j, 1 - j))
            at = pl.multiple_of((slab * SLAB + (q ^ r)) * kept, 8)
            begin = (2 * r + j) * rows
            placed[pl.ds(at, kept), :] = total[begin:begin + kept, :]
    out[...] = (residual[...].astype(jnp.float32) + column * placed[...]).astype(jnp.bfloat16)


def output(place, blocks, pieces, residual, scale):
    count = blocks[0].shape[1]
    rows, depth = pieces[0].shape[1:]
    share = residual.shape[0]
    scale = jnp.pad(scale, (0, -share % 128))[None]
    return pl.pallas_call(
        out_kernel,
        out_shape=jax.ShapeDtypeStruct((share, count), jnp.bfloat16),
        in_specs=[SMEM] + [HBM] * 16 + [VMEM] * 2,
        out_specs=VMEM,
        scratch_shapes=[
            pltpu.VMEM((2, depth, count), jnp.bfloat16),
            pltpu.VMEM((2, 2 * SLAB * rows, depth), jnp.bfloat16),
            pltpu.VMEM((2 * SLAB * rows, count), jnp.float32),
            pltpu.VMEM((share, count), jnp.float32),
            pltpu.SemaphoreType.DMA((SLAB, 2)),
            pltpu.SemaphoreType.DMA((SLAB, 2, 2)),
        ],
        compiler_params=pltpu.CompilerParams(vmem_limit_bytes=KERNEL_VMEM),
        cost_estimate=pl.CostEstimate(
            flops=4 * share * count * depth,
            bytes_accessed=4 * share * depth,
            transcendentals=0,
        ),
        name="output",
    )(place, *blocks, *pieces, residual, scale)


def rows_of_slab(q, got):
    placed = []
    for b in range(SLAB):
        piece = got[b]
        for other in range(1, SLAB):
            piece = jnp.where(q == other, got[b ^ other], piece)
        placed.append(piece)
    return jnp.concatenate(placed, axis=1)


def slab_plan(tokens, norm_gain, qkv_weight, q_gain, k_gain, out_weight, layer_scale, segment_ids):
    count = tokens.shape[0]
    seq, tp = lax.axis_index("seq"), lax.axis_index("tp")
    slabs = lax.axis_size("seq") // SLAB
    z, q = seq // SLAB, seq % SLAB
    place = jnp.stack([z, q, tp]).astype(jnp.int32)
    width = qkv_weight.shape[2] // SLAB
    full_width = qkv_weight.shape[2] * lax.axis_size("tp")
    slab, half = SLAB * count, 2 * count
    inner, home = (z == 1) | (z == 2), z // 2 == tp

    by_kind = jnp.transpose(qkv_weight, (1, 0, 2))
    cut = [lax.dynamic_slice_in_dim(by_kind, (q ^ r) * width, width, 2) for r in range(SLAB)]
    got = [cut[0]] + [in_slab(cut[r], r) for r in range(1, SLAB)]
    x0 = norm(tokens, norm_gain, slabs)
    out_own = jnp.pad(jnp.transpose(out_weight), ((0, -out_weight.shape[1] % 16), (0, 0)))
    own = rows_of_slab(q, got)
    out_near, out_mid1 = even_pair(out_own), odd_pair(out_own)
    out_end1, out_mid2 = even_pair(out_mid1), odd_pair(out_near)
    gains = [lax.dynamic_slice_in_dim(g, q * width, width, 0)[None] for g in (q_gain, k_gain)]

    def over_tp(close, far):
        keep, give = jnp.where(home, close, far), jnp.where(home, far, close)
        return keep, across(give)

    own, x0, out_end1, out_mid2, *gains = tied(own, x0, out_end1, out_mid2, *gains)
    near, middle1 = even_pair(own), odd_pair(own)
    x2 = in_slab(x0, 2)
    out_end2 = even_pair(out_mid2)
    keep0, got0 = over_tp(out_own, jnp.where(inner, out_mid1, out_end1))
    near, middle1, x0, x2, keep0, got0, out_end2 = tied(
        near, middle1, x0, x2, keep0, got0, out_end2
    )
    end1, middle2 = even_pair(middle1), odd_pair(near)
    x1, x3 = in_slab(x0, 1), in_slab(x2, 1)
    x1, out_end2, keep0, got0 = tied(x1, out_end2, keep0, got0)
    wa0 = jnp.stack([keep0, got0])
    wc0 = in_slab(wa0, 2)
    keep1, got1 = over_tp(out_near, jnp.where(inner, out_mid2, out_end2))
    end1, middle2, x1, x3, wa0, wc0, keep1, got1 = tied(
        end1, middle2, x1, x3, wa0, wc0, keep1, got1
    )
    end2 = even_pair(middle2)
    wa1 = jnp.stack([keep1, got1])
    wc1 = in_slab(wa1, 2)
    wb0, wd0 = in_slab(wa0, 1), in_slab(wc0, 1)
    xs = (x0, x1, x2, x3)
    acc = early(place, xs, own, near, middle1, end1)
    acc, wc1, wa1 = tied(acc, wc1, wa1)
    wb1, wd1 = in_slab(wa1, 1), in_slab(wc1, 1)
    end2, acc, wb0, wd0, wb1, wd1 = tied(end2, acc, wb0, wd0, wb1, wd1)
    pieces = (wa0, wa1, wb0, wb1, wc0, wc1, wd0, wd1)

    query, keys, values, squares, even, odd = late(place, xs, acc, middle2, end2, *gains)
    even, odd = even_pair(even), odd_pair(odd)
    sums = squares
    for r in range(1, SLAB):
        sums = sums + in_slab(squares, r)
    sums = sums + across(sums)
    sums = (sums, even_pair(sums), odd_pair(sums))

    outside = jnp.full((half,), -1, jnp.int32)
    seg = jnp.concatenate([outside, segment_ids, outside], axis=0)
    seg = lax.dynamic_slice_in_dim(seg, z * slab, slab + 2 * half, 0)
    seg = seg.astype(jnp.float32)[None]
    blocks = attend(full_width, place, query, keys, values, even, odd, sums, seg)
    spread = []
    for r, i in ((2, 0), (0, 1), (3, 1), (3, 0), (1, 1), (2, 1), (1, 0), (0, 0)):
        to = functools.partial(lambda r, i, z, q, y: (z, q ^ r, y ^ i), r, i)
        spread.append(permuted(blocks[r], to) if r or i else blocks[r])

    share = layer_scale.shape[0]
    residual = jnp.transpose(lax.dynamic_slice_in_dim(tokens, tp * share, share, 1))
    return jnp.transpose(output(place, spread, pieces, residual, layer_scale))


def solution(mesh):
    def shards(*args):
        heads = args[2].shape[2] // HEAD_DIM
        slab = mesh.shape["seq"] == 16 and mesh.shape["tp"] == 2 and heads % SLAB == 0
        return (slab_plan if slab else row_plan)(*args)

    return jax.shard_map(
        shards,
        mesh=mesh,
        in_specs=(
            P("seq", None),
            P(),
            P("seq", None, "tp"),
            P("tp"),
            P("tp"),
            P("tp", "seq"),
            P("tp"),
            P(),
        ),
        out_specs=P("seq", "tp"),
        check_vma=False,
    )
```

```python
import functools
import math

import jax
import jax.numpy as jnp
from jax import lax
from jax.experimental import pallas as pl
from jax.experimental.pallas import tpu as pltpu
from jax.sharding import PartitionSpec as P

HEAD_DIM = 128
SLAB = 4

eps = 1e-06
floor_score = -1e30


def passed_along(x, axis, by):
    size = lax.axis_size(axis)
    pairs = [(i, i + by) for i in range(size) if 0 <= i + by < size]
    return lax.ppermute(x, axis, pairs)


def masked_scores(query, keys, query_seg, key_seg):
    scores = jnp.einsum(
        "qhd,khd->hqk", query, keys, preferred_element_type=jnp.float32
    ) * HEAD_DIM ** (-0.5)
    mask = (query_seg[:, None] == key_seg[None, :])[None]
    return (jnp.where(mask, scores, floor_score), mask)


def row_plan(tokens, norm_gain, qkv_weight, q_gain, k_gain, out_weight, layer_scale, segment_ids):
    count = tokens.shape[0]
    source = tokens.astype(jnp.float32)
    normed = (
        source * lax.rsqrt(jnp.mean(source * source, axis=-1, keepdims=True) + eps) * norm_gain
    ).astype(jnp.bfloat16)
    local_width = qkv_weight.shape[2]
    heads = local_width // HEAD_DIM
    joined = jnp.einsum(
        "td,dch->tch",
        normed,
        lax.all_gather(qkv_weight, "seq", axis=0, tiled=True),
        preferred_element_type=jnp.float32,
    )
    query = joined[:, 0]
    keys = joined[:, 1]
    values = joined[:, 2]
    query_sq, key_sq = lax.psum(
        (jnp.sum(query * query, axis=-1), jnp.sum(keys * keys, axis=-1)), "tp"
    )
    full_width = local_width * lax.axis_size("tp")
    query_normed = (query * lax.rsqrt(query_sq / full_width + eps)[:, None] * q_gain).astype(
        jnp.bfloat16
    )
    key_normed = (keys * lax.rsqrt(key_sq / full_width + eps)[:, None] * k_gain).astype(
        jnp.bfloat16
    )
    paired = jnp.stack([key_normed, values.astype(jnp.bfloat16)], axis=1)
    pieces = []
    for offset in (2, 1, 0, -1, -2):
        if offset == 0:
            pieces.append(paired)
        else:
            pieces.append(passed_along(paired, "seq", offset))
    widened = jnp.concatenate(pieces, axis=0)
    position = lax.axis_index("seq")
    outside = jnp.full((2 * count,), -1, jnp.int32)
    seg_pad = jnp.concatenate([outside, segment_ids, outside], axis=0)
    key_seg = lax.dynamic_slice_in_dim(seg_pad, position * count, 5 * count, 0)
    query_seg = lax.dynamic_slice_in_dim(segment_ids, position * count, count, 0)
    query_heads = query_normed.reshape(count, heads, HEAD_DIM)
    key_heads = widened[:, 0].reshape(5 * count, heads, HEAD_DIM)
    value_heads = widened[:, 1].reshape(5 * count, heads, HEAD_DIM)
    scores, mask = masked_scores(query_heads, key_heads, query_seg, key_seg)
    peak = jnp.max(scores, axis=-1, keepdims=True)
    weights = jnp.where(mask, jnp.exp(scores - peak), 0.0)
    total = jnp.sum(weights, axis=-1)
    probs = weights.astype(jnp.bfloat16)
    summed = jnp.einsum("hqk,khd->qhd", probs, value_heads, preferred_element_type=jnp.float32)
    context = (
        (summed / jnp.transpose(total)[:, :, None]).reshape(count, local_width).astype(jnp.bfloat16)
    )
    terms = jnp.dot(
        context,
        lax.all_gather(out_weight, "seq", axis=1, tiled=True),
        preferred_element_type=jnp.float32,
    )
    projected = lax.psum_scatter(terms, "tp", scatter_dimension=1, tiled=True)
    share = layer_scale.shape[0]
    residual = lax.dynamic_slice_in_dim(source, lax.axis_index("tp") * share, share, 1)
    return (residual + layer_scale * projected).astype(jnp.bfloat16)


ANY = pl.BlockSpec(memory_space=pl.ANY)
VMEM = pl.BlockSpec(memory_space=pltpu.VMEM)
SMEM = pl.BlockSpec(memory_space=pltpu.SMEM)
HBM = pl.BlockSpec(memory_space=pltpu.HBM)
KERNEL_VMEM = 60 * 1024 * 1024


def permuted(x, to):
    slabs, tps = lax.axis_size("seq") // SLAB, lax.axis_size("tp")
    pairs = []
    for i in range(slabs * SLAB * tps):
        z, q, y = to(i // (SLAB * tps), i // tps % SLAB, i % tps)
        pairs.append((i, (z * SLAB + q) * tps + y))
    return lax.ppermute(x, ("seq", "tp"), pairs)


def in_slab(x, flip):
    return permuted(x, lambda z, q, y: (z, q ^ flip, y))


def across(x):
    return permuted(x, lambda z, q, y: (z, q, 1 - y))


def even_pair(x):
    return permuted(x, lambda z, q, y: (z ^ 1, q, y))


def odd_pair(x):
    return permuted(x, lambda z, q, y: (3 - z, q, y) if z in (1, 2) else (z, q ^ 1, y))


def half_pair(x):
    return permuted(x, lambda z, q, y: (z ^ 2, q, y))


def tied(*arrays):
    return lax.optimization_barrier(arrays)


def as_row(column):
    wide = jnp.broadcast_to(column, (column.shape[0], 128))
    return jnp.transpose(wide)[:8]


def as_column(row):
    return jnp.transpose(jnp.broadcast_to(row, (128, row.shape[1])))


def start(copies):
    for copy in copies:
        copy.start()


def wait(copies):
    for copy in copies:
        copy.wait()


def norm_kernel(tokens, gain, out):
    part = tokens.shape[1] // out.shape[0]
    source = tokens[...].astype(jnp.float32)
    mean = jnp.mean(source * source, axis=1, keepdims=True)
    normed = source * lax.rsqrt(mean + eps) * gain[...]
    for j in range(out.shape[0]):
        out[j, :, :part] = normed[:, j * part:(j + 1) * part].astype(jnp.bfloat16)
        out[j, :, part:] = jnp.zeros((out.shape[1], out.shape[2] - part), jnp.bfloat16)


def norm(tokens, gain, slabs):
    count, depth = tokens.shape
    shape = (slabs, count, pl.cdiv(depth // slabs, 128) * 128)
    return pl.pallas_call(
        norm_kernel,
        out_shape=jax.ShapeDtypeStruct(shape, jnp.bfloat16),
        in_specs=[VMEM, VMEM],
        out_specs=VMEM,
        compiler_params=pltpu.CompilerParams(vmem_limit_bytes=KERNEL_VMEM),
        name="norm",
    )(tokens, gain[None])


def token_copies(xs, at, out, sems):
    return [
        pltpu.make_async_copy(x.at[at], out.at[r], sems.at[r]) for r, x in enumerate(xs)
    ]


def blank_tail(w, rows):
    tail = w.shape[-2] - rows
    w[..., rows:, :] = jnp.zeros(w.shape[:-2] + (tail, w.shape[-1]), w.dtype)


def early_kernel(
    place, xa, xb, xc, xd, own, near, far, acc, x_all, w_all, held, x_sem, w_sem, sems,
):
    z = place[0]
    kinds, rows = own.shape[:2]
    copies = []
    for i, w in enumerate((own, near, far)):
        dst = w_all.at[i, :, pl.ds(0, rows), :]
        copies.append([pltpu.make_async_copy(w, dst, w_sem.at[i])])
        copies[i] += token_copies((xa, xb, xc, xd), z ^ i, x_all.at[i], x_sem.at[i])
        start(copies[i])
    blank_tail(w_all, rows)
    stores = []
    for step in range(3):
        wait(copies[step])
        for r in range(SLAB):
            x = x_all[step, r]
            for kind in range(kinds):
                term = jnp.dot(x, w_all[step, kind], preferred_element_type=jnp.float32)
                held[r, kind] = term if step == 0 else held[r, kind] + term
            if step == 2:
                stores.append(pltpu.make_async_copy(held.at[r], acc.at[r], sems.at[r]))
                stores[-1].start()
    wait(stores)


def early(place, xs, own, near, far):
    kinds, rows, width = own.shape
    slabs, count, wide = xs[0].shape
    return pl.pallas_call(
        early_kernel,
        out_shape=jax.ShapeDtypeStruct((SLAB, kinds, count, width), jnp.float32),
        in_specs=[SMEM] + [HBM] * 7,
        out_specs=HBM,
        scratch_shapes=[
            pltpu.VMEM((3, SLAB, count, wide), jnp.bfloat16),
            pltpu.VMEM((3, kinds, wide, width), jnp.bfloat16),
            pltpu.VMEM((SLAB, kinds, count, width), jnp.float32),
            pltpu.SemaphoreType.DMA((3, SLAB)),
            pltpu.SemaphoreType.DMA((3,)),
            pltpu.SemaphoreType.DMA((SLAB,)),
        ],
        compiler_params=pltpu.CompilerParams(vmem_limit_bytes=KERNEL_VMEM),
        cost_estimate=pl.CostEstimate(
            flops=12 * kinds * SLAB * count * rows * width,
            bytes_accessed=6 * kinds * rows * width + 6 * SLAB * count * rows,
            transcendentals=0,
        ),
        name="early",
    )(place, *xs, own, near, far)


def late_kernel(
    place, xa, xb, xc, xd, acc, last, q_gain, k_gain,
    query, keys, values, squares, even, odd,
    x_all, w_all, held, q_all, k_all, v_all, x_sem, w_sem, acc_sem, sems,
):
    z, q = place[0], place[1]
    rows = last.shape[1]
    w_copy = pltpu.make_async_copy(last, w_all.at[:, pl.ds(0, rows), :], w_sem)
    w_copy.start()
    copies = token_copies((xa, xb, xc, xd), z ^ 3, x_all, x_sem)
    loads = [pltpu.make_async_copy(acc.at[r], held.at[r], acc_sem.at[r]) for r in range(SLAB)]
    for r in range(SLAB):
        copies[r].start()
        loads[r].start()
    count = held.shape[2]
    stores = []
    blank_tail(w_all, rows)
    w_copy.wait()
    for r in range(SLAB):
        copies[r].wait()
        loads[r].wait()
        x = x_all[r]
        rows = pl.ds(pl.multiple_of((q ^ r) * count, count), count)
        for kind in range(3):
            part = held[r, kind] + jnp.dot(x, w_all[kind], preferred_element_type=jnp.float32)
            if kind < 2:
                summed = as_row(jnp.sum(part * part, axis=1, keepdims=True))
                squares[kind:kind + 1, rows] = summed[:1]
                part = part * (q_gain, k_gain)[kind][...]
            held_out, out = ((q_all, query), (k_all, keys), (v_all, values))[kind]
            held_out[rows, :] = part.astype(held_out.dtype)
            store = pltpu.make_async_copy(held_out.at[rows, :], out.at[rows, :], sems.at[3 * r + kind])
            store.start()
            stores.append(store)
    reach = even.shape[1]
    for n, (out, at) in enumerate(((even, 1 - z % 2), (odd, z % 2))):
        rows = pl.ds(pl.multiple_of(at * reach, reach), reach)
        for k, src in enumerate((k_all, v_all)):
            sem = sems.at[3 * SLAB + 2 * n + k]
            stores.append(pltpu.make_async_copy(src.at[rows, :], out.at[k], sem))
            stores[-1].start()
    wait(stores)


def late(place, xs, acc, last, q_gain, k_gain):
    kinds, rows, width = last.shape
    count, wide = xs[0].shape[1:]
    slab = SLAB * count
    f32, bf16 = jnp.float32, jnp.bfloat16
    return pl.pallas_call(
        late_kernel,
        out_shape=(
            jax.ShapeDtypeStruct((slab, width), f32),
            jax.ShapeDtypeStruct((slab, width), bf16),
            jax.ShapeDtypeStruct((slab, width), bf16),
            jax.ShapeDtypeStruct((2, slab), f32),
            jax.ShapeDtypeStruct((2, 2 * count, width), bf16),
            jax.ShapeDtypeStruct((2, 2 * count, width), bf16),
        ),
        in_specs=[SMEM] + [HBM] * 6 + [VMEM] * 2,
        out_specs=(HBM, HBM, HBM, VMEM, HBM, HBM),
        scratch_shapes=[
            pltpu.VMEM((SLAB, count, wide), bf16),
            pltpu.VMEM((kinds, wide, width), bf16),
            pltpu.VMEM((SLAB, kinds, count, width), f32),
            pltpu.VMEM((slab, width), f32),
            pltpu.VMEM((slab, width), bf16),
            pltpu.VMEM((slab, width), bf16),
            pltpu.SemaphoreType.DMA((SLAB,)),
            pltpu.SemaphoreType.DMA,
            pltpu.SemaphoreType.DMA((SLAB,)),
            pltpu.SemaphoreType.DMA((3 * SLAB + 4,)),
        ],
        compiler_params=pltpu.CompilerParams(vmem_limit_bytes=KERNEL_VMEM),
        cost_estimate=pl.CostEstimate(
            flops=2 * kinds * slab * rows * width,
            bytes_accessed=2 * kinds * rows * width + 2 * slab * rows,
            transcendentals=0,
        ),
        name="late",
    )(place, *xs, acc, last, q_gain, k_gain)


def attend_kernel(
    full_width, place, query, keys, values, even, odd, mine, near, mid, seg, o0, o1, o2, o3,
    q_all, k_all, v_all, k_turned, scale_all, sems,
):
    z, q = place[0], place[1]
    slab = query.shape[0]
    count = slab // SLAB
    half = even.shape[1]
    upper = half + slab
    is_even = z % 2 == 0
    even_at = pl.multiple_of(jnp.where(is_even, upper, 0), half)
    odd_at = pl.multiple_of(jnp.where(is_even, 0, upper), half)
    copies = [pltpu.make_async_copy(query, q_all, sems.at[0])]
    for k, (whole, out) in enumerate(((keys, k_all), (values, v_all))):
        for n, (src, at) in enumerate(((whole, half), (even.at[k], even_at), (odd.at[k], odd_at))):
            dst = out.at[pl.ds(at, src.shape[0]), :]
            copies.append(pltpu.make_async_copy(src, dst, sems.at[1 + 3 * k + n]))
    start(copies)
    scale = [lax.rsqrt(sums[...] / full_width + eps) for sums in (mine, near, mid)]
    scale_all[:, half:upper] = scale[0]
    scale_all[:, :half] = jnp.where(is_even, scale[2], scale[1])[:, slab - half:]
    scale_all[:, upper:] = jnp.where(is_even, scale[1], scale[2])[:, :half]
    wait(copies)
    for at in range(0, k_all.shape[0], count):
        k_turned[:, at:at + count] = jnp.transpose(k_all[at:at + count, :])
    window = count + 2 * half
    heads = query.shape[1] // HEAD_DIM
    factor = HEAD_DIM ** (-0.5) * math.log2(math.e)
    for r, out in ((2, o2), (3, o3), (1, o1), (0, o0)):
        begin = pl.multiple_of((q ^ r) * count, count)
        at_query = pl.multiple_of((q ^ r) * count + half, count)
        key_seg = seg[:, pl.ds(begin, window)]
        query_seg = as_column(seg[:, pl.ds(at_query, count)])
        k_scale = scale_all[1:2, pl.ds(begin, window)] * factor
        q_scale = as_column(scale_all[0:1, pl.ds(at_query, count)])
        mask = jnp.tile(query_seg, (1, window // 128)) == key_seg
        for h in range(heads):
            cols = slice(h * HEAD_DIM, (h + 1) * HEAD_DIM)
            q_low = (q_all[pl.ds(begin, count), cols] * q_scale).astype(jnp.bfloat16)
            scores = jnp.dot(
                q_low, k_turned[cols, pl.ds(begin, window)], preferred_element_type=jnp.float32
            )
            scores = jnp.where(mask, scores * k_scale, floor_score)
            peak = jnp.max(scores, axis=1, keepdims=True)
            weights = jnp.exp2(scores - peak)
            total = jnp.sum(weights, axis=1, keepdims=True)
            summed = jnp.dot(
                weights.astype(jnp.bfloat16), v_all[pl.ds(begin, window), cols],
                preferred_element_type=jnp.float32,
            )
            out[cols, :] = jnp.transpose(summed / total).astype(jnp.bfloat16)


def attend(full_width, place, query, keys, values, even, odd, sums, seg):
    slab, width = query.shape
    half = even.shape[1]
    count = slab // SLAB
    ext = slab + 2 * half
    bf16 = jnp.bfloat16
    window = count + 2 * half
    return pl.pallas_call(
        functools.partial(attend_kernel, full_width),
        out_shape=(jax.ShapeDtypeStruct((width, count), bf16),) * SLAB,
        in_specs=[SMEM] + [HBM] * 5 + [VMEM] * 4,
        out_specs=(VMEM,) * SLAB,
        scratch_shapes=[
            pltpu.VMEM((slab, width), jnp.float32),
            pltpu.VMEM((ext, width), bf16),
            pltpu.VMEM((ext, width), bf16),
            pltpu.VMEM((width, ext), bf16),
            pltpu.VMEM((2, ext), jnp.float32),
            pltpu.SemaphoreType.DMA((7,)),
        ],
        compiler_params=pltpu.CompilerParams(vmem_limit_bytes=KERNEL_VMEM),
        cost_estimate=pl.CostEstimate(
            flops=SLAB * 4 * count * window * width,
            bytes_accessed=4 * ext * width + 4 * slab * width,
            transcendentals=SLAB * count * window * width // HEAD_DIM,
        ),
        name="attend",
    )(place, query, keys, values, even, odd, *sums, seg)


def out_kernel(
    place, c20, c01, c31, c30, c11, c21, c10, c00, wa, wb, wc, wd,
    residual, scale, out, c_all, w_all, total, placed, c_sem, w_sem,
):
    z, q = place[0], place[1]
    width = c00.shape[0]
    c_copies = []
    for i in range(2):
        for r, pair in enumerate(((c00, c01), (c10, c11), (c20, c21), (c30, c31))):
            at = pl.multiple_of((q ^ r) * width, width)
            dst = c_all.at[i, pl.ds(at, width), :]
            c_copies.append(pltpu.make_async_copy(pair[i], dst, c_sem.at[r, i]))
    start(c_copies)
    rows = wa.shape[2]
    w_copies = []
    for i in range(2):
        for r, w in enumerate((wa, wb, wc, wd)):
            for j in range(2):
                dst = w_all.at[i, pl.ds((2 * r + j) * rows, rows), :]
                w_copies.append(pltpu.make_async_copy(w.at[i, j], dst, w_sem.at[r, j, i]))
    start(w_copies)
    column = as_column(scale[...])[:out.shape[0]]
    column = jnp.tile(column, (1, out.shape[1] // 128))
    wait(c_copies[:SLAB] + w_copies[:2 * SLAB])
    total[...] = jnp.dot(w_all[0], c_all[0], preferred_element_type=jnp.float32)
    wait(c_copies[SLAB:] + w_copies[2 * SLAB:])
    total[...] += jnp.dot(w_all[1], c_all[1], preferred_element_type=jnp.float32)
    kept = out.shape[0] // (2 * SLAB)
    for r in range(SLAB):
        for j in range(2):
            at = pl.multiple_of((((z % 2) ^ j) * SLAB + (q ^ r)) * kept, 8)
            begin = (2 * r + j) * rows
            placed[pl.ds(at, kept), :] = total[begin:begin + kept, :]
    out[...] = (residual[...].astype(jnp.float32) + column * placed[...]).astype(jnp.bfloat16)


def output(place, blocks, pieces, residual, scale):
    count = blocks[0].shape[1]
    rows, depth = pieces[0].shape[2:]
    share = residual.shape[0]
    scale = jnp.pad(scale, (0, -share % 128))[None]
    return pl.pallas_call(
        out_kernel,
        out_shape=jax.ShapeDtypeStruct((share, count), jnp.bfloat16),
        in_specs=[SMEM] + [HBM] * 12 + [VMEM] * 2,
        out_specs=VMEM,
        scratch_shapes=[
            pltpu.VMEM((2, depth, count), jnp.bfloat16),
            pltpu.VMEM((2, 2 * SLAB * rows, depth), jnp.bfloat16),
            pltpu.VMEM((2 * SLAB * rows, count), jnp.float32),
            pltpu.VMEM((share, count), jnp.float32),
            pltpu.SemaphoreType.DMA((SLAB, 2)),
            pltpu.SemaphoreType.DMA((SLAB, 2, 2)),
        ],
        compiler_params=pltpu.CompilerParams(vmem_limit_bytes=KERNEL_VMEM),
        cost_estimate=pl.CostEstimate(
            flops=4 * share * count * depth,
            bytes_accessed=4 * share * depth,
            transcendentals=0,
        ),
        name="output",
    )(place, *blocks, *pieces, residual, scale)


def rows_of_slab(q, got):
    placed = []
    for b in range(SLAB):
        piece = got[b]
        for other in range(1, SLAB):
            piece = jnp.where(q == other, got[b ^ other], piece)
        placed.append(piece)
    return jnp.concatenate(placed, axis=1)


def slab_plan(tokens, norm_gain, qkv_weight, q_gain, k_gain, out_weight, layer_scale, segment_ids):
    count = tokens.shape[0]
    seq, tp = lax.axis_index("seq"), lax.axis_index("tp")
    slabs = lax.axis_size("seq") // SLAB
    z, q = seq // SLAB, seq % SLAB
    place = jnp.stack([z, q, tp]).astype(jnp.int32)
    width = qkv_weight.shape[2] // SLAB
    full_width = qkv_weight.shape[2] * lax.axis_size("tp")
    slab, half = SLAB * count, 2 * count
    home = z // 2 == tp

    by_kind = jnp.transpose(qkv_weight, (1, 0, 2))
    cut = [lax.dynamic_slice_in_dim(by_kind, (q ^ r) * width, width, 2) for r in range(SLAB)]
    got = [cut[0]] + [in_slab(cut[r], r) for r in range(1, SLAB)]
    x0 = norm(tokens, norm_gain, slabs)
    out_own = jnp.pad(jnp.transpose(out_weight), ((0, -out_weight.shape[1] % 16), (0, 0)))
    own = rows_of_slab(q, got)
    out_near, out_far = even_pair(out_own), half_pair(out_own)
    gains = [lax.dynamic_slice_in_dim(g, q * width, width, 0)[None] for g in (q_gain, k_gain)]

    own, x0, out_near, out_far, *gains = tied(own, x0, out_near, out_far, *gains)
    out_last = even_pair(out_far)
    near, far = even_pair(own), half_pair(own)
    x1, x2 = in_slab(x0, 1), in_slab(x0, 2)
    out_last, x1 = tied(out_last, x1)
    close, away = jnp.stack([out_own, out_near]), jnp.stack([out_far, out_last])
    keep, give = jnp.where(home, close, away), jnp.where(home, away, close)
    wa = jnp.stack([keep, across(give)])
    near, far, x2, wa = tied(near, far, x2, wa)
    last = even_pair(far)
    x3 = in_slab(x2, 1)
    wc, wb = in_slab(wa, 2), in_slab(wa, 1)
    xs = (x0, x1, x2, x3)
    acc = early(place, xs, own, near, far)
    last, acc, wb = tied(last, acc, wb)

    query, keys, values, squares, even, odd = late(place, xs, acc, last, *gains)
    even, odd = even_pair(even), odd_pair(odd)
    sums = squares + in_slab(squares, 1)
    sums = sums + in_slab(sums, 2)
    sums = sums + across(sums)
    sums = (sums, even_pair(sums), odd_pair(sums))
    query, wc = tied(query, wc)
    wd = in_slab(wc, 1)

    outside = jnp.full((half,), -1, jnp.int32)
    seg = jnp.concatenate([outside, segment_ids, outside], axis=0)
    seg = lax.dynamic_slice_in_dim(seg, z * slab, slab + 2 * half, 0)
    seg = seg.astype(jnp.float32)[None]
    blocks = attend(full_width, place, query, keys, values, even, odd, sums, seg)
    *blocks, wd = tied(*blocks, wd)
    pieces = (wa, wb, wc, wd)
    spread = []
    for r, i in ((2, 0), (0, 1), (3, 1), (3, 0), (1, 1), (2, 1), (1, 0), (0, 0)):
        to = functools.partial(lambda r, i, z, q, y: (z, q ^ r, y ^ i), r, i)
        spread.append(permuted(blocks[r], to) if r or i else blocks[r])

    share = layer_scale.shape[0]
    residual = jnp.transpose(lax.dynamic_slice_in_dim(tokens, tp * share, share, 1))
    return jnp.transpose(output(place, spread, pieces, residual, layer_scale))


def solution(mesh):
    def shards(*args):
        heads = args[2].shape[2] // HEAD_DIM
        slab = mesh.shape["seq"] == 16 and mesh.shape["tp"] == 2 and heads % SLAB == 0
        return (slab_plan if slab else row_plan)(*args)

    return jax.shard_map(
        shards,
        mesh=mesh,
        in_specs=(
            P("seq", None),
            P(),
            P("seq", None, "tp"),
            P("tp"),
            P("tp"),
            P("tp", "seq"),
            P("tp"),
            P(),
        ),
        out_specs=P("seq", "tp"),
        check_vma=False,
    )
```

```python
import functools
import math

import jax
import jax.numpy as jnp
from jax import lax
from jax.experimental import pallas as pl
from jax.experimental.pallas import tpu as pltpu
from jax.sharding import PartitionSpec as P

HEAD_DIM = 128
SLAB = 4

eps = 1e-06
floor_score = -1e30


def passed_along(x, axis, by):
    size = lax.axis_size(axis)
    pairs = [(i, i + by) for i in range(size) if 0 <= i + by < size]
    return lax.ppermute(x, axis, pairs)


def masked_scores(query, keys, query_seg, key_seg):
    scores = jnp.einsum(
        "qhd,khd->hqk", query, keys, preferred_element_type=jnp.float32
    ) * HEAD_DIM ** (-0.5)
    mask = (query_seg[:, None] == key_seg[None, :])[None]
    return (jnp.where(mask, scores, floor_score), mask)


def row_plan(tokens, norm_gain, qkv_weight, q_gain, k_gain, out_weight, layer_scale, segment_ids):
    count = tokens.shape[0]
    source = tokens.astype(jnp.float32)
    normed = (
        source * lax.rsqrt(jnp.mean(source * source, axis=-1, keepdims=True) + eps) * norm_gain
    ).astype(jnp.bfloat16)
    local_width = qkv_weight.shape[2]
    heads = local_width // HEAD_DIM
    joined = jnp.einsum(
        "td,dch->tch",
        normed,
        lax.all_gather(qkv_weight, "seq", axis=0, tiled=True),
        preferred_element_type=jnp.float32,
    )
    query = joined[:, 0]
    keys = joined[:, 1]
    values = joined[:, 2]
    query_sq, key_sq = lax.psum(
        (jnp.sum(query * query, axis=-1), jnp.sum(keys * keys, axis=-1)), "tp"
    )
    full_width = local_width * lax.axis_size("tp")
    query_normed = (query * lax.rsqrt(query_sq / full_width + eps)[:, None] * q_gain).astype(
        jnp.bfloat16
    )
    key_normed = (keys * lax.rsqrt(key_sq / full_width + eps)[:, None] * k_gain).astype(
        jnp.bfloat16
    )
    paired = jnp.stack([key_normed, values.astype(jnp.bfloat16)], axis=1)
    pieces = []
    for offset in (2, 1, 0, -1, -2):
        if offset == 0:
            pieces.append(paired)
        else:
            pieces.append(passed_along(paired, "seq", offset))
    widened = jnp.concatenate(pieces, axis=0)
    position = lax.axis_index("seq")
    outside = jnp.full((2 * count,), -1, jnp.int32)
    seg_pad = jnp.concatenate([outside, segment_ids, outside], axis=0)
    key_seg = lax.dynamic_slice_in_dim(seg_pad, position * count, 5 * count, 0)
    query_seg = lax.dynamic_slice_in_dim(segment_ids, position * count, count, 0)
    query_heads = query_normed.reshape(count, heads, HEAD_DIM)
    key_heads = widened[:, 0].reshape(5 * count, heads, HEAD_DIM)
    value_heads = widened[:, 1].reshape(5 * count, heads, HEAD_DIM)
    scores, mask = masked_scores(query_heads, key_heads, query_seg, key_seg)
    peak = jnp.max(scores, axis=-1, keepdims=True)
    weights = jnp.where(mask, jnp.exp(scores - peak), 0.0)
    total = jnp.sum(weights, axis=-1)
    probs = weights.astype(jnp.bfloat16)
    summed = jnp.einsum("hqk,khd->qhd", probs, value_heads, preferred_element_type=jnp.float32)
    context = (
        (summed / jnp.transpose(total)[:, :, None]).reshape(count, local_width).astype(jnp.bfloat16)
    )
    terms = jnp.dot(
        context,
        lax.all_gather(out_weight, "seq", axis=1, tiled=True),
        preferred_element_type=jnp.float32,
    )
    projected = lax.psum_scatter(terms, "tp", scatter_dimension=1, tiled=True)
    share = layer_scale.shape[0]
    residual = lax.dynamic_slice_in_dim(source, lax.axis_index("tp") * share, share, 1)
    return (residual + layer_scale * projected).astype(jnp.bfloat16)


ANY = pl.BlockSpec(memory_space=pl.ANY)
VMEM = pl.BlockSpec(memory_space=pltpu.VMEM)
SMEM = pl.BlockSpec(memory_space=pltpu.SMEM)
HBM = pl.BlockSpec(memory_space=pltpu.HBM)
KERNEL_VMEM = 60 * 1024 * 1024


def permuted(x, to):
    slabs, tps = lax.axis_size("seq") // SLAB, lax.axis_size("tp")
    pairs = []
    for i in range(slabs * SLAB * tps):
        z, q, y = to(i // (SLAB * tps), i // tps % SLAB, i % tps)
        pairs.append((i, (z * SLAB + q) * tps + y))
    return lax.ppermute(x, ("seq", "tp"), pairs)


def in_slab(x, flip):
    return permuted(x, lambda z, q, y: (z, q ^ flip, y))


def across(x):
    return permuted(x, lambda z, q, y: (z, q, 1 - y))


def even_pair(x):
    return permuted(x, lambda z, q, y: (z ^ 1, q, y))


def odd_pair(x):
    return permuted(x, lambda z, q, y: (3 - z, q, y) if z in (1, 2) else (z, q ^ 1, y))


def half_pair(x):
    return permuted(x, lambda z, q, y: (z ^ 2, q, y))


def tied(*arrays):
    return lax.optimization_barrier(arrays)


def as_row(column):
    wide = jnp.broadcast_to(column, (column.shape[0], 128))
    return jnp.transpose(wide)[:8]


def as_column(row):
    return jnp.transpose(jnp.broadcast_to(row, (128, row.shape[1])))


def start(copies):
    for copy in copies:
        copy.start()


def wait(copies):
    for copy in copies:
        copy.wait()


def norm_kernel(tokens, gain, out):
    part = tokens.shape[1] // out.shape[0]
    source = tokens[...].astype(jnp.float32)
    mean = jnp.mean(source * source, axis=1, keepdims=True)
    normed = source * lax.rsqrt(mean + eps) * gain[...]
    for j in range(out.shape[0]):
        out[j, :, :part] = normed[:, j * part:(j + 1) * part].astype(jnp.bfloat16)
        out[j, :, part:] = jnp.zeros((out.shape[1], out.shape[2] - part), jnp.bfloat16)


def norm(tokens, gain, slabs):
    count, depth = tokens.shape
    shape = (slabs, count, pl.cdiv(depth // slabs, 128) * 128)
    return pl.pallas_call(
        norm_kernel,
        out_shape=jax.ShapeDtypeStruct(shape, jnp.bfloat16),
        in_specs=[VMEM, VMEM],
        out_specs=VMEM,
        compiler_params=pltpu.CompilerParams(vmem_limit_bytes=KERNEL_VMEM),
        name="norm",
    )(tokens, gain[None])


def token_copies(xs, at, out, sems):
    return [
        pltpu.make_async_copy(x.at[at], out.at[r], sems.at[r]) for r, x in enumerate(xs)
    ]


def blank_tail(w, rows):
    tail = w.shape[-2] - rows
    w[..., rows:, :] = jnp.zeros(w.shape[:-2] + (tail, w.shape[-1]), w.dtype)


def early_kernel(
    place, xa, xb, xc, xd, own, near, far, acc, x_all, w_all, held, x_sem, w_sem, sems,
):
    z = place[0]
    kinds, rows = own.shape[:2]
    copies = []
    for i, w in enumerate((own, near, far)):
        dst = w_all.at[i, :, pl.ds(0, rows), :]
        copies.append([pltpu.make_async_copy(w, dst, w_sem.at[i])])
        copies[i] += token_copies((xa, xb, xc, xd), z ^ i, x_all.at[i], x_sem.at[i])
        start(copies[i])
    blank_tail(w_all, rows)
    stores = []
    for step in range(3):
        wait(copies[step])
        for r in range(SLAB):
            x = x_all[step, r]
            for kind in range(kinds):
                term = jnp.dot(x, w_all[step, kind], preferred_element_type=jnp.float32)
                held[r, kind] = term if step == 0 else held[r, kind] + term
            if step == 2:
                stores.append(pltpu.make_async_copy(held.at[r], acc.at[r], sems.at[r]))
                stores[-1].start()
    wait(stores)


def early(place, xs, own, near, far):
    kinds, rows, width = own.shape
    slabs, count, wide = xs[0].shape
    return pl.pallas_call(
        early_kernel,
        out_shape=jax.ShapeDtypeStruct((SLAB, kinds, count, width), jnp.float32),
        in_specs=[SMEM] + [HBM] * 7,
        out_specs=HBM,
        scratch_shapes=[
            pltpu.VMEM((3, SLAB, count, wide), jnp.bfloat16),
            pltpu.VMEM((3, kinds, wide, width), jnp.bfloat16),
            pltpu.VMEM((SLAB, kinds, count, width), jnp.float32),
            pltpu.SemaphoreType.DMA((3, SLAB)),
            pltpu.SemaphoreType.DMA((3,)),
            pltpu.SemaphoreType.DMA((SLAB,)),
        ],
        compiler_params=pltpu.CompilerParams(vmem_limit_bytes=KERNEL_VMEM),
        cost_estimate=pl.CostEstimate(
            flops=12 * kinds * SLAB * count * rows * width,
            bytes_accessed=6 * kinds * rows * width + 6 * SLAB * count * rows,
            transcendentals=0,
        ),
        name="early",
    )(place, *xs, own, near, far)


def late_kernel(
    place, xa, xb, xc, xd, acc, last, q_gain, k_gain,
    query, keys, values, squares, even, odd,
    x_all, w_all, held, q_all, k_all, v_all, x_sem, w_sem, acc_sem, sems,
):
    z, q = place[0], place[1]
    rows = last.shape[1]
    w_copy = pltpu.make_async_copy(last, w_all.at[:, pl.ds(0, rows), :], w_sem)
    w_copy.start()
    copies = token_copies((xa, xb, xc, xd), z ^ 3, x_all, x_sem)
    loads = [pltpu.make_async_copy(acc.at[r], held.at[r], acc_sem.at[r]) for r in range(SLAB)]
    for r in range(SLAB):
        copies[r].start()
        loads[r].start()
    count = held.shape[2]
    stores = []
    blank_tail(w_all, rows)
    w_copy.wait()
    for r in range(SLAB):
        copies[r].wait()
        loads[r].wait()
        x = x_all[r]
        rows = pl.ds(pl.multiple_of((q ^ r) * count, count), count)
        for kind in range(3):
            part = held[r, kind] + jnp.dot(x, w_all[kind], preferred_element_type=jnp.float32)
            if kind < 2:
                summed = as_row(jnp.sum(part * part, axis=1, keepdims=True))
                squares[kind:kind + 1, rows] = summed[:1]
                part = part * (q_gain, k_gain)[kind][...]
            held_out, out = ((q_all, query), (k_all, keys), (v_all, values))[kind]
            held_out[rows, :] = part.astype(held_out.dtype)
            store = pltpu.make_async_copy(held_out.at[rows, :], out.at[rows, :], sems.at[3 * r + kind])
            store.start()
            stores.append(store)
    reach = even.shape[1]
    for n, (out, at) in enumerate(((even, 1 - z % 2), (odd, z % 2))):
        rows = pl.ds(pl.multiple_of(at * reach, reach), reach)
        for k, src in enumerate((k_all, v_all)):
            sem = sems.at[3 * SLAB + 2 * n + k]
            stores.append(pltpu.make_async_copy(src.at[rows, :], out.at[k], sem))
            stores[-1].start()
    wait(stores)


def late(place, xs, acc, last, q_gain, k_gain):
    kinds, rows, width = last.shape
    count, wide = xs[0].shape[1:]
    slab = SLAB * count
    f32, bf16 = jnp.float32, jnp.bfloat16
    return pl.pallas_call(
        late_kernel,
        out_shape=(
            jax.ShapeDtypeStruct((slab, width), f32),
            jax.ShapeDtypeStruct((slab, width), bf16),
            jax.ShapeDtypeStruct((slab, width), bf16),
            jax.ShapeDtypeStruct((2, slab), f32),
            jax.ShapeDtypeStruct((2, 2 * count, width), bf16),
            jax.ShapeDtypeStruct((2, 2 * count, width), bf16),
        ),
        in_specs=[SMEM] + [HBM] * 6 + [VMEM] * 2,
        out_specs=(HBM, HBM, HBM, VMEM, HBM, HBM),
        scratch_shapes=[
            pltpu.VMEM((SLAB, count, wide), bf16),
            pltpu.VMEM((kinds, wide, width), bf16),
            pltpu.VMEM((SLAB, kinds, count, width), f32),
            pltpu.VMEM((slab, width), f32),
            pltpu.VMEM((slab, width), bf16),
            pltpu.VMEM((slab, width), bf16),
            pltpu.SemaphoreType.DMA((SLAB,)),
            pltpu.SemaphoreType.DMA,
            pltpu.SemaphoreType.DMA((SLAB,)),
            pltpu.SemaphoreType.DMA((3 * SLAB + 4,)),
        ],
        compiler_params=pltpu.CompilerParams(vmem_limit_bytes=KERNEL_VMEM),
        cost_estimate=pl.CostEstimate(
            flops=2 * kinds * slab * rows * width,
            bytes_accessed=2 * kinds * rows * width + 2 * slab * rows,
            transcendentals=0,
        ),
        name="late",
    )(place, *xs, acc, last, q_gain, k_gain)


def attend_kernel(
    full_width, place, spans, query, keys, values, even, odd, mine, near, mid, seg, o0, o1, o2, o3,
    q_all, k_all, v_all, o_all, scale_all, sems,
):
    z, q = place[0], place[1]
    slab = query.shape[0]
    count = slab // SLAB
    half = even.shape[1]
    upper = half + slab
    is_even = z % 2 == 0
    even_at = pl.multiple_of(jnp.where(is_even, upper, 0), half)
    odd_at = pl.multiple_of(jnp.where(is_even, 0, upper), half)
    copies = [pltpu.make_async_copy(query, q_all, sems.at[0])]
    for k, (whole, out) in enumerate(((keys, k_all), (values, v_all))):
        for n, (src, at) in enumerate(((whole, half), (even.at[k], even_at), (odd.at[k], odd_at))):
            dst = out.at[pl.ds(at, src.shape[0]), :]
            copies.append(pltpu.make_async_copy(src, dst, sems.at[1 + 3 * k + n]))
    start(copies)
    scale = [lax.rsqrt(sums[...] / full_width + eps) for sums in (mine, near, mid)]
    scale_all[:, half:upper] = scale[0]
    scale_all[:, :half] = jnp.where(is_even, scale[2], scale[1])[:, slab - half:]
    scale_all[:, upper:] = jnp.where(is_even, scale[1], scale[2])[:, :half]
    wait(copies)
    ext = k_all.shape[0]
    heads = query.shape[1] // HEAD_DIM
    factor = HEAD_DIM ** (-0.5) * math.log2(math.e)

    def block(r, _):
        b = q ^ r
        at_query = pl.multiple_of(b * count + half, count)
        query_seg = as_column(seg[:, pl.ds(at_query, count)])
        q_scale = as_column(scale_all[0:1, pl.ds(at_query, count)])
        for tiles in range(2, 2 * half // count + 2):
            @pl.when(spans[b, 1] == tiles)
            def _():
                width = tiles * count
                begin = pl.multiple_of(spans[b, 0], 128)
                keys_at = pl.ds(begin, width)
                mask = jnp.tile(query_seg, (1, width // 128)) == seg[:, keys_at]
                k_scale = scale_all[1:2, keys_at] * factor
                for h in range(heads):
                    cols = slice(h * HEAD_DIM, (h + 1) * HEAD_DIM)
                    q_low = q_all[pl.ds(pl.multiple_of(b * count, count), count), cols] * q_scale
                    scores = lax.dot_general(
                        q_low.astype(jnp.bfloat16), k_all[keys_at, cols],
                        (((1,), (1,)), ((), ())), preferred_element_type=jnp.float32,
                    )
                    scores = jnp.where(mask, scores * k_scale, floor_score)
                    peak = jnp.max(scores, axis=1, keepdims=True)
                    weights = jnp.exp2(scores - peak)
                    total = jnp.sum(weights, axis=1, keepdims=True)
                    summed = jnp.dot(
                        weights.astype(jnp.bfloat16), v_all[keys_at, cols],
                        preferred_element_type=jnp.float32,
                    )
                    o_all[r, cols, :] = jnp.transpose(summed / total).astype(jnp.bfloat16)

        return 0

    lax.fori_loop(0, SLAB, block, 0)
    stores = [
        pltpu.make_async_copy(o_all.at[r], out, sems.at[r]) for r, out in enumerate((o0, o1, o2, o3))
    ]
    start(stores)
    wait(stores)


def key_spans(seg, slab, count, half):
    ext = seg.shape[0]
    index = jnp.arange(ext, dtype=jnp.int32)
    blocks = seg[half:half + slab].reshape(-1, count)
    first, last = blocks[:, :1], blocks[:, -1:]
    begin = jnp.min(jnp.where(seg == first, index, ext), axis=1) // 128 * 128
    end = jnp.max(jnp.where(seg == last, index, -1), axis=1) + 1
    tiles = jnp.maximum((end - begin + count - 1) // count, 2)
    return jnp.stack([jnp.minimum(begin, ext - tiles * count), tiles], axis=1)


def attend(full_width, place, spans, query, keys, values, even, odd, sums, seg):
    slab, width = query.shape
    half = even.shape[1]
    count = slab // SLAB
    ext = slab + 2 * half
    bf16 = jnp.bfloat16
    window = count + 2 * half
    return pl.pallas_call(
        functools.partial(attend_kernel, full_width),
        out_shape=(jax.ShapeDtypeStruct((width, count), bf16),) * SLAB,
        in_specs=[SMEM] * 2 + [HBM] * 5 + [VMEM] * 4,
        out_specs=(HBM,) * SLAB,
        scratch_shapes=[
            pltpu.VMEM((slab, width), jnp.float32),
            pltpu.VMEM((ext, width), bf16),
            pltpu.VMEM((ext, width), bf16),
            pltpu.VMEM((SLAB, width, count), bf16),
            pltpu.VMEM((2, ext), jnp.float32),
            pltpu.SemaphoreType.DMA((7,)),
        ],
        compiler_params=pltpu.CompilerParams(vmem_limit_bytes=KERNEL_VMEM),
        cost_estimate=pl.CostEstimate(
            flops=SLAB * 4 * count * window * width,
            bytes_accessed=4 * ext * width + 4 * slab * width,
            transcendentals=SLAB * count * window * width // HEAD_DIM,
        ),
        name="attend",
    )(place, spans, query, keys, values, even, odd, *sums, seg)


def out_kernel(
    place, c20, c01, c31, c30, c11, c21, c10, c00, wa, wb, wc, wd,
    residual, scale, out, c_all, w_all, total, placed, c_sem, w_sem,
):
    z, q = place[0], place[1]
    width = c00.shape[0]
    c_copies = []
    for i in range(2):
        for r, pair in enumerate(((c00, c01), (c10, c11), (c20, c21), (c30, c31))):
            at = pl.multiple_of((q ^ r) * width, width)
            dst = c_all.at[i, pl.ds(at, width), :]
            c_copies.append(pltpu.make_async_copy(pair[i], dst, c_sem.at[r, i]))
    start(c_copies)
    rows = wa.shape[2]
    w_copies = []
    for i in range(2):
        for r, w in enumerate((wa, wb, wc, wd)):
            for j in range(2):
                dst = w_all.at[i, pl.ds((2 * r + j) * rows, rows), :]
                w_copies.append(pltpu.make_async_copy(w.at[i, j], dst, w_sem.at[r, j, i]))
    start(w_copies)
    column = as_column(scale[...])[:out.shape[0]]
    column = jnp.tile(column, (1, out.shape[1] // 128))
    wait(c_copies[:SLAB] + w_copies[:2 * SLAB])
    total[...] = jnp.dot(w_all[0], c_all[0], preferred_element_type=jnp.float32)
    wait(c_copies[SLAB:] + w_copies[2 * SLAB:])
    total[...] += jnp.dot(w_all[1], c_all[1], preferred_element_type=jnp.float32)
    kept = out.shape[0] // (2 * SLAB)
    for r in range(SLAB):
        for j in range(2):
            at = pl.multiple_of((((z % 2) ^ j) * SLAB + (q ^ r)) * kept, 8)
            begin = (2 * r + j) * rows
            placed[pl.ds(at, kept), :] = total[begin:begin + kept, :]
    out[...] = (residual[...].astype(jnp.float32) + column * placed[...]).astype(jnp.bfloat16)


def output(place, blocks, pieces, residual, scale):
    count = blocks[0].shape[1]
    rows, depth = pieces[0].shape[2:]
    share = residual.shape[0]
    scale = jnp.pad(scale, (0, -share % 128))[None]
    return pl.pallas_call(
        out_kernel,
        out_shape=jax.ShapeDtypeStruct((share, count), jnp.bfloat16),
        in_specs=[SMEM] + [HBM] * 12 + [VMEM] * 2,
        out_specs=VMEM,
        scratch_shapes=[
            pltpu.VMEM((2, depth, count), jnp.bfloat16),
            pltpu.VMEM((2, 2 * SLAB * rows, depth), jnp.bfloat16),
            pltpu.VMEM((2 * SLAB * rows, count), jnp.float32),
            pltpu.VMEM((share, count), jnp.float32),
            pltpu.SemaphoreType.DMA((SLAB, 2)),
            pltpu.SemaphoreType.DMA((SLAB, 2, 2)),
        ],
        compiler_params=pltpu.CompilerParams(vmem_limit_bytes=KERNEL_VMEM),
        cost_estimate=pl.CostEstimate(
            flops=4 * share * count * depth,
            bytes_accessed=4 * share * depth,
            transcendentals=0,
        ),
        name="output",
    )(place, *blocks, *pieces, residual, scale)


def rows_of_slab(q, got):
    placed = []
    for b in range(SLAB):
        piece = got[b]
        for other in range(1, SLAB):
            piece = jnp.where(q == other, got[b ^ other], piece)
        placed.append(piece)
    return jnp.concatenate(placed, axis=1)


def slab_plan(tokens, norm_gain, qkv_weight, q_gain, k_gain, out_weight, layer_scale, segment_ids):
    count = tokens.shape[0]
    seq, tp = lax.axis_index("seq"), lax.axis_index("tp")
    slabs = lax.axis_size("seq") // SLAB
    z, q = seq // SLAB, seq % SLAB
    place = jnp.stack([z, q, tp]).astype(jnp.int32)
    width = qkv_weight.shape[2] // SLAB
    full_width = qkv_weight.shape[2] * lax.axis_size("tp")
    slab, half = SLAB * count, 2 * count
    home = z // 2 == tp

    by_kind = jnp.transpose(qkv_weight, (1, 0, 2))
    cut = [lax.dynamic_slice_in_dim(by_kind, (q ^ r) * width, width, 2) for r in range(SLAB)]
    got = [cut[0]] + [in_slab(cut[r], r) for r in range(1, SLAB)]
    x0 = norm(tokens, norm_gain, slabs)
    out_own = jnp.pad(jnp.transpose(out_weight), ((0, -out_weight.shape[1] % 16), (0, 0)))
    own = rows_of_slab(q, got)
    out_near, out_far = even_pair(out_own), half_pair(out_own)
    gains = [lax.dynamic_slice_in_dim(g, q * width, width, 0)[None] for g in (q_gain, k_gain)]

    own, x0, out_near, out_far, *gains = tied(own, x0, out_near, out_far, *gains)
    out_last = even_pair(out_far)
    near, far = even_pair(own), half_pair(own)
    x1, x2 = in_slab(x0, 1), in_slab(x0, 2)
    out_last, x1 = tied(out_last, x1)
    close, away = jnp.stack([out_own, out_near]), jnp.stack([out_far, out_last])
    keep, give = jnp.where(home, close, away), jnp.where(home, away, close)
    wa = jnp.stack([keep, across(give)])
    near, far, x2, wa = tied(near, far, x2, wa)
    last = even_pair(far)
    x3 = in_slab(x2, 1)
    wc, wb = in_slab(wa, 2), in_slab(wa, 1)
    xs = (x0, x1, x2, x3)
    acc = early(place, xs, own, near, far)
    last, acc, wb = tied(last, acc, wb)

    query, keys, values, squares, even, odd = late(place, xs, acc, last, *gains)
    even, odd = even_pair(even), odd_pair(odd)
    squares, wc = tied(squares, wc)
    sums = squares
    for r in range(1, SLAB):
        sums = sums + in_slab(squares, r)
    sums = sums + across(sums)
    sums = (sums, even_pair(sums), odd_pair(sums))

    outside = jnp.full((half,), -1, jnp.int32)
    seg = jnp.concatenate([outside, segment_ids, outside], axis=0)
    seg = lax.dynamic_slice_in_dim(seg, z * slab, slab + 2 * half, 0)
    spans = key_spans(seg, slab, count, half)
    seg = seg.astype(jnp.float32)[None]
    blocks = attend(full_width, place, spans, query, keys, values, even, odd, sums, seg)
    *blocks, wc = tied(*blocks, wc)
    pieces = (wa, wb, wc, in_slab(wc, 1))
    spread = []
    for r, i in ((2, 0), (0, 1), (3, 1), (3, 0), (1, 1), (2, 1), (1, 0), (0, 0)):
        to = functools.partial(lambda r, i, z, q, y: (z, q ^ r, y ^ i), r, i)
        spread.append(permuted(blocks[r], to) if r or i else blocks[r])

    share = layer_scale.shape[0]
    residual = jnp.transpose(lax.dynamic_slice_in_dim(tokens, tp * share, share, 1))
    return jnp.transpose(output(place, spread, pieces, residual, layer_scale))


def solution(mesh):
    def shards(*args):
        heads = args[2].shape[2] // HEAD_DIM
        slab = mesh.shape["seq"] == 16 and mesh.shape["tp"] == 2 and heads % SLAB == 0
        return (slab_plan if slab else row_plan)(*args)

    return jax.shard_map(
        shards,
        mesh=mesh,
        in_specs=(
            P("seq", None),
            P(),
            P("seq", None, "tp"),
            P("tp"),
            P("tp"),
            P("tp", "seq"),
            P("tp"),
            P(),
        ),
        out_specs=P("seq", "tp"),
        check_vma=False,
    )
```

```python
import functools
import math

import jax
import jax.numpy as jnp
from jax import lax
from jax.experimental import pallas as pl
from jax.experimental.pallas import tpu as pltpu
from jax.sharding import PartitionSpec as P

HEAD_DIM = 128
SLAB = 4

eps = 1e-06
floor_score = -1e30


def passed_along(x, axis, by):
    size = lax.axis_size(axis)
    pairs = [(i, i + by) for i in range(size) if 0 <= i + by < size]
    return lax.ppermute(x, axis, pairs)


def masked_scores(query, keys, query_seg, key_seg):
    scores = jnp.einsum(
        "qhd,khd->hqk", query, keys, preferred_element_type=jnp.float32
    ) * HEAD_DIM ** (-0.5)
    mask = (query_seg[:, None] == key_seg[None, :])[None]
    return (jnp.where(mask, scores, floor_score), mask)


def row_plan(tokens, norm_gain, qkv_weight, q_gain, k_gain, out_weight, layer_scale, segment_ids):
    count = tokens.shape[0]
    source = tokens.astype(jnp.float32)
    normed = (
        source * lax.rsqrt(jnp.mean(source * source, axis=-1, keepdims=True) + eps) * norm_gain
    ).astype(jnp.bfloat16)
    local_width = qkv_weight.shape[2]
    heads = local_width // HEAD_DIM
    joined = jnp.einsum(
        "td,dch->tch",
        normed,
        lax.all_gather(qkv_weight, "seq", axis=0, tiled=True),
        preferred_element_type=jnp.float32,
    )
    query = joined[:, 0]
    keys = joined[:, 1]
    values = joined[:, 2]
    query_sq, key_sq = lax.psum(
        (jnp.sum(query * query, axis=-1), jnp.sum(keys * keys, axis=-1)), "tp"
    )
    full_width = local_width * lax.axis_size("tp")
    query_normed = (query * lax.rsqrt(query_sq / full_width + eps)[:, None] * q_gain).astype(
        jnp.bfloat16
    )
    key_normed = (keys * lax.rsqrt(key_sq / full_width + eps)[:, None] * k_gain).astype(
        jnp.bfloat16
    )
    paired = jnp.stack([key_normed, values.astype(jnp.bfloat16)], axis=1)
    pieces = []
    for offset in (2, 1, 0, -1, -2):
        if offset == 0:
            pieces.append(paired)
        else:
            pieces.append(passed_along(paired, "seq", offset))
    widened = jnp.concatenate(pieces, axis=0)
    position = lax.axis_index("seq")
    outside = jnp.full((2 * count,), -1, jnp.int32)
    seg_pad = jnp.concatenate([outside, segment_ids, outside], axis=0)
    key_seg = lax.dynamic_slice_in_dim(seg_pad, position * count, 5 * count, 0)
    query_seg = lax.dynamic_slice_in_dim(segment_ids, position * count, count, 0)
    query_heads = query_normed.reshape(count, heads, HEAD_DIM)
    key_heads = widened[:, 0].reshape(5 * count, heads, HEAD_DIM)
    value_heads = widened[:, 1].reshape(5 * count, heads, HEAD_DIM)
    scores, mask = masked_scores(query_heads, key_heads, query_seg, key_seg)
    peak = jnp.max(scores, axis=-1, keepdims=True)
    weights = jnp.where(mask, jnp.exp(scores - peak), 0.0)
    total = jnp.sum(weights, axis=-1)
    probs = weights.astype(jnp.bfloat16)
    summed = jnp.einsum("hqk,khd->qhd", probs, value_heads, preferred_element_type=jnp.float32)
    context = (
        (summed / jnp.transpose(total)[:, :, None]).reshape(count, local_width).astype(jnp.bfloat16)
    )
    terms = jnp.dot(
        context,
        lax.all_gather(out_weight, "seq", axis=1, tiled=True),
        preferred_element_type=jnp.float32,
    )
    projected = lax.psum_scatter(terms, "tp", scatter_dimension=1, tiled=True)
    share = layer_scale.shape[0]
    residual = lax.dynamic_slice_in_dim(source, lax.axis_index("tp") * share, share, 1)
    return (residual + layer_scale * projected).astype(jnp.bfloat16)


ANY = pl.BlockSpec(memory_space=pl.ANY)
VMEM = pl.BlockSpec(memory_space=pltpu.VMEM)
SMEM = pl.BlockSpec(memory_space=pltpu.SMEM)
HBM = pl.BlockSpec(memory_space=pltpu.HBM)
KERNEL_VMEM = 60 * 1024 * 1024


def permuted(x, to):
    slabs, tps = lax.axis_size("seq") // SLAB, lax.axis_size("tp")
    pairs = []
    for i in range(slabs * SLAB * tps):
        z, q, y = to(i // (SLAB * tps), i // tps % SLAB, i % tps)
        pairs.append((i, (z * SLAB + q) * tps + y))
    return lax.ppermute(x, ("seq", "tp"), pairs)


def in_slab(x, flip):
    return permuted(x, lambda z, q, y: (z, q ^ flip, y))


def across(x):
    return permuted(x, lambda z, q, y: (z, q, 1 - y))


def even_pair(x):
    return permuted(x, lambda z, q, y: (z ^ 1, q, y))


def odd_pair(x):
    return permuted(x, lambda z, q, y: (3 - z, q, y) if z in (1, 2) else (z, q ^ 1, y))


def half_pair(x):
    return permuted(x, lambda z, q, y: (z ^ 2, q, y))


def tied(*arrays):
    return lax.optimization_barrier(arrays)


def as_row(column):
    wide = jnp.broadcast_to(column, (column.shape[0], 128))
    return jnp.transpose(wide)[:8]


def as_column(row):
    return jnp.transpose(jnp.broadcast_to(row, (128, row.shape[1])))


def start(copies):
    for copy in copies:
        copy.start()


def wait(copies):
    for copy in copies:
        copy.wait()


def norm_kernel(tokens, gain, out):
    part = tokens.shape[1] // out.shape[0]
    source = tokens[...].astype(jnp.float32)
    mean = jnp.mean(source * source, axis=1, keepdims=True)
    normed = source * lax.rsqrt(mean + eps) * gain[...]
    for j in range(out.shape[0]):
        out[j, :, :part] = normed[:, j * part:(j + 1) * part].astype(jnp.bfloat16)
        out[j, :, part:] = jnp.zeros((out.shape[1], out.shape[2] - part), jnp.bfloat16)


def norm(tokens, gain, slabs):
    count, depth = tokens.shape
    shape = (slabs, count, pl.cdiv(depth // slabs, 128) * 128)
    return pl.pallas_call(
        norm_kernel,
        out_shape=jax.ShapeDtypeStruct(shape, jnp.bfloat16),
        in_specs=[VMEM, VMEM],
        out_specs=VMEM,
        compiler_params=pltpu.CompilerParams(vmem_limit_bytes=KERNEL_VMEM),
        name="norm",
    )(tokens, gain[None])


def token_copies(xs, at, out, sems):
    return [
        pltpu.make_async_copy(x.at[at], out.at[r], sems.at[r]) for r, x in enumerate(xs)
    ]


def blank_tail(w, rows):
    tail = w.shape[-2] - rows
    w[..., rows:, :] = jnp.zeros(w.shape[:-2] + (tail, w.shape[-1]), w.dtype)


def early_kernel(
    place, xa, xb, xc, xd, own, near, far, acc, x_all, w_all, held, x_sem, w_sem, sems,
):
    z = place[0]
    kinds, rows = own.shape[:2]
    copies = []
    for i, w in enumerate((own, near, far)):
        dst = w_all.at[i, :, pl.ds(0, rows), :]
        copies.append([pltpu.make_async_copy(w, dst, w_sem.at[i])])
        copies[i] += token_copies((xa, xb, xc, xd), z ^ i, x_all.at[i], x_sem.at[i])
        start(copies[i])
    blank_tail(w_all, rows)
    stores = []
    for step in range(3):
        wait(copies[step])
        for r in range(SLAB):
            x = x_all[step, r]
            for kind in range(kinds):
                term = jnp.dot(x, w_all[step, kind], preferred_element_type=jnp.float32)
                held[r, kind] = term if step == 0 else held[r, kind] + term
            if step == 2:
                stores.append(pltpu.make_async_copy(held.at[r], acc.at[r], sems.at[r]))
                stores[-1].start()
    wait(stores)


def early(place, xs, own, near, far):
    kinds, rows, width = own.shape
    slabs, count, wide = xs[0].shape
    return pl.pallas_call(
        early_kernel,
        out_shape=jax.ShapeDtypeStruct((SLAB, kinds, count, width), jnp.float32),
        in_specs=[SMEM] + [HBM] * 7,
        out_specs=HBM,
        scratch_shapes=[
            pltpu.VMEM((3, SLAB, count, wide), jnp.bfloat16),
            pltpu.VMEM((3, kinds, wide, width), jnp.bfloat16),
            pltpu.VMEM((SLAB, kinds, count, width), jnp.float32),
            pltpu.SemaphoreType.DMA((3, SLAB)),
            pltpu.SemaphoreType.DMA((3,)),
            pltpu.SemaphoreType.DMA((SLAB,)),
        ],
        compiler_params=pltpu.CompilerParams(vmem_limit_bytes=KERNEL_VMEM),
        cost_estimate=pl.CostEstimate(
            flops=12 * kinds * SLAB * count * rows * width,
            bytes_accessed=6 * kinds * rows * width + 6 * SLAB * count * rows,
            transcendentals=0,
        ),
        name="early",
    )(place, *xs, own, near, far)


def late_kernel(
    place, xa, xb, xc, xd, acc, last, q_gain, k_gain,
    query, keys, values, squares, even, odd,
    x_all, w_all, held, q_all, k_all, v_all, x_sem, w_sem, acc_sem, sems,
):
    z, q = place[0], place[1]
    rows = last.shape[1]
    w_copy = pltpu.make_async_copy(last, w_all.at[:, pl.ds(0, rows), :], w_sem)
    w_copy.start()
    copies = token_copies((xa, xb, xc, xd), z ^ 3, x_all, x_sem)
    loads = [pltpu.make_async_copy(acc.at[r], held.at[r], acc_sem.at[r]) for r in range(SLAB)]
    for r in range(SLAB):
        copies[r].start()
        loads[r].start()
    count = held.shape[2]
    stores = []
    blank_tail(w_all, rows)
    w_copy.wait()
    for r in range(SLAB):
        copies[r].wait()
        loads[r].wait()
        x = x_all[r]
        rows = pl.ds(pl.multiple_of((q ^ r) * count, count), count)
        for kind in range(3):
            part = held[r, kind] + jnp.dot(x, w_all[kind], preferred_element_type=jnp.float32)
            if kind < 2:
                summed = as_row(jnp.sum(part * part, axis=1, keepdims=True))
                squares[kind:kind + 1, rows] = summed[:1]
                part = part * (q_gain, k_gain)[kind][...]
            held_out, out = ((q_all, query), (k_all, keys), (v_all, values))[kind]
            held_out[rows, :] = part.astype(held_out.dtype)
            store = pltpu.make_async_copy(held_out.at[rows, :], out.at[rows, :], sems.at[3 * r + kind])
            store.start()
            stores.append(store)
    reach = even.shape[1]
    for n, (out, at) in enumerate(((even, 1 - z % 2), (odd, z % 2))):
        rows = pl.ds(pl.multiple_of(at * reach, reach), reach)
        for k, src in enumerate((k_all, v_all)):
            sem = sems.at[3 * SLAB + 2 * n + k]
            stores.append(pltpu.make_async_copy(src.at[rows, :], out.at[k], sem))
            stores[-1].start()
    wait(stores)


def late(place, xs, acc, last, q_gain, k_gain):
    kinds, rows, width = last.shape
    count, wide = xs[0].shape[1:]
    slab = SLAB * count
    f32, bf16 = jnp.float32, jnp.bfloat16
    return pl.pallas_call(
        late_kernel,
        out_shape=(
            jax.ShapeDtypeStruct((slab, width), f32),
            jax.ShapeDtypeStruct((slab, width), bf16),
            jax.ShapeDtypeStruct((slab, width), bf16),
            jax.ShapeDtypeStruct((2, slab), f32),
            jax.ShapeDtypeStruct((2, 2 * count, width), bf16),
            jax.ShapeDtypeStruct((2, 2 * count, width), bf16),
        ),
        in_specs=[SMEM] + [HBM] * 6 + [VMEM] * 2,
        out_specs=(HBM, HBM, HBM, VMEM, HBM, HBM),
        scratch_shapes=[
            pltpu.VMEM((SLAB, count, wide), bf16),
            pltpu.VMEM((kinds, wide, width), bf16),
            pltpu.VMEM((SLAB, kinds, count, width), f32),
            pltpu.VMEM((slab, width), f32),
            pltpu.VMEM((slab, width), bf16),
            pltpu.VMEM((slab, width), bf16),
            pltpu.SemaphoreType.DMA((SLAB,)),
            pltpu.SemaphoreType.DMA,
            pltpu.SemaphoreType.DMA((SLAB,)),
            pltpu.SemaphoreType.DMA((3 * SLAB + 4,)),
        ],
        compiler_params=pltpu.CompilerParams(vmem_limit_bytes=KERNEL_VMEM),
        cost_estimate=pl.CostEstimate(
            flops=2 * kinds * slab * rows * width,
            bytes_accessed=2 * kinds * rows * width + 2 * slab * rows,
            transcendentals=0,
        ),
        name="late",
    )(place, *xs, acc, last, q_gain, k_gain)


def attend_kernel(
    full_width, place, spans, query, keys, values, even, odd, mine, near, mid, seg, o0, o1, o2, o3,
    q_all, k_all, v_all, o_all, scale_all, sems,
):
    z, q = place[0], place[1]
    slab = query.shape[0]
    count = slab // SLAB
    half = even.shape[1]
    upper = half + slab
    is_even = z % 2 == 0
    even_at = pl.multiple_of(jnp.where(is_even, upper, 0), half)
    odd_at = pl.multiple_of(jnp.where(is_even, 0, upper), half)
    copies = [pltpu.make_async_copy(query, q_all, sems.at[0])]
    for k, (whole, out) in enumerate(((keys, k_all), (values, v_all))):
        for n, (src, at) in enumerate(((whole, half), (even.at[k], even_at), (odd.at[k], odd_at))):
            dst = out.at[pl.ds(at, src.shape[0]), :]
            copies.append(pltpu.make_async_copy(src, dst, sems.at[1 + 3 * k + n]))
    start(copies)
    scale = [lax.rsqrt(sums[...] / full_width + eps) for sums in (mine, near, mid)]
    scale_all[:, half:upper] = scale[0]
    scale_all[:, :half] = jnp.where(is_even, scale[2], scale[1])[:, slab - half:]
    scale_all[:, upper:] = jnp.where(is_even, scale[1], scale[2])[:, :half]
    wait(copies)
    ext = k_all.shape[0]
    heads = query.shape[1] // HEAD_DIM
    factor = HEAD_DIM ** (-0.5) * math.log2(math.e)

    def block(r, _):
        b = q ^ r
        at_query = pl.multiple_of(b * count + half, count)
        query_seg = as_column(seg[:, pl.ds(at_query, count)])
        q_scale = as_column(scale_all[0:1, pl.ds(at_query, count)])
        for tiles in range(2, 2 * half // count + 2):
            @pl.when(spans[b, 1] == tiles)
            def _():
                width = tiles * count
                begin = pl.multiple_of(spans[b, 0], 128)
                keys_at = pl.ds(begin, width)
                mask = jnp.tile(query_seg, (1, width // 128)) == seg[:, keys_at]
                k_scale = scale_all[1:2, keys_at] * factor
                for h in range(heads):
                    cols = slice(h * HEAD_DIM, (h + 1) * HEAD_DIM)
                    q_low = q_all[pl.ds(pl.multiple_of(b * count, count), count), cols] * q_scale
                    scores = lax.dot_general(
                        q_low.astype(jnp.bfloat16), k_all[keys_at, cols],
                        (((1,), (1,)), ((), ())), preferred_element_type=jnp.float32,
                    )
                    scores = jnp.where(mask, scores * k_scale, floor_score)
                    peak = jnp.max(scores, axis=1, keepdims=True)
                    weights = jnp.exp2(scores - peak)
                    total = jnp.sum(weights, axis=1, keepdims=True)
                    summed = jnp.dot(
                        weights.astype(jnp.bfloat16), v_all[keys_at, cols],
                        preferred_element_type=jnp.float32,
                    )
                    o_all[r, cols, :] = jnp.transpose(summed / total).astype(jnp.bfloat16)

        return 0

    lax.fori_loop(0, SLAB, block, 0)
    stores = [
        pltpu.make_async_copy(o_all.at[r], out, sems.at[r]) for r, out in enumerate((o0, o1, o2, o3))
    ]
    start(stores)
    wait(stores)


def key_spans(seg, slab, count, half):
    ext = seg.shape[0]
    index = jnp.arange(ext, dtype=jnp.int32)
    blocks = seg[half:half + slab].reshape(-1, count)
    first, last = blocks[:, :1], blocks[:, -1:]
    begin = jnp.min(jnp.where(seg == first, index, ext), axis=1) // 128 * 128
    end = jnp.max(jnp.where(seg == last, index, -1), axis=1) + 1
    tiles = jnp.maximum((end - begin + count - 1) // count, 2)
    return jnp.stack([jnp.minimum(begin, ext - tiles * count), tiles], axis=1)


def attend(full_width, place, spans, query, keys, values, even, odd, sums, seg):
    slab, width = query.shape
    half = even.shape[1]
    count = slab // SLAB
    ext = slab + 2 * half
    bf16 = jnp.bfloat16
    window = count + 2 * half
    return pl.pallas_call(
        functools.partial(attend_kernel, full_width),
        out_shape=(jax.ShapeDtypeStruct((width, count), bf16),) * SLAB,
        in_specs=[SMEM] * 2 + [HBM] * 5 + [VMEM] * 4,
        out_specs=(HBM,) * SLAB,
        scratch_shapes=[
            pltpu.VMEM((slab, width), jnp.float32),
            pltpu.VMEM((ext, width), bf16),
            pltpu.VMEM((ext, width), bf16),
            pltpu.VMEM((SLAB, width, count), bf16),
            pltpu.VMEM((2, ext), jnp.float32),
            pltpu.SemaphoreType.DMA((7,)),
        ],
        compiler_params=pltpu.CompilerParams(vmem_limit_bytes=KERNEL_VMEM),
        cost_estimate=pl.CostEstimate(
            flops=64 * SLAB * count * window * width,
            bytes_accessed=4 * ext * width + 4 * slab * width,
            transcendentals=SLAB * count * window * width // HEAD_DIM,
        ),
        name="attend",
    )(place, spans, query, keys, values, even, odd, *sums, seg)


def out_kernel(
    place, c20, c01, c31, c30, c11, c21, c10, c00, wa, wb, wc, wd,
    residual, scale, out, c_all, w_all, total, placed, c_sem, w_sem,
):
    z, q = place[0], place[1]
    width = c00.shape[0]
    c_copies = []
    for i in range(2):
        for r, pair in enumerate(((c00, c01), (c10, c11), (c20, c21), (c30, c31))):
            at = pl.multiple_of((q ^ r) * width, width)
            dst = c_all.at[i, pl.ds(at, width), :]
            c_copies.append(pltpu.make_async_copy(pair[i], dst, c_sem.at[r, i]))
    start(c_copies)
    rows = wa.shape[2]
    w_copies = []
    for i in range(2):
        for r, w in enumerate((wa, wb, wc, wd)):
            for j in range(2):
                dst = w_all.at[i, pl.ds((2 * r + j) * rows, rows), :]
                w_copies.append(pltpu.make_async_copy(w.at[i, j], dst, w_sem.at[r, j, i]))
    start(w_copies)
    column = as_column(scale[...])[:out.shape[0]]
    column = jnp.tile(column, (1, out.shape[1] // 128))
    wait(c_copies[:SLAB] + w_copies[:2 * SLAB])
    total[...] = jnp.dot(w_all[0], c_all[0], preferred_element_type=jnp.float32)
    wait(c_copies[SLAB:] + w_copies[2 * SLAB:])
    total[...] += jnp.dot(w_all[1], c_all[1], preferred_element_type=jnp.float32)
    kept = out.shape[0] // (2 * SLAB)
    for r in range(SLAB):
        for j in range(2):
            at = pl.multiple_of((((z % 2) ^ j) * SLAB + (q ^ r)) * kept, 8)
            begin = (2 * r + j) * rows
            placed[pl.ds(at, kept), :] = total[begin:begin + kept, :]
    out[...] = (residual[...].astype(jnp.float32) + column * placed[...]).astype(jnp.bfloat16)


def output(place, blocks, pieces, residual, scale):
    count = blocks[0].shape[1]
    rows, depth = pieces[0].shape[2:]
    share = residual.shape[0]
    scale = jnp.pad(scale, (0, -share % 128))[None]
    return pl.pallas_call(
        out_kernel,
        out_shape=jax.ShapeDtypeStruct((share, count), jnp.bfloat16),
        in_specs=[SMEM] + [HBM] * 12 + [VMEM] * 2,
        out_specs=VMEM,
        scratch_shapes=[
            pltpu.VMEM((2, depth, count), jnp.bfloat16),
            pltpu.VMEM((2, 2 * SLAB * rows, depth), jnp.bfloat16),
            pltpu.VMEM((2 * SLAB * rows, count), jnp.float32),
            pltpu.VMEM((share, count), jnp.float32),
            pltpu.SemaphoreType.DMA((SLAB, 2)),
            pltpu.SemaphoreType.DMA((SLAB, 2, 2)),
        ],
        compiler_params=pltpu.CompilerParams(vmem_limit_bytes=KERNEL_VMEM),
        cost_estimate=pl.CostEstimate(
            flops=4 * share * count * depth,
            bytes_accessed=4 * share * depth,
            transcendentals=0,
        ),
        name="output",
    )(place, *blocks, *pieces, residual, scale)


def rows_of_slab(q, got):
    placed = []
    for b in range(SLAB):
        piece = got[b]
        for other in range(1, SLAB):
            piece = jnp.where(q == other, got[b ^ other], piece)
        placed.append(piece)
    return jnp.concatenate(placed, axis=1)


def slab_plan(tokens, norm_gain, qkv_weight, q_gain, k_gain, out_weight, layer_scale, segment_ids):
    count = tokens.shape[0]
    seq, tp = lax.axis_index("seq"), lax.axis_index("tp")
    slabs = lax.axis_size("seq") // SLAB
    z, q = seq // SLAB, seq % SLAB
    place = jnp.stack([z, q, tp]).astype(jnp.int32)
    width = qkv_weight.shape[2] // SLAB
    full_width = qkv_weight.shape[2] * lax.axis_size("tp")
    slab, half = SLAB * count, 2 * count
    home = z // 2 == tp

    by_kind = jnp.transpose(qkv_weight, (1, 0, 2))
    cut = [lax.dynamic_slice_in_dim(by_kind, (q ^ r) * width, width, 2) for r in range(SLAB)]
    got = [cut[0]] + [in_slab(cut[r], r) for r in range(1, SLAB)]
    x0 = norm(tokens, norm_gain, slabs)
    out_own = jnp.pad(jnp.transpose(out_weight), ((0, -out_weight.shape[1] % 16), (0, 0)))
    own = rows_of_slab(q, got)
    out_near, out_far = even_pair(out_own), half_pair(out_own)
    gains = [lax.dynamic_slice_in_dim(g, q * width, width, 0)[None] for g in (q_gain, k_gain)]

    x0, out_near, out_far, *gains = tied(x0, out_near, out_far, *gains)
    out_last = even_pair(out_far)
    x2 = in_slab(x0, 2)
    out_last, own, x0 = tied(out_last, own, x0)
    near, far = even_pair(own), half_pair(own)
    x1 = in_slab(x0, 1)
    out_last, x1 = tied(out_last, x1)
    close, away = jnp.stack([out_own, out_near]), jnp.stack([out_far, out_last])
    keep, give = jnp.where(home, close, away), jnp.where(home, away, close)
    got = across(give)
    keep_x = in_slab(keep, 2)
    near, far, x1, x2, got, keep_x = tied(near, far, x1, x2, got, keep_x)
    last = even_pair(far)
    x3, got_x = in_slab(x2, 1), in_slab(got, 2)
    wa = jnp.stack([keep, got])
    wb = in_slab(wa, 1)
    xs = (x0, x1, x2, x3)
    acc = early(place, xs, own, near, far)
    last, acc, wb, got_x = tied(last, acc, wb, got_x)
    wc = jnp.stack([keep_x, got_x])

    query, keys, values, squares, even, odd = late(place, xs, acc, last, *gains)
    even, odd = even_pair(even), odd_pair(odd)
    sums = squares
    for r in range(1, SLAB):
        sums = sums + in_slab(squares, r)
    sums = sums + across(sums)
    sums = (sums, even_pair(sums), odd_pair(sums))
    query, wc = tied(query, wc)
    wd = in_slab(wc, 1)

    outside = jnp.full((half,), -1, jnp.int32)
    seg = jnp.concatenate([outside, segment_ids, outside], axis=0)
    seg = lax.dynamic_slice_in_dim(seg, z * slab, slab + 2 * half, 0)
    spans = key_spans(seg, slab, count, half)
    seg = seg.astype(jnp.float32)[None]
    blocks = attend(full_width, place, spans, query, keys, values, even, odd, sums, seg)
    *blocks, wd = tied(*blocks, wd)
    pieces = (wa, wb, wc, wd)
    spread = []
    for r, i in ((2, 0), (0, 1), (3, 1), (3, 0), (1, 1), (2, 1), (1, 0), (0, 0)):
        to = functools.partial(lambda r, i, z, q, y: (z, q ^ r, y ^ i), r, i)
        spread.append(permuted(blocks[r], to) if r or i else blocks[r])

    share = layer_scale.shape[0]
    residual = jnp.transpose(lax.dynamic_slice_in_dim(tokens, tp * share, share, 1))
    return jnp.transpose(output(place, spread, pieces, residual, layer_scale))


def solution(mesh):
    def shards(*args):
        heads = args[2].shape[2] // HEAD_DIM
        slab = mesh.shape["seq"] == 16 and mesh.shape["tp"] == 2 and heads % SLAB == 0
        return (slab_plan if slab else row_plan)(*args)

    return jax.shard_map(
        shards,
        mesh=mesh,
        in_specs=(
            P("seq", None),
            P(),
            P("seq", None, "tp"),
            P("tp"),
            P("tp"),
            P("tp", "seq"),
            P("tp"),
            P(),
        ),
        out_specs=P("seq", "tp"),
        check_vma=False,
    )
```

```python
import functools
import math

import jax
import jax.numpy as jnp
from jax import lax
from jax.experimental import pallas as pl
from jax.experimental.pallas import tpu as pltpu
from jax.sharding import PartitionSpec as P

HEAD_DIM = 128
SLAB = 4

eps = 1e-06
floor_score = -1e30


def passed_along(x, axis, by):
    size = lax.axis_size(axis)
    pairs = [(i, i + by) for i in range(size) if 0 <= i + by < size]
    return lax.ppermute(x, axis, pairs)


def masked_scores(query, keys, query_seg, key_seg):
    scores = jnp.einsum(
        "qhd,khd->hqk", query, keys, preferred_element_type=jnp.float32
    ) * HEAD_DIM ** (-0.5)
    mask = (query_seg[:, None] == key_seg[None, :])[None]
    return (jnp.where(mask, scores, floor_score), mask)


def row_plan(tokens, norm_gain, qkv_weight, q_gain, k_gain, out_weight, layer_scale, segment_ids):
    count = tokens.shape[0]
    source = tokens.astype(jnp.float32)
    normed = (
        source * lax.rsqrt(jnp.mean(source * source, axis=-1, keepdims=True) + eps) * norm_gain
    ).astype(jnp.bfloat16)
    local_width = qkv_weight.shape[2]
    heads = local_width // HEAD_DIM
    joined = jnp.einsum(
        "td,dch->tch",
        normed,
        lax.all_gather(qkv_weight, "seq", axis=0, tiled=True),
        preferred_element_type=jnp.float32,
    )
    query = joined[:, 0]
    keys = joined[:, 1]
    values = joined[:, 2]
    query_sq, key_sq = lax.psum(
        (jnp.sum(query * query, axis=-1), jnp.sum(keys * keys, axis=-1)), "tp"
    )
    full_width = local_width * lax.axis_size("tp")
    query_normed = (query * lax.rsqrt(query_sq / full_width + eps)[:, None] * q_gain).astype(
        jnp.bfloat16
    )
    key_normed = (keys * lax.rsqrt(key_sq / full_width + eps)[:, None] * k_gain).astype(
        jnp.bfloat16
    )
    paired = jnp.stack([key_normed, values.astype(jnp.bfloat16)], axis=1)
    pieces = []
    for offset in (2, 1, 0, -1, -2):
        if offset == 0:
            pieces.append(paired)
        else:
            pieces.append(passed_along(paired, "seq", offset))
    widened = jnp.concatenate(pieces, axis=0)
    position = lax.axis_index("seq")
    outside = jnp.full((2 * count,), -1, jnp.int32)
    seg_pad = jnp.concatenate([outside, segment_ids, outside], axis=0)
    key_seg = lax.dynamic_slice_in_dim(seg_pad, position * count, 5 * count, 0)
    query_seg = lax.dynamic_slice_in_dim(segment_ids, position * count, count, 0)
    query_heads = query_normed.reshape(count, heads, HEAD_DIM)
    key_heads = widened[:, 0].reshape(5 * count, heads, HEAD_DIM)
    value_heads = widened[:, 1].reshape(5 * count, heads, HEAD_DIM)
    scores, mask = masked_scores(query_heads, key_heads, query_seg, key_seg)
    peak = jnp.max(scores, axis=-1, keepdims=True)
    weights = jnp.where(mask, jnp.exp(scores - peak), 0.0)
    total = jnp.sum(weights, axis=-1)
    probs = weights.astype(jnp.bfloat16)
    summed = jnp.einsum("hqk,khd->qhd", probs, value_heads, preferred_element_type=jnp.float32)
    context = (
        (summed / jnp.transpose(total)[:, :, None]).reshape(count, local_width).astype(jnp.bfloat16)
    )
    terms = jnp.dot(
        context,
        lax.all_gather(out_weight, "seq", axis=1, tiled=True),
        preferred_element_type=jnp.float32,
    )
    projected = lax.psum_scatter(terms, "tp", scatter_dimension=1, tiled=True)
    share = layer_scale.shape[0]
    residual = lax.dynamic_slice_in_dim(source, lax.axis_index("tp") * share, share, 1)
    return (residual + layer_scale * projected).astype(jnp.bfloat16)


ANY = pl.BlockSpec(memory_space=pl.ANY)
VMEM = pl.BlockSpec(memory_space=pltpu.VMEM)
SMEM = pl.BlockSpec(memory_space=pltpu.SMEM)
HBM = pl.BlockSpec(memory_space=pltpu.HBM)
KERNEL_VMEM = 60 * 1024 * 1024
HELD_VMEM = 24 * 1024 * 1024


def permuted(x, to):
    slabs, tps = lax.axis_size("seq") // SLAB, lax.axis_size("tp")
    pairs = []
    for i in range(slabs * SLAB * tps):
        z, q, y = to(i // (SLAB * tps), i // tps % SLAB, i % tps)
        pairs.append((i, (z * SLAB + q) * tps + y))
    return lax.ppermute(x, ("seq", "tp"), pairs)


def in_slab(x, flip):
    return permuted(x, lambda z, q, y: (z, q ^ flip, y))


def across(x):
    return permuted(x, lambda z, q, y: (z, q, 1 - y))


def even_pair(x):
    return permuted(x, lambda z, q, y: (z ^ 1, q, y))


def odd_pair(x):
    return permuted(x, lambda z, q, y: (3 - z, q, y) if z in (1, 2) else (z, q ^ 1, y))


def half_pair(x):
    return permuted(x, lambda z, q, y: (z ^ 2, q, y))


def tied(*arrays):
    return lax.optimization_barrier(arrays)


def as_row(column):
    wide = jnp.broadcast_to(column, (column.shape[0], 128))
    return jnp.transpose(wide)[:8]


def as_column(row):
    return jnp.transpose(jnp.broadcast_to(row, (128, row.shape[1])))


def start(copies):
    for copy in copies:
        copy.start()


def wait(copies):
    for copy in copies:
        copy.wait()


def norm_kernel(tokens, gain, out):
    part = tokens.shape[1] // out.shape[0]
    source = tokens[...].astype(jnp.float32)
    mean = jnp.mean(source * source, axis=1, keepdims=True)
    normed = source * lax.rsqrt(mean + eps) * gain[...]
    for j in range(out.shape[0]):
        out[j, :, :part] = normed[:, j * part:(j + 1) * part].astype(jnp.bfloat16)
        out[j, :, part:] = jnp.zeros((out.shape[1], out.shape[2] - part), jnp.bfloat16)


def norm(tokens, gain, slabs):
    count, depth = tokens.shape
    shape = (slabs, count, pl.cdiv(depth // slabs, 128) * 128)
    return pl.pallas_call(
        norm_kernel,
        out_shape=jax.ShapeDtypeStruct(shape, jnp.bfloat16),
        in_specs=[VMEM, VMEM],
        out_specs=VMEM,
        compiler_params=pltpu.CompilerParams(vmem_limit_bytes=KERNEL_VMEM),
        name="norm",
    )(tokens, gain[None])


def token_copies(xs, at, out, sems):
    return [
        pltpu.make_async_copy(x.at[at], out.at[r], sems.at[r]) for r, x in enumerate(xs)
    ]


def blank_tail(w, rows):
    tail = w.shape[-2] - rows
    w[..., rows:, :] = jnp.zeros(w.shape[:-2] + (tail, w.shape[-1]), w.dtype)


def early_kernel(
    place, xa, xb, xc, xd, own, near, far, acc, x_last, x_all, w_all, x_sem, w_sem, last_sem,
):
    z = place[0]
    kinds, rows = own.shape[:2]
    copies = []
    for i, w in enumerate((own, near, far)):
        dst = w_all.at[i, :, pl.ds(0, rows), :]
        copies.append([pltpu.make_async_copy(w, dst, w_sem.at[i])])
        copies[i] += token_copies((xa, xb, xc, xd), z ^ i, x_all.at[i], x_sem.at[i])
        start(copies[i])
    last_copies = token_copies((xa, xb, xc, xd), z ^ 3, x_last, last_sem)
    start(last_copies)
    blank_tail(w_all, rows)
    for step in range(3):
        wait(copies[step])
        for r in range(SLAB):
            x = x_all[step, r]
            for kind in range(kinds):
                term = jnp.dot(x, w_all[step, kind], preferred_element_type=jnp.float32)
                acc[r, kind] = term if step == 0 else acc[r, kind] + term
    wait(last_copies)


def early(place, xs, own, near, far):
    kinds, rows, width = own.shape
    slabs, count, wide = xs[0].shape
    return pl.pallas_call(
        early_kernel,
        out_shape=(
            jax.ShapeDtypeStruct((SLAB, kinds, count, width), jnp.float32),
            jax.ShapeDtypeStruct((SLAB, count, wide), jnp.bfloat16),
        ),
        in_specs=[SMEM] + [HBM] * 7,
        out_specs=(VMEM, VMEM),
        scratch_shapes=[
            pltpu.VMEM((3, SLAB, count, wide), jnp.bfloat16),
            pltpu.VMEM((3, kinds, wide, width), jnp.bfloat16),
            pltpu.SemaphoreType.DMA((3, SLAB)),
            pltpu.SemaphoreType.DMA((3,)),
            pltpu.SemaphoreType.DMA((SLAB,)),
        ],
        compiler_params=pltpu.CompilerParams(vmem_limit_bytes=HELD_VMEM),
        cost_estimate=pl.CostEstimate(
            flops=12 * kinds * SLAB * count * rows * width,
            bytes_accessed=6 * kinds * rows * width + 6 * SLAB * count * rows,
            transcendentals=0,
        ),
        name="early",
    )(place, *xs, own, near, far)


def late_kernel(
    place, x_last, acc, last, q_gain, k_gain, query, keys, values, squares, even, odd,
    w_all, q_all, k_all, v_all, sems,
):
    z, q = place[0], place[1]
    rows = last.shape[1]
    w_all[:, :rows, :] = last[...]
    blank_tail(w_all, rows)
    count = acc.shape[2]
    stores = []
    for r in range(SLAB):
        rows = pl.ds(pl.multiple_of((q ^ r) * count, count), count)
        for kind in range(3):
            part = acc[r, kind] + jnp.dot(
                x_last[r], w_all[kind], preferred_element_type=jnp.float32
            )
            if kind < 2:
                summed = as_row(jnp.sum(part * part, axis=1, keepdims=True))
                squares[kind:kind + 1, rows] = summed[:1]
                part = part * (q_gain, k_gain)[kind][...]
            held_out, out = ((q_all, query), (k_all, keys), (v_all, values))[kind]
            held_out[rows, :] = part.astype(held_out.dtype)
            store = pltpu.make_async_copy(held_out.at[rows, :], out.at[rows, :], sems.at[3 * r + kind])
            store.start()
            stores.append(store)
    reach = even.shape[1]
    for n, (out, at) in enumerate(((even, 1 - z % 2), (odd, z % 2))):
        rows = pl.ds(pl.multiple_of(at * reach, reach), reach)
        for k, src in enumerate((k_all, v_all)):
            sem = sems.at[3 * SLAB + 2 * n + k]
            stores.append(pltpu.make_async_copy(src.at[rows, :], out.at[k], sem))
            stores[-1].start()
    wait(stores)


def late(place, x_last, acc, last, q_gain, k_gain):
    kinds, rows, width = last.shape
    count, wide = x_last.shape[1:]
    slab = SLAB * count
    f32, bf16 = jnp.float32, jnp.bfloat16
    return pl.pallas_call(
        late_kernel,
        out_shape=(
            jax.ShapeDtypeStruct((slab, width), f32),
            jax.ShapeDtypeStruct((slab, width), bf16),
            jax.ShapeDtypeStruct((slab, width), bf16),
            jax.ShapeDtypeStruct((2, slab), f32),
            jax.ShapeDtypeStruct((2, 2 * count, width), bf16),
            jax.ShapeDtypeStruct((2, 2 * count, width), bf16),
        ),
        in_specs=[SMEM] + [VMEM] * 5,
        out_specs=(HBM, HBM, HBM, VMEM, HBM, HBM),
        scratch_shapes=[
            pltpu.VMEM((kinds, wide, width), bf16),
            pltpu.VMEM((slab, width), f32),
            pltpu.VMEM((slab, width), bf16),
            pltpu.VMEM((slab, width), bf16),
            pltpu.SemaphoreType.DMA((3 * SLAB + 4,)),
        ],
        compiler_params=pltpu.CompilerParams(vmem_limit_bytes=HELD_VMEM),
        cost_estimate=pl.CostEstimate(
            flops=2 * kinds * slab * rows * width,
            bytes_accessed=2 * kinds * rows * width + 2 * slab * rows,
            transcendentals=0,
        ),
        name="late",
    )(place, x_last, acc, last, q_gain, k_gain)


def attend_kernel(
    full_width, place, spans, query, keys, values, even, odd, mine, near, mid, seg, o0, o1, o2, o3,
    q_all, k_all, v_all, o_all, scale_all, sems,
):
    z, q = place[0], place[1]
    slab = query.shape[0]
    count = slab // SLAB
    half = even.shape[1]
    upper = half + slab
    is_even = z % 2 == 0
    even_at = pl.multiple_of(jnp.where(is_even, upper, 0), half)
    odd_at = pl.multiple_of(jnp.where(is_even, 0, upper), half)
    copies = [pltpu.make_async_copy(query, q_all, sems.at[0])]
    for k, (whole, out) in enumerate(((keys, k_all), (values, v_all))):
        for n, (src, at) in enumerate(((whole, half), (even.at[k], even_at), (odd.at[k], odd_at))):
            dst = out.at[pl.ds(at, src.shape[0]), :]
            copies.append(pltpu.make_async_copy(src, dst, sems.at[1 + 3 * k + n]))
    start(copies)
    scale = [lax.rsqrt(sums[...] / full_width + eps) for sums in (mine, near, mid)]
    scale_all[:, half:upper] = scale[0]
    scale_all[:, :half] = jnp.where(is_even, scale[2], scale[1])[:, slab - half:]
    scale_all[:, upper:] = jnp.where(is_even, scale[1], scale[2])[:, :half]
    wait(copies)
    ext = k_all.shape[0]
    heads = query.shape[1] // HEAD_DIM
    factor = HEAD_DIM ** (-0.5) * math.log2(math.e)

    def block(r, _):
        b = q ^ r
        at_query = pl.multiple_of(b * count + half, count)
        query_seg = as_column(seg[:, pl.ds(at_query, count)])
        q_scale = as_column(scale_all[0:1, pl.ds(at_query, count)])
        for tiles in range(2, 2 * half // count + 2):
            @pl.when(spans[b, 1] == tiles)
            def _():
                width = tiles * count
                begin = pl.multiple_of(spans[b, 0], 128)
                keys_at = pl.ds(begin, width)
                mask = jnp.tile(query_seg, (1, width // 128)) == seg[:, keys_at]
                k_scale = scale_all[1:2, keys_at] * factor
                for h in range(heads):
                    cols = slice(h * HEAD_DIM, (h + 1) * HEAD_DIM)
                    q_low = q_all[pl.ds(pl.multiple_of(b * count, count), count), cols] * q_scale
                    scores = lax.dot_general(
                        q_low.astype(jnp.bfloat16), k_all[keys_at, cols],
                        (((1,), (1,)), ((), ())), preferred_element_type=jnp.float32,
                    )
                    scores = jnp.where(mask, scores * k_scale, floor_score)
                    peak = jnp.max(scores, axis=1, keepdims=True)
                    weights = jnp.exp2(scores - peak)
                    total = jnp.sum(weights, axis=1, keepdims=True)
                    summed = jnp.dot(
                        weights.astype(jnp.bfloat16), v_all[keys_at, cols],
                        preferred_element_type=jnp.float32,
                    )
                    o_all[r, cols, :] = jnp.transpose(summed / total).astype(jnp.bfloat16)

        return 0

    lax.fori_loop(0, SLAB, block, 0)
    stores = [
        pltpu.make_async_copy(o_all.at[r], out, sems.at[r]) for r, out in enumerate((o0, o1, o2, o3))
    ]
    start(stores)
    wait(stores)


def key_spans(seg, slab, count, half):
    ext = seg.shape[0]
    index = jnp.arange(ext, dtype=jnp.int32)
    blocks = seg[half:half + slab].reshape(-1, count)
    first, last = blocks[:, :1], blocks[:, -1:]
    begin = jnp.min(jnp.where(seg == first, index, ext), axis=1) // 128 * 128
    end = jnp.max(jnp.where(seg == last, index, -1), axis=1) + 1
    tiles = jnp.maximum((end - begin + count - 1) // count, 2)
    return jnp.stack([jnp.minimum(begin, ext - tiles * count), tiles], axis=1)


def attend(full_width, place, spans, query, keys, values, even, odd, sums, seg):
    slab, width = query.shape
    half = even.shape[1]
    count = slab // SLAB
    ext = slab + 2 * half
    bf16 = jnp.bfloat16
    window = count + 2 * half
    return pl.pallas_call(
        functools.partial(attend_kernel, full_width),
        out_shape=(jax.ShapeDtypeStruct((width, count), bf16),) * SLAB,
        in_specs=[SMEM] * 2 + [HBM] * 5 + [VMEM] * 4,
        out_specs=(HBM,) * SLAB,
        scratch_shapes=[
            pltpu.VMEM((slab, width), jnp.float32),
            pltpu.VMEM((ext, width), bf16),
            pltpu.VMEM((ext, width), bf16),
            pltpu.VMEM((SLAB, width, count), bf16),
            pltpu.VMEM((2, ext), jnp.float32),
            pltpu.SemaphoreType.DMA((7,)),
        ],
        compiler_params=pltpu.CompilerParams(vmem_limit_bytes=HELD_VMEM),
        cost_estimate=pl.CostEstimate(
            flops=64 * SLAB * count * window * width,
            bytes_accessed=4 * ext * width + 4 * slab * width,
            transcendentals=SLAB * count * window * width // HEAD_DIM,
        ),
        name="attend",
    )(place, spans, query, keys, values, even, odd, *sums, seg)


def out_kernel(
    place, c20, c01, c31, c30, c11, c21, c10, c00, wa0, wb0, wc0, wd0, wa1, wb1, wc1, wd1,
    residual, scale, out, c_all, w_all, total, placed, c_sem, w_sem,
):
    z, q = place[0], place[1]
    width = c00.shape[0]
    c_copies = []
    for i in range(2):
        for r, pair in enumerate(((c00, c01), (c10, c11), (c20, c21), (c30, c31))):
            at = pl.multiple_of((q ^ r) * width, width)
            dst = c_all.at[i, pl.ds(at, width), :]
            c_copies.append(pltpu.make_async_copy(pair[i], dst, c_sem.at[r, i]))
    start(c_copies)
    rows = wa0.shape[1]
    w_copies = []
    for i in range(2):
        for r, w in enumerate(((wa0, wb0, wc0, wd0), (wa1, wb1, wc1, wd1))[i]):
            for j in range(2):
                dst = w_all.at[i, pl.ds((2 * r + j) * rows, rows), :]
                w_copies.append(pltpu.make_async_copy(w.at[j], dst, w_sem.at[r, j, i]))
    start(w_copies)
    column = as_column(scale[...])[:out.shape[0]]
    column = jnp.tile(column, (1, out.shape[1] // 128))
    wait(c_copies[:SLAB] + w_copies[:2 * SLAB])
    total[...] = jnp.dot(w_all[0], c_all[0], preferred_element_type=jnp.float32)
    wait(c_copies[SLAB:] + w_copies[2 * SLAB:])
    total[...] += jnp.dot(w_all[1], c_all[1], preferred_element_type=jnp.float32)
    kept = out.shape[0] // (2 * SLAB)
    for r in range(SLAB):
        for j in range(2):
            at = pl.multiple_of((((z % 2) ^ j) * SLAB + (q ^ r)) * kept, 8)
            begin = (2 * r + j) * rows
            placed[pl.ds(at, kept), :] = total[begin:begin + kept, :]
    out[...] = (residual[...].astype(jnp.float32) + column * placed[...]).astype(jnp.bfloat16)


def output(place, blocks, pieces, residual, scale):
    count = blocks[0].shape[1]
    rows, depth = pieces[0].shape[1:]
    share = residual.shape[0]
    scale = jnp.pad(scale, (0, -share % 128))[None]
    return pl.pallas_call(
        out_kernel,
        out_shape=jax.ShapeDtypeStruct((share, count), jnp.bfloat16),
        in_specs=[SMEM] + [HBM] * 16 + [VMEM] * 2,
        out_specs=VMEM,
        scratch_shapes=[
            pltpu.VMEM((2, depth, count), jnp.bfloat16),
            pltpu.VMEM((2, 2 * SLAB * rows, depth), jnp.bfloat16),
            pltpu.VMEM((2 * SLAB * rows, count), jnp.float32),
            pltpu.VMEM((share, count), jnp.float32),
            pltpu.SemaphoreType.DMA((SLAB, 2)),
            pltpu.SemaphoreType.DMA((SLAB, 2, 2)),
        ],
        compiler_params=pltpu.CompilerParams(vmem_limit_bytes=HELD_VMEM),
        cost_estimate=pl.CostEstimate(
            flops=4 * share * count * depth,
            bytes_accessed=4 * share * depth,
            transcendentals=0,
        ),
        name="output",
    )(place, *blocks, *pieces, residual, scale)


def rows_of_slab(q, got):
    placed = []
    for b in range(SLAB):
        piece = got[b]
        for other in range(1, SLAB):
            piece = jnp.where(q == other, got[b ^ other], piece)
        placed.append(piece)
    return jnp.concatenate(placed, axis=1)


def slab_plan(tokens, norm_gain, qkv_weight, q_gain, k_gain, out_weight, layer_scale, segment_ids):
    count = tokens.shape[0]
    seq, tp = lax.axis_index("seq"), lax.axis_index("tp")
    slabs = lax.axis_size("seq") // SLAB
    z, q = seq // SLAB, seq % SLAB
    place = jnp.stack([z, q, tp]).astype(jnp.int32)
    width = qkv_weight.shape[2] // SLAB
    full_width = qkv_weight.shape[2] * lax.axis_size("tp")
    slab, half = SLAB * count, 2 * count
    home = z // 2 == tp

    by_kind = jnp.transpose(qkv_weight, (1, 0, 2))
    cut = [lax.dynamic_slice_in_dim(by_kind, (q ^ r) * width, width, 2) for r in range(SLAB)]
    got = [cut[0]] + [in_slab(cut[r], r) for r in range(1, SLAB)]
    x0 = norm(tokens, norm_gain, slabs)
    out_own = jnp.pad(jnp.transpose(out_weight), ((0, -out_weight.shape[1] % 16), (0, 0)))
    own = rows_of_slab(q, got)
    out_near, out_far = even_pair(out_own), half_pair(out_own)
    gains = [lax.dynamic_slice_in_dim(g, q * width, width, 0)[None] for g in (q_gain, k_gain)]

    outside = jnp.full((half,), -1, jnp.int32)
    seg = jnp.concatenate([outside, segment_ids, outside], axis=0)
    seg = lax.dynamic_slice_in_dim(seg, z * slab, slab + 2 * half, 0)
    spans = key_spans(seg, slab, count, half)
    seg = seg.astype(jnp.float32)[None]
    x0, out_near, out_far, seg, spans, *gains = tied(x0, out_near, out_far, seg, spans, *gains)
    out_last = even_pair(out_far)
    x2 = in_slab(x0, 2)
    out_last, own, x0 = tied(out_last, own, x0)
    near, far = even_pair(own), half_pair(own)
    x1 = in_slab(x0, 1)
    out_last, x1 = tied(out_last, x1)
    close, away = jnp.stack([out_own, out_near]), jnp.stack([out_far, out_last])
    keep, give = jnp.where(home, close, away), jnp.where(home, away, close)
    got = across(give)
    keep_x = in_slab(keep, 2)
    near, far, x1, x2, got, keep_x = tied(near, far, x1, x2, got, keep_x)
    last = even_pair(far)
    x3 = in_slab(x2, 1)
    got_x, got_c, keep_c = in_slab(got, 2), in_slab(got, 1), in_slab(keep, 1)
    keep_xc = in_slab(tied(keep_x, x3)[0], 1)
    xs = (x0, x1, x2, x3)
    acc, x_last = early(place, xs, own, near, far)
    last, acc, x_last = tied(last, acc, x_last)
    query, keys, values, squares, even, odd = late(place, x_last, acc, last, *gains)
    even, odd = even_pair(even), odd_pair(odd)
    squares, got_x, got_c, keep_c, keep_xc = tied(squares, got_x, got_c, keep_c, keep_xc)
    sums = squares
    for r in range(1, SLAB):
        sums = sums + in_slab(squares, r)
    sums = sums + across(sums)
    sums = (sums, even_pair(sums), odd_pair(sums))
    got_xc = in_slab(got_x, 1)

    blocks = attend(full_width, place, spans, query, keys, values, even, odd, sums, seg)
    *blocks, got_xc = tied(*blocks, got_xc)
    pieces = (keep, keep_c, keep_x, keep_xc, got, got_c, got_x, got_xc)
    spread = []
    for r, i in ((2, 0), (0, 1), (3, 1), (3, 0), (1, 1), (2, 1), (1, 0), (0, 0)):
        to = functools.partial(lambda r, i, z, q, y: (z, q ^ r, y ^ i), r, i)
        spread.append(permuted(blocks[r], to) if r or i else blocks[r])

    share = layer_scale.shape[0]
    residual = jnp.transpose(lax.dynamic_slice_in_dim(tokens, tp * share, share, 1))
    return jnp.transpose(output(place, spread, pieces, residual, layer_scale))


def solution(mesh):
    def shards(*args):
        heads = args[2].shape[2] // HEAD_DIM
        slab = mesh.shape["seq"] == 16 and mesh.shape["tp"] == 2 and heads % SLAB == 0
        return (slab_plan if slab else row_plan)(*args)

    return jax.shard_map(
        shards,
        mesh=mesh,
        in_specs=(
            P("seq", None),
            P(),
            P("seq", None, "tp"),
            P("tp"),
            P("tp"),
            P("tp", "seq"),
            P("tp"),
            P(),
        ),
        out_specs=P("seq", "tp"),
        check_vma=False,
    )
```

```python
import functools
import math

import jax
import jax.numpy as jnp
from jax import lax
from jax.experimental import pallas as pl
from jax.experimental.pallas import tpu as pltpu
from jax.sharding import PartitionSpec as P

HEAD_DIM = 128
SLAB = 4

eps = 1e-06
floor_score = -1e30


def passed_along(x, axis, by):
    size = lax.axis_size(axis)
    pairs = [(i, i + by) for i in range(size) if 0 <= i + by < size]
    return lax.ppermute(x, axis, pairs)


def masked_scores(query, keys, query_seg, key_seg):
    scores = jnp.einsum(
        "qhd,khd->hqk", query, keys, preferred_element_type=jnp.float32
    ) * HEAD_DIM ** (-0.5)
    mask = (query_seg[:, None] == key_seg[None, :])[None]
    return (jnp.where(mask, scores, floor_score), mask)


def row_plan(tokens, norm_gain, qkv_weight, q_gain, k_gain, out_weight, layer_scale, segment_ids):
    count = tokens.shape[0]
    source = tokens.astype(jnp.float32)
    normed = (
        source * lax.rsqrt(jnp.mean(source * source, axis=-1, keepdims=True) + eps) * norm_gain
    ).astype(jnp.bfloat16)
    local_width = qkv_weight.shape[2]
    heads = local_width // HEAD_DIM
    joined = jnp.einsum(
        "td,dch->tch",
        normed,
        lax.all_gather(qkv_weight, "seq", axis=0, tiled=True),
        preferred_element_type=jnp.float32,
    )
    query = joined[:, 0]
    keys = joined[:, 1]
    values = joined[:, 2]
    query_sq, key_sq = lax.psum(
        (jnp.sum(query * query, axis=-1), jnp.sum(keys * keys, axis=-1)), "tp"
    )
    full_width = local_width * lax.axis_size("tp")
    query_normed = (query * lax.rsqrt(query_sq / full_width + eps)[:, None] * q_gain).astype(
        jnp.bfloat16
    )
    key_normed = (keys * lax.rsqrt(key_sq / full_width + eps)[:, None] * k_gain).astype(
        jnp.bfloat16
    )
    paired = jnp.stack([key_normed, values.astype(jnp.bfloat16)], axis=1)
    pieces = []
    for offset in (2, 1, 0, -1, -2):
        if offset == 0:
            pieces.append(paired)
        else:
            pieces.append(passed_along(paired, "seq", offset))
    widened = jnp.concatenate(pieces, axis=0)
    position = lax.axis_index("seq")
    outside = jnp.full((2 * count,), -1, jnp.int32)
    seg_pad = jnp.concatenate([outside, segment_ids, outside], axis=0)
    key_seg = lax.dynamic_slice_in_dim(seg_pad, position * count, 5 * count, 0)
    query_seg = lax.dynamic_slice_in_dim(segment_ids, position * count, count, 0)
    query_heads = query_normed.reshape(count, heads, HEAD_DIM)
    key_heads = widened[:, 0].reshape(5 * count, heads, HEAD_DIM)
    value_heads = widened[:, 1].reshape(5 * count, heads, HEAD_DIM)
    scores, mask = masked_scores(query_heads, key_heads, query_seg, key_seg)
    peak = jnp.max(scores, axis=-1, keepdims=True)
    weights = jnp.where(mask, jnp.exp(scores - peak), 0.0)
    total = jnp.sum(weights, axis=-1)
    probs = weights.astype(jnp.bfloat16)
    summed = jnp.einsum("hqk,khd->qhd", probs, value_heads, preferred_element_type=jnp.float32)
    context = (
        (summed / jnp.transpose(total)[:, :, None]).reshape(count, local_width).astype(jnp.bfloat16)
    )
    terms = jnp.dot(
        context,
        lax.all_gather(out_weight, "seq", axis=1, tiled=True),
        preferred_element_type=jnp.float32,
    )
    projected = lax.psum_scatter(terms, "tp", scatter_dimension=1, tiled=True)
    share = layer_scale.shape[0]
    residual = lax.dynamic_slice_in_dim(source, lax.axis_index("tp") * share, share, 1)
    return (residual + layer_scale * projected).astype(jnp.bfloat16)


ANY = pl.BlockSpec(memory_space=pl.ANY)
VMEM = pl.BlockSpec(memory_space=pltpu.VMEM)
SMEM = pl.BlockSpec(memory_space=pltpu.SMEM)
HBM = pl.BlockSpec(memory_space=pltpu.HBM)
KERNEL_VMEM = 60 * 1024 * 1024
HELD_VMEM = 24 * 1024 * 1024


def permuted(x, to):
    slabs, tps = lax.axis_size("seq") // SLAB, lax.axis_size("tp")
    pairs = []
    for i in range(slabs * SLAB * tps):
        z, q, y = to(i // (SLAB * tps), i // tps % SLAB, i % tps)
        pairs.append((i, (z * SLAB + q) * tps + y))
    return lax.ppermute(x, ("seq", "tp"), pairs)


def in_slab(x, flip):
    return permuted(x, lambda z, q, y: (z, q ^ flip, y))


def across(x):
    return permuted(x, lambda z, q, y: (z, q, 1 - y))


def even_pair(x):
    return permuted(x, lambda z, q, y: (z ^ 1, q, y))


def odd_pair(x):
    return permuted(x, lambda z, q, y: (3 - z, q, y) if z in (1, 2) else (z, q ^ 1, y))


def half_pair(x):
    return permuted(x, lambda z, q, y: (z ^ 2, q, y))


def tied(*arrays):
    return lax.optimization_barrier(arrays)


def as_row(column):
    wide = jnp.broadcast_to(column, (column.shape[0], 128))
    return jnp.transpose(wide)[:8]


def as_column(row):
    return jnp.transpose(jnp.broadcast_to(row, (128, row.shape[1])))


def start(copies):
    for copy in copies:
        copy.start()


def wait(copies):
    for copy in copies:
        copy.wait()


def norm_kernel(tokens, gain, out):
    part = tokens.shape[1] // out.shape[0]
    source = tokens[...].astype(jnp.float32)
    mean = jnp.mean(source * source, axis=1, keepdims=True)
    normed = source * lax.rsqrt(mean + eps) * gain[...]
    for j in range(out.shape[0]):
        out[j, :, :part] = normed[:, j * part:(j + 1) * part].astype(jnp.bfloat16)
        out[j, :, part:] = jnp.zeros((out.shape[1], out.shape[2] - part), jnp.bfloat16)


def norm(tokens, gain, slabs):
    count, depth = tokens.shape
    shape = (slabs, count, pl.cdiv(depth // slabs, 128) * 128)
    return pl.pallas_call(
        norm_kernel,
        out_shape=jax.ShapeDtypeStruct(shape, jnp.bfloat16),
        in_specs=[VMEM, VMEM],
        out_specs=VMEM,
        compiler_params=pltpu.CompilerParams(vmem_limit_bytes=KERNEL_VMEM),
        name="norm",
    )(tokens, gain[None])


def token_copies(xs, at, out, sems):
    return [
        pltpu.make_async_copy(x.at[at], out.at[r], sems.at[r]) for r, x in enumerate(xs)
    ]


def blank_tail(w, rows):
    tail = w.shape[-2] - rows
    w[..., rows:, :] = jnp.zeros(w.shape[:-2] + (tail, w.shape[-1]), w.dtype)


def early_kernel(
    place, xa, xb, xc, xd, own, near, far, acc, x_last, x_all, w_all, x_sem, w_sem, last_sem,
):
    z = place[0]
    kinds, rows = own.shape[:2]
    copies = []
    for i, w in enumerate((own, near, far)):
        dst = w_all.at[i, :, pl.ds(0, rows), :]
        copies.append([pltpu.make_async_copy(w, dst, w_sem.at[i])])
        copies[i] += token_copies((xa, xb, xc, xd), z ^ i, x_all.at[i], x_sem.at[i])
        start(copies[i])
    last_copies = token_copies((xa, xb, xc, xd), z ^ 3, x_last, last_sem)
    start(last_copies)
    blank_tail(w_all, rows)
    for step in range(3):
        wait(copies[step])
        for r in range(SLAB):
            x = x_all[step, r]
            for kind in range(kinds):
                term = jnp.dot(x, w_all[step, kind], preferred_element_type=jnp.float32)
                acc[r, kind] = term if step == 0 else acc[r, kind] + term
    wait(last_copies)


def early(place, xs, own, near, far):
    kinds, rows, width = own.shape
    slabs, count, wide = xs[0].shape
    return pl.pallas_call(
        early_kernel,
        out_shape=(
            jax.ShapeDtypeStruct((SLAB, kinds, count, width), jnp.float32),
            jax.ShapeDtypeStruct((SLAB, count, wide), jnp.bfloat16),
        ),
        in_specs=[SMEM] + [HBM] * 7,
        out_specs=(VMEM, VMEM),
        scratch_shapes=[
            pltpu.VMEM((3, SLAB, count, wide), jnp.bfloat16),
            pltpu.VMEM((3, kinds, wide, width), jnp.bfloat16),
            pltpu.SemaphoreType.DMA((3, SLAB)),
            pltpu.SemaphoreType.DMA((3,)),
            pltpu.SemaphoreType.DMA((SLAB,)),
        ],
        compiler_params=pltpu.CompilerParams(vmem_limit_bytes=HELD_VMEM),
        cost_estimate=pl.CostEstimate(
            flops=12 * kinds * SLAB * count * rows * width,
            bytes_accessed=6 * kinds * rows * width + 6 * SLAB * count * rows,
            transcendentals=0,
        ),
        name="early",
    )(place, *xs, own, near, far)


def late_kernel(
    place, x_last, acc, last, q_gain, k_gain, query, keys, values, squares, even, odd, w_all,
):
    z, q = place[0], place[1]
    rows = last.shape[1]
    w_all[:, :rows, :] = last[...]
    blank_tail(w_all, rows)
    count = acc.shape[2]
    for r in range(SLAB):
        rows = pl.ds(pl.multiple_of((q ^ r) * count, count), count)
        for kind in range(3):
            part = acc[r, kind] + jnp.dot(
                x_last[r], w_all[kind], preferred_element_type=jnp.float32
            )
            if kind < 2:
                summed = as_row(jnp.sum(part * part, axis=1, keepdims=True))
                squares[kind:kind + 1, rows] = summed[:1]
                part = part * (q_gain, k_gain)[kind][...]
            out = (query, keys, values)[kind]
            out[rows, :] = part.astype(out.dtype)
    reach = even.shape[1]
    for out, at in ((even, 1 - z % 2), (odd, z % 2)):
        rows = pl.ds(pl.multiple_of(at * reach, reach), reach)
        out[0] = keys[rows, :]
        out[1] = values[rows, :]


def late(place, x_last, acc, last, q_gain, k_gain):
    kinds, rows, width = last.shape
    count, wide = x_last.shape[1:]
    slab = SLAB * count
    f32, bf16 = jnp.float32, jnp.bfloat16
    return pl.pallas_call(
        late_kernel,
        out_shape=(
            jax.ShapeDtypeStruct((slab, width), f32),
            jax.ShapeDtypeStruct((slab, width), bf16),
            jax.ShapeDtypeStruct((slab, width), bf16),
            jax.ShapeDtypeStruct((2, slab), f32),
            jax.ShapeDtypeStruct((2, 2 * count, width), bf16),
            jax.ShapeDtypeStruct((2, 2 * count, width), bf16),
        ),
        in_specs=[SMEM] + [VMEM] * 5,
        out_specs=(VMEM,) * 6,
        scratch_shapes=[
            pltpu.VMEM((kinds, wide, width), bf16),
        ],
        compiler_params=pltpu.CompilerParams(vmem_limit_bytes=HELD_VMEM),
        cost_estimate=pl.CostEstimate(
            flops=2 * kinds * slab * rows * width,
            bytes_accessed=2 * kinds * rows * width + 2 * slab * rows,
            transcendentals=0,
        ),
        name="late",
    )(place, x_last, acc, last, q_gain, k_gain)


def attend_kernel(
    full_width, place, spans, query, keys, values, even, odd, mine, near, mid, seg, o0, o1, o2, o3,
    q_all, k_all, v_all, o_all, scale_all, sems,
):
    z, q = place[0], place[1]
    slab = query.shape[0]
    count = slab // SLAB
    half = even.shape[1]
    upper = half + slab
    is_even = z % 2 == 0
    even_at = pl.multiple_of(jnp.where(is_even, upper, 0), half)
    odd_at = pl.multiple_of(jnp.where(is_even, 0, upper), half)
    copies = [pltpu.make_async_copy(query, q_all, sems.at[0])]
    for k, (whole, out) in enumerate(((keys, k_all), (values, v_all))):
        for n, (src, at) in enumerate(((whole, half), (even.at[k], even_at), (odd.at[k], odd_at))):
            dst = out.at[pl.ds(at, src.shape[0]), :]
            copies.append(pltpu.make_async_copy(src, dst, sems.at[1 + 3 * k + n]))
    start(copies)
    scale = [lax.rsqrt(sums[...] / full_width + eps) for sums in (mine, near, mid)]
    scale_all[:, half:upper] = scale[0]
    scale_all[:, :half] = jnp.where(is_even, scale[2], scale[1])[:, slab - half:]
    scale_all[:, upper:] = jnp.where(is_even, scale[1], scale[2])[:, :half]
    wait(copies)
    ext = k_all.shape[0]
    heads = query.shape[1] // HEAD_DIM
    factor = HEAD_DIM ** (-0.5) * math.log2(math.e)

    def block(r, _):
        b = q ^ r
        at_query = pl.multiple_of(b * count + half, count)
        query_seg = as_column(seg[:, pl.ds(at_query, count)])
        q_scale = as_column(scale_all[0:1, pl.ds(at_query, count)])
        for tiles in range(2, 2 * half // count + 2):
            @pl.when(spans[b, 1] == tiles)
            def _():
                width = tiles * count
                begin = pl.multiple_of(spans[b, 0], 128)
                keys_at = pl.ds(begin, width)
                mask = jnp.tile(query_seg, (1, width // 128)) == seg[:, keys_at]
                k_scale = scale_all[1:2, keys_at] * factor
                for h in range(heads):
                    cols = slice(h * HEAD_DIM, (h + 1) * HEAD_DIM)
                    q_low = q_all[pl.ds(pl.multiple_of(b * count, count), count), cols] * q_scale
                    scores = lax.dot_general(
                        q_low.astype(jnp.bfloat16), k_all[keys_at, cols],
                        (((1,), (1,)), ((), ())), preferred_element_type=jnp.float32,
                    )
                    scores = jnp.where(mask, scores * k_scale, floor_score)
                    peak = jnp.max(scores, axis=1, keepdims=True)
                    weights = jnp.exp2(scores - peak)
                    total = jnp.sum(weights, axis=1, keepdims=True)
                    summed = jnp.dot(
                        weights.astype(jnp.bfloat16), v_all[keys_at, cols],
                        preferred_element_type=jnp.float32,
                    )
                    o_all[r, cols, :] = jnp.transpose(summed / total).astype(jnp.bfloat16)

        return 0

    lax.fori_loop(0, SLAB, block, 0)
    stores = [
        pltpu.make_async_copy(o_all.at[r], out, sems.at[r]) for r, out in enumerate((o0, o1, o2, o3))
    ]
    start(stores)
    wait(stores)


def key_spans(seg, slab, count, half):
    ext = seg.shape[0]
    index = jnp.arange(ext, dtype=jnp.int32)
    blocks = seg[half:half + slab].reshape(-1, count)
    first, last = blocks[:, :1], blocks[:, -1:]
    begin = jnp.min(jnp.where(seg == first, index, ext), axis=1) // 128 * 128
    end = jnp.max(jnp.where(seg == last, index, -1), axis=1) + 1
    tiles = jnp.maximum((end - begin + count - 1) // count, 2)
    return jnp.stack([jnp.minimum(begin, ext - tiles * count), tiles], axis=1)


def attend(full_width, place, spans, query, keys, values, even, odd, sums, seg):
    slab, width = query.shape
    half = even.shape[1]
    count = slab // SLAB
    ext = slab + 2 * half
    bf16 = jnp.bfloat16
    window = count + 2 * half
    return pl.pallas_call(
        functools.partial(attend_kernel, full_width),
        out_shape=(jax.ShapeDtypeStruct((width, count), bf16),) * SLAB,
        in_specs=[SMEM] * 2 + [HBM] * 5 + [VMEM] * 4,
        out_specs=(HBM,) * SLAB,
        scratch_shapes=[
            pltpu.VMEM((slab, width), jnp.float32),
            pltpu.VMEM((ext, width), bf16),
            pltpu.VMEM((ext, width), bf16),
            pltpu.VMEM((SLAB, width, count), bf16),
            pltpu.VMEM((2, ext), jnp.float32),
            pltpu.SemaphoreType.DMA((7,)),
        ],
        compiler_params=pltpu.CompilerParams(vmem_limit_bytes=HELD_VMEM),
        cost_estimate=pl.CostEstimate(
            flops=64 * SLAB * count * window * width,
            bytes_accessed=4 * ext * width + 4 * slab * width,
            transcendentals=SLAB * count * window * width // HEAD_DIM,
        ),
        name="attend",
    )(place, spans, query, keys, values, even, odd, *sums, seg)


def out_kernel(
    place, c20, c01, c31, c30, c11, c21, c10, c00, wa0, wb0, wc0, wd0, wa1, wb1, wc1, wd1,
    residual, scale, out, c_all, w_all, total, placed, c_sem, w_sem,
):
    z, q = place[0], place[1]
    width = c00.shape[0]
    c_copies = []
    for i in range(2):
        for r, pair in enumerate(((c00, c01), (c10, c11), (c20, c21), (c30, c31))):
            at = pl.multiple_of((q ^ r) * width, width)
            dst = c_all.at[i, pl.ds(at, width), :]
            c_copies.append(pltpu.make_async_copy(pair[i], dst, c_sem.at[r, i]))
    start(c_copies)
    rows = wa0.shape[1]
    w_copies = []
    for i in range(2):
        for r, w in enumerate(((wa0, wb0, wc0, wd0), (wa1, wb1, wc1, wd1))[i]):
            for j in range(2):
                dst = w_all.at[i, pl.ds((2 * r + j) * rows, rows), :]
                w_copies.append(pltpu.make_async_copy(w.at[j], dst, w_sem.at[r, j, i]))
    start(w_copies)
    column = as_column(scale[...])[:out.shape[0]]
    column = jnp.tile(column, (1, out.shape[1] // 128))
    wait(c_copies[:SLAB] + w_copies[:2 * SLAB])
    total[...] = jnp.dot(w_all[0], c_all[0], preferred_element_type=jnp.float32)
    wait(c_copies[SLAB:] + w_copies[2 * SLAB:])
    total[...] += jnp.dot(w_all[1], c_all[1], preferred_element_type=jnp.float32)
    kept = out.shape[0] // (2 * SLAB)
    for r in range(SLAB):
        for j in range(2):
            at = pl.multiple_of((((z % 2) ^ j) * SLAB + (q ^ r)) * kept, 8)
            begin = (2 * r + j) * rows
            placed[pl.ds(at, kept), :] = total[begin:begin + kept, :]
    out[...] = (residual[...].astype(jnp.float32) + column * placed[...]).astype(jnp.bfloat16)


def output(place, blocks, pieces, residual, scale):
    count = blocks[0].shape[1]
    rows, depth = pieces[0].shape[1:]
    share = residual.shape[0]
    scale = jnp.pad(scale, (0, -share % 128))[None]
    return pl.pallas_call(
        out_kernel,
        out_shape=jax.ShapeDtypeStruct((share, count), jnp.bfloat16),
        in_specs=[SMEM] + [HBM] * 16 + [VMEM] * 2,
        out_specs=VMEM,
        scratch_shapes=[
            pltpu.VMEM((2, depth, count), jnp.bfloat16),
            pltpu.VMEM((2, 2 * SLAB * rows, depth), jnp.bfloat16),
            pltpu.VMEM((2 * SLAB * rows, count), jnp.float32),
            pltpu.VMEM((share, count), jnp.float32),
            pltpu.SemaphoreType.DMA((SLAB, 2)),
            pltpu.SemaphoreType.DMA((SLAB, 2, 2)),
        ],
        compiler_params=pltpu.CompilerParams(vmem_limit_bytes=KERNEL_VMEM),
        cost_estimate=pl.CostEstimate(
            flops=4 * share * count * depth,
            bytes_accessed=4 * share * depth,
            transcendentals=0,
        ),
        name="output",
    )(place, *blocks, *pieces, residual, scale)


def rows_of_slab(q, got):
    placed = []
    for b in range(SLAB):
        piece = got[b]
        for other in range(1, SLAB):
            piece = jnp.where(q == other, got[b ^ other], piece)
        placed.append(piece)
    return jnp.concatenate(placed, axis=1)


def slab_plan(tokens, norm_gain, qkv_weight, q_gain, k_gain, out_weight, layer_scale, segment_ids):
    count = tokens.shape[0]
    seq, tp = lax.axis_index("seq"), lax.axis_index("tp")
    slabs = lax.axis_size("seq") // SLAB
    z, q = seq // SLAB, seq % SLAB
    place = jnp.stack([z, q, tp]).astype(jnp.int32)
    width = qkv_weight.shape[2] // SLAB
    full_width = qkv_weight.shape[2] * lax.axis_size("tp")
    slab, half = SLAB * count, 2 * count
    home = z // 2 == tp

    by_kind = jnp.transpose(qkv_weight, (1, 0, 2))
    cut = [lax.dynamic_slice_in_dim(by_kind, (q ^ r) * width, width, 2) for r in range(SLAB)]
    got = [cut[0]] + [in_slab(cut[r], r) for r in range(1, SLAB)]
    x0 = norm(tokens, norm_gain, slabs)
    out_own = jnp.pad(jnp.transpose(out_weight), ((0, -out_weight.shape[1] % 16), (0, 0)))
    own = rows_of_slab(q, got)
    out_near, out_far = even_pair(out_own), half_pair(out_own)
    gains = [lax.dynamic_slice_in_dim(g, q * width, width, 0)[None] for g in (q_gain, k_gain)]

    outside = jnp.full((half,), -1, jnp.int32)
    seg = jnp.concatenate([outside, segment_ids, outside], axis=0)
    seg = lax.dynamic_slice_in_dim(seg, z * slab, slab + 2 * half, 0)
    spans = key_spans(seg, slab, count, half)
    seg = seg.astype(jnp.float32)[None]
    x0, out_near, out_far, seg, spans, *gains = tied(x0, out_near, out_far, seg, spans, *gains)
    out_last = even_pair(out_far)
    x2 = in_slab(x0, 2)
    out_last, own, x0 = tied(out_last, own, x0)
    near, far = even_pair(own), half_pair(own)
    x1 = in_slab(x0, 1)
    out_last, x1 = tied(out_last, x1)
    close, away = jnp.stack([out_own, out_near]), jnp.stack([out_far, out_last])
    keep, give = jnp.where(home, close, away), jnp.where(home, away, close)
    got = across(give)
    keep_x = in_slab(keep, 2)
    near, far, x1, x2, got, keep_x = tied(near, far, x1, x2, got, keep_x)
    last = even_pair(far)
    x3 = in_slab(x2, 1)
    got_x, got_c, keep_c = in_slab(got, 2), in_slab(got, 1), in_slab(keep, 1)
    keep_xc = in_slab(tied(keep_x, x3)[0], 1)
    xs = (x0, x1, x2, x3)
    acc, x_last = early(place, xs, own, near, far)
    last, acc, x_last = tied(last, acc, x_last)
    query, keys, values, squares, even, odd = late(place, x_last, acc, last, *gains)
    even, odd = even_pair(even), odd_pair(odd)
    squares, got_x, got_c, keep_c, keep_xc = tied(squares, got_x, got_c, keep_c, keep_xc)
    sums = squares
    for r in range(1, SLAB):
        sums = sums + in_slab(squares, r)
    sums = sums + across(sums)
    sums = (sums, even_pair(sums), odd_pair(sums))
    got_xc = in_slab(got_x, 1)

    blocks = attend(full_width, place, spans, query, keys, values, even, odd, sums, seg)
    *blocks, got_xc = tied(*blocks, got_xc)
    pieces = (keep, keep_c, keep_x, keep_xc, got, got_c, got_x, got_xc)
    spread = []
    for r, i in ((2, 0), (0, 1), (3, 1), (3, 0), (1, 1), (2, 1), (1, 0), (0, 0)):
        to = functools.partial(lambda r, i, z, q, y: (z, q ^ r, y ^ i), r, i)
        spread.append(permuted(blocks[r], to) if r or i else blocks[r])

    share = layer_scale.shape[0]
    residual = jnp.transpose(lax.dynamic_slice_in_dim(tokens, tp * share, share, 1))
    return jnp.transpose(output(place, spread, pieces, residual, layer_scale))


def solution(mesh):
    def shards(*args):
        heads = args[2].shape[2] // HEAD_DIM
        slab = mesh.shape["seq"] == 16 and mesh.shape["tp"] == 2 and heads % SLAB == 0
        return (slab_plan if slab else row_plan)(*args)

    return jax.shard_map(
        shards,
        mesh=mesh,
        in_specs=(
            P("seq", None),
            P(),
            P("seq", None, "tp"),
            P("tp"),
            P("tp"),
            P("tp", "seq"),
            P("tp"),
            P(),
        ),
        out_specs=P("seq", "tp"),
        check_vma=False,
    )
```

```python
import functools
import math

import jax
import jax.numpy as jnp
from jax import lax
from jax.experimental import pallas as pl
from jax.experimental.pallas import tpu as pltpu
from jax.sharding import PartitionSpec as P

HEAD_DIM = 128
SLAB = 4

eps = 1e-06
floor_score = -1e30


def passed_along(x, axis, by):
    size = lax.axis_size(axis)
    pairs = [(i, i + by) for i in range(size) if 0 <= i + by < size]
    return lax.ppermute(x, axis, pairs)


def masked_scores(query, keys, query_seg, key_seg):
    scores = jnp.einsum(
        "qhd,khd->hqk", query, keys, preferred_element_type=jnp.float32
    ) * HEAD_DIM ** (-0.5)
    mask = (query_seg[:, None] == key_seg[None, :])[None]
    return (jnp.where(mask, scores, floor_score), mask)


def row_plan(tokens, norm_gain, qkv_weight, q_gain, k_gain, out_weight, layer_scale, segment_ids):
    count = tokens.shape[0]
    source = tokens.astype(jnp.float32)
    normed = (
        source * lax.rsqrt(jnp.mean(source * source, axis=-1, keepdims=True) + eps) * norm_gain
    ).astype(jnp.bfloat16)
    local_width = qkv_weight.shape[2]
    heads = local_width // HEAD_DIM
    joined = jnp.einsum(
        "td,dch->tch",
        normed,
        lax.all_gather(qkv_weight, "seq", axis=0, tiled=True),
        preferred_element_type=jnp.float32,
    )
    query = joined[:, 0]
    keys = joined[:, 1]
    values = joined[:, 2]
    query_sq, key_sq = lax.psum(
        (jnp.sum(query * query, axis=-1), jnp.sum(keys * keys, axis=-1)), "tp"
    )
    full_width = local_width * lax.axis_size("tp")
    query_normed = (query * lax.rsqrt(query_sq / full_width + eps)[:, None] * q_gain).astype(
        jnp.bfloat16
    )
    key_normed = (keys * lax.rsqrt(key_sq / full_width + eps)[:, None] * k_gain).astype(
        jnp.bfloat16
    )
    paired = jnp.stack([key_normed, values.astype(jnp.bfloat16)], axis=1)
    pieces = []
    for offset in (2, 1, 0, -1, -2):
        if offset == 0:
            pieces.append(paired)
        else:
            pieces.append(passed_along(paired, "seq", offset))
    widened = jnp.concatenate(pieces, axis=0)
    position = lax.axis_index("seq")
    outside = jnp.full((2 * count,), -1, jnp.int32)
    seg_pad = jnp.concatenate([outside, segment_ids, outside], axis=0)
    key_seg = lax.dynamic_slice_in_dim(seg_pad, position * count, 5 * count, 0)
    query_seg = lax.dynamic_slice_in_dim(segment_ids, position * count, count, 0)
    query_heads = query_normed.reshape(count, heads, HEAD_DIM)
    key_heads = widened[:, 0].reshape(5 * count, heads, HEAD_DIM)
    value_heads = widened[:, 1].reshape(5 * count, heads, HEAD_DIM)
    scores, mask = masked_scores(query_heads, key_heads, query_seg, key_seg)
    peak = jnp.max(scores, axis=-1, keepdims=True)
    weights = jnp.where(mask, jnp.exp(scores - peak), 0.0)
    total = jnp.sum(weights, axis=-1)
    probs = weights.astype(jnp.bfloat16)
    summed = jnp.einsum("hqk,khd->qhd", probs, value_heads, preferred_element_type=jnp.float32)
    context = (
        (summed / jnp.transpose(total)[:, :, None]).reshape(count, local_width).astype(jnp.bfloat16)
    )
    terms = jnp.dot(
        context,
        lax.all_gather(out_weight, "seq", axis=1, tiled=True),
        preferred_element_type=jnp.float32,
    )
    projected = lax.psum_scatter(terms, "tp", scatter_dimension=1, tiled=True)
    share = layer_scale.shape[0]
    residual = lax.dynamic_slice_in_dim(source, lax.axis_index("tp") * share, share, 1)
    return (residual + layer_scale * projected).astype(jnp.bfloat16)


ANY = pl.BlockSpec(memory_space=pl.ANY)
VMEM = pl.BlockSpec(memory_space=pltpu.VMEM)
SMEM = pl.BlockSpec(memory_space=pltpu.SMEM)
HBM = pl.BlockSpec(memory_space=pltpu.HBM)
KERNEL_VMEM = 60 * 1024 * 1024
HELD_VMEM = 24 * 1024 * 1024


def permuted(x, to):
    slabs, tps = lax.axis_size("seq") // SLAB, lax.axis_size("tp")
    pairs = []
    for i in range(slabs * SLAB * tps):
        z, q, y = to(i // (SLAB * tps), i // tps % SLAB, i % tps)
        pairs.append((i, (z * SLAB + q) * tps + y))
    return lax.ppermute(x, ("seq", "tp"), pairs)


def in_slab(x, flip):
    return permuted(x, lambda z, q, y: (z, q ^ flip, y))


def across(x):
    return permuted(x, lambda z, q, y: (z, q, 1 - y))


def even_pair(x):
    return permuted(x, lambda z, q, y: (z ^ 1, q, y))


def odd_pair(x):
    return permuted(x, lambda z, q, y: (3 - z, q, y) if z in (1, 2) else (z, q ^ 1, y))


def half_pair(x):
    return permuted(x, lambda z, q, y: (z ^ 2, q, y))


def tied(*arrays):
    return lax.optimization_barrier(arrays)


def as_row(column):
    wide = jnp.broadcast_to(column, (column.shape[0], 128))
    return jnp.transpose(wide)[:8]


def as_column(row):
    return jnp.transpose(jnp.broadcast_to(row, (128, row.shape[1])))


def start(copies):
    for copy in copies:
        copy.start()


def wait(copies):
    for copy in copies:
        copy.wait()


def norm_kernel(tokens, gain, out):
    part = tokens.shape[1] // out.shape[0]
    source = tokens[...].astype(jnp.float32)
    mean = jnp.mean(source * source, axis=1, keepdims=True)
    normed = source * lax.rsqrt(mean + eps) * gain[...]
    for j in range(out.shape[0]):
        out[j, :, :part] = normed[:, j * part:(j + 1) * part].astype(jnp.bfloat16)
        out[j, :, part:] = jnp.zeros((out.shape[1], out.shape[2] - part), jnp.bfloat16)


def norm(tokens, gain, slabs):
    count, depth = tokens.shape
    shape = (slabs, count, pl.cdiv(depth // slabs, 128) * 128)
    return pl.pallas_call(
        norm_kernel,
        out_shape=jax.ShapeDtypeStruct(shape, jnp.bfloat16),
        in_specs=[VMEM, VMEM],
        out_specs=VMEM,
        compiler_params=pltpu.CompilerParams(vmem_limit_bytes=KERNEL_VMEM),
        name="norm",
    )(tokens, gain[None])


def token_copies(xs, at, out, sems):
    return [
        pltpu.make_async_copy(x.at[at], out.at[r], sems.at[r]) for r, x in enumerate(xs)
    ]


def blank_tail(w, rows):
    tail = w.shape[-2] - rows
    w[..., rows:, :] = jnp.zeros(w.shape[:-2] + (tail, w.shape[-1]), w.dtype)


def early_kernel(
    place, xa, xb, xc, xd, own, near, far, acc, x_last, x_all, w_all, x_sem, w_sem, last_sem,
):
    z = place[0]
    kinds, rows = own.shape[:2]
    copies = []
    for i, w in enumerate((own, near, far)):
        dst = w_all.at[i, :, pl.ds(0, rows), :]
        copies.append([pltpu.make_async_copy(w, dst, w_sem.at[i])])
        copies[i] += token_copies((xa, xb, xc, xd), z ^ i, x_all.at[i], x_sem.at[i])
        start(copies[i])
    last_copies = token_copies((xa, xb, xc, xd), z ^ 3, x_last, last_sem)
    start(last_copies)
    blank_tail(w_all, rows)
    for step in range(3):
        wait(copies[step])
        for r in range(SLAB):
            x = x_all[step, r]
            for kind in range(kinds):
                term = jnp.dot(x, w_all[step, kind], preferred_element_type=jnp.float32)
                acc[r, kind] = term if step == 0 else acc[r, kind] + term
    wait(last_copies)


def early(place, xs, own, near, far):
    kinds, rows, width = own.shape
    slabs, count, wide = xs[0].shape
    return pl.pallas_call(
        early_kernel,
        out_shape=(
            jax.ShapeDtypeStruct((SLAB, kinds, count, width), jnp.float32),
            jax.ShapeDtypeStruct((SLAB, count, wide), jnp.bfloat16),
        ),
        in_specs=[SMEM] + [HBM] * 7,
        out_specs=(VMEM, VMEM),
        scratch_shapes=[
            pltpu.VMEM((3, SLAB, count, wide), jnp.bfloat16),
            pltpu.VMEM((3, kinds, wide, width), jnp.bfloat16),
            pltpu.SemaphoreType.DMA((3, SLAB)),
            pltpu.SemaphoreType.DMA((3,)),
            pltpu.SemaphoreType.DMA((SLAB,)),
        ],
        compiler_params=pltpu.CompilerParams(vmem_limit_bytes=HELD_VMEM),
        cost_estimate=pl.CostEstimate(
            flops=12 * kinds * SLAB * count * rows * width,
            bytes_accessed=6 * kinds * rows * width + 6 * SLAB * count * rows,
            transcendentals=0,
        ),
        name="early",
    )(place, *xs, own, near, far)


def late_kernel(
    place, x_last, acc, last, q_gain, k_gain, query, keys, values, squares, even, odd, w_all,
):
    z, q = place[0], place[1]
    rows = last.shape[1]
    w_all[:, :rows, :] = last[...]
    blank_tail(w_all, rows)
    count = acc.shape[2]
    for r in range(SLAB):
        rows = pl.ds(pl.multiple_of((q ^ r) * count, count), count)
        for kind in range(3):
            part = acc[r, kind] + jnp.dot(
                x_last[r], w_all[kind], preferred_element_type=jnp.float32
            )
            if kind < 2:
                summed = as_row(jnp.sum(part * part, axis=1, keepdims=True))
                squares[kind:kind + 1, rows] = summed[:1]
                part = part * (q_gain, k_gain)[kind][...]
            out = (query, keys, values)[kind]
            out[rows, :] = part.astype(out.dtype)
    reach = even.shape[1]
    for out, at in ((even, 1 - z % 2), (odd, z % 2)):
        rows = pl.ds(pl.multiple_of(at * reach, reach), reach)
        out[0] = keys[rows, :]
        out[1] = values[rows, :]


def late(place, x_last, acc, last, q_gain, k_gain):
    kinds, rows, width = last.shape
    count, wide = x_last.shape[1:]
    slab = SLAB * count
    f32, bf16 = jnp.float32, jnp.bfloat16
    return pl.pallas_call(
        late_kernel,
        out_shape=(
            jax.ShapeDtypeStruct((slab, width), f32),
            jax.ShapeDtypeStruct((slab, width), bf16),
            jax.ShapeDtypeStruct((slab, width), bf16),
            jax.ShapeDtypeStruct((2, slab), f32),
            jax.ShapeDtypeStruct((2, 2 * count, width), bf16),
            jax.ShapeDtypeStruct((2, 2 * count, width), bf16),
        ),
        in_specs=[SMEM] + [VMEM] * 5,
        out_specs=(VMEM,) * 6,
        scratch_shapes=[
            pltpu.VMEM((kinds, wide, width), bf16),
        ],
        compiler_params=pltpu.CompilerParams(vmem_limit_bytes=HELD_VMEM),
        cost_estimate=pl.CostEstimate(
            flops=2 * kinds * slab * rows * width,
            bytes_accessed=2 * kinds * rows * width + 2 * slab * rows,
            transcendentals=0,
        ),
        name="late",
    )(place, x_last, acc, last, q_gain, k_gain)


def attend_kernel(
    full_width, place, spans, query, keys, values, even, odd, mine, near, mid, seg, o0, o1, o2, o3,
    k_all, v_all, o_all, scale_all,
):
    z, q = place[0], place[1]
    slab = query.shape[0]
    count = slab // SLAB
    half = even.shape[1]
    upper = half + slab
    is_even = z % 2 == 0
    even_at = pl.multiple_of(jnp.where(is_even, upper, 0), half)
    odd_at = pl.multiple_of(jnp.where(is_even, 0, upper), half)
    for k, (whole, out) in enumerate(((keys, k_all), (values, v_all))):
        out[half:upper, :] = whole[...]
        out[pl.ds(even_at, half), :] = even[k]
        out[pl.ds(odd_at, half), :] = odd[k]
    scale = [lax.rsqrt(sums[...] / full_width + eps) for sums in (mine, near, mid)]
    scale_all[:, half:upper] = scale[0]
    scale_all[:, :half] = jnp.where(is_even, scale[2], scale[1])[:, slab - half:]
    scale_all[:, upper:] = jnp.where(is_even, scale[1], scale[2])[:, :half]
    heads = query.shape[1] // HEAD_DIM
    factor = HEAD_DIM ** (-0.5) * math.log2(math.e)

    def block(r, _):
        b = q ^ r
        at_query = pl.multiple_of(b * count + half, count)
        query_seg = as_column(seg[:, pl.ds(at_query, count)])
        q_scale = as_column(scale_all[0:1, pl.ds(at_query, count)])
        for tiles in range(2, 2 * half // count + 2):
            @pl.when(spans[b, 1] == tiles)
            def _():
                width = tiles * count
                begin = pl.multiple_of(spans[b, 0], 128)
                keys_at = pl.ds(begin, width)
                mask = jnp.tile(query_seg, (1, width // 128)) == seg[:, keys_at]
                k_scale = scale_all[1:2, keys_at] * factor
                for h in range(heads):
                    cols = slice(h * HEAD_DIM, (h + 1) * HEAD_DIM)
                    q_low = query[pl.ds(pl.multiple_of(b * count, count), count), cols] * q_scale
                    scores = lax.dot_general(
                        q_low.astype(jnp.bfloat16), k_all[keys_at, cols],
                        (((1,), (1,)), ((), ())), preferred_element_type=jnp.float32,
                    )
                    scores = jnp.where(mask, scores * k_scale, floor_score)
                    peak = jnp.max(scores, axis=1, keepdims=True)
                    weights = jnp.exp2(scores - peak)
                    total = jnp.sum(weights, axis=1, keepdims=True)
                    summed = jnp.dot(
                        weights.astype(jnp.bfloat16), v_all[keys_at, cols],
                        preferred_element_type=jnp.float32,
                    )
                    o_all[r, cols, :] = jnp.transpose(summed / total).astype(jnp.bfloat16)

        return 0

    lax.fori_loop(0, SLAB, block, 0)
    for r, out in enumerate((o0, o1, o2, o3)):
        out[...] = o_all[r]


def key_spans(seg, slab, count, half):
    ext = seg.shape[0]
    index = jnp.arange(ext, dtype=jnp.int32)
    blocks = seg[half:half + slab].reshape(-1, count)
    first, last = blocks[:, :1], blocks[:, -1:]
    begin = jnp.min(jnp.where(seg == first, index, ext), axis=1) // 128 * 128
    end = jnp.max(jnp.where(seg == last, index, -1), axis=1) + 1
    tiles = jnp.maximum((end - begin + count - 1) // count, 2)
    return jnp.stack([jnp.minimum(begin, ext - tiles * count), tiles], axis=1)


def attend(full_width, place, spans, query, keys, values, even, odd, sums, seg):
    slab, width = query.shape
    half = even.shape[1]
    count = slab // SLAB
    ext = slab + 2 * half
    bf16 = jnp.bfloat16
    window = count + 2 * half
    return pl.pallas_call(
        functools.partial(attend_kernel, full_width),
        out_shape=(jax.ShapeDtypeStruct((width, count), bf16),) * SLAB,
        in_specs=[SMEM] * 2 + [VMEM] * 9,
        out_specs=(VMEM,) * SLAB,
        scratch_shapes=[
            pltpu.VMEM((ext, width), bf16),
            pltpu.VMEM((ext, width), bf16),
            pltpu.VMEM((SLAB, width, count), bf16),
            pltpu.VMEM((2, ext), jnp.float32),
        ],
        compiler_params=pltpu.CompilerParams(vmem_limit_bytes=HELD_VMEM),
        cost_estimate=pl.CostEstimate(
            flops=64 * SLAB * count * window * width,
            bytes_accessed=4 * ext * width + 4 * slab * width,
            transcendentals=SLAB * count * window * width // HEAD_DIM,
        ),
        name="attend",
    )(place, spans, query, keys, values, even, odd, *sums, seg)


def collect_kernel(wa0, wb0, wc0, wd0, wa1, wb1, wc1, wd1, out, sems):
    rows = wa0.shape[1]
    copies = []
    for i, ws in enumerate(((wa0, wb0, wc0, wd0), (wa1, wb1, wc1, wd1))):
        for r, w in enumerate(ws):
            for j in range(2):
                dst = out.at[i, pl.ds((2 * r + j) * rows, rows), :]
                copies.append(pltpu.make_async_copy(w.at[j], dst, sems.at[i, r, j]))
    start(copies)
    wait(copies)


def collect(pieces):
    rows, depth = pieces[0].shape[1:]
    return pl.pallas_call(
        collect_kernel,
        out_shape=jax.ShapeDtypeStruct((2, 2 * SLAB * rows, depth), jnp.bfloat16),
        in_specs=[HBM] * 8,
        out_specs=VMEM,
        scratch_shapes=[pltpu.SemaphoreType.DMA((2, SLAB, 2))],
        compiler_params=pltpu.CompilerParams(vmem_limit_bytes=HELD_VMEM),
        cost_estimate=pl.CostEstimate(
            flops=0, bytes_accessed=16 * SLAB * rows * depth, transcendentals=0
        ),
        name="collect",
    )(*pieces)


def out_kernel(
    place, c20, c01, c31, c30, c11, c21, c10, c00, w, residual, scale, out, c_all, total, placed,
):
    z, q = place[0], place[1]
    width = c00.shape[0]
    for i, blocks in enumerate(((c00, c10, c20, c30), (c01, c11, c21, c31))):
        for r, c in enumerate(blocks):
            c_all[i, pl.ds(pl.multiple_of((q ^ r) * width, width), width), :] = c[...]
    column = as_column(scale[...])[:out.shape[0]]
    column = jnp.tile(column, (1, out.shape[1] // 128))
    total[...] = jnp.dot(w[0], c_all[0], preferred_element_type=jnp.float32)
    total[...] += jnp.dot(w[1], c_all[1], preferred_element_type=jnp.float32)
    rows, kept = w.shape[1] // (2 * SLAB), out.shape[0] // (2 * SLAB)
    for r in range(SLAB):
        for j in range(2):
            at = pl.multiple_of((((z % 2) ^ j) * SLAB + (q ^ r)) * kept, 8)
            begin = (2 * r + j) * rows
            placed[pl.ds(at, kept), :] = total[begin:begin + kept, :]
    out[...] = (residual[...].astype(jnp.float32) + column * placed[...]).astype(jnp.bfloat16)


def output(place, blocks, w, residual, scale):
    count = blocks[0].shape[1]
    rows, depth = w.shape[1:]
    share = residual.shape[0]
    return pl.pallas_call(
        out_kernel,
        out_shape=jax.ShapeDtypeStruct((share, count), jnp.bfloat16),
        in_specs=[SMEM] + [VMEM] * 11,
        out_specs=VMEM,
        scratch_shapes=[
            pltpu.VMEM((2, depth, count), jnp.bfloat16),
            pltpu.VMEM((rows, count), jnp.float32),
            pltpu.VMEM((share, count), jnp.float32),
        ],
        compiler_params=pltpu.CompilerParams(vmem_limit_bytes=HELD_VMEM),
        cost_estimate=pl.CostEstimate(
            flops=4 * share * count * depth,
            bytes_accessed=4 * share * depth,
            transcendentals=0,
        ),
        name="output",
    )(place, *blocks, w, residual, scale)


def rows_of_slab(q, got):
    placed = []
    for b in range(SLAB):
        piece = got[b]
        for other in range(1, SLAB):
            piece = jnp.where(q == other, got[b ^ other], piece)
        placed.append(piece)
    return jnp.concatenate(placed, axis=1)


def slab_plan(tokens, norm_gain, qkv_weight, q_gain, k_gain, out_weight, layer_scale, segment_ids):
    count = tokens.shape[0]
    seq, tp = lax.axis_index("seq"), lax.axis_index("tp")
    slabs = lax.axis_size("seq") // SLAB
    z, q = seq // SLAB, seq % SLAB
    place = jnp.stack([z, q, tp]).astype(jnp.int32)
    width = qkv_weight.shape[2] // SLAB
    full_width = qkv_weight.shape[2] * lax.axis_size("tp")
    slab, half = SLAB * count, 2 * count
    home = z // 2 == tp

    by_kind = jnp.transpose(qkv_weight, (1, 0, 2))
    cut = [lax.dynamic_slice_in_dim(by_kind, (q ^ r) * width, width, 2) for r in range(SLAB)]
    got = [cut[0]] + [in_slab(cut[r], r) for r in range(1, SLAB)]
    x0 = norm(tokens, norm_gain, slabs)
    out_own = jnp.pad(jnp.transpose(out_weight), ((0, -out_weight.shape[1] % 16), (0, 0)))
    own = rows_of_slab(q, got)
    out_near, out_far = even_pair(out_own), half_pair(out_own)
    gains = [lax.dynamic_slice_in_dim(g, q * width, width, 0)[None] for g in (q_gain, k_gain)]

    outside = jnp.full((half,), -1, jnp.int32)
    seg = jnp.concatenate([outside, segment_ids, outside], axis=0)
    seg = lax.dynamic_slice_in_dim(seg, z * slab, slab + 2 * half, 0)
    spans = key_spans(seg, slab, count, half)
    seg = seg.astype(jnp.float32)[None]
    share = layer_scale.shape[0]
    residual = jnp.transpose(lax.dynamic_slice_in_dim(tokens, tp * share, share, 1))
    scale = jnp.pad(layer_scale, (0, -share % 128))[None]
    x0, out_near, out_far, seg, spans, residual, scale, *gains = tied(
        x0, out_near, out_far, seg, spans, residual, scale, *gains
    )
    out_last = even_pair(out_far)
    x2 = in_slab(x0, 2)
    out_last, own, x0 = tied(out_last, own, x0)
    near, far = even_pair(own), half_pair(own)
    x1 = in_slab(x0, 1)
    out_last, x1 = tied(out_last, x1)
    close, away = jnp.stack([out_own, out_near]), jnp.stack([out_far, out_last])
    keep, give = jnp.where(home, close, away), jnp.where(home, away, close)
    got = across(give)
    keep_x = in_slab(keep, 2)
    near, far, x1, x2, got, keep_x = tied(near, far, x1, x2, got, keep_x)
    last = even_pair(far)
    x3 = in_slab(x2, 1)
    got_x, got_c, keep_c = in_slab(got, 2), in_slab(got, 1), in_slab(keep, 1)
    keep_xc = in_slab(tied(keep_x, x3)[0], 1)
    xs = (x0, x1, x2, x3)
    acc, x_last = early(place, xs, own, near, far)
    last, acc, x_last = tied(last, acc, x_last)
    query, keys, values, squares, even, odd = late(place, x_last, acc, last, *gains)
    even, odd = even_pair(even), odd_pair(odd)
    squares, got_x, got_c, keep_c, keep_xc = tied(squares, got_x, got_c, keep_c, keep_xc)
    sums = squares
    for r in range(1, SLAB):
        sums = sums + in_slab(squares, r)
    sums = sums + across(sums)
    sums = (sums, even_pair(sums), odd_pair(sums))
    got_xc = in_slab(got_x, 1)

    blocks = attend(full_width, place, spans, query, keys, values, even, odd, sums, seg)
    *blocks, got_xc = tied(*blocks, got_xc)
    pieces = (keep, keep_c, keep_x, keep_xc, got, got_c, got_x, got_xc)
    spread = []
    for r, i in ((2, 0), (0, 1), (3, 1), (3, 0), (1, 1), (2, 1), (1, 0), (0, 0)):
        to = functools.partial(lambda r, i, z, q, y: (z, q ^ r, y ^ i), r, i)
        spread.append(permuted(blocks[r], to) if r or i else blocks[r])

    return jnp.transpose(output(place, spread, collect(pieces), residual, scale))


def solution(mesh):
    def shards(*args):
        heads = args[2].shape[2] // HEAD_DIM
        slab = mesh.shape["seq"] == 16 and mesh.shape["tp"] == 2 and heads % SLAB == 0
        return (slab_plan if slab else row_plan)(*args)

    return jax.shard_map(
        shards,
        mesh=mesh,
        in_specs=(
            P("seq", None),
            P(),
            P("seq", None, "tp"),
            P("tp"),
            P("tp"),
            P("tp", "seq"),
            P("tp"),
            P(),
        ),
        out_specs=P("seq", "tp"),
        check_vma=False,
    )
```

```python
import functools
import math

import jax
import jax.numpy as jnp
from jax import lax
from jax.experimental import pallas as pl
from jax.experimental.pallas import tpu as pltpu
from jax.sharding import PartitionSpec as P

HEAD_DIM = 128
SLAB = 4

eps = 1e-06
floor_score = -1e30


def passed_along(x, axis, by):
    size = lax.axis_size(axis)
    pairs = [(i, i + by) for i in range(size) if 0 <= i + by < size]
    return lax.ppermute(x, axis, pairs)


def masked_scores(query, keys, query_seg, key_seg):
    scores = jnp.einsum(
        "qhd,khd->hqk", query, keys, preferred_element_type=jnp.float32
    ) * HEAD_DIM ** (-0.5)
    mask = (query_seg[:, None] == key_seg[None, :])[None]
    return (jnp.where(mask, scores, floor_score), mask)


def row_plan(tokens, norm_gain, qkv_weight, q_gain, k_gain, out_weight, layer_scale, segment_ids):
    count = tokens.shape[0]
    source = tokens.astype(jnp.float32)
    normed = (
        source * lax.rsqrt(jnp.mean(source * source, axis=-1, keepdims=True) + eps) * norm_gain
    ).astype(jnp.bfloat16)
    local_width = qkv_weight.shape[2]
    heads = local_width // HEAD_DIM
    joined = jnp.einsum(
        "td,dch->tch",
        normed,
        lax.all_gather(qkv_weight, "seq", axis=0, tiled=True),
        preferred_element_type=jnp.float32,
    )
    query = joined[:, 0]
    keys = joined[:, 1]
    values = joined[:, 2]
    query_sq, key_sq = lax.psum(
        (jnp.sum(query * query, axis=-1), jnp.sum(keys * keys, axis=-1)), "tp"
    )
    full_width = local_width * lax.axis_size("tp")
    query_normed = (query * lax.rsqrt(query_sq / full_width + eps)[:, None] * q_gain).astype(
        jnp.bfloat16
    )
    key_normed = (keys * lax.rsqrt(key_sq / full_width + eps)[:, None] * k_gain).astype(
        jnp.bfloat16
    )
    paired = jnp.stack([key_normed, values.astype(jnp.bfloat16)], axis=1)
    pieces = []
    for offset in (2, 1, 0, -1, -2):
        if offset == 0:
            pieces.append(paired)
        else:
            pieces.append(passed_along(paired, "seq", offset))
    widened = jnp.concatenate(pieces, axis=0)
    position = lax.axis_index("seq")
    outside = jnp.full((2 * count,), -1, jnp.int32)
    seg_pad = jnp.concatenate([outside, segment_ids, outside], axis=0)
    key_seg = lax.dynamic_slice_in_dim(seg_pad, position * count, 5 * count, 0)
    query_seg = lax.dynamic_slice_in_dim(segment_ids, position * count, count, 0)
    query_heads = query_normed.reshape(count, heads, HEAD_DIM)
    key_heads = widened[:, 0].reshape(5 * count, heads, HEAD_DIM)
    value_heads = widened[:, 1].reshape(5 * count, heads, HEAD_DIM)
    scores, mask = masked_scores(query_heads, key_heads, query_seg, key_seg)
    peak = jnp.max(scores, axis=-1, keepdims=True)
    weights = jnp.where(mask, jnp.exp(scores - peak), 0.0)
    total = jnp.sum(weights, axis=-1)
    probs = weights.astype(jnp.bfloat16)
    summed = jnp.einsum("hqk,khd->qhd", probs, value_heads, preferred_element_type=jnp.float32)
    context = (
        (summed / jnp.transpose(total)[:, :, None]).reshape(count, local_width).astype(jnp.bfloat16)
    )
    terms = jnp.dot(
        context,
        lax.all_gather(out_weight, "seq", axis=1, tiled=True),
        preferred_element_type=jnp.float32,
    )
    projected = lax.psum_scatter(terms, "tp", scatter_dimension=1, tiled=True)
    share = layer_scale.shape[0]
    residual = lax.dynamic_slice_in_dim(source, lax.axis_index("tp") * share, share, 1)
    return (residual + layer_scale * projected).astype(jnp.bfloat16)


ANY = pl.BlockSpec(memory_space=pl.ANY)
VMEM = pl.BlockSpec(memory_space=pltpu.VMEM)
SMEM = pl.BlockSpec(memory_space=pltpu.SMEM)
HBM = pl.BlockSpec(memory_space=pltpu.HBM)
KERNEL_VMEM = 60 * 1024 * 1024
HELD_VMEM = 24 * 1024 * 1024


def permuted(x, to):
    slabs, tps = lax.axis_size("seq") // SLAB, lax.axis_size("tp")
    pairs = []
    for i in range(slabs * SLAB * tps):
        z, q, y = to(i // (SLAB * tps), i // tps % SLAB, i % tps)
        pairs.append((i, (z * SLAB + q) * tps + y))
    return lax.ppermute(x, ("seq", "tp"), pairs)


def in_slab(x, flip):
    return permuted(x, lambda z, q, y: (z, q ^ flip, y))


def across(x):
    return permuted(x, lambda z, q, y: (z, q, 1 - y))


def even_pair(x):
    return permuted(x, lambda z, q, y: (z ^ 1, q, y))


def odd_pair(x):
    return permuted(x, lambda z, q, y: (3 - z, q, y) if z in (1, 2) else (z, q ^ 1, y))


def half_pair(x):
    return permuted(x, lambda z, q, y: (z ^ 2, q, y))


def tied(*arrays):
    return lax.optimization_barrier(arrays)


def as_row(column):
    wide = jnp.broadcast_to(column, (column.shape[0], 128))
    return jnp.transpose(wide)[:8]


def as_column(row):
    return jnp.transpose(jnp.broadcast_to(row, (128, row.shape[1])))


def start(copies):
    for copy in copies:
        copy.start()


def wait(copies):
    for copy in copies:
        copy.wait()


def norm_kernel(tokens, gain, out):
    part = tokens.shape[1] // out.shape[0]
    source = tokens[...].astype(jnp.float32)
    mean = jnp.mean(source * source, axis=1, keepdims=True)
    normed = source * lax.rsqrt(mean + eps) * gain[...]
    for j in range(out.shape[0]):
        out[j, :, :part] = normed[:, j * part:(j + 1) * part].astype(jnp.bfloat16)
        out[j, :, part:] = jnp.zeros((out.shape[1], out.shape[2] - part), jnp.bfloat16)


def norm(tokens, gain, slabs):
    count, depth = tokens.shape
    shape = (slabs, count, pl.cdiv(depth // slabs, 128) * 128)
    return pl.pallas_call(
        norm_kernel,
        out_shape=jax.ShapeDtypeStruct(shape, jnp.bfloat16),
        in_specs=[VMEM, VMEM],
        out_specs=VMEM,
        compiler_params=pltpu.CompilerParams(vmem_limit_bytes=KERNEL_VMEM),
        name="norm",
    )(tokens, gain[None])


def token_copies(xs, at, out, sems):
    return [
        pltpu.make_async_copy(x.at[at], out.at[r], sems.at[r]) for r, x in enumerate(xs)
    ]


def blank_tail(w, rows):
    tail = w.shape[-2] - rows
    w[..., rows:, :] = jnp.zeros(w.shape[:-2] + (tail, w.shape[-1]), w.dtype)


def early_kernel(
    place, xa, xb, xc, xd, own, near, far, acc, x_last, x_all, w_all, x_sem, w_sem, last_sem,
):
    z = place[0]
    kinds, rows = own.shape[:2]
    copies = []
    for i, w in enumerate((own, near, far)):
        dst = w_all.at[i, :, pl.ds(0, rows), :]
        copies.append([pltpu.make_async_copy(w, dst, w_sem.at[i])])
        copies[i] += token_copies((xa, xb, xc, xd), z ^ i, x_all.at[i], x_sem.at[i])
        start(copies[i])
    last_copies = token_copies((xa, xb, xc, xd), z ^ 3, x_last, last_sem)
    start(last_copies)
    blank_tail(w_all, rows)
    for step in range(3):
        wait(copies[step])
        for r in range(SLAB):
            x = x_all[step, r]
            for kind in range(kinds):
                term = jnp.dot(x, w_all[step, kind], preferred_element_type=jnp.float32)
                acc[r, kind] = term if step == 0 else acc[r, kind] + term
    wait(last_copies)


def early(place, xs, own, near, far):
    kinds, rows, width = own.shape
    slabs, count, wide = xs[0].shape
    return pl.pallas_call(
        early_kernel,
        out_shape=(
            jax.ShapeDtypeStruct((SLAB, kinds, count, width), jnp.float32),
            jax.ShapeDtypeStruct((SLAB, count, wide), jnp.bfloat16),
        ),
        in_specs=[SMEM] + [HBM] * 7,
        out_specs=(VMEM, VMEM),
        scratch_shapes=[
            pltpu.VMEM((3, SLAB, count, wide), jnp.bfloat16),
            pltpu.VMEM((3, kinds, wide, width), jnp.bfloat16),
            pltpu.SemaphoreType.DMA((3, SLAB)),
            pltpu.SemaphoreType.DMA((3,)),
            pltpu.SemaphoreType.DMA((SLAB,)),
        ],
        compiler_params=pltpu.CompilerParams(vmem_limit_bytes=HELD_VMEM),
        cost_estimate=pl.CostEstimate(
            flops=12 * kinds * SLAB * count * rows * width,
            bytes_accessed=6 * kinds * rows * width + 6 * SLAB * count * rows,
            transcendentals=0,
        ),
        name="early",
    )(place, *xs, own, near, far)


def late_kernel(
    place, x_last, acc, last, q_gain, k_gain, query, keys, values, squares, even, odd, w_all,
):
    z, q = place[0], place[1]
    rows = last.shape[1]
    w_all[:, :rows, :] = last[...]
    blank_tail(w_all, rows)
    count = acc.shape[2]
    for r in range(SLAB):
        rows = pl.ds(pl.multiple_of((q ^ r) * count, count), count)
        for kind in range(3):
            part = acc[r, kind] + jnp.dot(
                x_last[r], w_all[kind], preferred_element_type=jnp.float32
            )
            if kind < 2:
                summed = as_row(jnp.sum(part * part, axis=1, keepdims=True))
                squares[kind:kind + 1, rows] = summed[:1]
                part = part * (q_gain, k_gain)[kind][...]
            out = (query, keys, values)[kind]
            out[rows, :] = part.astype(out.dtype)
    reach = even.shape[1]
    for out, at in ((even, 1 - z % 2), (odd, z % 2)):
        rows = pl.ds(pl.multiple_of(at * reach, reach), reach)
        out[0] = keys[rows, :]
        out[1] = values[rows, :]


def late(place, x_last, acc, last, q_gain, k_gain):
    kinds, rows, width = last.shape
    count, wide = x_last.shape[1:]
    slab = SLAB * count
    f32, bf16 = jnp.float32, jnp.bfloat16
    return pl.pallas_call(
        late_kernel,
        out_shape=(
            jax.ShapeDtypeStruct((slab, width), f32),
            jax.ShapeDtypeStruct((slab, width), bf16),
            jax.ShapeDtypeStruct((slab, width), bf16),
            jax.ShapeDtypeStruct((2, slab), f32),
            jax.ShapeDtypeStruct((2, 2 * count, width), bf16),
            jax.ShapeDtypeStruct((2, 2 * count, width), bf16),
        ),
        in_specs=[SMEM] + [VMEM] * 5,
        out_specs=(VMEM,) * 6,
        scratch_shapes=[
            pltpu.VMEM((kinds, wide, width), bf16),
        ],
        compiler_params=pltpu.CompilerParams(vmem_limit_bytes=HELD_VMEM),
        cost_estimate=pl.CostEstimate(
            flops=2 * kinds * slab * rows * width,
            bytes_accessed=2 * kinds * rows * width + 2 * slab * rows,
            transcendentals=0,
        ),
        name="late",
    )(place, x_last, acc, last, q_gain, k_gain)


def attend_kernel(
    full_width, place, spans, query, keys, values, even, odd, mine, near, mid, seg, o0, o1, o2, o3,
    k_all, v_all, o_all, scale_all,
):
    z, q = place[0], place[1]
    slab = query.shape[0]
    count = slab // SLAB
    half = even.shape[1]
    upper = half + slab
    is_even = z % 2 == 0
    even_at = pl.multiple_of(jnp.where(is_even, upper, 0), half)
    odd_at = pl.multiple_of(jnp.where(is_even, 0, upper), half)
    for k, (whole, out) in enumerate(((keys, k_all), (values, v_all))):
        out[half:upper, :] = whole[...]
        out[pl.ds(even_at, half), :] = even[k]
        out[pl.ds(odd_at, half), :] = odd[k]
    scale = [lax.rsqrt(sums[...] / full_width + eps) for sums in (mine, near, mid)]
    scale_all[:, half:upper] = scale[0]
    scale_all[:, :half] = jnp.where(is_even, scale[2], scale[1])[:, slab - half:]
    scale_all[:, upper:] = jnp.where(is_even, scale[1], scale[2])[:, :half]
    heads = query.shape[1] // HEAD_DIM
    factor = HEAD_DIM ** (-0.5) * math.log2(math.e)

    def block(r, _):
        b = q ^ r
        at_query = pl.multiple_of(b * count + half, count)
        query_seg = as_column(seg[:, pl.ds(at_query, count)])
        q_scale = as_column(scale_all[0:1, pl.ds(at_query, count)])
        for tiles in range(2, 2 * half // count + 2):
            @pl.when(spans[b, 1] == tiles)
            def _():
                width = tiles * count
                begin = pl.multiple_of(spans[b, 0], 128)
                keys_at = pl.ds(begin, width)
                mask = jnp.tile(query_seg, (1, width // 128)) == seg[:, keys_at]
                k_scale = scale_all[1:2, keys_at] * factor
                for h in range(heads):
                    cols = slice(h * HEAD_DIM, (h + 1) * HEAD_DIM)
                    q_low = query[pl.ds(pl.multiple_of(b * count, count), count), cols] * q_scale
                    scores = lax.dot_general(
                        q_low.astype(jnp.bfloat16), k_all[keys_at, cols],
                        (((1,), (1,)), ((), ())), preferred_element_type=jnp.float32,
                    )
                    scores = jnp.where(mask, scores * k_scale, floor_score)
                    peak = jnp.max(scores, axis=1, keepdims=True)
                    weights = jnp.exp2(scores - peak)
                    total = jnp.sum(weights, axis=1, keepdims=True)
                    summed = jnp.dot(
                        weights.astype(jnp.bfloat16), v_all[keys_at, cols],
                        preferred_element_type=jnp.float32,
                    )
                    o_all[r, cols, :] = jnp.transpose(summed / total).astype(jnp.bfloat16)

        return 0

    lax.fori_loop(0, SLAB, block, 0)
    for r, out in enumerate((o0, o1, o2, o3)):
        out[...] = o_all[r]


def key_spans(seg, slab, count, half):
    ext = seg.shape[0]
    index = jnp.arange(ext, dtype=jnp.int32)
    blocks = seg[half:half + slab].reshape(-1, count)
    first, last = blocks[:, :1], blocks[:, -1:]
    begin = jnp.min(jnp.where(seg == first, index, ext), axis=1) // 128 * 128
    end = jnp.max(jnp.where(seg == last, index, -1), axis=1) + 1
    tiles = jnp.maximum((end - begin + count - 1) // count, 2)
    return jnp.stack([jnp.minimum(begin, ext - tiles * count), tiles], axis=1)


def attend(full_width, place, spans, query, keys, values, even, odd, sums, seg):
    slab, width = query.shape
    half = even.shape[1]
    count = slab // SLAB
    ext = slab + 2 * half
    bf16 = jnp.bfloat16
    window = count + 2 * half
    return pl.pallas_call(
        functools.partial(attend_kernel, full_width),
        out_shape=(jax.ShapeDtypeStruct((width, count), bf16),) * SLAB,
        in_specs=[SMEM] * 2 + [VMEM] * 9,
        out_specs=(VMEM,) * SLAB,
        scratch_shapes=[
            pltpu.VMEM((ext, width), bf16),
            pltpu.VMEM((ext, width), bf16),
            pltpu.VMEM((SLAB, width, count), bf16),
            pltpu.VMEM((2, ext), jnp.float32),
        ],
        compiler_params=pltpu.CompilerParams(vmem_limit_bytes=HELD_VMEM),
        cost_estimate=pl.CostEstimate(
            flops=64 * SLAB * count * window * width,
            bytes_accessed=4 * ext * width + 4 * slab * width,
            transcendentals=SLAB * count * window * width // HEAD_DIM,
        ),
        name="attend",
    )(place, spans, query, keys, values, even, odd, *sums, seg)


def collect_kernel(wa0, wb0, wc0, wd0, wa1, wb1, wc1, wd1, out, sems):
    rows = wa0.shape[1]
    copies = []
    for i, ws in enumerate(((wa0, wb0, wc0, wd0), (wa1, wb1, wc1, wd1))):
        for r, w in enumerate(ws):
            for j in range(2):
                dst = out.at[i, pl.ds((2 * r + j) * rows, rows), :]
                copies.append(pltpu.make_async_copy(w.at[j], dst, sems.at[i, r, j]))
    start(copies)
    wait(copies)


def collect(pieces):
    rows, depth = pieces[0].shape[1:]
    return pl.pallas_call(
        collect_kernel,
        out_shape=jax.ShapeDtypeStruct((2, 2 * SLAB * rows, depth), jnp.bfloat16),
        in_specs=[HBM] * 8,
        out_specs=VMEM,
        scratch_shapes=[pltpu.SemaphoreType.DMA((2, SLAB, 2))],
        compiler_params=pltpu.CompilerParams(vmem_limit_bytes=HELD_VMEM),
        cost_estimate=pl.CostEstimate(
            flops=0, bytes_accessed=16 * SLAB * rows * depth, transcendentals=0
        ),
        name="collect",
    )(*pieces)


def out_kernel(
    place, c20, c01, c31, c30, c11, c21, c10, c00, w, residual, scale, out, c_all, total, placed,
):
    z, q = place[0], place[1]
    width = c00.shape[0]
    for i, blocks in enumerate(((c00, c10, c20, c30), (c01, c11, c21, c31))):
        for r, c in enumerate(blocks):
            c_all[i, pl.ds(pl.multiple_of((q ^ r) * width, width), width), :] = c[...]
    column = as_column(scale[...])[:out.shape[0]]
    column = jnp.tile(column, (1, out.shape[1] // 128))
    total[...] = jnp.dot(w[0], c_all[0], preferred_element_type=jnp.float32)
    total[...] += jnp.dot(w[1], c_all[1], preferred_element_type=jnp.float32)
    rows, kept = w.shape[1] // (2 * SLAB), out.shape[0] // (2 * SLAB)
    for r in range(SLAB):
        for j in range(2):
            at = pl.multiple_of((((z % 2) ^ j) * SLAB + (q ^ r)) * kept, 8)
            begin = (2 * r + j) * rows
            placed[pl.ds(at, kept), :] = total[begin:begin + kept, :]
    out[...] = (residual[...].astype(jnp.float32) + column * placed[...]).astype(jnp.bfloat16)


def output(place, blocks, w, residual, scale):
    count = blocks[0].shape[1]
    rows, depth = w.shape[1:]
    share = residual.shape[0]
    return pl.pallas_call(
        out_kernel,
        out_shape=jax.ShapeDtypeStruct((share, count), jnp.bfloat16),
        in_specs=[SMEM] + [VMEM] * 11,
        out_specs=VMEM,
        scratch_shapes=[
            pltpu.VMEM((2, depth, count), jnp.bfloat16),
            pltpu.VMEM((rows, count), jnp.float32),
            pltpu.VMEM((share, count), jnp.float32),
        ],
        compiler_params=pltpu.CompilerParams(vmem_limit_bytes=HELD_VMEM),
        cost_estimate=pl.CostEstimate(
            flops=4 * share * count * depth,
            bytes_accessed=4 * share * depth,
            transcendentals=0,
        ),
        name="output",
    )(place, *blocks, w, residual, scale)


def rows_of_slab(q, got):
    placed = []
    for b in range(SLAB):
        piece = got[b]
        for other in range(1, SLAB):
            piece = jnp.where(q == other, got[b ^ other], piece)
        placed.append(piece)
    return jnp.concatenate(placed, axis=1)


def slab_plan(tokens, norm_gain, qkv_weight, q_gain, k_gain, out_weight, layer_scale, segment_ids):
    count = tokens.shape[0]
    seq, tp = lax.axis_index("seq"), lax.axis_index("tp")
    slabs = lax.axis_size("seq") // SLAB
    z, q = seq // SLAB, seq % SLAB
    place = jnp.stack([z, q, tp]).astype(jnp.int32)
    width = qkv_weight.shape[2] // SLAB
    full_width = qkv_weight.shape[2] * lax.axis_size("tp")
    slab, half = SLAB * count, 2 * count
    home = z // 2 == tp

    by_kind = jnp.transpose(qkv_weight, (1, 0, 2))
    cut = [lax.dynamic_slice_in_dim(by_kind, (q ^ r) * width, width, 2) for r in range(SLAB)]
    got = [cut[0]] + [in_slab(cut[r], r) for r in range(1, SLAB)]
    x0 = norm(tokens, norm_gain, slabs)
    out_own = jnp.transpose(out_weight)
    own = rows_of_slab(q, got)
    out_near, out_far = even_pair(out_own), half_pair(out_own)
    gains = [lax.dynamic_slice_in_dim(g, q * width, width, 0)[None] for g in (q_gain, k_gain)]

    outside = jnp.full((half,), -1, jnp.int32)
    seg = jnp.concatenate([outside, segment_ids, outside], axis=0)
    seg = lax.dynamic_slice_in_dim(seg, z * slab, slab + 2 * half, 0)
    spans = key_spans(seg, slab, count, half)
    seg = seg.astype(jnp.float32)[None]
    share = layer_scale.shape[0]
    residual = jnp.transpose(lax.dynamic_slice_in_dim(tokens, tp * share, share, 1))
    scale = jnp.pad(layer_scale, (0, -share % 128))[None]
    x0, out_near, out_far, seg, spans, residual, scale, *gains = tied(
        x0, out_near, out_far, seg, spans, residual, scale, *gains
    )
    out_last = even_pair(out_far)
    x2 = in_slab(x0, 2)
    out_last, own, x0 = tied(out_last, own, x0)
    far, near = half_pair(own), even_pair(own)
    x1 = in_slab(x0, 1)
    out_last, x1 = tied(out_last, x1)
    close, away = jnp.stack([out_own, out_near]), jnp.stack([out_far, out_last])
    pad = ((0, 0), (0, -close.shape[1] % 16), (0, 0))
    keep = jnp.pad(jnp.where(home, close, away), pad)
    got = across(jnp.pad(jnp.where(home, away, close), pad))
    keep_x = in_slab(keep, 2)
    near, far, x1, x2, got, keep_x = tied(near, far, x1, x2, got, keep_x)
    last = even_pair(far)
    x3 = in_slab(x2, 1)
    got_x, got_c, keep_c = in_slab(got, 2), in_slab(got, 1), in_slab(keep, 1)
    keep_xc = in_slab(tied(keep_x, x3)[0], 1)
    xs = (x0, x1, x2, x3)
    acc, x_last = early(place, xs, own, near, far)
    last, acc, x_last = tied(last, acc, x_last)
    query, keys, values, squares, even, odd = late(place, x_last, acc, last, *gains)
    even, odd = even_pair(even), odd_pair(odd)
    squares, got_x, got_c, keep_c, keep_xc = tied(squares, got_x, got_c, keep_c, keep_xc)
    sums = squares
    for r in range(1, SLAB):
        sums = sums + in_slab(squares, r)
    sums = sums + across(sums)
    sums = (sums, even_pair(sums), odd_pair(sums))
    got_xc = in_slab(got_x, 1)

    blocks = attend(full_width, place, spans, query, keys, values, even, odd, sums, seg)
    *blocks, got_xc = tied(*blocks, got_xc)
    pieces = (keep, keep_c, keep_x, keep_xc, got, got_c, got_x, got_xc)
    spread = []
    for r, i in ((2, 0), (0, 1), (3, 1), (3, 0), (1, 1), (2, 1), (1, 0), (0, 0)):
        to = functools.partial(lambda r, i, z, q, y: (z, q ^ r, y ^ i), r, i)
        spread.append(permuted(blocks[r], to) if r or i else blocks[r])

    return jnp.transpose(output(place, spread, collect(pieces), residual, scale))


def solution(mesh):
    def shards(*args):
        heads = args[2].shape[2] // HEAD_DIM
        slab = mesh.shape["seq"] == 16 and mesh.shape["tp"] == 2 and heads % SLAB == 0
        return (slab_plan if slab else row_plan)(*args)

    return jax.shard_map(
        shards,
        mesh=mesh,
        in_specs=(
            P("seq", None),
            P(),
            P("seq", None, "tp"),
            P("tp"),
            P("tp"),
            P("tp", "seq"),
            P("tp"),
            P(),
        ),
        out_specs=P("seq", "tp"),
        check_vma=False,
    )
```

```python
import functools
import math

import jax
import jax.numpy as jnp
from jax import lax
from jax.experimental import pallas as pl
from jax.experimental.pallas import tpu as pltpu
from jax.sharding import PartitionSpec as P

HEAD_DIM = 128
SLAB = 4

eps = 1e-06
floor_score = -1e30


def passed_along(x, axis, by):
    size = lax.axis_size(axis)
    pairs = [(i, i + by) for i in range(size) if 0 <= i + by < size]
    return lax.ppermute(x, axis, pairs)


def masked_scores(query, keys, query_seg, key_seg):
    scores = jnp.einsum(
        "qhd,khd->hqk", query, keys, preferred_element_type=jnp.float32
    ) * HEAD_DIM ** (-0.5)
    mask = (query_seg[:, None] == key_seg[None, :])[None]
    return (jnp.where(mask, scores, floor_score), mask)


def row_plan(tokens, norm_gain, qkv_weight, q_gain, k_gain, out_weight, layer_scale, segment_ids):
    count = tokens.shape[0]
    source = tokens.astype(jnp.float32)
    normed = (
        source * lax.rsqrt(jnp.mean(source * source, axis=-1, keepdims=True) + eps) * norm_gain
    ).astype(jnp.bfloat16)
    local_width = qkv_weight.shape[2]
    heads = local_width // HEAD_DIM
    joined = jnp.einsum(
        "td,dch->tch",
        normed,
        lax.all_gather(qkv_weight, "seq", axis=0, tiled=True),
        preferred_element_type=jnp.float32,
    )
    query = joined[:, 0]
    keys = joined[:, 1]
    values = joined[:, 2]
    query_sq, key_sq = lax.psum(
        (jnp.sum(query * query, axis=-1), jnp.sum(keys * keys, axis=-1)), "tp"
    )
    full_width = local_width * lax.axis_size("tp")
    query_normed = (query * lax.rsqrt(query_sq / full_width + eps)[:, None] * q_gain).astype(
        jnp.bfloat16
    )
    key_normed = (keys * lax.rsqrt(key_sq / full_width + eps)[:, None] * k_gain).astype(
        jnp.bfloat16
    )
    paired = jnp.stack([key_normed, values.astype(jnp.bfloat16)], axis=1)
    pieces = []
    for offset in (2, 1, 0, -1, -2):
        if offset == 0:
            pieces.append(paired)
        else:
            pieces.append(passed_along(paired, "seq", offset))
    widened = jnp.concatenate(pieces, axis=0)
    position = lax.axis_index("seq")
    outside = jnp.full((2 * count,), -1, jnp.int32)
    seg_pad = jnp.concatenate([outside, segment_ids, outside], axis=0)
    key_seg = lax.dynamic_slice_in_dim(seg_pad, position * count, 5 * count, 0)
    query_seg = lax.dynamic_slice_in_dim(segment_ids, position * count, count, 0)
    query_heads = query_normed.reshape(count, heads, HEAD_DIM)
    key_heads = widened[:, 0].reshape(5 * count, heads, HEAD_DIM)
    value_heads = widened[:, 1].reshape(5 * count, heads, HEAD_DIM)
    scores, mask = masked_scores(query_heads, key_heads, query_seg, key_seg)
    peak = jnp.max(scores, axis=-1, keepdims=True)
    weights = jnp.where(mask, jnp.exp(scores - peak), 0.0)
    total = jnp.sum(weights, axis=-1)
    probs = weights.astype(jnp.bfloat16)
    summed = jnp.einsum("hqk,khd->qhd", probs, value_heads, preferred_element_type=jnp.float32)
    context = (
        (summed / jnp.transpose(total)[:, :, None]).reshape(count, local_width).astype(jnp.bfloat16)
    )
    terms = jnp.dot(
        context,
        lax.all_gather(out_weight, "seq", axis=1, tiled=True),
        preferred_element_type=jnp.float32,
    )
    projected = lax.psum_scatter(terms, "tp", scatter_dimension=1, tiled=True)
    share = layer_scale.shape[0]
    residual = lax.dynamic_slice_in_dim(source, lax.axis_index("tp") * share, share, 1)
    return (residual + layer_scale * projected).astype(jnp.bfloat16)


ANY = pl.BlockSpec(memory_space=pl.ANY)
VMEM = pl.BlockSpec(memory_space=pltpu.VMEM)
SMEM = pl.BlockSpec(memory_space=pltpu.SMEM)
HBM = pl.BlockSpec(memory_space=pltpu.HBM)
KERNEL_VMEM = 60 * 1024 * 1024
HELD_VMEM = 24 * 1024 * 1024


def permuted(x, to):
    slabs, tps = lax.axis_size("seq") // SLAB, lax.axis_size("tp")
    pairs = []
    for i in range(slabs * SLAB * tps):
        z, q, y = to(i // (SLAB * tps), i // tps % SLAB, i % tps)
        pairs.append((i, (z * SLAB + q) * tps + y))
    return lax.ppermute(x, ("seq", "tp"), pairs)


def in_slab(x, flip):
    return permuted(x, lambda z, q, y: (z, q ^ flip, y))


def across(x):
    return permuted(x, lambda z, q, y: (z, q, 1 - y))


def even_pair(x):
    return permuted(x, lambda z, q, y: (z ^ 1, q, y))


def odd_pair(x):
    return permuted(x, lambda z, q, y: (3 - z, q, y) if z in (1, 2) else (z, q ^ 1, y))


def half_pair(x):
    return permuted(x, lambda z, q, y: (z ^ 2, q, y))


def tied(*arrays):
    return lax.optimization_barrier(arrays)


def as_row(column):
    wide = jnp.broadcast_to(column, (column.shape[0], 128))
    return jnp.transpose(wide)[:8]


def as_column(row):
    return jnp.transpose(jnp.broadcast_to(row, (128, row.shape[1])))


def start(copies):
    for copy in copies:
        copy.start()


def wait(copies):
    for copy in copies:
        copy.wait()


def norm_kernel(tokens, gain, out):
    part = tokens.shape[1] // out.shape[0]
    source = tokens[...].astype(jnp.float32)
    mean = jnp.mean(source * source, axis=1, keepdims=True)
    normed = source * lax.rsqrt(mean + eps) * gain[...]
    for j in range(out.shape[0]):
        out[j, :, :part] = normed[:, j * part:(j + 1) * part].astype(jnp.bfloat16)
        out[j, :, part:] = jnp.zeros((out.shape[1], out.shape[2] - part), jnp.bfloat16)


def norm(tokens, gain, slabs):
    count, depth = tokens.shape
    shape = (slabs, count, pl.cdiv(depth // slabs, 128) * 128)
    return pl.pallas_call(
        norm_kernel,
        out_shape=jax.ShapeDtypeStruct(shape, jnp.bfloat16),
        in_specs=[VMEM, VMEM],
        out_specs=VMEM,
        compiler_params=pltpu.CompilerParams(vmem_limit_bytes=KERNEL_VMEM),
        name="norm",
    )(tokens, gain[None])


def token_copies(xs, at, out, sems):
    return [
        pltpu.make_async_copy(x.at[at], out.at[r], sems.at[r]) for r, x in enumerate(xs)
    ]


def blank_tail(w, rows):
    tail = w.shape[-2] - rows
    w[..., rows:, :] = jnp.zeros(w.shape[:-2] + (tail, w.shape[-1]), w.dtype)


def early_kernel(
    place, xa, xb, xc, xd, own, near, far, acc, x_last, x_all, w_all, x_sem, w_sem, last_sem,
):
    z = place[0]
    kinds, rows = own.shape[:2]
    copies = []
    for i, w in enumerate((own, near, far)):
        dst = w_all.at[i, :, pl.ds(0, rows), :]
        copies.append([pltpu.make_async_copy(w, dst, w_sem.at[i])])
        copies[i] += token_copies((xa, xb, xc, xd), z ^ i, x_all.at[i], x_sem.at[i])
        start(copies[i])
    last_copies = token_copies((xa, xb, xc, xd), z ^ 3, x_last, last_sem)
    start(last_copies)
    blank_tail(w_all, rows)
    for step in range(3):
        wait(copies[step])
        for r in range(SLAB):
            x = x_all[step, r]
            for kind in range(kinds):
                term = jnp.dot(x, w_all[step, kind], preferred_element_type=jnp.float32)
                acc[r, kind] = term if step == 0 else acc[r, kind] + term
    wait(last_copies)


def early(place, xs, own, near, far):
    kinds, rows, width = own.shape
    slabs, count, wide = xs[0].shape
    return pl.pallas_call(
        early_kernel,
        out_shape=(
            jax.ShapeDtypeStruct((SLAB, kinds, count, width), jnp.float32),
            jax.ShapeDtypeStruct((SLAB, count, wide), jnp.bfloat16),
        ),
        in_specs=[SMEM] + [HBM] * 7,
        out_specs=(VMEM, VMEM),
        scratch_shapes=[
            pltpu.VMEM((3, SLAB, count, wide), jnp.bfloat16),
            pltpu.VMEM((3, kinds, wide, width), jnp.bfloat16),
            pltpu.SemaphoreType.DMA((3, SLAB)),
            pltpu.SemaphoreType.DMA((3,)),
            pltpu.SemaphoreType.DMA((SLAB,)),
        ],
        compiler_params=pltpu.CompilerParams(vmem_limit_bytes=HELD_VMEM),
        cost_estimate=pl.CostEstimate(
            flops=12 * kinds * SLAB * count * rows * width,
            bytes_accessed=6 * kinds * rows * width + 6 * SLAB * count * rows,
            transcendentals=0,
        ),
        name="early",
    )(place, *xs, own, near, far)


def late_kernel(
    place, x_last, acc, last, q_gain, k_gain, query, keys, values, squares, even, odd, w_all,
):
    z, q = place[0], place[1]
    rows = last.shape[1]
    w_all[:, :rows, :] = last[...]
    blank_tail(w_all, rows)
    count = acc.shape[2]
    for r in range(SLAB):
        rows = pl.ds(pl.multiple_of((q ^ r) * count, count), count)
        for kind in range(3):
            part = acc[r, kind] + jnp.dot(
                x_last[r], w_all[kind], preferred_element_type=jnp.float32
            )
            if kind < 2:
                summed = as_row(jnp.sum(part * part, axis=1, keepdims=True))
                squares[kind:kind + 1, rows] = summed[:1]
                part = part * (q_gain, k_gain)[kind][...]
            out = (query, keys, values)[kind]
            out[rows, :] = part.astype(out.dtype)
    reach = even.shape[1]
    for out, at in ((even, 1 - z % 2), (odd, z % 2)):
        rows = pl.ds(pl.multiple_of(at * reach, reach), reach)
        out[0] = keys[rows, :]
        out[1] = values[rows, :]


def late(place, x_last, acc, last, q_gain, k_gain):
    kinds, rows, width = last.shape
    count, wide = x_last.shape[1:]
    slab = SLAB * count
    f32, bf16 = jnp.float32, jnp.bfloat16
    return pl.pallas_call(
        late_kernel,
        out_shape=(
            jax.ShapeDtypeStruct((slab, width), f32),
            jax.ShapeDtypeStruct((slab, width), bf16),
            jax.ShapeDtypeStruct((slab, width), bf16),
            jax.ShapeDtypeStruct((2, slab), f32),
            jax.ShapeDtypeStruct((2, 2 * count, width), bf16),
            jax.ShapeDtypeStruct((2, 2 * count, width), bf16),
        ),
        in_specs=[SMEM] + [VMEM] * 5,
        out_specs=(VMEM,) * 6,
        scratch_shapes=[
            pltpu.VMEM((kinds, wide, width), bf16),
        ],
        compiler_params=pltpu.CompilerParams(vmem_limit_bytes=HELD_VMEM),
        cost_estimate=pl.CostEstimate(
            flops=2 * kinds * slab * rows * width,
            bytes_accessed=2 * kinds * rows * width + 2 * slab * rows,
            transcendentals=0,
        ),
        name="late",
    )(place, x_last, acc, last, q_gain, k_gain)


def attend_kernel(
    full_width, place, spans, query, keys, values, even, odd, mine, near, mid, seg, o0, o1, o2, o3,
    k_all, v_all, o_all, scale_all,
):
    z, q = place[0], place[1]
    slab = query.shape[0]
    count = slab // SLAB
    half = even.shape[1]
    upper = half + slab
    is_even = z % 2 == 0
    even_at = pl.multiple_of(jnp.where(is_even, upper, 0), half)
    odd_at = pl.multiple_of(jnp.where(is_even, 0, upper), half)
    for k, (whole, out) in enumerate(((keys, k_all), (values, v_all))):
        out[half:upper, :] = whole[...]
        out[pl.ds(even_at, half), :] = even[k]
        out[pl.ds(odd_at, half), :] = odd[k]
    scale = [lax.rsqrt(sums[...] / full_width + eps) for sums in (mine, near, mid)]
    scale_all[:, half:upper] = scale[0]
    scale_all[:, :half] = jnp.where(is_even, scale[2], scale[1])[:, slab - half:]
    scale_all[:, upper:] = jnp.where(is_even, scale[1], scale[2])[:, :half]
    heads = query.shape[1] // HEAD_DIM
    factor = HEAD_DIM ** (-0.5) * math.log2(math.e)

    def block(r, _):
        b = q ^ r
        at_query = pl.multiple_of(b * count + half, count)
        query_seg = as_column(seg[:, pl.ds(at_query, count)])
        q_scale = as_column(scale_all[0:1, pl.ds(at_query, count)])
        for tiles in range(2, 2 * half // count + 2):
            @pl.when(spans[b, 1] == tiles)
            def _():
                width = tiles * count
                begin = pl.multiple_of(spans[b, 0], 128)
                keys_at = pl.ds(begin, width)
                mask = jnp.tile(query_seg, (1, width // 128)) == seg[:, keys_at]
                k_scale = scale_all[1:2, keys_at] * factor
                for h in range(heads):
                    cols = slice(h * HEAD_DIM, (h + 1) * HEAD_DIM)
                    q_low = query[pl.ds(pl.multiple_of(b * count, count), count), cols] * q_scale
                    scores = lax.dot_general(
                        q_low.astype(jnp.bfloat16), k_all[keys_at, cols],
                        (((1,), (1,)), ((), ())), preferred_element_type=jnp.float32,
                    )
                    scores = jnp.where(mask, scores * k_scale, floor_score)
                    peak = jnp.max(scores, axis=1, keepdims=True)
                    weights = jnp.exp2(scores - peak)
                    total = jnp.sum(weights, axis=1, keepdims=True)
                    summed = jnp.dot(
                        weights.astype(jnp.bfloat16), v_all[keys_at, cols],
                        preferred_element_type=jnp.float32,
                    )
                    o_all[r, cols, :] = jnp.transpose(summed / total).astype(jnp.bfloat16)

        return 0

    lax.fori_loop(0, SLAB, block, 0)
    for r, out in enumerate((o0, o1, o2, o3)):
        out[...] = o_all[r]


def key_spans(seg, slab, count, half):
    ext = seg.shape[0]
    index = jnp.arange(ext, dtype=jnp.int32)
    blocks = seg[half:half + slab].reshape(-1, count)
    first, last = blocks[:, :1], blocks[:, -1:]
    begin = jnp.min(jnp.where(seg == first, index, ext), axis=1) // 128 * 128
    end = jnp.max(jnp.where(seg == last, index, -1), axis=1) + 1
    tiles = jnp.maximum((end - begin + count - 1) // count, 2)
    return jnp.stack([jnp.minimum(begin, ext - tiles * count), tiles], axis=1)


def attend(full_width, place, spans, query, keys, values, even, odd, sums, seg):
    slab, width = query.shape
    half = even.shape[1]
    count = slab // SLAB
    ext = slab + 2 * half
    bf16 = jnp.bfloat16
    window = count + 2 * half
    return pl.pallas_call(
        functools.partial(attend_kernel, full_width),
        out_shape=(jax.ShapeDtypeStruct((width, count), bf16),) * SLAB,
        in_specs=[SMEM] * 2 + [VMEM] * 9,
        out_specs=(VMEM,) * SLAB,
        scratch_shapes=[
            pltpu.VMEM((ext, width), bf16),
            pltpu.VMEM((ext, width), bf16),
            pltpu.VMEM((SLAB, width, count), bf16),
            pltpu.VMEM((2, ext), jnp.float32),
        ],
        compiler_params=pltpu.CompilerParams(vmem_limit_bytes=HELD_VMEM),
        cost_estimate=pl.CostEstimate(
            flops=64 * SLAB * count * window * width,
            bytes_accessed=4 * ext * width + 4 * slab * width,
            transcendentals=SLAB * count * window * width // HEAD_DIM,
        ),
        name="attend",
    )(place, spans, query, keys, values, even, odd, *sums, seg)


def collect_kernel(wa0, wb0, wc0, wd0, wa1, wb1, wc1, wd1, out, sems):
    rows = wa0.shape[1]
    copies = []
    for i, ws in enumerate(((wa0, wb0, wc0, wd0), (wa1, wb1, wc1, wd1))):
        for r, w in enumerate(ws):
            for j in range(2):
                dst = out.at[i, pl.ds((2 * r + j) * rows, rows), :]
                copies.append(pltpu.make_async_copy(w.at[j], dst, sems.at[i, r, j]))
    start(copies)
    wait(copies)


def collect(pieces):
    rows, depth = pieces[0].shape[1:]
    return pl.pallas_call(
        collect_kernel,
        out_shape=jax.ShapeDtypeStruct((2, 2 * SLAB * rows, depth), jnp.bfloat16),
        in_specs=[HBM] * 8,
        out_specs=VMEM,
        scratch_shapes=[pltpu.SemaphoreType.DMA((2, SLAB, 2))],
        compiler_params=pltpu.CompilerParams(vmem_limit_bytes=HELD_VMEM),
        cost_estimate=pl.CostEstimate(
            flops=0, bytes_accessed=16 * SLAB * rows * depth, transcendentals=0
        ),
        name="collect",
    )(*pieces)


def out_kernel(
    place, c20, c01, c31, c30, c11, c21, c10, c00, w, residual, scale, out, c_all, total, placed,
):
    z, q = place[0], place[1]
    width = c00.shape[0]
    for i, blocks in enumerate(((c00, c10, c20, c30), (c01, c11, c21, c31))):
        for r, c in enumerate(blocks):
            c_all[i, pl.ds(pl.multiple_of((q ^ r) * width, width), width), :] = c[...]
    column = as_column(scale[...])[:out.shape[0]]
    column = jnp.tile(column, (1, out.shape[1] // 128))
    total[...] = jnp.dot(w[0], c_all[0], preferred_element_type=jnp.float32)
    total[...] += jnp.dot(w[1], c_all[1], preferred_element_type=jnp.float32)
    rows, kept = w.shape[1] // (2 * SLAB), out.shape[0] // (2 * SLAB)
    for r in range(SLAB):
        for j in range(2):
            at = pl.multiple_of((((z % 2) ^ j) * SLAB + (q ^ r)) * kept, 8)
            begin = (2 * r + j) * rows
            placed[pl.ds(at, kept), :] = total[begin:begin + kept, :]
    out[...] = (residual[...].astype(jnp.float32) + column * placed[...]).astype(jnp.bfloat16)


def output(place, blocks, w, residual, scale):
    count = blocks[0].shape[1]
    rows, depth = w.shape[1:]
    share = residual.shape[0]
    return pl.pallas_call(
        out_kernel,
        out_shape=jax.ShapeDtypeStruct((share, count), jnp.bfloat16),
        in_specs=[SMEM] + [VMEM] * 11,
        out_specs=VMEM,
        scratch_shapes=[
            pltpu.VMEM((2, depth, count), jnp.bfloat16),
            pltpu.VMEM((rows, count), jnp.float32),
            pltpu.VMEM((share, count), jnp.float32),
        ],
        compiler_params=pltpu.CompilerParams(vmem_limit_bytes=HELD_VMEM),
        cost_estimate=pl.CostEstimate(
            flops=4 * share * count * depth,
            bytes_accessed=4 * share * depth,
            transcendentals=0,
        ),
        name="output",
    )(place, *blocks, w, residual, scale)


def rows_of_slab(q, got):
    placed = []
    for b in range(SLAB):
        piece = got[b]
        for other in range(1, SLAB):
            piece = jnp.where(q == other, got[b ^ other], piece)
        placed.append(piece)
    return jnp.concatenate(placed, axis=1)


def slab_plan(tokens, norm_gain, qkv_weight, q_gain, k_gain, out_weight, layer_scale, segment_ids):
    count = tokens.shape[0]
    seq, tp = lax.axis_index("seq"), lax.axis_index("tp")
    slabs = lax.axis_size("seq") // SLAB
    z, q = seq // SLAB, seq % SLAB
    place = jnp.stack([z, q, tp]).astype(jnp.int32)
    width = qkv_weight.shape[2] // SLAB
    full_width = qkv_weight.shape[2] * lax.axis_size("tp")
    slab, half = SLAB * count, 2 * count
    home = z // 2 == tp

    by_kind = jnp.transpose(qkv_weight, (1, 0, 2))
    cut = [lax.dynamic_slice_in_dim(by_kind, (q ^ r) * width, width, 2) for r in range(SLAB)]
    got = [cut[0]] + [in_slab(cut[r], r) for r in range(1, SLAB)]
    x0 = norm(tokens, norm_gain, slabs)
    out_own = jnp.transpose(out_weight)
    own = rows_of_slab(q, got)
    out_near, out_far = even_pair(out_own), half_pair(out_own)
    gains = [lax.dynamic_slice_in_dim(g, q * width, width, 0)[None] for g in (q_gain, k_gain)]

    outside = jnp.full((half,), -1, jnp.int32)
    seg = jnp.concatenate([outside, segment_ids, outside], axis=0)
    seg = lax.dynamic_slice_in_dim(seg, z * slab, slab + 2 * half, 0)
    spans = key_spans(seg, slab, count, half)
    seg = seg.astype(jnp.float32)[None]
    share = layer_scale.shape[0]
    residual = jnp.transpose(lax.dynamic_slice_in_dim(tokens, tp * share, share, 1))
    scale = jnp.pad(layer_scale, (0, -share % 128))[None]
    own, x0, out_near, out_far, seg, spans, residual, scale, *gains = tied(
        own, x0, out_near, out_far, seg, spans, residual, scale, *gains
    )
    out_last = even_pair(out_far)
    x2 = in_slab(x0, 2)
    far, x1 = half_pair(own), in_slab(x0, 1)
    out_last, own, x1 = tied(out_last, own, x1)
    near = even_pair(own)
    close, away = jnp.stack([out_own, out_near]), jnp.stack([out_far, out_last])
    pad = ((0, 0), (0, -close.shape[1] % 16), (0, 0))
    keep = jnp.pad(jnp.where(home, close, away), pad)
    got = across(jnp.pad(jnp.where(home, away, close), pad))
    keep_x = in_slab(keep, 2)
    near, far, x1, x2, got, keep_x = tied(near, far, x1, x2, got, keep_x)
    last = even_pair(far)
    x3 = in_slab(x2, 1)
    got_x, got_c, keep_c = in_slab(got, 2), in_slab(got, 1), in_slab(keep, 1)
    keep_xc = in_slab(tied(keep_x, x3)[0], 1)
    xs = (x0, x1, x2, x3)
    acc, x_last = early(place, xs, own, near, far)
    last, acc, x_last = tied(last, acc, x_last)
    query, keys, values, squares, even, odd = late(place, x_last, acc, last, *gains)
    even, odd = even_pair(even), odd_pair(odd)
    squares, got_x, got_c, keep_c, keep_xc = tied(squares, got_x, got_c, keep_c, keep_xc)
    sums = squares
    for r in range(1, SLAB):
        sums = sums + in_slab(squares, r)
    sums = sums + across(sums)
    sums = (sums, even_pair(sums), odd_pair(sums))
    got_xc = in_slab(got_x, 1)

    blocks = attend(full_width, place, spans, query, keys, values, even, odd, sums, seg)
    *blocks, got_xc = tied(*blocks, got_xc)
    pieces = (keep, keep_c, keep_x, keep_xc, got, got_c, got_x, got_xc)
    spread = []
    for r, i in ((2, 0), (0, 1), (3, 1), (3, 0), (1, 1), (2, 1), (1, 0), (0, 0)):
        to = functools.partial(lambda r, i, z, q, y: (z, q ^ r, y ^ i), r, i)
        spread.append(permuted(blocks[r], to) if r or i else blocks[r])

    return jnp.transpose(output(place, spread, collect(pieces), residual, scale))


def solution(mesh):
    def shards(*args):
        heads = args[2].shape[2] // HEAD_DIM
        slab = mesh.shape["seq"] == 16 and mesh.shape["tp"] == 2 and heads % SLAB == 0
        return (slab_plan if slab else row_plan)(*args)

    return jax.shard_map(
        shards,
        mesh=mesh,
        in_specs=(
            P("seq", None),
            P(),
            P("seq", None, "tp"),
            P("tp"),
            P("tp"),
            P("tp", "seq"),
            P("tp"),
            P(),
        ),
        out_specs=P("seq", "tp"),
        check_vma=False,
    )
```

```python
import functools
import math

import jax
import jax.numpy as jnp
from jax import lax
from jax.experimental import pallas as pl
from jax.experimental.pallas import tpu as pltpu
from jax.sharding import PartitionSpec as P

HEAD_DIM = 128
SLAB = 4

eps = 1e-06
floor_score = -1e30


def passed_along(x, axis, by):
    size = lax.axis_size(axis)
    pairs = [(i, i + by) for i in range(size) if 0 <= i + by < size]
    return lax.ppermute(x, axis, pairs)


def masked_scores(query, keys, query_seg, key_seg):
    scores = jnp.einsum(
        "qhd,khd->hqk", query, keys, preferred_element_type=jnp.float32
    ) * HEAD_DIM ** (-0.5)
    mask = (query_seg[:, None] == key_seg[None, :])[None]
    return (jnp.where(mask, scores, floor_score), mask)


def row_plan(tokens, norm_gain, qkv_weight, q_gain, k_gain, out_weight, layer_scale, segment_ids):
    count = tokens.shape[0]
    source = tokens.astype(jnp.float32)
    normed = (
        source * lax.rsqrt(jnp.mean(source * source, axis=-1, keepdims=True) + eps) * norm_gain
    ).astype(jnp.bfloat16)
    local_width = qkv_weight.shape[2]
    heads = local_width // HEAD_DIM
    joined = jnp.einsum(
        "td,dch->tch",
        normed,
        lax.all_gather(qkv_weight, "seq", axis=0, tiled=True),
        preferred_element_type=jnp.float32,
    )
    query = joined[:, 0]
    keys = joined[:, 1]
    values = joined[:, 2]
    query_sq, key_sq = lax.psum(
        (jnp.sum(query * query, axis=-1), jnp.sum(keys * keys, axis=-1)), "tp"
    )
    full_width = local_width * lax.axis_size("tp")
    query_normed = (query * lax.rsqrt(query_sq / full_width + eps)[:, None] * q_gain).astype(
        jnp.bfloat16
    )
    key_normed = (keys * lax.rsqrt(key_sq / full_width + eps)[:, None] * k_gain).astype(
        jnp.bfloat16
    )
    paired = jnp.stack([key_normed, values.astype(jnp.bfloat16)], axis=1)
    pieces = []
    for offset in (2, 1, 0, -1, -2):
        if offset == 0:
            pieces.append(paired)
        else:
            pieces.append(passed_along(paired, "seq", offset))
    widened = jnp.concatenate(pieces, axis=0)
    position = lax.axis_index("seq")
    outside = jnp.full((2 * count,), -1, jnp.int32)
    seg_pad = jnp.concatenate([outside, segment_ids, outside], axis=0)
    key_seg = lax.dynamic_slice_in_dim(seg_pad, position * count, 5 * count, 0)
    query_seg = lax.dynamic_slice_in_dim(segment_ids, position * count, count, 0)
    query_heads = query_normed.reshape(count, heads, HEAD_DIM)
    key_heads = widened[:, 0].reshape(5 * count, heads, HEAD_DIM)
    value_heads = widened[:, 1].reshape(5 * count, heads, HEAD_DIM)
    scores, mask = masked_scores(query_heads, key_heads, query_seg, key_seg)
    peak = jnp.max(scores, axis=-1, keepdims=True)
    weights = jnp.where(mask, jnp.exp(scores - peak), 0.0)
    total = jnp.sum(weights, axis=-1)
    probs = weights.astype(jnp.bfloat16)
    summed = jnp.einsum("hqk,khd->qhd", probs, value_heads, preferred_element_type=jnp.float32)
    context = (
        (summed / jnp.transpose(total)[:, :, None]).reshape(count, local_width).astype(jnp.bfloat16)
    )
    terms = jnp.dot(
        context,
        lax.all_gather(out_weight, "seq", axis=1, tiled=True),
        preferred_element_type=jnp.float32,
    )
    projected = lax.psum_scatter(terms, "tp", scatter_dimension=1, tiled=True)
    share = layer_scale.shape[0]
    residual = lax.dynamic_slice_in_dim(source, lax.axis_index("tp") * share, share, 1)
    return (residual + layer_scale * projected).astype(jnp.bfloat16)


ANY = pl.BlockSpec(memory_space=pl.ANY)
VMEM = pl.BlockSpec(memory_space=pltpu.VMEM)
SMEM = pl.BlockSpec(memory_space=pltpu.SMEM)
HBM = pl.BlockSpec(memory_space=pltpu.HBM)
KERNEL_VMEM = 60 * 1024 * 1024
HELD_VMEM = 24 * 1024 * 1024


def permuted(x, to):
    slabs, tps = lax.axis_size("seq") // SLAB, lax.axis_size("tp")
    pairs = []
    for i in range(slabs * SLAB * tps):
        z, q, y = to(i // (SLAB * tps), i // tps % SLAB, i % tps)
        pairs.append((i, (z * SLAB + q) * tps + y))
    return lax.ppermute(x, ("seq", "tp"), pairs)


def in_slab(x, flip):
    return permuted(x, lambda z, q, y: (z, q ^ flip, y))


def across(x):
    return permuted(x, lambda z, q, y: (z, q, 1 - y))


def even_pair(x):
    return permuted(x, lambda z, q, y: (z ^ 1, q, y))


def odd_pair(x):
    return permuted(x, lambda z, q, y: (3 - z, q, y) if z in (1, 2) else (z, q ^ 1, y))


def half_pair(x):
    return permuted(x, lambda z, q, y: (z ^ 2, q, y))


def tied(*arrays):
    return lax.optimization_barrier(arrays)


def as_row(column):
    wide = jnp.broadcast_to(column, (column.shape[0], 128))
    return jnp.transpose(wide)[:8]


def as_column(row):
    return jnp.transpose(jnp.broadcast_to(row, (128, row.shape[1])))


def start(copies):
    for copy in copies:
        copy.start()


def wait(copies):
    for copy in copies:
        copy.wait()


def norm_kernel(tokens, gain, out):
    part = tokens.shape[1] // out.shape[0]
    source = tokens[...].astype(jnp.float32)
    mean = jnp.mean(source * source, axis=1, keepdims=True)
    normed = source * lax.rsqrt(mean + eps) * gain[...]
    for j in range(out.shape[0]):
        out[j, :, :part] = normed[:, j * part:(j + 1) * part].astype(jnp.bfloat16)
        out[j, :, part:] = jnp.zeros((out.shape[1], out.shape[2] - part), jnp.bfloat16)


def norm(tokens, gain, slabs):
    count, depth = tokens.shape
    shape = (slabs, count, pl.cdiv(depth // slabs, 128) * 128)
    return pl.pallas_call(
        norm_kernel,
        out_shape=jax.ShapeDtypeStruct(shape, jnp.bfloat16),
        in_specs=[VMEM, VMEM],
        out_specs=VMEM,
        compiler_params=pltpu.CompilerParams(vmem_limit_bytes=KERNEL_VMEM),
        name="norm",
    )(tokens, gain[None])


def token_copies(xs, at, out, sems):
    return [
        pltpu.make_async_copy(x.at[at], out.at[r], sems.at[r]) for r, x in enumerate(xs)
    ]


def blank_tail(w, rows):
    tail = w.shape[-2] - rows
    w[..., rows:, :] = jnp.zeros(w.shape[:-2] + (tail, w.shape[-1]), w.dtype)


def early_kernel(
    place, xa, xb, xc, xd, own, near, far, acc, x_last, x_all, w_all, x_sem, w_sem, last_sem,
):
    z = place[0]
    kinds, rows = own.shape[:2]
    copies = []
    for i, w in enumerate((own, near, far)):
        dst = w_all.at[i, :, pl.ds(0, rows), :]
        copies.append([pltpu.make_async_copy(w, dst, w_sem.at[i])])
        copies[i] += token_copies((xa, xb, xc, xd), z ^ i, x_all.at[i], x_sem.at[i])
        start(copies[i])
    last_copies = token_copies((xa, xb, xc, xd), z ^ 3, x_last, last_sem)
    start(last_copies)
    blank_tail(w_all, rows)
    for step in range(3):
        wait(copies[step])
        for r in range(SLAB):
            x = x_all[step, r]
            for kind in range(kinds):
                term = jnp.dot(x, w_all[step, kind], preferred_element_type=jnp.float32)
                acc[r, kind] = term if step == 0 else acc[r, kind] + term
    wait(last_copies)


def early(place, xs, own, near, far):
    kinds, rows, width = own.shape
    slabs, count, wide = xs[0].shape
    return pl.pallas_call(
        early_kernel,
        out_shape=(
            jax.ShapeDtypeStruct((SLAB, kinds, count, width), jnp.float32),
            jax.ShapeDtypeStruct((SLAB, count, wide), jnp.bfloat16),
        ),
        in_specs=[SMEM] + [HBM] * 7,
        out_specs=(VMEM, VMEM),
        scratch_shapes=[
            pltpu.VMEM((3, SLAB, count, wide), jnp.bfloat16),
            pltpu.VMEM((3, kinds, wide, width), jnp.bfloat16),
            pltpu.SemaphoreType.DMA((3, SLAB)),
            pltpu.SemaphoreType.DMA((3,)),
            pltpu.SemaphoreType.DMA((SLAB,)),
        ],
        compiler_params=pltpu.CompilerParams(vmem_limit_bytes=HELD_VMEM),
        cost_estimate=pl.CostEstimate(
            flops=12 * kinds * SLAB * count * rows * width,
            bytes_accessed=6 * kinds * rows * width + 6 * SLAB * count * rows,
            transcendentals=0,
        ),
        name="early",
    )(place, *xs, own, near, far)


def late_kernel(
    place, x_last, acc, last, q_gain, k_gain, query, keys, values, squares, even, odd, w_all,
):
    z, q = place[0], place[1]
    rows = last.shape[1]
    w_all[:, :rows, :] = last[...]
    blank_tail(w_all, rows)
    count = acc.shape[2]
    for r in range(SLAB):
        rows = pl.ds(pl.multiple_of((q ^ r) * count, count), count)
        for kind in range(3):
            part = acc[r, kind] + jnp.dot(
                x_last[r], w_all[kind], preferred_element_type=jnp.float32
            )
            if kind < 2:
                summed = as_row(jnp.sum(part * part, axis=1, keepdims=True))
                squares[kind:kind + 1, rows] = summed[:1]
                part = part * (q_gain, k_gain)[kind][...]
            out = (query, keys, values)[kind]
            out[rows, :] = part.astype(out.dtype)
    reach = even.shape[1]
    for out, at in ((even, 1 - z % 2), (odd, z % 2)):
        rows = pl.ds(pl.multiple_of(at * reach, reach), reach)
        out[0] = keys[rows, :]
        out[1] = values[rows, :]


def late(place, x_last, acc, last, q_gain, k_gain):
    kinds, rows, width = last.shape
    count, wide = x_last.shape[1:]
    slab = SLAB * count
    f32, bf16 = jnp.float32, jnp.bfloat16
    return pl.pallas_call(
        late_kernel,
        out_shape=(
            jax.ShapeDtypeStruct((slab, width), f32),
            jax.ShapeDtypeStruct((slab, width), bf16),
            jax.ShapeDtypeStruct((slab, width), bf16),
            jax.ShapeDtypeStruct((2, slab), f32),
            jax.ShapeDtypeStruct((2, 2 * count, width), bf16),
            jax.ShapeDtypeStruct((2, 2 * count, width), bf16),
        ),
        in_specs=[SMEM] + [VMEM] * 5,
        out_specs=(VMEM,) * 6,
        scratch_shapes=[
            pltpu.VMEM((kinds, wide, width), bf16),
        ],
        compiler_params=pltpu.CompilerParams(vmem_limit_bytes=HELD_VMEM),
        cost_estimate=pl.CostEstimate(
            flops=2 * kinds * slab * rows * width,
            bytes_accessed=2 * kinds * rows * width + 2 * slab * rows,
            transcendentals=0,
        ),
        name="late",
    )(place, x_last, acc, last, q_gain, k_gain)


def attend_kernel(
    full_width, place, spans, query, keys, values, even, odd, mine, near, mid, seg, o0, o1, o2, o3,
    k_all, v_all, o_all, scale_all,
):
    z, q = place[0], place[1]
    slab = query.shape[0]
    count = slab // SLAB
    half = even.shape[1]
    upper = half + slab
    is_even = z % 2 == 0
    even_at = pl.multiple_of(jnp.where(is_even, upper, 0), half)
    odd_at = pl.multiple_of(jnp.where(is_even, 0, upper), half)
    for k, (whole, out) in enumerate(((keys, k_all), (values, v_all))):
        out[half:upper, :] = whole[...]
        out[pl.ds(even_at, half), :] = even[k]
        out[pl.ds(odd_at, half), :] = odd[k]
    scale = [lax.rsqrt(sums[...] / full_width + eps) for sums in (mine, near, mid)]
    scale_all[:, half:upper] = scale[0]
    scale_all[:, :half] = jnp.where(is_even, scale[2], scale[1])[:, slab - half:]
    scale_all[:, upper:] = jnp.where(is_even, scale[1], scale[2])[:, :half]
    heads = query.shape[1] // HEAD_DIM
    factor = HEAD_DIM ** (-0.5) * math.log2(math.e)

    def block(r, _):
        b = q ^ r
        at_query = pl.multiple_of(b * count + half, count)
        query_seg = as_column(seg[:, pl.ds(at_query, count)])
        q_scale = as_column(scale_all[0:1, pl.ds(at_query, count)])
        for tiles in range(2, 2 * half // count + 2):
            @pl.when(spans[b, 1] == tiles)
            def _():
                width = tiles * count
                begin = pl.multiple_of(spans[b, 0], 128)
                keys_at = pl.ds(begin, width)
                mask = jnp.tile(query_seg, (1, width // 128)) == seg[:, keys_at]
                k_scale = scale_all[1:2, keys_at] * factor
                for h in range(heads):
                    cols = slice(h * HEAD_DIM, (h + 1) * HEAD_DIM)
                    q_low = query[pl.ds(pl.multiple_of(b * count, count), count), cols] * q_scale
                    scores = lax.dot_general(
                        q_low.astype(jnp.bfloat16), k_all[keys_at, cols],
                        (((1,), (1,)), ((), ())), preferred_element_type=jnp.float32,
                    )
                    scores = jnp.where(mask, scores * k_scale, floor_score)
                    peak = jnp.max(scores, axis=1, keepdims=True)
                    weights = jnp.exp2(scores - peak)
                    total = jnp.sum(weights, axis=1, keepdims=True)
                    summed = jnp.dot(
                        weights.astype(jnp.bfloat16), v_all[keys_at, cols],
                        preferred_element_type=jnp.float32,
                    )
                    o_all[r, cols, :] = jnp.transpose(summed / total).astype(jnp.bfloat16)

        return 0

    lax.fori_loop(0, SLAB, block, 0)
    for r, out in enumerate((o0, o1, o2, o3)):
        out[...] = o_all[r]


def key_spans(seg, slab, count, half):
    ext = seg.shape[0]
    index = jnp.arange(ext, dtype=jnp.int32)
    blocks = seg[half:half + slab].reshape(-1, count)
    first, last = blocks[:, :1], blocks[:, -1:]
    begin = jnp.min(jnp.where(seg == first, index, ext), axis=1) // 128 * 128
    end = jnp.max(jnp.where(seg == last, index, -1), axis=1) + 1
    tiles = jnp.maximum((end - begin + count - 1) // count, 2)
    return jnp.stack([jnp.minimum(begin, ext - tiles * count), tiles], axis=1)


def attend(full_width, place, spans, query, keys, values, even, odd, sums, seg):
    slab, width = query.shape
    half = even.shape[1]
    count = slab // SLAB
    ext = slab + 2 * half
    bf16 = jnp.bfloat16
    window = count + 2 * half
    return pl.pallas_call(
        functools.partial(attend_kernel, full_width),
        out_shape=(jax.ShapeDtypeStruct((width, count), bf16),) * SLAB,
        in_specs=[SMEM] * 2 + [VMEM] * 9,
        out_specs=(VMEM,) * SLAB,
        scratch_shapes=[
            pltpu.VMEM((ext, width), bf16),
            pltpu.VMEM((ext, width), bf16),
            pltpu.VMEM((SLAB, width, count), bf16),
            pltpu.VMEM((2, ext), jnp.float32),
        ],
        compiler_params=pltpu.CompilerParams(vmem_limit_bytes=HELD_VMEM),
        cost_estimate=pl.CostEstimate(
            flops=64 * SLAB * count * window * width,
            bytes_accessed=4 * ext * width + 4 * slab * width,
            transcendentals=SLAB * count * window * width // HEAD_DIM,
        ),
        name="attend",
    )(place, spans, query, keys, values, even, odd, *sums, seg)


def collect_kernel(wa0, wb0, wc0, wd0, wa1, wb1, wc1, wd1, out, sems):
    rows = wa0.shape[1]
    copies = []
    for i, ws in enumerate(((wa0, wb0, wc0, wd0), (wa1, wb1, wc1, wd1))):
        for r, w in enumerate(ws):
            for j in range(2):
                dst = out.at[i, pl.ds((2 * r + j) * rows, rows), :]
                copies.append(pltpu.make_async_copy(w.at[j], dst, sems.at[i, r, j]))
    start(copies)
    wait(copies)


def collect(pieces):
    rows, depth = pieces[0].shape[1:]
    return pl.pallas_call(
        collect_kernel,
        out_shape=jax.ShapeDtypeStruct((2, 2 * SLAB * rows, depth), jnp.bfloat16),
        in_specs=[HBM] * 8,
        out_specs=VMEM,
        scratch_shapes=[pltpu.SemaphoreType.DMA((2, SLAB, 2))],
        compiler_params=pltpu.CompilerParams(vmem_limit_bytes=HELD_VMEM),
        cost_estimate=pl.CostEstimate(
            flops=0, bytes_accessed=16 * SLAB * rows * depth, transcendentals=0
        ),
        name="collect",
    )(*pieces)


def out_kernel(
    place, c20, c01, c31, c30, c11, c21, c10, c00, w, residual, scale, out, c_all, total, placed,
):
    z, q = place[0], place[1]
    width = c00.shape[0]
    for i, blocks in enumerate(((c00, c10, c20, c30), (c01, c11, c21, c31))):
        for r, c in enumerate(blocks):
            c_all[i, pl.ds(pl.multiple_of((q ^ r) * width, width), width), :] = c[...]
    column = as_column(scale[...])[:out.shape[0]]
    column = jnp.tile(column, (1, out.shape[1] // 128))
    total[...] = jnp.dot(w[0], c_all[0], preferred_element_type=jnp.float32)
    total[...] += jnp.dot(w[1], c_all[1], preferred_element_type=jnp.float32)
    rows, kept = w.shape[1] // (2 * SLAB), out.shape[0] // (2 * SLAB)
    for r in range(SLAB):
        for j in range(2):
            at = pl.multiple_of((((z % 2) ^ j) * SLAB + (q ^ r)) * kept, 8)
            begin = (2 * r + j) * rows
            placed[pl.ds(at, kept), :] = total[begin:begin + kept, :]
    out[...] = (residual[...].astype(jnp.float32) + column * placed[...]).astype(jnp.bfloat16)


def output(place, blocks, w, residual, scale):
    count = blocks[0].shape[1]
    rows, depth = w.shape[1:]
    share = residual.shape[0]
    return pl.pallas_call(
        out_kernel,
        out_shape=jax.ShapeDtypeStruct((share, count), jnp.bfloat16),
        in_specs=[SMEM] + [VMEM] * 11,
        out_specs=VMEM,
        scratch_shapes=[
            pltpu.VMEM((2, depth, count), jnp.bfloat16),
            pltpu.VMEM((rows, count), jnp.float32),
            pltpu.VMEM((share, count), jnp.float32),
        ],
        compiler_params=pltpu.CompilerParams(vmem_limit_bytes=HELD_VMEM),
        cost_estimate=pl.CostEstimate(
            flops=4 * share * count * depth,
            bytes_accessed=4 * share * depth,
            transcendentals=0,
        ),
        name="output",
    )(place, *blocks, w, residual, scale)


def rows_of_slab(q, got):
    placed = []
    for b in range(SLAB):
        piece = got[b]
        for other in range(1, SLAB):
            piece = jnp.where(q == other, got[b ^ other], piece)
        placed.append(piece)
    return jnp.concatenate(placed, axis=1)


def slab_plan(tokens, norm_gain, qkv_weight, q_gain, k_gain, out_weight, layer_scale, segment_ids):
    count = tokens.shape[0]
    seq, tp = lax.axis_index("seq"), lax.axis_index("tp")
    slabs = lax.axis_size("seq") // SLAB
    z, q = seq // SLAB, seq % SLAB
    place = jnp.stack([z, q, tp]).astype(jnp.int32)
    width = qkv_weight.shape[2] // SLAB
    full_width = qkv_weight.shape[2] * lax.axis_size("tp")
    slab, half = SLAB * count, 2 * count
    home = z // 2 == tp

    by_kind = jnp.transpose(qkv_weight, (1, 0, 2))
    cut = [lax.dynamic_slice_in_dim(by_kind, (q ^ r) * width, width, 2) for r in range(SLAB)]
    got = [cut[0]] + [in_slab(cut[r], r) for r in range(1, SLAB)]
    x0 = norm(tokens, norm_gain, slabs)
    out_own = jnp.transpose(out_weight)
    own = rows_of_slab(q, got)
    out_near, out_far = even_pair(out_own), half_pair(out_own)
    gains = [lax.dynamic_slice_in_dim(g, q * width, width, 0)[None] for g in (q_gain, k_gain)]

    outside = jnp.full((half,), -1, jnp.int32)
    seg = jnp.concatenate([outside, segment_ids, outside], axis=0)
    seg = lax.dynamic_slice_in_dim(seg, z * slab, slab + 2 * half, 0)
    spans = key_spans(seg, slab, count, half)
    seg = seg.astype(jnp.float32)[None]
    share = layer_scale.shape[0]
    residual = jnp.transpose(lax.dynamic_slice_in_dim(tokens, tp * share, share, 1))
    scale = jnp.pad(layer_scale, (0, -share % 128))[None]
    own, x0, out_near, out_far, seg, spans, residual, scale, *gains = tied(
        own, x0, out_near, out_far, seg, spans, residual, scale, *gains
    )
    out_last = even_pair(out_far)
    x2 = in_slab(x0, 2)
    far, near = half_pair(own), even_pair(own)
    close, away = jnp.stack([out_own, out_near]), jnp.stack([out_far, out_last])
    pad = ((0, 0), (0, -close.shape[1] % 16), (0, 0))
    keep = jnp.pad(jnp.where(home, close, away), pad)
    got = across(jnp.pad(jnp.where(home, away, close), pad))
    keep_x = in_slab(keep, 2)
    near, far, x0, x2, got, keep_x = tied(near, far, x0, x2, got, keep_x)
    last = even_pair(far)
    x1, x3 = in_slab(x0, 1), in_slab(x2, 1)
    got_x, got_c, keep_c = in_slab(got, 2), in_slab(got, 1), in_slab(keep, 1)
    keep_xc = in_slab(tied(keep_x, x3)[0], 1)
    xs = (x0, x1, x2, x3)
    acc, x_last = early(place, xs, own, near, far)
    last, acc, x_last = tied(last, acc, x_last)
    query, keys, values, squares, even, odd = late(place, x_last, acc, last, *gains)
    even, odd = even_pair(even), odd_pair(odd)
    squares, got_x, got_c, keep_c, keep_xc = tied(squares, got_x, got_c, keep_c, keep_xc)
    sums = squares
    for r in range(1, SLAB):
        sums = sums + in_slab(squares, r)
    sums = sums + across(sums)
    sums = (sums, even_pair(sums), odd_pair(sums))
    got_xc = in_slab(got_x, 1)

    blocks = attend(full_width, place, spans, query, keys, values, even, odd, sums, seg)
    *blocks, got_xc = tied(*blocks, got_xc)
    pieces = (keep, keep_c, keep_x, keep_xc, got, got_c, got_x, got_xc)
    spread = []
    for r, i in ((2, 0), (0, 1), (3, 1), (3, 0), (1, 1), (2, 1), (1, 0), (0, 0)):
        to = functools.partial(lambda r, i, z, q, y: (z, q ^ r, y ^ i), r, i)
        spread.append(permuted(blocks[r], to) if r or i else blocks[r])

    return jnp.transpose(output(place, spread, collect(pieces), residual, scale))


def solution(mesh):
    def shards(*args):
        heads = args[2].shape[2] // HEAD_DIM
        slab = mesh.shape["seq"] == 16 and mesh.shape["tp"] == 2 and heads % SLAB == 0
        return (slab_plan if slab else row_plan)(*args)

    return jax.shard_map(
        shards,
        mesh=mesh,
        in_specs=(
            P("seq", None),
            P(),
            P("seq", None, "tp"),
            P("tp"),
            P("tp"),
            P("tp", "seq"),
            P("tp"),
            P(),
        ),
        out_specs=P("seq", "tp"),
        check_vma=False,
    )
```

```python
import functools
import math

import jax
import jax.numpy as jnp
from jax import lax
from jax.experimental import pallas as pl
from jax.experimental.pallas import tpu as pltpu
from jax.sharding import PartitionSpec as P

HEAD_DIM = 128
SLAB = 4

eps = 1e-06
floor_score = -1e30


def passed_along(x, axis, by):
    size = lax.axis_size(axis)
    pairs = [(i, i + by) for i in range(size) if 0 <= i + by < size]
    return lax.ppermute(x, axis, pairs)


def masked_scores(query, keys, query_seg, key_seg):
    scores = jnp.einsum(
        "qhd,khd->hqk", query, keys, preferred_element_type=jnp.float32
    ) * HEAD_DIM ** (-0.5)
    mask = (query_seg[:, None] == key_seg[None, :])[None]
    return (jnp.where(mask, scores, floor_score), mask)


def row_plan(tokens, norm_gain, qkv_weight, q_gain, k_gain, out_weight, layer_scale, segment_ids):
    count = tokens.shape[0]
    source = tokens.astype(jnp.float32)
    normed = (
        source * lax.rsqrt(jnp.mean(source * source, axis=-1, keepdims=True) + eps) * norm_gain
    ).astype(jnp.bfloat16)
    local_width = qkv_weight.shape[2]
    heads = local_width // HEAD_DIM
    joined = jnp.einsum(
        "td,dch->tch",
        normed,
        lax.all_gather(qkv_weight, "seq", axis=0, tiled=True),
        preferred_element_type=jnp.float32,
    )
    query = joined[:, 0]
    keys = joined[:, 1]
    values = joined[:, 2]
    query_sq, key_sq = lax.psum(
        (jnp.sum(query * query, axis=-1), jnp.sum(keys * keys, axis=-1)), "tp"
    )
    full_width = local_width * lax.axis_size("tp")
    query_normed = (query * lax.rsqrt(query_sq / full_width + eps)[:, None] * q_gain).astype(
        jnp.bfloat16
    )
    key_normed = (keys * lax.rsqrt(key_sq / full_width + eps)[:, None] * k_gain).astype(
        jnp.bfloat16
    )
    paired = jnp.stack([key_normed, values.astype(jnp.bfloat16)], axis=1)
    pieces = []
    for offset in (2, 1, 0, -1, -2):
        if offset == 0:
            pieces.append(paired)
        else:
            pieces.append(passed_along(paired, "seq", offset))
    widened = jnp.concatenate(pieces, axis=0)
    position = lax.axis_index("seq")
    outside = jnp.full((2 * count,), -1, jnp.int32)
    seg_pad = jnp.concatenate([outside, segment_ids, outside], axis=0)
    key_seg = lax.dynamic_slice_in_dim(seg_pad, position * count, 5 * count, 0)
    query_seg = lax.dynamic_slice_in_dim(segment_ids, position * count, count, 0)
    query_heads = query_normed.reshape(count, heads, HEAD_DIM)
    key_heads = widened[:, 0].reshape(5 * count, heads, HEAD_DIM)
    value_heads = widened[:, 1].reshape(5 * count, heads, HEAD_DIM)
    scores, mask = masked_scores(query_heads, key_heads, query_seg, key_seg)
    peak = jnp.max(scores, axis=-1, keepdims=True)
    weights = jnp.where(mask, jnp.exp(scores - peak), 0.0)
    total = jnp.sum(weights, axis=-1)
    probs = weights.astype(jnp.bfloat16)
    summed = jnp.einsum("hqk,khd->qhd", probs, value_heads, preferred_element_type=jnp.float32)
    context = (
        (summed / jnp.transpose(total)[:, :, None]).reshape(count, local_width).astype(jnp.bfloat16)
    )
    terms = jnp.dot(
        context,
        lax.all_gather(out_weight, "seq", axis=1, tiled=True),
        preferred_element_type=jnp.float32,
    )
    projected = lax.psum_scatter(terms, "tp", scatter_dimension=1, tiled=True)
    share = layer_scale.shape[0]
    residual = lax.dynamic_slice_in_dim(source, lax.axis_index("tp") * share, share, 1)
    return (residual + layer_scale * projected).astype(jnp.bfloat16)


ANY = pl.BlockSpec(memory_space=pl.ANY)
VMEM = pl.BlockSpec(memory_space=pltpu.VMEM)
SMEM = pl.BlockSpec(memory_space=pltpu.SMEM)
HBM = pl.BlockSpec(memory_space=pltpu.HBM)
KERNEL_VMEM = 60 * 1024 * 1024
HELD_VMEM = 24 * 1024 * 1024


def permuted(x, to):
    slabs, tps = lax.axis_size("seq") // SLAB, lax.axis_size("tp")
    pairs = []
    for i in range(slabs * SLAB * tps):
        z, q, y = to(i // (SLAB * tps), i // tps % SLAB, i % tps)
        pairs.append((i, (z * SLAB + q) * tps + y))
    return lax.ppermute(x, ("seq", "tp"), pairs)


def in_slab(x, flip):
    return permuted(x, lambda z, q, y: (z, q ^ flip, y))


def across(x):
    return permuted(x, lambda z, q, y: (z, q, 1 - y))


def even_pair(x):
    return permuted(x, lambda z, q, y: (z ^ 1, q, y))


def odd_pair(x):
    return permuted(x, lambda z, q, y: (3 - z, q, y) if z in (1, 2) else (z, q ^ 1, y))


def half_pair(x):
    return permuted(x, lambda z, q, y: (z ^ 2, q, y))


def tied(*arrays):
    return lax.optimization_barrier(arrays)


def as_row(column):
    wide = jnp.broadcast_to(column, (column.shape[0], 128))
    return jnp.transpose(wide)[:8]


def as_column(row):
    return jnp.transpose(jnp.broadcast_to(row, (128, row.shape[1])))


def start(copies):
    for copy in copies:
        copy.start()


def wait(copies):
    for copy in copies:
        copy.wait()


def norm_kernel(tokens, gain, out):
    part = tokens.shape[1] // out.shape[0]
    source = tokens[...].astype(jnp.float32)
    mean = jnp.mean(source * source, axis=1, keepdims=True)
    normed = source * lax.rsqrt(mean + eps) * gain[...]
    for j in range(out.shape[0]):
        out[j, :, :part] = normed[:, j * part:(j + 1) * part].astype(jnp.bfloat16)
        out[j, :, part:] = jnp.zeros((out.shape[1], out.shape[2] - part), jnp.bfloat16)


def norm(tokens, gain, slabs):
    count, depth = tokens.shape
    shape = (slabs, count, pl.cdiv(depth // slabs, 128) * 128)
    return pl.pallas_call(
        norm_kernel,
        out_shape=jax.ShapeDtypeStruct(shape, jnp.bfloat16),
        in_specs=[VMEM, VMEM],
        out_specs=VMEM,
        compiler_params=pltpu.CompilerParams(vmem_limit_bytes=KERNEL_VMEM),
        name="norm",
    )(tokens, gain[None])


def token_copies(xs, at, out, sems):
    return [
        pltpu.make_async_copy(x.at[at], out.at[r], sems.at[r]) for r, x in enumerate(xs)
    ]


def blank_tail(w, rows):
    tail = w.shape[-2] - rows
    w[..., rows:, :] = jnp.zeros(w.shape[:-2] + (tail, w.shape[-1]), w.dtype)


def early_kernel(
    place, xa, xb, xc, xd, own, near, far, acc, x_last, x_all, w_all, x_sem, w_sem, last_sem,
):
    z = place[0]
    kinds, rows = own.shape[:2]
    copies = []
    for i, w in enumerate((own, near, far)):
        dst = w_all.at[i, :, pl.ds(0, rows), :]
        copies.append([pltpu.make_async_copy(w, dst, w_sem.at[i])])
        copies[i] += token_copies((xa, xb, xc, xd), z ^ i, x_all.at[i], x_sem.at[i])
        start(copies[i])
    last_copies = token_copies((xa, xb, xc, xd), z ^ 3, x_last, last_sem)
    start(last_copies)
    blank_tail(w_all, rows)
    for step in range(3):
        wait(copies[step])
        for r in range(SLAB):
            x = x_all[step, r]
            for kind in range(kinds):
                term = jnp.dot(x, w_all[step, kind], preferred_element_type=jnp.float32)
                acc[r, kind] = term if step == 0 else acc[r, kind] + term
    wait(last_copies)


def early(place, xs, own, near, far):
    kinds, rows, width = own.shape
    slabs, count, wide = xs[0].shape
    return pl.pallas_call(
        early_kernel,
        out_shape=(
            jax.ShapeDtypeStruct((SLAB, kinds, count, width), jnp.float32),
            jax.ShapeDtypeStruct((SLAB, count, wide), jnp.bfloat16),
        ),
        in_specs=[SMEM] + [HBM] * 7,
        out_specs=(VMEM, VMEM),
        scratch_shapes=[
            pltpu.VMEM((3, SLAB, count, wide), jnp.bfloat16),
            pltpu.VMEM((3, kinds, wide, width), jnp.bfloat16),
            pltpu.SemaphoreType.DMA((3, SLAB)),
            pltpu.SemaphoreType.DMA((3,)),
            pltpu.SemaphoreType.DMA((SLAB,)),
        ],
        compiler_params=pltpu.CompilerParams(vmem_limit_bytes=HELD_VMEM),
        cost_estimate=pl.CostEstimate(
            flops=12 * kinds * SLAB * count * rows * width,
            bytes_accessed=6 * kinds * rows * width + 6 * SLAB * count * rows,
            transcendentals=0,
        ),
        name="early",
    )(place, *xs, own, near, far)


def late_kernel(
    place, x_last, acc, last, q_gain, k_gain, query, keys, values, squares, even, odd, w_all,
):
    z, q = place[0], place[1]
    rows = last.shape[1]
    w_all[:, :rows, :] = last[...]
    blank_tail(w_all, rows)
    count = acc.shape[2]
    for r in range(SLAB):
        rows = pl.ds(pl.multiple_of((q ^ r) * count, count), count)
        for kind in range(3):
            part = acc[r, kind] + jnp.dot(
                x_last[r], w_all[kind], preferred_element_type=jnp.float32
            )
            if kind < 2:
                summed = as_row(jnp.sum(part * part, axis=1, keepdims=True))
                squares[kind:kind + 1, rows] = summed[:1]
                part = part * (q_gain, k_gain)[kind][...]
            out = (query, keys, values)[kind]
            out[rows, :] = part.astype(out.dtype)
    reach = even.shape[1]
    for out, at in ((even, 1 - z % 2), (odd, z % 2)):
        rows = pl.ds(pl.multiple_of(at * reach, reach), reach)
        out[0] = keys[rows, :]
        out[1] = values[rows, :]


def late(place, x_last, acc, last, q_gain, k_gain):
    kinds, rows, width = last.shape
    count, wide = x_last.shape[1:]
    slab = SLAB * count
    f32, bf16 = jnp.float32, jnp.bfloat16
    return pl.pallas_call(
        late_kernel,
        out_shape=(
            jax.ShapeDtypeStruct((slab, width), f32),
            jax.ShapeDtypeStruct((slab, width), bf16),
            jax.ShapeDtypeStruct((slab, width), bf16),
            jax.ShapeDtypeStruct((2, slab), f32),
            jax.ShapeDtypeStruct((2, 2 * count, width), bf16),
            jax.ShapeDtypeStruct((2, 2 * count, width), bf16),
        ),
        in_specs=[SMEM] + [VMEM] * 5,
        out_specs=(VMEM,) * 6,
        scratch_shapes=[
            pltpu.VMEM((kinds, wide, width), bf16),
        ],
        compiler_params=pltpu.CompilerParams(vmem_limit_bytes=HELD_VMEM),
        cost_estimate=pl.CostEstimate(
            flops=2 * kinds * slab * rows * width,
            bytes_accessed=2 * kinds * rows * width + 2 * slab * rows,
            transcendentals=0,
        ),
        name="late",
    )(place, x_last, acc, last, q_gain, k_gain)


def attend_kernel(
    full_width, place, spans, query, keys, values, even, odd, mine, near, mid, seg, o0, o1, o2, o3,
    k_all, v_all, o_all, scale_all,
):
    z, q = place[0], place[1]
    slab = query.shape[0]
    count = slab // SLAB
    half = even.shape[1]
    upper = half + slab
    is_even = z % 2 == 0
    even_at = pl.multiple_of(jnp.where(is_even, upper, 0), half)
    odd_at = pl.multiple_of(jnp.where(is_even, 0, upper), half)
    for k, (whole, out) in enumerate(((keys, k_all), (values, v_all))):
        out[half:upper, :] = whole[...]
        out[pl.ds(even_at, half), :] = even[k]
        out[pl.ds(odd_at, half), :] = odd[k]
    scale = [lax.rsqrt(sums[...] / full_width + eps) for sums in (mine, near, mid)]
    scale_all[:, half:upper] = scale[0]
    scale_all[:, :half] = jnp.where(is_even, scale[2], scale[1])[:, slab - half:]
    scale_all[:, upper:] = jnp.where(is_even, scale[1], scale[2])[:, :half]
    heads = query.shape[1] // HEAD_DIM
    factor = HEAD_DIM ** (-0.5) * math.log2(math.e)

    def block(r, _):
        b = q ^ r
        at_query = pl.multiple_of(b * count + half, count)
        query_seg = as_column(seg[:, pl.ds(at_query, count)])
        q_scale = as_column(scale_all[0:1, pl.ds(at_query, count)])
        for tiles in range(2, 2 * half // count + 2):
            @pl.when(spans[b, 1] == tiles)
            def _():
                width = tiles * count
                begin = pl.multiple_of(spans[b, 0], 128)
                keys_at = pl.ds(begin, width)
                mask = jnp.tile(query_seg, (1, width // 128)) == seg[:, keys_at]
                k_scale = scale_all[1:2, keys_at] * factor
                for h in range(heads):
                    cols = slice(h * HEAD_DIM, (h + 1) * HEAD_DIM)
                    q_low = query[pl.ds(pl.multiple_of(b * count, count), count), cols] * q_scale
                    scores = lax.dot_general(
                        q_low.astype(jnp.bfloat16), k_all[keys_at, cols],
                        (((1,), (1,)), ((), ())), preferred_element_type=jnp.float32,
                    )
                    scores = jnp.where(mask, scores * k_scale, floor_score)
                    peak = jnp.max(scores, axis=1, keepdims=True)
                    weights = jnp.exp2(scores - peak)
                    total = jnp.sum(weights, axis=1, keepdims=True)
                    summed = jnp.dot(
                        weights.astype(jnp.bfloat16), v_all[keys_at, cols],
                        preferred_element_type=jnp.float32,
                    )
                    o_all[r, cols, :] = jnp.transpose(summed / total).astype(jnp.bfloat16)

        return 0

    lax.fori_loop(0, SLAB, block, 0)
    for r, out in enumerate((o0, o1, o2, o3)):
        out[...] = o_all[r]


def key_spans(seg, slab, count, half):
    ext = seg.shape[0]
    index = jnp.arange(ext, dtype=jnp.int32)
    blocks = seg[half:half + slab].reshape(-1, count)
    first, last = blocks[:, :1], blocks[:, -1:]
    begin = jnp.min(jnp.where(seg == first, index, ext), axis=1) // 128 * 128
    end = jnp.max(jnp.where(seg == last, index, -1), axis=1) + 1
    tiles = jnp.maximum((end - begin + count - 1) // count, 2)
    return jnp.stack([jnp.minimum(begin, ext - tiles * count), tiles], axis=1)


def attend(full_width, place, spans, query, keys, values, even, odd, sums, seg):
    slab, width = query.shape
    half = even.shape[1]
    count = slab // SLAB
    ext = slab + 2 * half
    bf16 = jnp.bfloat16
    window = count + 2 * half
    return pl.pallas_call(
        functools.partial(attend_kernel, full_width),
        out_shape=(jax.ShapeDtypeStruct((width, count), bf16),) * SLAB,
        in_specs=[SMEM] * 2 + [VMEM] * 9,
        out_specs=(VMEM,) * SLAB,
        scratch_shapes=[
            pltpu.VMEM((ext, width), bf16),
            pltpu.VMEM((ext, width), bf16),
            pltpu.VMEM((SLAB, width, count), bf16),
            pltpu.VMEM((2, ext), jnp.float32),
        ],
        compiler_params=pltpu.CompilerParams(vmem_limit_bytes=HELD_VMEM),
        cost_estimate=pl.CostEstimate(
            flops=64 * SLAB * count * window * width,
            bytes_accessed=4 * ext * width + 4 * slab * width,
            transcendentals=SLAB * count * window * width // HEAD_DIM,
        ),
        name="attend",
    )(place, spans, query, keys, values, even, odd, *sums, seg)


def collect_kernel(wa0, wb0, wc0, wd0, wa1, wb1, wc1, wd1, out, sems):
    rows = wa0.shape[1]
    copies = []
    for i, ws in enumerate(((wa0, wb0, wc0, wd0), (wa1, wb1, wc1, wd1))):
        for r, w in enumerate(ws):
            for j in range(2):
                dst = out.at[i, pl.ds((2 * r + j) * rows, rows), :]
                copies.append(pltpu.make_async_copy(w.at[j], dst, sems.at[i, r, j]))
    start(copies)
    wait(copies)


def collect(pieces):
    rows, depth = pieces[0].shape[1:]
    return pl.pallas_call(
        collect_kernel,
        out_shape=jax.ShapeDtypeStruct((2, 2 * SLAB * rows, depth), jnp.bfloat16),
        in_specs=[HBM] * 8,
        out_specs=VMEM,
        scratch_shapes=[pltpu.SemaphoreType.DMA((2, SLAB, 2))],
        compiler_params=pltpu.CompilerParams(vmem_limit_bytes=HELD_VMEM),
        cost_estimate=pl.CostEstimate(
            flops=0, bytes_accessed=16 * SLAB * rows * depth, transcendentals=0
        ),
        name="collect",
    )(*pieces)


def out_kernel(
    place, c20, c01, c31, c30, c11, c21, c10, c00, w, residual, scale, out, c_all, total, placed,
):
    z, q = place[0], place[1]
    width = c00.shape[0]
    for i, blocks in enumerate(((c00, c10, c20, c30), (c01, c11, c21, c31))):
        for r, c in enumerate(blocks):
            c_all[i, pl.ds(pl.multiple_of((q ^ r) * width, width), width), :] = c[...]
    column = as_column(scale[...])[:out.shape[0]]
    column = jnp.tile(column, (1, out.shape[1] // 128))
    total[...] = jnp.dot(w[0], c_all[0], preferred_element_type=jnp.float32)
    total[...] += jnp.dot(w[1], c_all[1], preferred_element_type=jnp.float32)
    rows, kept = w.shape[1] // (2 * SLAB), out.shape[0] // (2 * SLAB)
    for r in range(SLAB):
        for j in range(2):
            at = pl.multiple_of((((z % 2) ^ j) * SLAB + (q ^ r)) * kept, 8)
            begin = (2 * r + j) * rows
            placed[pl.ds(at, kept), :] = total[begin:begin + kept, :]
    out[...] = (residual[...].astype(jnp.float32) + column * placed[...]).astype(jnp.bfloat16)


def output(place, blocks, w, residual, scale):
    count = blocks[0].shape[1]
    rows, depth = w.shape[1:]
    share = residual.shape[0]
    return pl.pallas_call(
        out_kernel,
        out_shape=jax.ShapeDtypeStruct((share, count), jnp.bfloat16),
        in_specs=[SMEM] + [VMEM] * 11,
        out_specs=VMEM,
        scratch_shapes=[
            pltpu.VMEM((2, depth, count), jnp.bfloat16),
            pltpu.VMEM((rows, count), jnp.float32),
            pltpu.VMEM((share, count), jnp.float32),
        ],
        compiler_params=pltpu.CompilerParams(vmem_limit_bytes=HELD_VMEM),
        cost_estimate=pl.CostEstimate(
            flops=4 * share * count * depth,
            bytes_accessed=4 * share * depth,
            transcendentals=0,
        ),
        name="output",
    )(place, *blocks, w, residual, scale)


def rows_of_slab(q, got):
    placed = []
    for b in range(SLAB):
        piece = got[b]
        for other in range(1, SLAB):
            piece = jnp.where(q == other, got[b ^ other], piece)
        placed.append(piece)
    return jnp.concatenate(placed, axis=1)


def slab_plan(tokens, norm_gain, qkv_weight, q_gain, k_gain, out_weight, layer_scale, segment_ids):
    count = tokens.shape[0]
    seq, tp = lax.axis_index("seq"), lax.axis_index("tp")
    slabs = lax.axis_size("seq") // SLAB
    z, q = seq // SLAB, seq % SLAB
    place = jnp.stack([z, q, tp]).astype(jnp.int32)
    width = qkv_weight.shape[2] // SLAB
    full_width = qkv_weight.shape[2] * lax.axis_size("tp")
    slab, half = SLAB * count, 2 * count
    home = z // 2 == tp

    by_kind = jnp.transpose(qkv_weight, (1, 0, 2))
    cut = [lax.dynamic_slice_in_dim(by_kind, (q ^ r) * width, width, 2) for r in range(SLAB)]
    *cut, out_own = tied(*cut, jnp.transpose(out_weight))
    got = [cut[0]] + [in_slab(cut[r], r) for r in range(1, SLAB)]
    x0 = norm(tokens, norm_gain, slabs)
    own = rows_of_slab(q, got)
    out_near, out_far = even_pair(out_own), half_pair(out_own)
    gains = [lax.dynamic_slice_in_dim(g, q * width, width, 0)[None] for g in (q_gain, k_gain)]

    outside = jnp.full((half,), -1, jnp.int32)
    seg = jnp.concatenate([outside, segment_ids, outside], axis=0)
    seg = lax.dynamic_slice_in_dim(seg, z * slab, slab + 2 * half, 0)
    spans = key_spans(seg, slab, count, half)
    seg = seg.astype(jnp.float32)[None]
    share = layer_scale.shape[0]
    residual = jnp.transpose(lax.dynamic_slice_in_dim(tokens, tp * share, share, 1))
    scale = jnp.pad(layer_scale, (0, -share % 128))[None]
    x0, out_near, out_far, seg, spans, residual, scale, *gains = tied(
        x0, out_near, out_far, seg, spans, residual, scale, *gains
    )
    out_last = even_pair(out_far)
    x2 = in_slab(x0, 2)
    far, near = half_pair(own), even_pair(own)
    close, away = jnp.stack([out_own, out_near]), jnp.stack([out_far, out_last])
    pad = ((0, 0), (0, -close.shape[1] % 16), (0, 0))
    keep = jnp.pad(jnp.where(home, close, away), pad)
    got = across(jnp.pad(jnp.where(home, away, close), pad))
    keep_x = in_slab(keep, 2)
    near, far, x0, x2, got, keep_x = tied(near, far, x0, x2, got, keep_x)
    last = even_pair(far)
    x1, x3 = in_slab(x0, 1), in_slab(x2, 1)
    got_x, got_c, keep_c = in_slab(got, 2), in_slab(got, 1), in_slab(keep, 1)
    keep_xc = in_slab(tied(keep_x, x3)[0], 1)
    xs = (x0, x1, x2, x3)
    acc, x_last = early(place, xs, own, near, far)
    last, acc, x_last = tied(last, acc, x_last)
    query, keys, values, squares, even, odd = late(place, x_last, acc, last, *gains)
    even, odd = even_pair(even), odd_pair(odd)
    squares, got_x, got_c, keep_c, keep_xc = tied(squares, got_x, got_c, keep_c, keep_xc)
    sums = squares
    for r in range(1, SLAB):
        sums = sums + in_slab(squares, r)
    sums = sums + across(sums)
    sums = (sums, even_pair(sums), odd_pair(sums))
    got_xc = in_slab(got_x, 1)

    blocks = attend(full_width, place, spans, query, keys, values, even, odd, sums, seg)
    *blocks, got_xc = tied(*blocks, got_xc)
    pieces = (keep, keep_c, keep_x, keep_xc, got, got_c, got_x, got_xc)
    spread = []
    for r, i in ((2, 0), (0, 1), (3, 1), (3, 0), (1, 1), (2, 1), (1, 0), (0, 0)):
        to = functools.partial(lambda r, i, z, q, y: (z, q ^ r, y ^ i), r, i)
        spread.append(permuted(blocks[r], to) if r or i else blocks[r])

    return jnp.transpose(output(place, spread, collect(pieces), residual, scale))


def solution(mesh):
    def shards(*args):
        heads = args[2].shape[2] // HEAD_DIM
        slab = mesh.shape["seq"] == 16 and mesh.shape["tp"] == 2 and heads % SLAB == 0
        return (slab_plan if slab else row_plan)(*args)

    return jax.shard_map(
        shards,
        mesh=mesh,
        in_specs=(
            P("seq", None),
            P(),
            P("seq", None, "tp"),
            P("tp"),
            P("tp"),
            P("tp", "seq"),
            P("tp"),
            P(),
        ),
        out_specs=P("seq", "tp"),
        check_vma=False,
    )
```

```python
import functools
import math

import jax
import jax.numpy as jnp
from jax import lax
from jax.experimental import pallas as pl
from jax.experimental.pallas import tpu as pltpu
from jax.sharding import PartitionSpec as P

HEAD_DIM = 128
SLAB = 4

eps = 1e-06
floor_score = -1e30


def passed_along(x, axis, by):
    size = lax.axis_size(axis)
    pairs = [(i, i + by) for i in range(size) if 0 <= i + by < size]
    return lax.ppermute(x, axis, pairs)


def masked_scores(query, keys, query_seg, key_seg):
    scores = jnp.einsum(
        "qhd,khd->hqk", query, keys, preferred_element_type=jnp.float32
    ) * HEAD_DIM ** (-0.5)
    mask = (query_seg[:, None] == key_seg[None, :])[None]
    return (jnp.where(mask, scores, floor_score), mask)


def row_plan(tokens, norm_gain, qkv_weight, q_gain, k_gain, out_weight, layer_scale, segment_ids):
    count = tokens.shape[0]
    source = tokens.astype(jnp.float32)
    normed = (
        source * lax.rsqrt(jnp.mean(source * source, axis=-1, keepdims=True) + eps) * norm_gain
    ).astype(jnp.bfloat16)
    local_width = qkv_weight.shape[2]
    heads = local_width // HEAD_DIM
    joined = jnp.einsum(
        "td,dch->tch",
        normed,
        lax.all_gather(qkv_weight, "seq", axis=0, tiled=True),
        preferred_element_type=jnp.float32,
    )
    query = joined[:, 0]
    keys = joined[:, 1]
    values = joined[:, 2]
    query_sq, key_sq = lax.psum(
        (jnp.sum(query * query, axis=-1), jnp.sum(keys * keys, axis=-1)), "tp"
    )
    full_width = local_width * lax.axis_size("tp")
    query_normed = (query * lax.rsqrt(query_sq / full_width + eps)[:, None] * q_gain).astype(
        jnp.bfloat16
    )
    key_normed = (keys * lax.rsqrt(key_sq / full_width + eps)[:, None] * k_gain).astype(
        jnp.bfloat16
    )
    paired = jnp.stack([key_normed, values.astype(jnp.bfloat16)], axis=1)
    pieces = []
    for offset in (2, 1, 0, -1, -2):
        if offset == 0:
            pieces.append(paired)
        else:
            pieces.append(passed_along(paired, "seq", offset))
    widened = jnp.concatenate(pieces, axis=0)
    position = lax.axis_index("seq")
    outside = jnp.full((2 * count,), -1, jnp.int32)
    seg_pad = jnp.concatenate([outside, segment_ids, outside], axis=0)
    key_seg = lax.dynamic_slice_in_dim(seg_pad, position * count, 5 * count, 0)
    query_seg = lax.dynamic_slice_in_dim(segment_ids, position * count, count, 0)
    query_heads = query_normed.reshape(count, heads, HEAD_DIM)
    key_heads = widened[:, 0].reshape(5 * count, heads, HEAD_DIM)
    value_heads = widened[:, 1].reshape(5 * count, heads, HEAD_DIM)
    scores, mask = masked_scores(query_heads, key_heads, query_seg, key_seg)
    peak = jnp.max(scores, axis=-1, keepdims=True)
    weights = jnp.where(mask, jnp.exp(scores - peak), 0.0)
    total = jnp.sum(weights, axis=-1)
    probs = weights.astype(jnp.bfloat16)
    summed = jnp.einsum("hqk,khd->qhd", probs, value_heads, preferred_element_type=jnp.float32)
    context = (
        (summed / jnp.transpose(total)[:, :, None]).reshape(count, local_width).astype(jnp.bfloat16)
    )
    terms = jnp.dot(
        context,
        lax.all_gather(out_weight, "seq", axis=1, tiled=True),
        preferred_element_type=jnp.float32,
    )
    projected = lax.psum_scatter(terms, "tp", scatter_dimension=1, tiled=True)
    share = layer_scale.shape[0]
    residual = lax.dynamic_slice_in_dim(source, lax.axis_index("tp") * share, share, 1)
    return (residual + layer_scale * projected).astype(jnp.bfloat16)


ANY = pl.BlockSpec(memory_space=pl.ANY)
VMEM = pl.BlockSpec(memory_space=pltpu.VMEM)
SMEM = pl.BlockSpec(memory_space=pltpu.SMEM)
HBM = pl.BlockSpec(memory_space=pltpu.HBM)
KERNEL_VMEM = 60 * 1024 * 1024
HELD_VMEM = 24 * 1024 * 1024


def permuted(x, to):
    slabs, tps = lax.axis_size("seq") // SLAB, lax.axis_size("tp")
    pairs = []
    for i in range(slabs * SLAB * tps):
        z, q, y = to(i // (SLAB * tps), i // tps % SLAB, i % tps)
        pairs.append((i, (z * SLAB + q) * tps + y))
    return lax.ppermute(x, ("seq", "tp"), pairs)


def in_slab(x, flip):
    return permuted(x, lambda z, q, y: (z, q ^ flip, y))


def across(x):
    return permuted(x, lambda z, q, y: (z, q, 1 - y))


def even_pair(x):
    return permuted(x, lambda z, q, y: (z ^ 1, q, y))


def odd_pair(x):
    return permuted(x, lambda z, q, y: (3 - z, q, y) if z in (1, 2) else (z, q ^ 1, y))


def half_pair(x):
    return permuted(x, lambda z, q, y: (z ^ 2, q, y))


def tied(*arrays):
    return lax.optimization_barrier(arrays)


def as_row(column):
    wide = jnp.broadcast_to(column, (column.shape[0], 128))
    return jnp.transpose(wide)[:8]


def as_column(row):
    return jnp.transpose(jnp.broadcast_to(row, (128, row.shape[1])))


def start(copies):
    for copy in copies:
        copy.start()


def wait(copies):
    for copy in copies:
        copy.wait()


def norm_kernel(tokens, gain, out):
    part = tokens.shape[1] // out.shape[0]
    source = tokens[...].astype(jnp.float32)
    mean = jnp.mean(source * source, axis=1, keepdims=True)
    normed = source * lax.rsqrt(mean + eps) * gain[...]
    for j in range(out.shape[0]):
        out[j, :, :part] = normed[:, j * part:(j + 1) * part].astype(jnp.bfloat16)
        out[j, :, part:] = jnp.zeros((out.shape[1], out.shape[2] - part), jnp.bfloat16)


def norm(tokens, gain, slabs):
    count, depth = tokens.shape
    shape = (slabs, count, pl.cdiv(depth // slabs, 128) * 128)
    return pl.pallas_call(
        norm_kernel,
        out_shape=jax.ShapeDtypeStruct(shape, jnp.bfloat16),
        in_specs=[VMEM, VMEM],
        out_specs=VMEM,
        compiler_params=pltpu.CompilerParams(vmem_limit_bytes=KERNEL_VMEM),
        name="norm",
    )(tokens, gain[None])


def token_copies(xs, at, out, sems):
    return [
        pltpu.make_async_copy(x.at[at], out.at[r], sems.at[r]) for r, x in enumerate(xs)
    ]


def blank_tail(w, rows):
    tail = w.shape[-2] - rows
    w[..., rows:, :] = jnp.zeros(w.shape[:-2] + (tail, w.shape[-1]), w.dtype)


def early_kernel(
    place, xa, xb, xc, xd, own, near, far, acc, x_last, x_all, w_all, x_sem, w_sem, last_sem,
):
    z = place[0]
    kinds, rows = own.shape[:2]
    copies = []
    for i, w in enumerate((own, near, far)):
        dst = w_all.at[i, :, pl.ds(0, rows), :]
        copies.append([pltpu.make_async_copy(w, dst, w_sem.at[i])])
        copies[i] += token_copies((xa, xb, xc, xd), z ^ i, x_all.at[i], x_sem.at[i])
        start(copies[i])
    last_copies = token_copies((xa, xb, xc, xd), z ^ 3, x_last, last_sem)
    start(last_copies)
    blank_tail(w_all, rows)
    for step in range(3):
        wait(copies[step])
        for r in range(SLAB):
            x = x_all[step, r]
            for kind in range(kinds):
                term = jnp.dot(x, w_all[step, kind], preferred_element_type=jnp.float32)
                acc[r, kind] = term if step == 0 else acc[r, kind] + term
    wait(last_copies)


def early(place, xs, own, near, far):
    kinds, rows, width = own.shape
    slabs, count, wide = xs[0].shape
    return pl.pallas_call(
        early_kernel,
        out_shape=(
            jax.ShapeDtypeStruct((SLAB, kinds, count, width), jnp.float32),
            jax.ShapeDtypeStruct((SLAB, count, wide), jnp.bfloat16),
        ),
        in_specs=[SMEM] + [HBM] * 7,
        out_specs=(VMEM, VMEM),
        scratch_shapes=[
            pltpu.VMEM((3, SLAB, count, wide), jnp.bfloat16),
            pltpu.VMEM((3, kinds, wide, width), jnp.bfloat16),
            pltpu.SemaphoreType.DMA((3, SLAB)),
            pltpu.SemaphoreType.DMA((3,)),
            pltpu.SemaphoreType.DMA((SLAB,)),
        ],
        compiler_params=pltpu.CompilerParams(vmem_limit_bytes=HELD_VMEM),
        cost_estimate=pl.CostEstimate(
            flops=12 * kinds * SLAB * count * rows * width,
            bytes_accessed=6 * kinds * rows * width + 6 * SLAB * count * rows,
            transcendentals=0,
        ),
        name="early",
    )(place, *xs, own, near, far)


def late_kernel(
    place, x_last, acc, last, q_gain, k_gain, query, keys, values, squares, even, odd, w_all,
):
    z, q = place[0], place[1]
    rows = last.shape[1]
    w_all[:, :rows, :] = last[...]
    blank_tail(w_all, rows)
    count = acc.shape[2]
    for r in range(SLAB):
        rows = pl.ds(pl.multiple_of((q ^ r) * count, count), count)
        for kind in range(3):
            part = acc[r, kind] + jnp.dot(
                x_last[r], w_all[kind], preferred_element_type=jnp.float32
            )
            if kind < 2:
                summed = as_row(jnp.sum(part * part, axis=1, keepdims=True))
                squares[kind:kind + 1, rows] = summed[:1]
                part = part * (q_gain, k_gain)[kind][...]
            out = (query, keys, values)[kind]
            out[rows, :] = part.astype(out.dtype)
    reach = even.shape[1]
    for out, at in ((even, 1 - z % 2), (odd, z % 2)):
        rows = pl.ds(pl.multiple_of(at * reach, reach), reach)
        out[0] = keys[rows, :]
        out[1] = values[rows, :]


def late(place, x_last, acc, last, q_gain, k_gain):
    kinds, rows, width = last.shape
    count, wide = x_last.shape[1:]
    slab = SLAB * count
    f32, bf16 = jnp.float32, jnp.bfloat16
    return pl.pallas_call(
        late_kernel,
        out_shape=(
            jax.ShapeDtypeStruct((slab, width), f32),
            jax.ShapeDtypeStruct((slab, width), bf16),
            jax.ShapeDtypeStruct((slab, width), bf16),
            jax.ShapeDtypeStruct((2, slab), f32),
            jax.ShapeDtypeStruct((2, 2 * count, width), bf16),
            jax.ShapeDtypeStruct((2, 2 * count, width), bf16),
        ),
        in_specs=[SMEM] + [VMEM] * 5,
        out_specs=(VMEM,) * 6,
        scratch_shapes=[
            pltpu.VMEM((kinds, wide, width), bf16),
        ],
        compiler_params=pltpu.CompilerParams(vmem_limit_bytes=HELD_VMEM),
        cost_estimate=pl.CostEstimate(
            flops=2 * kinds * slab * rows * width,
            bytes_accessed=2 * kinds * rows * width + 2 * slab * rows,
            transcendentals=0,
        ),
        name="late",
    )(place, x_last, acc, last, q_gain, k_gain)


def attend_kernel(
    full_width, place, spans, query, keys, values, even, odd, mine, near, mid, seg, o0, o1, o2, o3,
    k_all, v_all, o_all, scale_all,
):
    z, q = place[0], place[1]
    slab = query.shape[0]
    count = slab // SLAB
    half = even.shape[1]
    upper = half + slab
    is_even = z % 2 == 0
    even_at = pl.multiple_of(jnp.where(is_even, upper, 0), half)
    odd_at = pl.multiple_of(jnp.where(is_even, 0, upper), half)
    for k, (whole, out) in enumerate(((keys, k_all), (values, v_all))):
        out[half:upper, :] = whole[...]
        out[pl.ds(even_at, half), :] = even[k]
        out[pl.ds(odd_at, half), :] = odd[k]
    scale = [lax.rsqrt(sums[...] / full_width + eps) for sums in (mine, near, mid)]
    scale_all[:, half:upper] = scale[0]
    scale_all[:, :half] = jnp.where(is_even, scale[2], scale[1])[:, slab - half:]
    scale_all[:, upper:] = jnp.where(is_even, scale[1], scale[2])[:, :half]
    heads = query.shape[1] // HEAD_DIM
    factor = HEAD_DIM ** (-0.5) * math.log2(math.e)

    def block(r, _):
        b = q ^ r
        at_query = pl.multiple_of(b * count + half, count)
        query_seg = as_column(seg[:, pl.ds(at_query, count)])
        q_scale = as_column(scale_all[0:1, pl.ds(at_query, count)])
        for tiles in range(2, 2 * half // count + 2):
            @pl.when(spans[b, 1] == tiles)
            def _():
                width = tiles * count
                begin = pl.multiple_of(spans[b, 0], 128)
                keys_at = pl.ds(begin, width)
                mask = jnp.tile(query_seg, (1, width // 128)) == seg[:, keys_at]
                k_scale = scale_all[1:2, keys_at] * factor
                all_cols = [slice(h * HEAD_DIM, (h + 1) * HEAD_DIM) for h in range(heads)]
                rows = pl.ds(pl.multiple_of(b * count, count), count)
                scores = [
                    lax.dot_general(
                        (query[rows, cols] * q_scale).astype(jnp.bfloat16), k_all[keys_at, cols],
                        (((1,), (1,)), ((), ())), preferred_element_type=jnp.float32,
                    )
                    for cols in all_cols
                ]
                for cols, s in zip(all_cols, scores):
                    s = jnp.where(mask, s * k_scale, floor_score)
                    peak = jnp.max(s, axis=1, keepdims=True)
                    weights = jnp.exp2(s - peak)
                    total = jnp.sum(weights, axis=1, keepdims=True)
                    summed = jnp.dot(
                        weights.astype(jnp.bfloat16), v_all[keys_at, cols],
                        preferred_element_type=jnp.float32,
                    )
                    o_all[r, cols, :] = jnp.transpose(summed / total).astype(jnp.bfloat16)

        return 0

    lax.fori_loop(0, SLAB, block, 0)
    for r, out in enumerate((o0, o1, o2, o3)):
        out[...] = o_all[r]


def key_spans(seg, slab, count, half):
    ext = seg.shape[0]
    index = jnp.arange(ext, dtype=jnp.int32)
    blocks = seg[half:half + slab].reshape(-1, count)
    first, last = blocks[:, :1], blocks[:, -1:]
    begin = jnp.min(jnp.where(seg == first, index, ext), axis=1) // 128 * 128
    end = jnp.max(jnp.where(seg == last, index, -1), axis=1) + 1
    tiles = jnp.maximum((end - begin + count - 1) // count, 2)
    return jnp.stack([jnp.minimum(begin, ext - tiles * count), tiles], axis=1)


def attend(full_width, place, spans, query, keys, values, even, odd, sums, seg):
    slab, width = query.shape
    half = even.shape[1]
    count = slab // SLAB
    ext = slab + 2 * half
    bf16 = jnp.bfloat16
    window = count + 2 * half
    return pl.pallas_call(
        functools.partial(attend_kernel, full_width),
        out_shape=(jax.ShapeDtypeStruct((width, count), bf16),) * SLAB,
        in_specs=[SMEM] * 2 + [VMEM] * 9,
        out_specs=(VMEM,) * SLAB,
        scratch_shapes=[
            pltpu.VMEM((ext, width), bf16),
            pltpu.VMEM((ext, width), bf16),
            pltpu.VMEM((SLAB, width, count), bf16),
            pltpu.VMEM((2, ext), jnp.float32),
        ],
        compiler_params=pltpu.CompilerParams(vmem_limit_bytes=HELD_VMEM),
        cost_estimate=pl.CostEstimate(
            flops=64 * SLAB * count * window * width,
            bytes_accessed=4 * ext * width + 4 * slab * width,
            transcendentals=SLAB * count * window * width // HEAD_DIM,
        ),
        name="attend",
    )(place, spans, query, keys, values, even, odd, *sums, seg)


def collect_kernel(wa0, wb0, wc0, wd0, wa1, wb1, wc1, wd1, out, sems):
    rows = wa0.shape[1]
    copies = []
    for i, ws in enumerate(((wa0, wb0, wc0, wd0), (wa1, wb1, wc1, wd1))):
        for r, w in enumerate(ws):
            for j in range(2):
                dst = out.at[i, pl.ds((2 * r + j) * rows, rows), :]
                copies.append(pltpu.make_async_copy(w.at[j], dst, sems.at[i, r, j]))
    start(copies)
    wait(copies)


def collect(pieces):
    rows, depth = pieces[0].shape[1:]
    return pl.pallas_call(
        collect_kernel,
        out_shape=jax.ShapeDtypeStruct((2, 2 * SLAB * rows, depth), jnp.bfloat16),
        in_specs=[HBM] * 8,
        out_specs=VMEM,
        scratch_shapes=[pltpu.SemaphoreType.DMA((2, SLAB, 2))],
        compiler_params=pltpu.CompilerParams(vmem_limit_bytes=HELD_VMEM),
        cost_estimate=pl.CostEstimate(
            flops=0, bytes_accessed=16 * SLAB * rows * depth, transcendentals=0
        ),
        name="collect",
    )(*pieces)


def out_kernel(
    place, c20, c01, c31, c30, c11, c21, c10, c00, w, residual, scale, out, c_all, total, placed,
):
    z, q = place[0], place[1]
    width = c00.shape[0]
    for i, blocks in enumerate(((c00, c10, c20, c30), (c01, c11, c21, c31))):
        for r, c in enumerate(blocks):
            c_all[i, pl.ds(pl.multiple_of((q ^ r) * width, width), width), :] = c[...]
    column = as_column(scale[...])[:out.shape[0]]
    column = jnp.tile(column, (1, out.shape[1] // 128))
    total[...] = jnp.dot(w[0], c_all[0], preferred_element_type=jnp.float32)
    total[...] += jnp.dot(w[1], c_all[1], preferred_element_type=jnp.float32)
    rows, kept = w.shape[1] // (2 * SLAB), out.shape[0] // (2 * SLAB)
    for r in range(SLAB):
        for j in range(2):
            at = pl.multiple_of((((z % 2) ^ j) * SLAB + (q ^ r)) * kept, 8)
            begin = (2 * r + j) * rows
            placed[pl.ds(at, kept), :] = total[begin:begin + kept, :]
    out[...] = (residual[...].astype(jnp.float32) + column * placed[...]).astype(jnp.bfloat16)


def output(place, blocks, w, residual, scale):
    count = blocks[0].shape[1]
    rows, depth = w.shape[1:]
    share = residual.shape[0]
    return pl.pallas_call(
        out_kernel,
        out_shape=jax.ShapeDtypeStruct((share, count), jnp.bfloat16),
        in_specs=[SMEM] + [VMEM] * 11,
        out_specs=VMEM,
        scratch_shapes=[
            pltpu.VMEM((2, depth, count), jnp.bfloat16),
            pltpu.VMEM((rows, count), jnp.float32),
            pltpu.VMEM((share, count), jnp.float32),
        ],
        compiler_params=pltpu.CompilerParams(vmem_limit_bytes=HELD_VMEM),
        cost_estimate=pl.CostEstimate(
            flops=4 * share * count * depth,
            bytes_accessed=4 * share * depth,
            transcendentals=0,
        ),
        name="output",
    )(place, *blocks, w, residual, scale)


def rows_of_slab(q, got):
    placed = []
    for b in range(SLAB):
        piece = got[b]
        for other in range(1, SLAB):
            piece = jnp.where(q == other, got[b ^ other], piece)
        placed.append(piece)
    return jnp.concatenate(placed, axis=1)


def slab_plan(tokens, norm_gain, qkv_weight, q_gain, k_gain, out_weight, layer_scale, segment_ids):
    count = tokens.shape[0]
    seq, tp = lax.axis_index("seq"), lax.axis_index("tp")
    slabs = lax.axis_size("seq") // SLAB
    z, q = seq // SLAB, seq % SLAB
    place = jnp.stack([z, q, tp]).astype(jnp.int32)
    width = qkv_weight.shape[2] // SLAB
    full_width = qkv_weight.shape[2] * lax.axis_size("tp")
    slab, half = SLAB * count, 2 * count
    home = z // 2 == tp

    by_kind = jnp.transpose(qkv_weight, (1, 0, 2))
    cut = [lax.dynamic_slice_in_dim(by_kind, (q ^ r) * width, width, 2) for r in range(SLAB)]
    got = [cut[0]] + [in_slab(cut[r], r) for r in range(1, SLAB)]
    x0 = norm(tokens, norm_gain, slabs)
    out_own = jnp.transpose(out_weight)
    own = rows_of_slab(q, got)
    out_near, out_far = even_pair(out_own), half_pair(out_own)
    gains = [lax.dynamic_slice_in_dim(g, q * width, width, 0)[None] for g in (q_gain, k_gain)]

    outside = jnp.full((half,), -1, jnp.int32)
    seg = jnp.concatenate([outside, segment_ids, outside], axis=0)
    seg = lax.dynamic_slice_in_dim(seg, z * slab, slab + 2 * half, 0)
    spans = key_spans(seg, slab, count, half)
    seg = seg.astype(jnp.float32)[None]
    share = layer_scale.shape[0]
    residual = jnp.transpose(lax.dynamic_slice_in_dim(tokens, tp * share, share, 1))
    scale = jnp.pad(layer_scale, (0, -share % 128))[None]
    x0, out_near, out_far, seg, spans, residual, scale, *gains = tied(
        x0, out_near, out_far, seg, spans, residual, scale, *gains
    )
    out_last = even_pair(out_far)
    x2 = in_slab(x0, 2)
    far, near = half_pair(own), even_pair(own)
    close, away = jnp.stack([out_own, out_near]), jnp.stack([out_far, out_last])
    pad = ((0, 0), (0, -close.shape[1] % 16), (0, 0))
    keep = jnp.pad(jnp.where(home, close, away), pad)
    got = across(jnp.pad(jnp.where(home, away, close), pad))
    keep_x = in_slab(keep, 2)
    near, far, x0, x2, got, keep_x = tied(near, far, x0, x2, got, keep_x)
    last = even_pair(far)
    x1, x3 = in_slab(x0, 1), in_slab(x2, 1)
    got_x, got_c, keep_c = in_slab(got, 2), in_slab(got, 1), in_slab(keep, 1)
    keep_xc = in_slab(tied(keep_x, x3)[0], 1)
    xs = (x0, x1, x2, x3)
    acc, x_last = early(place, xs, own, near, far)
    last, acc, x_last = tied(last, acc, x_last)
    query, keys, values, squares, even, odd = late(place, x_last, acc, last, *gains)
    even, odd = even_pair(even), odd_pair(odd)
    squares, got_x, got_c, keep_c, keep_xc = tied(squares, got_x, got_c, keep_c, keep_xc)
    sums = squares
    for r in range(1, SLAB):
        sums = sums + in_slab(squares, r)
    sums = sums + across(sums)
    sums = (sums, even_pair(sums), odd_pair(sums))
    got_xc = in_slab(got_x, 1)

    blocks = attend(full_width, place, spans, query, keys, values, even, odd, sums, seg)
    *blocks, got_xc = tied(*blocks, got_xc)
    pieces = (keep, keep_c, keep_x, keep_xc, got, got_c, got_x, got_xc)
    spread = []
    for r, i in ((2, 0), (0, 1), (3, 1), (3, 0), (1, 1), (2, 1), (1, 0), (0, 0)):
        to = functools.partial(lambda r, i, z, q, y: (z, q ^ r, y ^ i), r, i)
        spread.append(permuted(blocks[r], to) if r or i else blocks[r])

    return jnp.transpose(output(place, spread, collect(pieces), residual, scale))


def solution(mesh):
    def shards(*args):
        heads = args[2].shape[2] // HEAD_DIM
        slab = mesh.shape["seq"] == 16 and mesh.shape["tp"] == 2 and heads % SLAB == 0
        return (slab_plan if slab else row_plan)(*args)

    return jax.shard_map(
        shards,
        mesh=mesh,
        in_specs=(
            P("seq", None),
            P(),
            P("seq", None, "tp"),
            P("tp"),
            P("tp"),
            P("tp", "seq"),
            P("tp"),
            P(),
        ),
        out_specs=P("seq", "tp"),
        check_vma=False,
    )
```

```python
import functools
import math

import jax
import jax.numpy as jnp
from jax import lax
from jax.experimental import pallas as pl
from jax.experimental.pallas import tpu as pltpu
from jax.sharding import PartitionSpec as P

HEAD_DIM = 128
SLAB = 4

eps = 1e-06
floor_score = -1e30


def passed_along(x, axis, by):
    size = lax.axis_size(axis)
    pairs = [(i, i + by) for i in range(size) if 0 <= i + by < size]
    return lax.ppermute(x, axis, pairs)


def masked_scores(query, keys, query_seg, key_seg):
    scores = jnp.einsum(
        "qhd,khd->hqk", query, keys, preferred_element_type=jnp.float32
    ) * HEAD_DIM ** (-0.5)
    mask = (query_seg[:, None] == key_seg[None, :])[None]
    return (jnp.where(mask, scores, floor_score), mask)


def row_plan(tokens, norm_gain, qkv_weight, q_gain, k_gain, out_weight, layer_scale, segment_ids):
    count = tokens.shape[0]
    source = tokens.astype(jnp.float32)
    normed = (
        source * lax.rsqrt(jnp.mean(source * source, axis=-1, keepdims=True) + eps) * norm_gain
    ).astype(jnp.bfloat16)
    local_width = qkv_weight.shape[2]
    heads = local_width // HEAD_DIM
    joined = jnp.einsum(
        "td,dch->tch",
        normed,
        lax.all_gather(qkv_weight, "seq", axis=0, tiled=True),
        preferred_element_type=jnp.float32,
    )
    query = joined[:, 0]
    keys = joined[:, 1]
    values = joined[:, 2]
    query_sq, key_sq = lax.psum(
        (jnp.sum(query * query, axis=-1), jnp.sum(keys * keys, axis=-1)), "tp"
    )
    full_width = local_width * lax.axis_size("tp")
    query_normed = (query * lax.rsqrt(query_sq / full_width + eps)[:, None] * q_gain).astype(
        jnp.bfloat16
    )
    key_normed = (keys * lax.rsqrt(key_sq / full_width + eps)[:, None] * k_gain).astype(
        jnp.bfloat16
    )
    paired = jnp.stack([key_normed, values.astype(jnp.bfloat16)], axis=1)
    pieces = []
    for offset in (2, 1, 0, -1, -2):
        if offset == 0:
            pieces.append(paired)
        else:
            pieces.append(passed_along(paired, "seq", offset))
    widened = jnp.concatenate(pieces, axis=0)
    position = lax.axis_index("seq")
    outside = jnp.full((2 * count,), -1, jnp.int32)
    seg_pad = jnp.concatenate([outside, segment_ids, outside], axis=0)
    key_seg = lax.dynamic_slice_in_dim(seg_pad, position * count, 5 * count, 0)
    query_seg = lax.dynamic_slice_in_dim(segment_ids, position * count, count, 0)
    query_heads = query_normed.reshape(count, heads, HEAD_DIM)
    key_heads = widened[:, 0].reshape(5 * count, heads, HEAD_DIM)
    value_heads = widened[:, 1].reshape(5 * count, heads, HEAD_DIM)
    scores, mask = masked_scores(query_heads, key_heads, query_seg, key_seg)
    peak = jnp.max(scores, axis=-1, keepdims=True)
    weights = jnp.where(mask, jnp.exp(scores - peak), 0.0)
    total = jnp.sum(weights, axis=-1)
    probs = weights.astype(jnp.bfloat16)
    summed = jnp.einsum("hqk,khd->qhd", probs, value_heads, preferred_element_type=jnp.float32)
    context = (
        (summed / jnp.transpose(total)[:, :, None]).reshape(count, local_width).astype(jnp.bfloat16)
    )
    terms = jnp.dot(
        context,
        lax.all_gather(out_weight, "seq", axis=1, tiled=True),
        preferred_element_type=jnp.float32,
    )
    projected = lax.psum_scatter(terms, "tp", scatter_dimension=1, tiled=True)
    share = layer_scale.shape[0]
    residual = lax.dynamic_slice_in_dim(source, lax.axis_index("tp") * share, share, 1)
    return (residual + layer_scale * projected).astype(jnp.bfloat16)


ANY = pl.BlockSpec(memory_space=pl.ANY)
VMEM = pl.BlockSpec(memory_space=pltpu.VMEM)
SMEM = pl.BlockSpec(memory_space=pltpu.SMEM)
HBM = pl.BlockSpec(memory_space=pltpu.HBM)
KERNEL_VMEM = 60 * 1024 * 1024
HELD_VMEM = 24 * 1024 * 1024


def permuted(x, to):
    slabs, tps = lax.axis_size("seq") // SLAB, lax.axis_size("tp")
    pairs = []
    for i in range(slabs * SLAB * tps):
        z, q, y = to(i // (SLAB * tps), i // tps % SLAB, i % tps)
        pairs.append((i, (z * SLAB + q) * tps + y))
    return lax.ppermute(x, ("seq", "tp"), pairs)


def in_slab(x, flip):
    return permuted(x, lambda z, q, y: (z, q ^ flip, y))


def across(x):
    return permuted(x, lambda z, q, y: (z, q, 1 - y))


def even_pair(x):
    return permuted(x, lambda z, q, y: (z ^ 1, q, y))


def odd_pair(x):
    return permuted(x, lambda z, q, y: (3 - z, q, y) if z in (1, 2) else (z, q ^ 1, y))


def half_pair(x):
    return permuted(x, lambda z, q, y: (z ^ 2, q, y))


def tied(*arrays):
    return lax.optimization_barrier(arrays)


def as_row(column):
    wide = jnp.broadcast_to(column, (column.shape[0], 128))
    return jnp.transpose(wide)[:8]


def as_column(row):
    return jnp.transpose(jnp.broadcast_to(row, (128, row.shape[1])))


def start(copies):
    for copy in copies:
        copy.start()


def wait(copies):
    for copy in copies:
        copy.wait()


def norm_kernel(tokens, gain, out):
    part = tokens.shape[1] // out.shape[0]
    source = tokens[...].astype(jnp.float32)
    mean = jnp.mean(source * source, axis=1, keepdims=True)
    normed = source * lax.rsqrt(mean + eps) * gain[...]
    for j in range(out.shape[0]):
        out[j, :, :part] = normed[:, j * part:(j + 1) * part].astype(jnp.bfloat16)
        out[j, :, part:] = jnp.zeros((out.shape[1], out.shape[2] - part), jnp.bfloat16)


def norm(tokens, gain, slabs):
    count, depth = tokens.shape
    shape = (slabs, count, pl.cdiv(depth // slabs, 128) * 128)
    return pl.pallas_call(
        norm_kernel,
        out_shape=jax.ShapeDtypeStruct(shape, jnp.bfloat16),
        in_specs=[VMEM, VMEM],
        out_specs=VMEM,
        compiler_params=pltpu.CompilerParams(vmem_limit_bytes=KERNEL_VMEM),
        name="norm",
    )(tokens, gain[None])


def token_copies(xs, at, out, sems):
    return [
        pltpu.make_async_copy(x.at[at], out.at[r], sems.at[r]) for r, x in enumerate(xs)
    ]


def blank_tail(w, rows):
    tail = w.shape[-2] - rows
    w[..., rows:, :] = jnp.zeros(w.shape[:-2] + (tail, w.shape[-1]), w.dtype)


def early_kernel(
    place, xa, xb, xc, xd, own, near, far, acc, x_last, x_all, w_all, x_sem, w_sem, last_sem,
):
    z = place[0]
    kinds, rows = own.shape[:2]
    copies = []
    for i, w in enumerate((own, near, far)):
        dst = w_all.at[i, :, pl.ds(0, rows), :]
        copies.append([pltpu.make_async_copy(w, dst, w_sem.at[i])])
        copies[i] += token_copies((xa, xb, xc, xd), z ^ i, x_all.at[i], x_sem.at[i])
        start(copies[i])
    last_copies = token_copies((xa, xb, xc, xd), z ^ 3, x_last, last_sem)
    start(last_copies)
    blank_tail(w_all, rows)
    for step in range(3):
        wait(copies[step])
        for r in range(SLAB):
            x = x_all[step, r]
            for kind in range(kinds):
                term = jnp.dot(x, w_all[step, kind], preferred_element_type=jnp.float32)
                acc[r, kind] = term if step == 0 else acc[r, kind] + term
    wait(last_copies)


def early(place, xs, own, near, far):
    kinds, rows, width = own.shape
    slabs, count, wide = xs[0].shape
    return pl.pallas_call(
        early_kernel,
        out_shape=(
            jax.ShapeDtypeStruct((SLAB, kinds, count, width), jnp.float32),
            jax.ShapeDtypeStruct((SLAB, count, wide), jnp.bfloat16),
        ),
        in_specs=[SMEM] + [HBM] * 7,
        out_specs=(VMEM, VMEM),
        scratch_shapes=[
            pltpu.VMEM((3, SLAB, count, wide), jnp.bfloat16),
            pltpu.VMEM((3, kinds, wide, width), jnp.bfloat16),
            pltpu.SemaphoreType.DMA((3, SLAB)),
            pltpu.SemaphoreType.DMA((3,)),
            pltpu.SemaphoreType.DMA((SLAB,)),
        ],
        compiler_params=pltpu.CompilerParams(vmem_limit_bytes=HELD_VMEM),
        cost_estimate=pl.CostEstimate(
            flops=12 * kinds * SLAB * count * rows * width,
            bytes_accessed=6 * kinds * rows * width + 6 * SLAB * count * rows,
            transcendentals=0,
        ),
        name="early",
    )(place, *xs, own, near, far)


def late_kernel(
    place, x_last, acc, last, q_gain, k_gain, query, keys, values, squares, even, odd, w_all,
):
    z, q = place[0], place[1]
    rows = last.shape[1]
    w_all[:, :rows, :] = last[...]
    blank_tail(w_all, rows)
    count = acc.shape[2]
    for r in range(SLAB):
        rows = pl.ds(pl.multiple_of((q ^ r) * count, count), count)
        for kind in range(3):
            part = acc[r, kind] + jnp.dot(
                x_last[r], w_all[kind], preferred_element_type=jnp.float32
            )
            if kind < 2:
                summed = as_row(jnp.sum(part * part, axis=1, keepdims=True))
                squares[kind:kind + 1, rows] = summed[:1]
                part = part * (q_gain, k_gain)[kind][...]
            out = (query, keys, values)[kind]
            out[rows, :] = part.astype(out.dtype)
    reach = even.shape[1]
    for out, at in ((even, 1 - z % 2), (odd, z % 2)):
        rows = pl.ds(pl.multiple_of(at * reach, reach), reach)
        out[0] = keys[rows, :]
        out[1] = values[rows, :]


def late(place, x_last, acc, last, q_gain, k_gain):
    kinds, rows, width = last.shape
    count, wide = x_last.shape[1:]
    slab = SLAB * count
    f32, bf16 = jnp.float32, jnp.bfloat16
    return pl.pallas_call(
        late_kernel,
        out_shape=(
            jax.ShapeDtypeStruct((slab, width), f32),
            jax.ShapeDtypeStruct((slab, width), bf16),
            jax.ShapeDtypeStruct((slab, width), bf16),
            jax.ShapeDtypeStruct((2, slab), f32),
            jax.ShapeDtypeStruct((2, 2 * count, width), bf16),
            jax.ShapeDtypeStruct((2, 2 * count, width), bf16),
        ),
        in_specs=[SMEM] + [VMEM] * 5,
        out_specs=(VMEM,) * 6,
        scratch_shapes=[
            pltpu.VMEM((kinds, wide, width), bf16),
        ],
        compiler_params=pltpu.CompilerParams(vmem_limit_bytes=HELD_VMEM),
        cost_estimate=pl.CostEstimate(
            flops=2 * kinds * slab * rows * width,
            bytes_accessed=2 * kinds * rows * width + 2 * slab * rows,
            transcendentals=0,
        ),
        name="late",
    )(place, x_last, acc, last, q_gain, k_gain)


def attend_kernel(
    full_width, place, spans, query, keys, values, even, odd, mine, near, mid, seg, o0, o1, o2, o3,
    k_all, v_all, o_all, scale_all,
):
    z, q = place[0], place[1]
    slab = query.shape[0]
    count = slab // SLAB
    half = even.shape[1]
    upper = half + slab
    is_even = z % 2 == 0
    even_at = pl.multiple_of(jnp.where(is_even, upper, 0), half)
    odd_at = pl.multiple_of(jnp.where(is_even, 0, upper), half)
    for k, (whole, out) in enumerate(((keys, k_all), (values, v_all))):
        out[half:upper, :] = whole[...]
        out[pl.ds(even_at, half), :] = even[k]
        out[pl.ds(odd_at, half), :] = odd[k]
    scale = [lax.rsqrt(sums[...] / full_width + eps) for sums in (mine, near, mid)]
    scale_all[:, half:upper] = scale[0]
    scale_all[:, :half] = jnp.where(is_even, scale[2], scale[1])[:, slab - half:]
    scale_all[:, upper:] = jnp.where(is_even, scale[1], scale[2])[:, :half]
    heads = query.shape[1] // HEAD_DIM
    factor = HEAD_DIM ** (-0.5) * math.log2(math.e)

    def block(r, _):
        b = q ^ r
        at_query = pl.multiple_of(b * count + half, count)
        query_seg = as_column(seg[:, pl.ds(at_query, count)])
        q_scale = as_column(scale_all[0:1, pl.ds(at_query, count)])
        for tiles in range(2, 2 * half // count + 2):
            @pl.when(spans[b, 1] == tiles)
            def _():
                width = tiles * count
                begin = pl.multiple_of(spans[b, 0], 128)
                keys_at = pl.ds(begin, width)
                mask = jnp.tile(query_seg, (1, width // 128)) == seg[:, keys_at]
                k_scale = scale_all[1:2, keys_at] * factor
                all_cols = [slice(h * HEAD_DIM, (h + 1) * HEAD_DIM) for h in range(heads)]
                rows = pl.ds(pl.multiple_of(b * count, count), count)
                scores = [
                    lax.dot_general(
                        (query[rows, cols] * q_scale).astype(jnp.bfloat16), k_all[keys_at, cols],
                        (((1,), (1,)), ((), ())), preferred_element_type=jnp.float32,
                    )
                    for cols in all_cols
                ]
                parts = []
                for s in scores:
                    s = jnp.where(mask, s * k_scale, floor_score)
                    weights = jnp.exp2(s - jnp.max(s, axis=1, keepdims=True))
                    total = jnp.sum(weights, axis=1, keepdims=True)
                    parts.append((weights.astype(jnp.bfloat16), total))
                for cols, (probs, total) in zip(all_cols, parts):
                    summed = jnp.dot(
                        probs, v_all[keys_at, cols], preferred_element_type=jnp.float32
                    )
                    o_all[r, cols, :] = jnp.transpose(summed / total).astype(jnp.bfloat16)

        return 0

    lax.fori_loop(0, SLAB, block, 0)
    for r, out in enumerate((o0, o1, o2, o3)):
        out[...] = o_all[r]


def key_spans(seg, slab, count, half):
    ext = seg.shape[0]
    index = jnp.arange(ext, dtype=jnp.int32)
    blocks = seg[half:half + slab].reshape(-1, count)
    first, last = blocks[:, :1], blocks[:, -1:]
    begin = jnp.min(jnp.where(seg == first, index, ext), axis=1) // 128 * 128
    end = jnp.max(jnp.where(seg == last, index, -1), axis=1) + 1
    tiles = jnp.maximum((end - begin + count - 1) // count, 2)
    return jnp.stack([jnp.minimum(begin, ext - tiles * count), tiles], axis=1)


def attend(full_width, place, spans, query, keys, values, even, odd, sums, seg):
    slab, width = query.shape
    half = even.shape[1]
    count = slab // SLAB
    ext = slab + 2 * half
    bf16 = jnp.bfloat16
    window = count + 2 * half
    return pl.pallas_call(
        functools.partial(attend_kernel, full_width),
        out_shape=(jax.ShapeDtypeStruct((width, count), bf16),) * SLAB,
        in_specs=[SMEM] * 2 + [VMEM] * 9,
        out_specs=(VMEM,) * SLAB,
        scratch_shapes=[
            pltpu.VMEM((ext, width), bf16),
            pltpu.VMEM((ext, width), bf16),
            pltpu.VMEM((SLAB, width, count), bf16),
            pltpu.VMEM((2, ext), jnp.float32),
        ],
        compiler_params=pltpu.CompilerParams(vmem_limit_bytes=HELD_VMEM),
        cost_estimate=pl.CostEstimate(
            flops=64 * SLAB * count * window * width,
            bytes_accessed=4 * ext * width + 4 * slab * width,
            transcendentals=SLAB * count * window * width // HEAD_DIM,
        ),
        name="attend",
    )(place, spans, query, keys, values, even, odd, *sums, seg)


def collect_kernel(wa0, wb0, wc0, wd0, wa1, wb1, wc1, wd1, out, sems):
    rows, depth = wa0.shape[1:]
    copies = []
    for i, ws in enumerate(((wa0, wb0, wc0, wd0), (wa1, wb1, wc1, wd1))):
        for r, w in enumerate(ws):
            for j in range(2):
                dst = out.at[pl.ds((2 * r + j) * rows, rows), pl.ds(i * depth, depth)]
                copies.append(pltpu.make_async_copy(w.at[j], dst, sems.at[i, r, j]))
    start(copies)
    wait(copies)


def collect(pieces):
    rows, depth = pieces[0].shape[1:]
    return pl.pallas_call(
        collect_kernel,
        out_shape=jax.ShapeDtypeStruct((2 * SLAB * rows, 2 * depth), jnp.bfloat16),
        in_specs=[HBM] * 8,
        out_specs=VMEM,
        scratch_shapes=[pltpu.SemaphoreType.DMA((2, SLAB, 2))],
        compiler_params=pltpu.CompilerParams(vmem_limit_bytes=HELD_VMEM),
        cost_estimate=pl.CostEstimate(
            flops=0, bytes_accessed=16 * SLAB * rows * depth, transcendentals=0
        ),
        name="collect",
    )(*pieces)


def out_kernel(
    place, c20, c01, c31, c30, c11, c21, c10, c00, w, residual, scale, out, c_all, total, placed,
):
    z, q = place[0], place[1]
    width = c00.shape[0]
    for i, blocks in enumerate(((c00, c10, c20, c30), (c01, c11, c21, c31))):
        for r, c in enumerate(blocks):
            at = pl.multiple_of((i * SLAB + (q ^ r)) * width, width)
            c_all[pl.ds(at, width), :] = c[...]
    column = as_column(scale[...])[:out.shape[0]]
    column = jnp.tile(column, (1, out.shape[1] // 128))
    total[...] = jnp.dot(w[...], c_all[...], preferred_element_type=jnp.float32)
    rows, kept = w.shape[0] // (2 * SLAB), out.shape[0] // (2 * SLAB)
    for r in range(SLAB):
        for j in range(2):
            at = pl.multiple_of((((z % 2) ^ j) * SLAB + (q ^ r)) * kept, 8)
            begin = (2 * r + j) * rows
            placed[pl.ds(at, kept), :] = total[begin:begin + kept, :]
    out[...] = (residual[...].astype(jnp.float32) + column * placed[...]).astype(jnp.bfloat16)


def output(place, blocks, w, residual, scale):
    count = blocks[0].shape[1]
    rows, depth = w.shape
    share = residual.shape[0]
    return pl.pallas_call(
        out_kernel,
        out_shape=jax.ShapeDtypeStruct((share, count), jnp.bfloat16),
        in_specs=[SMEM] + [VMEM] * 11,
        out_specs=VMEM,
        scratch_shapes=[
            pltpu.VMEM((depth, count), jnp.bfloat16),
            pltpu.VMEM((rows, count), jnp.float32),
            pltpu.VMEM((share, count), jnp.float32),
        ],
        compiler_params=pltpu.CompilerParams(vmem_limit_bytes=HELD_VMEM),
        cost_estimate=pl.CostEstimate(
            flops=2 * share * count * depth,
            bytes_accessed=2 * share * depth,
            transcendentals=0,
        ),
        name="output",
    )(place, *blocks, w, residual, scale)


def rows_of_slab(q, got):
    placed = []
    for b in range(SLAB):
        piece = got[b]
        for other in range(1, SLAB):
            piece = jnp.where(q == other, got[b ^ other], piece)
        placed.append(piece)
    return jnp.concatenate(placed, axis=1)


def slab_plan(tokens, norm_gain, qkv_weight, q_gain, k_gain, out_weight, layer_scale, segment_ids):
    count = tokens.shape[0]
    seq, tp = lax.axis_index("seq"), lax.axis_index("tp")
    slabs = lax.axis_size("seq") // SLAB
    z, q = seq // SLAB, seq % SLAB
    place = jnp.stack([z, q, tp]).astype(jnp.int32)
    width = qkv_weight.shape[2] // SLAB
    full_width = qkv_weight.shape[2] * lax.axis_size("tp")
    slab, half = SLAB * count, 2 * count
    home = z // 2 == tp

    by_kind = jnp.transpose(qkv_weight, (1, 0, 2))
    cut = [lax.dynamic_slice_in_dim(by_kind, (q ^ r) * width, width, 2) for r in range(SLAB)]
    got = [cut[0]] + [in_slab(cut[r], r) for r in range(1, SLAB)]
    x0 = norm(tokens, norm_gain, slabs)
    out_own = jnp.transpose(out_weight)
    own = rows_of_slab(q, got)
    out_near, out_far = even_pair(out_own), half_pair(out_own)
    gains = [lax.dynamic_slice_in_dim(g, q * width, width, 0)[None] for g in (q_gain, k_gain)]

    outside = jnp.full((half,), -1, jnp.int32)
    seg = jnp.concatenate([outside, segment_ids, outside], axis=0)
    seg = lax.dynamic_slice_in_dim(seg, z * slab, slab + 2 * half, 0)
    spans = key_spans(seg, slab, count, half)
    seg = seg.astype(jnp.float32)[None]
    share = layer_scale.shape[0]
    residual = jnp.transpose(lax.dynamic_slice_in_dim(tokens, tp * share, share, 1))
    scale = jnp.pad(layer_scale, (0, -share % 128))[None]
    x0, out_near, out_far, seg, spans, residual, scale, *gains = tied(
        x0, out_near, out_far, seg, spans, residual, scale, *gains
    )
    out_last = even_pair(out_far)
    x2 = in_slab(x0, 2)
    far, near = half_pair(own), even_pair(own)
    close, away = jnp.stack([out_own, out_near]), jnp.stack([out_far, out_last])
    pad = ((0, 0), (0, -close.shape[1] % 16), (0, 0))
    keep = jnp.pad(jnp.where(home, close, away), pad)
    got = across(jnp.pad(jnp.where(home, away, close), pad))
    keep_x = in_slab(keep, 2)
    near, far, x0, x2, got, keep_x = tied(near, far, x0, x2, got, keep_x)
    last = even_pair(far)
    x1, x3 = in_slab(x0, 1), in_slab(x2, 1)
    got_x, got_c, keep_c = in_slab(got, 2), in_slab(got, 1), in_slab(keep, 1)
    keep_xc = in_slab(tied(keep_x, x3)[0], 1)
    xs = (x0, x1, x2, x3)
    acc, x_last = early(place, xs, own, near, far)
    last, acc, x_last = tied(last, acc, x_last)
    query, keys, values, squares, even, odd = late(place, x_last, acc, last, *gains)
    even, odd = even_pair(even), odd_pair(odd)
    squares, got_x, got_c, keep_c, keep_xc = tied(squares, got_x, got_c, keep_c, keep_xc)
    sums = squares
    for r in range(1, SLAB):
        sums = sums + in_slab(squares, r)
    sums = sums + across(sums)
    sums = (sums, even_pair(sums), odd_pair(sums))
    got_xc = in_slab(got_x, 1)

    blocks = attend(full_width, place, spans, query, keys, values, even, odd, sums, seg)
    *blocks, got_xc = tied(*blocks, got_xc)
    pieces = (keep, keep_c, keep_x, keep_xc, got, got_c, got_x, got_xc)
    spread = []
    for r, i in ((2, 0), (0, 1), (3, 1), (3, 0), (1, 1), (2, 1), (1, 0), (0, 0)):
        to = functools.partial(lambda r, i, z, q, y: (z, q ^ r, y ^ i), r, i)
        spread.append(permuted(blocks[r], to) if r or i else blocks[r])

    return jnp.transpose(output(place, spread, collect(pieces), residual, scale))


def solution(mesh):
    def shards(*args):
        heads = args[2].shape[2] // HEAD_DIM
        slab = mesh.shape["seq"] == 16 and mesh.shape["tp"] == 2 and heads % SLAB == 0
        return (slab_plan if slab else row_plan)(*args)

    return jax.shard_map(
        shards,
        mesh=mesh,
        in_specs=(
            P("seq", None),
            P(),
            P("seq", None, "tp"),
            P("tp"),
            P("tp"),
            P("tp", "seq"),
            P("tp"),
            P(),
        ),
        out_specs=P("seq", "tp"),
        check_vma=False,
    )
```

```python
import functools
import math

import jax
import jax.numpy as jnp
from jax import lax
from jax.experimental import pallas as pl
from jax.experimental.pallas import tpu as pltpu
from jax.sharding import PartitionSpec as P

HEAD_DIM = 128
SLAB = 4

eps = 1e-06
floor_score = -1e30


def passed_along(x, axis, by):
    size = lax.axis_size(axis)
    pairs = [(i, i + by) for i in range(size) if 0 <= i + by < size]
    return lax.ppermute(x, axis, pairs)


def masked_scores(query, keys, query_seg, key_seg):
    scores = jnp.einsum(
        "qhd,khd->hqk", query, keys, preferred_element_type=jnp.float32
    ) * HEAD_DIM ** (-0.5)
    mask = (query_seg[:, None] == key_seg[None, :])[None]
    return (jnp.where(mask, scores, floor_score), mask)


def row_plan(tokens, norm_gain, qkv_weight, q_gain, k_gain, out_weight, layer_scale, segment_ids):
    count = tokens.shape[0]
    source = tokens.astype(jnp.float32)
    normed = (
        source * lax.rsqrt(jnp.mean(source * source, axis=-1, keepdims=True) + eps) * norm_gain
    ).astype(jnp.bfloat16)
    local_width = qkv_weight.shape[2]
    heads = local_width // HEAD_DIM
    joined = jnp.einsum(
        "td,dch->tch",
        normed,
        lax.all_gather(qkv_weight, "seq", axis=0, tiled=True),
        preferred_element_type=jnp.float32,
    )
    query = joined[:, 0]
    keys = joined[:, 1]
    values = joined[:, 2]
    query_sq, key_sq = lax.psum(
        (jnp.sum(query * query, axis=-1), jnp.sum(keys * keys, axis=-1)), "tp"
    )
    full_width = local_width * lax.axis_size("tp")
    query_normed = (query * lax.rsqrt(query_sq / full_width + eps)[:, None] * q_gain).astype(
        jnp.bfloat16
    )
    key_normed = (keys * lax.rsqrt(key_sq / full_width + eps)[:, None] * k_gain).astype(
        jnp.bfloat16
    )
    paired = jnp.stack([key_normed, values.astype(jnp.bfloat16)], axis=1)
    pieces = []
    for offset in (2, 1, 0, -1, -2):
        if offset == 0:
            pieces.append(paired)
        else:
            pieces.append(passed_along(paired, "seq", offset))
    widened = jnp.concatenate(pieces, axis=0)
    position = lax.axis_index("seq")
    outside = jnp.full((2 * count,), -1, jnp.int32)
    seg_pad = jnp.concatenate([outside, segment_ids, outside], axis=0)
    key_seg = lax.dynamic_slice_in_dim(seg_pad, position * count, 5 * count, 0)
    query_seg = lax.dynamic_slice_in_dim(segment_ids, position * count, count, 0)
    query_heads = query_normed.reshape(count, heads, HEAD_DIM)
    key_heads = widened[:, 0].reshape(5 * count, heads, HEAD_DIM)
    value_heads = widened[:, 1].reshape(5 * count, heads, HEAD_DIM)
    scores, mask = masked_scores(query_heads, key_heads, query_seg, key_seg)
    peak = jnp.max(scores, axis=-1, keepdims=True)
    weights = jnp.where(mask, jnp.exp(scores - peak), 0.0)
    total = jnp.sum(weights, axis=-1)
    probs = weights.astype(jnp.bfloat16)
    summed = jnp.einsum("hqk,khd->qhd", probs, value_heads, preferred_element_type=jnp.float32)
    context = (
        (summed / jnp.transpose(total)[:, :, None]).reshape(count, local_width).astype(jnp.bfloat16)
    )
    terms = jnp.dot(
        context,
        lax.all_gather(out_weight, "seq", axis=1, tiled=True),
        preferred_element_type=jnp.float32,
    )
    projected = lax.psum_scatter(terms, "tp", scatter_dimension=1, tiled=True)
    share = layer_scale.shape[0]
    residual = lax.dynamic_slice_in_dim(source, lax.axis_index("tp") * share, share, 1)
    return (residual + layer_scale * projected).astype(jnp.bfloat16)


ANY = pl.BlockSpec(memory_space=pl.ANY)
VMEM = pl.BlockSpec(memory_space=pltpu.VMEM)
SMEM = pl.BlockSpec(memory_space=pltpu.SMEM)
HBM = pl.BlockSpec(memory_space=pltpu.HBM)
KERNEL_VMEM = 60 * 1024 * 1024
HELD_VMEM = 24 * 1024 * 1024


def permuted(x, to):
    slabs, tps = lax.axis_size("seq") // SLAB, lax.axis_size("tp")
    pairs = []
    for i in range(slabs * SLAB * tps):
        z, q, y = to(i // (SLAB * tps), i // tps % SLAB, i % tps)
        pairs.append((i, (z * SLAB + q) * tps + y))
    return lax.ppermute(x, ("seq", "tp"), pairs)


def in_slab(x, flip):
    return permuted(x, lambda z, q, y: (z, q ^ flip, y))


def across(x):
    return permuted(x, lambda z, q, y: (z, q, 1 - y))


def even_pair(x):
    return permuted(x, lambda z, q, y: (z ^ 1, q, y))


def odd_pair(x):
    return permuted(x, lambda z, q, y: (3 - z, q, y) if z in (1, 2) else (z, q ^ 1, y))


def half_pair(x):
    return permuted(x, lambda z, q, y: (z ^ 2, q, y))


def tied(*arrays):
    return lax.optimization_barrier(arrays)


def as_row(column):
    wide = jnp.broadcast_to(column, (column.shape[0], 128))
    return jnp.transpose(wide)[:8]


def as_column(row):
    return jnp.transpose(jnp.broadcast_to(row, (128, row.shape[1])))


def start(copies):
    for copy in copies:
        copy.start()


def wait(copies):
    for copy in copies:
        copy.wait()


def norm_kernel(tokens, gain, out):
    part = tokens.shape[1] // out.shape[0]
    source = tokens[...].astype(jnp.float32)
    mean = jnp.mean(source * source, axis=1, keepdims=True)
    normed = source * lax.rsqrt(mean + eps) * gain[...]
    for j in range(out.shape[0]):
        out[j, :, :part] = normed[:, j * part:(j + 1) * part].astype(jnp.bfloat16)
        out[j, :, part:] = jnp.zeros((out.shape[1], out.shape[2] - part), jnp.bfloat16)


def norm(tokens, gain, slabs):
    count, depth = tokens.shape
    shape = (slabs, count, pl.cdiv(depth // slabs, 128) * 128)
    return pl.pallas_call(
        norm_kernel,
        out_shape=jax.ShapeDtypeStruct(shape, jnp.bfloat16),
        in_specs=[VMEM, VMEM],
        out_specs=VMEM,
        compiler_params=pltpu.CompilerParams(vmem_limit_bytes=KERNEL_VMEM),
        name="norm",
    )(tokens, gain[None])


def token_copies(xs, at, out, sems):
    return [
        pltpu.make_async_copy(x.at[at], out.at[r], sems.at[r]) for r, x in enumerate(xs)
    ]


def blank_tail(w, rows):
    tail = w.shape[-2] - rows
    w[..., rows:, :] = jnp.zeros(w.shape[:-2] + (tail, w.shape[-1]), w.dtype)


def early_kernel(
    place, xa, xb, xc, xd, own, near, far, acc, x_last, x_all, w_all, x_sem, w_sem, last_sem,
):
    z = place[0]
    kinds, rows = own.shape[:2]
    copies = []
    for i, w in enumerate((own, near, far)):
        dst = w_all.at[i, :, pl.ds(0, rows), :]
        copies.append([pltpu.make_async_copy(w, dst, w_sem.at[i])])
        copies[i] += token_copies((xa, xb, xc, xd), z ^ i, x_all.at[i], x_sem.at[i])
        start(copies[i])
    last_copies = token_copies((xa, xb, xc, xd), z ^ 3, x_last, last_sem)
    start(last_copies)
    blank_tail(w_all, rows)
    for step in range(3):
        wait(copies[step])
        for r in range(SLAB):
            x = x_all[step, r]
            for kind in range(kinds):
                term = jnp.dot(x, w_all[step, kind], preferred_element_type=jnp.float32)
                acc[r, kind] = term if step == 0 else acc[r, kind] + term
    wait(last_copies)


def early(place, xs, own, near, far):
    kinds, rows, width = own.shape
    slabs, count, wide = xs[0].shape
    return pl.pallas_call(
        early_kernel,
        out_shape=(
            jax.ShapeDtypeStruct((SLAB, kinds, count, width), jnp.float32),
            jax.ShapeDtypeStruct((SLAB, count, wide), jnp.bfloat16),
        ),
        in_specs=[SMEM] + [HBM] * 7,
        out_specs=(VMEM, VMEM),
        scratch_shapes=[
            pltpu.VMEM((3, SLAB, count, wide), jnp.bfloat16),
            pltpu.VMEM((3, kinds, wide, width), jnp.bfloat16),
            pltpu.SemaphoreType.DMA((3, SLAB)),
            pltpu.SemaphoreType.DMA((3,)),
            pltpu.SemaphoreType.DMA((SLAB,)),
        ],
        compiler_params=pltpu.CompilerParams(vmem_limit_bytes=HELD_VMEM),
        cost_estimate=pl.CostEstimate(
            flops=12 * kinds * SLAB * count * rows * width,
            bytes_accessed=6 * kinds * rows * width + 6 * SLAB * count * rows,
            transcendentals=0,
        ),
        name="early",
    )(place, *xs, own, near, far)


def late_kernel(
    place, x_last, acc, last, q_gain, k_gain, query, keys, values, squares, even, odd, w_all,
):
    z, q = place[0], place[1]
    rows = last.shape[1]
    w_all[:, :rows, :] = last[...]
    blank_tail(w_all, rows)
    count = acc.shape[2]
    for r in range(SLAB):
        rows = pl.ds(pl.multiple_of((q ^ r) * count, count), count)
        for kind in range(3):
            part = acc[r, kind] + jnp.dot(
                x_last[r], w_all[kind], preferred_element_type=jnp.float32
            )
            if kind < 2:
                summed = as_row(jnp.sum(part * part, axis=1, keepdims=True))
                squares[kind:kind + 1, rows] = summed[:1]
                part = part * (q_gain, k_gain)[kind][...]
            out = (query, keys, values)[kind]
            out[rows, :] = part.astype(out.dtype)
    reach = even.shape[1]
    for out, at in ((even, 1 - z % 2), (odd, z % 2)):
        rows = pl.ds(pl.multiple_of(at * reach, reach), reach)
        out[0] = keys[rows, :]
        out[1] = values[rows, :]


def late(place, x_last, acc, last, q_gain, k_gain):
    kinds, rows, width = last.shape
    count, wide = x_last.shape[1:]
    slab = SLAB * count
    f32, bf16 = jnp.float32, jnp.bfloat16
    return pl.pallas_call(
        late_kernel,
        out_shape=(
            jax.ShapeDtypeStruct((slab, width), f32),
            jax.ShapeDtypeStruct((slab, width), bf16),
            jax.ShapeDtypeStruct((slab, width), bf16),
            jax.ShapeDtypeStruct((2, slab), f32),
            jax.ShapeDtypeStruct((2, 2 * count, width), bf16),
            jax.ShapeDtypeStruct((2, 2 * count, width), bf16),
        ),
        in_specs=[SMEM] + [VMEM] * 5,
        out_specs=(VMEM,) * 6,
        scratch_shapes=[
            pltpu.VMEM((kinds, wide, width), bf16),
        ],
        compiler_params=pltpu.CompilerParams(vmem_limit_bytes=HELD_VMEM),
        cost_estimate=pl.CostEstimate(
            flops=2 * kinds * slab * rows * width,
            bytes_accessed=2 * kinds * rows * width + 2 * slab * rows,
            transcendentals=0,
        ),
        name="late",
    )(place, x_last, acc, last, q_gain, k_gain)


def attend_kernel(
    full_width, place, spans, query, keys, values, even, odd, mine, near, mid, seg, o0, o1, o2, o3,
    k_all, v_all, o_all, scale_all,
):
    z, q = place[0], place[1]
    slab = query.shape[0]
    count = slab // SLAB
    half = even.shape[1]
    upper = half + slab
    is_even = z % 2 == 0
    even_at = pl.multiple_of(jnp.where(is_even, upper, 0), half)
    odd_at = pl.multiple_of(jnp.where(is_even, 0, upper), half)
    for k, (whole, out) in enumerate(((keys, k_all), (values, v_all))):
        out[half:upper, :] = whole[...]
        out[pl.ds(even_at, half), :] = even[k]
        out[pl.ds(odd_at, half), :] = odd[k]
    scale = [lax.rsqrt(sums[...] / full_width + eps) for sums in (mine, near, mid)]
    scale_all[:, half:upper] = scale[0]
    scale_all[:, :half] = jnp.where(is_even, scale[2], scale[1])[:, slab - half:]
    scale_all[:, upper:] = jnp.where(is_even, scale[1], scale[2])[:, :half]
    heads = query.shape[1] // HEAD_DIM
    factor = HEAD_DIM ** (-0.5) * math.log2(math.e)

    def block(r, _):
        b = q ^ r
        at_query = pl.multiple_of(b * count + half, count)
        query_seg = as_column(seg[:, pl.ds(at_query, count)])
        q_scale = as_column(scale_all[0:1, pl.ds(at_query, count)])
        for tiles in range(2, 2 * half // count + 2):
            @pl.when(spans[b, 1] == tiles)
            def _():
                width = tiles * count
                begin = pl.multiple_of(spans[b, 0], 128)
                keys_at = pl.ds(begin, width)
                mask = jnp.tile(query_seg, (1, width // 128)) == seg[:, keys_at]
                k_scale = scale_all[1:2, keys_at] * factor
                all_cols = [slice(h * HEAD_DIM, (h + 1) * HEAD_DIM) for h in range(heads)]
                rows = pl.ds(pl.multiple_of(b * count, count), count)
                scores = [
                    lax.dot_general(
                        (query[rows, cols] * q_scale).astype(jnp.bfloat16), k_all[keys_at, cols],
                        (((1,), (1,)), ((), ())), preferred_element_type=jnp.float32,
                    )
                    for cols in all_cols
                ]
                parts = []
                for s in scores:
                    s = jnp.where(mask, s * k_scale, floor_score)
                    weights = jnp.exp2(s - jnp.max(s, axis=1, keepdims=True))
                    total = jnp.sum(weights, axis=1, keepdims=True)
                    parts.append((weights.astype(jnp.bfloat16), total))
                for cols, (probs, total) in zip(all_cols, parts):
                    summed = jnp.dot(
                        probs, v_all[keys_at, cols], preferred_element_type=jnp.float32
                    )
                    o_all[r, cols, :] = jnp.transpose(summed / total).astype(jnp.bfloat16)

        return 0

    lax.fori_loop(0, SLAB, block, 0)
    for r, out in enumerate((o0, o1, o2, o3)):
        out[...] = o_all[r]


def key_spans(seg, slab, count, half):
    ext = seg.shape[0]
    index = jnp.arange(ext, dtype=jnp.int32)
    blocks = seg[half:half + slab].reshape(-1, count)
    first, last = blocks[:, :1], blocks[:, -1:]
    begin = jnp.min(jnp.where(seg == first, index, ext), axis=1) // 128 * 128
    end = jnp.max(jnp.where(seg == last, index, -1), axis=1) + 1
    tiles = jnp.maximum((end - begin + count - 1) // count, 2)
    return jnp.stack([jnp.minimum(begin, ext - tiles * count), tiles], axis=1)


def attend(full_width, place, spans, query, keys, values, even, odd, sums, seg):
    slab, width = query.shape
    half = even.shape[1]
    count = slab // SLAB
    ext = slab + 2 * half
    bf16 = jnp.bfloat16
    window = count + 2 * half
    return pl.pallas_call(
        functools.partial(attend_kernel, full_width),
        out_shape=(jax.ShapeDtypeStruct((width, count), bf16),) * SLAB,
        in_specs=[SMEM] * 2 + [VMEM] * 9,
        out_specs=(VMEM,) * SLAB,
        scratch_shapes=[
            pltpu.VMEM((ext, width), bf16),
            pltpu.VMEM((ext, width), bf16),
            pltpu.VMEM((SLAB, width, count), bf16),
            pltpu.VMEM((2, ext), jnp.float32),
        ],
        compiler_params=pltpu.CompilerParams(vmem_limit_bytes=HELD_VMEM),
        cost_estimate=pl.CostEstimate(
            flops=64 * SLAB * count * window * width,
            bytes_accessed=4 * ext * width + 4 * slab * width,
            transcendentals=SLAB * count * window * width // HEAD_DIM,
        ),
        name="attend",
    )(place, spans, query, keys, values, even, odd, *sums, seg)


def collect_kernel(wa0, wb0, wc0, wd0, wa1, wb1, wc1, wd1, out, sems):
    rows, depth = wa0.shape[1:]
    copies = []
    for i, ws in enumerate(((wa0, wb0, wc0, wd0), (wa1, wb1, wc1, wd1))):
        for r, w in enumerate(ws):
            for j in range(2):
                dst = out.at[pl.ds((2 * r + j) * rows, rows), pl.ds(i * depth, depth)]
                copies.append(pltpu.make_async_copy(w.at[j], dst, sems.at[i, r, j]))
    start(copies)
    wait(copies)


def collect(pieces):
    rows, depth = pieces[0].shape[1:]
    return pl.pallas_call(
        collect_kernel,
        out_shape=jax.ShapeDtypeStruct((2 * SLAB * rows, 2 * depth), jnp.bfloat16),
        in_specs=[HBM] * 8,
        out_specs=VMEM,
        scratch_shapes=[pltpu.SemaphoreType.DMA((2, SLAB, 2))],
        compiler_params=pltpu.CompilerParams(vmem_limit_bytes=HELD_VMEM),
        cost_estimate=pl.CostEstimate(
            flops=0, bytes_accessed=16 * SLAB * rows * depth, transcendentals=0
        ),
        name="collect",
    )(*pieces)


def out_kernel(
    place, c31, c21, c20, c01, c30, c11, c10, c00, w, residual, scale, out, c_all, total, placed,
):
    z, q = place[0], place[1]
    width = c00.shape[0]
    for i, blocks in enumerate(((c00, c10, c20, c30), (c01, c11, c21, c31))):
        for r, c in enumerate(blocks):
            at = pl.multiple_of((i * SLAB + (q ^ r)) * width, width)
            c_all[pl.ds(at, width), :] = c[...]
    column = as_column(scale[...])[:out.shape[0]]
    column = jnp.tile(column, (1, out.shape[1] // 128))
    total[...] = jnp.dot(w[...], c_all[...], preferred_element_type=jnp.float32)
    rows, kept = w.shape[0] // (2 * SLAB), out.shape[0] // (2 * SLAB)
    for r in range(SLAB):
        for j in range(2):
            at = pl.multiple_of((((z % 2) ^ j) * SLAB + (q ^ r)) * kept, 8)
            begin = (2 * r + j) * rows
            placed[pl.ds(at, kept), :] = total[begin:begin + kept, :]
    out[...] = (residual[...].astype(jnp.float32) + column * placed[...]).astype(jnp.bfloat16)


def output(place, blocks, w, residual, scale):
    count = blocks[0].shape[1]
    rows, depth = w.shape
    share = residual.shape[0]
    return pl.pallas_call(
        out_kernel,
        out_shape=jax.ShapeDtypeStruct((share, count), jnp.bfloat16),
        in_specs=[SMEM] + [VMEM] * 11,
        out_specs=VMEM,
        scratch_shapes=[
            pltpu.VMEM((depth, count), jnp.bfloat16),
            pltpu.VMEM((rows, count), jnp.float32),
            pltpu.VMEM((share, count), jnp.float32),
        ],
        compiler_params=pltpu.CompilerParams(vmem_limit_bytes=HELD_VMEM),
        cost_estimate=pl.CostEstimate(
            flops=2 * share * count * depth,
            bytes_accessed=2 * share * depth,
            transcendentals=0,
        ),
        name="output",
    )(place, *blocks, w, residual, scale)


def rows_of_slab(q, got):
    placed = []
    for b in range(SLAB):
        piece = got[b]
        for other in range(1, SLAB):
            piece = jnp.where(q == other, got[b ^ other], piece)
        placed.append(piece)
    return jnp.concatenate(placed, axis=1)


def slab_plan(tokens, norm_gain, qkv_weight, q_gain, k_gain, out_weight, layer_scale, segment_ids):
    count = tokens.shape[0]
    seq, tp = lax.axis_index("seq"), lax.axis_index("tp")
    slabs = lax.axis_size("seq") // SLAB
    z, q = seq // SLAB, seq % SLAB
    place = jnp.stack([z, q, tp]).astype(jnp.int32)
    width = qkv_weight.shape[2] // SLAB
    full_width = qkv_weight.shape[2] * lax.axis_size("tp")
    slab, half = SLAB * count, 2 * count
    home = z // 2 == tp

    by_kind = jnp.transpose(qkv_weight, (1, 0, 2))
    cut = [lax.dynamic_slice_in_dim(by_kind, (q ^ r) * width, width, 2) for r in range(SLAB)]
    got = [cut[0]] + [in_slab(cut[r], r) for r in range(1, SLAB)]
    x0 = norm(tokens, norm_gain, slabs)
    out_own = jnp.transpose(out_weight)
    own = rows_of_slab(q, got)
    out_near, out_far = even_pair(out_own), half_pair(out_own)
    gains = [lax.dynamic_slice_in_dim(g, q * width, width, 0)[None] for g in (q_gain, k_gain)]

    outside = jnp.full((half,), -1, jnp.int32)
    seg = jnp.concatenate([outside, segment_ids, outside], axis=0)
    seg = lax.dynamic_slice_in_dim(seg, z * slab, slab + 2 * half, 0)
    spans = key_spans(seg, slab, count, half)
    seg = seg.astype(jnp.float32)[None]
    share = layer_scale.shape[0]
    residual = jnp.transpose(lax.dynamic_slice_in_dim(tokens, tp * share, share, 1))
    scale = jnp.pad(layer_scale, (0, -share % 128))[None]
    x0, out_near, out_far, seg, spans, residual, scale, *gains = tied(
        x0, out_near, out_far, seg, spans, residual, scale, *gains
    )
    out_last = even_pair(out_far)
    x2 = in_slab(x0, 2)
    far, near = half_pair(own), even_pair(own)
    close, away = jnp.stack([out_own, out_near]), jnp.stack([out_far, out_last])
    pad = ((0, 0), (0, -close.shape[1] % 16), (0, 0))
    keep = jnp.pad(jnp.where(home, close, away), pad)
    got = across(jnp.pad(jnp.where(home, away, close), pad))
    keep_x = in_slab(keep, 2)
    near, far, x0, x2, got, keep_x = tied(near, far, x0, x2, got, keep_x)
    last = even_pair(far)
    x1, x3 = in_slab(x0, 1), in_slab(x2, 1)
    got_x, got_c, keep_c = in_slab(got, 2), in_slab(got, 1), in_slab(keep, 1)
    keep_xc = in_slab(tied(keep_x, x3)[0], 1)
    xs = (x0, x1, x2, x3)
    acc, x_last = early(place, xs, own, near, far)
    last, acc, x_last = tied(last, acc, x_last)
    query, keys, values, squares, even, odd = late(place, x_last, acc, last, *gains)
    even, odd = even_pair(even), odd_pair(odd)
    squares, got_x, got_c, keep_c, keep_xc = tied(squares, got_x, got_c, keep_c, keep_xc)
    sums = squares
    for r in range(1, SLAB):
        sums = sums + in_slab(squares, r)
    sums = sums + across(sums)
    sums = (sums, even_pair(sums), odd_pair(sums))
    got_xc = in_slab(got_x, 1)

    blocks = attend(full_width, place, spans, query, keys, values, even, odd, sums, seg)
    *blocks, got_xc = tied(*blocks, got_xc)
    pieces = (keep, keep_c, keep_x, keep_xc, got, got_c, got_x, got_xc)
    spread = []
    for r, i in ((3, 1), (2, 1), (2, 0), (0, 1), (3, 0), (1, 1), (1, 0), (0, 0)):
        to = functools.partial(lambda r, i, z, q, y: (z, q ^ r, y ^ i), r, i)
        spread.append(permuted(blocks[r], to) if r or i else blocks[r])

    return jnp.transpose(output(place, spread, collect(pieces), residual, scale))


def solution(mesh):
    def shards(*args):
        heads = args[2].shape[2] // HEAD_DIM
        slab = mesh.shape["seq"] == 16 and mesh.shape["tp"] == 2 and heads % SLAB == 0
        return (slab_plan if slab else row_plan)(*args)

    return jax.shard_map(
        shards,
        mesh=mesh,
        in_specs=(
            P("seq", None),
            P(),
            P("seq", None, "tp"),
            P("tp"),
            P("tp"),
            P("tp", "seq"),
            P("tp"),
            P(),
        ),
        out_specs=P("seq", "tp"),
        check_vma=False,
    )
```

```python
import functools
import math

import jax
import jax.numpy as jnp
from jax import lax
from jax.experimental import pallas as pl
from jax.experimental.pallas import tpu as pltpu
from jax.sharding import PartitionSpec as P

HEAD_DIM = 128
SLAB = 4

eps = 1e-06
floor_score = -1e30


def passed_along(x, axis, by):
    size = lax.axis_size(axis)
    pairs = [(i, i + by) for i in range(size) if 0 <= i + by < size]
    return lax.ppermute(x, axis, pairs)


def masked_scores(query, keys, query_seg, key_seg):
    scores = jnp.einsum(
        "qhd,khd->hqk", query, keys, preferred_element_type=jnp.float32
    ) * HEAD_DIM ** (-0.5)
    mask = (query_seg[:, None] == key_seg[None, :])[None]
    return (jnp.where(mask, scores, floor_score), mask)


def row_plan(tokens, norm_gain, qkv_weight, q_gain, k_gain, out_weight, layer_scale, segment_ids):
    count = tokens.shape[0]
    source = tokens.astype(jnp.float32)
    normed = (
        source * lax.rsqrt(jnp.mean(source * source, axis=-1, keepdims=True) + eps) * norm_gain
    ).astype(jnp.bfloat16)
    local_width = qkv_weight.shape[2]
    heads = local_width // HEAD_DIM
    joined = jnp.einsum(
        "td,dch->tch",
        normed,
        lax.all_gather(qkv_weight, "seq", axis=0, tiled=True),
        preferred_element_type=jnp.float32,
    )
    query = joined[:, 0]
    keys = joined[:, 1]
    values = joined[:, 2]
    query_sq, key_sq = lax.psum(
        (jnp.sum(query * query, axis=-1), jnp.sum(keys * keys, axis=-1)), "tp"
    )
    full_width = local_width * lax.axis_size("tp")
    query_normed = (query * lax.rsqrt(query_sq / full_width + eps)[:, None] * q_gain).astype(
        jnp.bfloat16
    )
    key_normed = (keys * lax.rsqrt(key_sq / full_width + eps)[:, None] * k_gain).astype(
        jnp.bfloat16
    )
    paired = jnp.stack([key_normed, values.astype(jnp.bfloat16)], axis=1)
    pieces = []
    for offset in (2, 1, 0, -1, -2):
        if offset == 0:
            pieces.append(paired)
        else:
            pieces.append(passed_along(paired, "seq", offset))
    widened = jnp.concatenate(pieces, axis=0)
    position = lax.axis_index("seq")
    outside = jnp.full((2 * count,), -1, jnp.int32)
    seg_pad = jnp.concatenate([outside, segment_ids, outside], axis=0)
    key_seg = lax.dynamic_slice_in_dim(seg_pad, position * count, 5 * count, 0)
    query_seg = lax.dynamic_slice_in_dim(segment_ids, position * count, count, 0)
    query_heads = query_normed.reshape(count, heads, HEAD_DIM)
    key_heads = widened[:, 0].reshape(5 * count, heads, HEAD_DIM)
    value_heads = widened[:, 1].reshape(5 * count, heads, HEAD_DIM)
    scores, mask = masked_scores(query_heads, key_heads, query_seg, key_seg)
    peak = jnp.max(scores, axis=-1, keepdims=True)
    weights = jnp.where(mask, jnp.exp(scores - peak), 0.0)
    total = jnp.sum(weights, axis=-1)
    probs = weights.astype(jnp.bfloat16)
    summed = jnp.einsum("hqk,khd->qhd", probs, value_heads, preferred_element_type=jnp.float32)
    context = (
        (summed / jnp.transpose(total)[:, :, None]).reshape(count, local_width).astype(jnp.bfloat16)
    )
    terms = jnp.dot(
        context,
        lax.all_gather(out_weight, "seq", axis=1, tiled=True),
        preferred_element_type=jnp.float32,
    )
    projected = lax.psum_scatter(terms, "tp", scatter_dimension=1, tiled=True)
    share = layer_scale.shape[0]
    residual = lax.dynamic_slice_in_dim(source, lax.axis_index("tp") * share, share, 1)
    return (residual + layer_scale * projected).astype(jnp.bfloat16)


ANY = pl.BlockSpec(memory_space=pl.ANY)
VMEM = pl.BlockSpec(memory_space=pltpu.VMEM)
SMEM = pl.BlockSpec(memory_space=pltpu.SMEM)
HBM = pl.BlockSpec(memory_space=pltpu.HBM)
KERNEL_VMEM = 60 * 1024 * 1024
HELD_VMEM = 24 * 1024 * 1024


def permuted(x, to):
    slabs, tps = lax.axis_size("seq") // SLAB, lax.axis_size("tp")
    pairs = []
    for i in range(slabs * SLAB * tps):
        z, q, y = to(i // (SLAB * tps), i // tps % SLAB, i % tps)
        pairs.append((i, (z * SLAB + q) * tps + y))
    return lax.ppermute(x, ("seq", "tp"), pairs)


def in_slab(x, flip):
    return permuted(x, lambda z, q, y: (z, q ^ flip, y))


def across(x):
    return permuted(x, lambda z, q, y: (z, q, 1 - y))


def even_pair(x):
    return permuted(x, lambda z, q, y: (z ^ 1, q, y))


def odd_pair(x):
    return permuted(x, lambda z, q, y: (3 - z, q, y) if z in (1, 2) else (z, q ^ 1, y))


def half_pair(x):
    return permuted(x, lambda z, q, y: (z ^ 2, q, y))


def tied(*arrays):
    return lax.optimization_barrier(arrays)


def as_row(column):
    wide = jnp.broadcast_to(column, (column.shape[0], 128))
    return jnp.transpose(wide)[:8]


def as_column(row):
    return jnp.transpose(jnp.broadcast_to(row, (128, row.shape[1])))


def start(copies):
    for copy in copies:
        copy.start()


def wait(copies):
    for copy in copies:
        copy.wait()


def norm_kernel(tokens, gain, out):
    part = tokens.shape[1] // out.shape[0]
    source = tokens[...].astype(jnp.float32)
    mean = jnp.mean(source * source, axis=1, keepdims=True)
    normed = source * lax.rsqrt(mean + eps) * gain[...]
    for j in range(out.shape[0]):
        out[j, :, :part] = normed[:, j * part:(j + 1) * part].astype(jnp.bfloat16)
        out[j, :, part:] = jnp.zeros((out.shape[1], out.shape[2] - part), jnp.bfloat16)


def norm(tokens, gain, slabs):
    count, depth = tokens.shape
    shape = (slabs, count, pl.cdiv(depth // slabs, 128) * 128)
    return pl.pallas_call(
        norm_kernel,
        out_shape=jax.ShapeDtypeStruct(shape, jnp.bfloat16),
        in_specs=[VMEM, VMEM],
        out_specs=VMEM,
        compiler_params=pltpu.CompilerParams(vmem_limit_bytes=KERNEL_VMEM),
        name="norm",
    )(tokens, gain[None])


def token_copies(xs, at, out, sems):
    return [
        pltpu.make_async_copy(x.at[at], out.at[r], sems.at[r]) for r, x in enumerate(xs)
    ]


def blank_tail(w, rows):
    tail = w.shape[-2] - rows
    w[..., rows:, :] = jnp.zeros(w.shape[:-2] + (tail, w.shape[-1]), w.dtype)


def early_kernel(
    place, xa, xb, xc, xd, own, near, far, acc, x_last, x_all, w_all, x_sem, w_sem, last_sem,
):
    z = place[0]
    kinds, rows = own.shape[:2]
    copies = []
    for i, w in enumerate((own, near, far)):
        dst = w_all.at[i, :, pl.ds(0, rows), :]
        copies.append([pltpu.make_async_copy(w, dst, w_sem.at[i])])
        copies[i] += token_copies((xa, xb, xc, xd), z ^ i, x_all.at[i], x_sem.at[i])
        start(copies[i])
    last_copies = token_copies((xa, xb, xc, xd), z ^ 3, x_last, last_sem)
    start(last_copies)
    blank_tail(w_all, rows)
    for step in range(3):
        wait(copies[step])
        for r in range(SLAB):
            x = x_all[step, r]
            for kind in range(kinds):
                term = jnp.dot(x, w_all[step, kind], preferred_element_type=jnp.float32)
                acc[r, kind] = term if step == 0 else acc[r, kind] + term
    wait(last_copies)


def early(place, xs, own, near, far):
    kinds, rows, width = own.shape
    slabs, count, wide = xs[0].shape
    return pl.pallas_call(
        early_kernel,
        out_shape=(
            jax.ShapeDtypeStruct((SLAB, kinds, count, width), jnp.float32),
            jax.ShapeDtypeStruct((SLAB, count, wide), jnp.bfloat16),
        ),
        in_specs=[SMEM] + [HBM] * 7,
        out_specs=(VMEM, VMEM),
        scratch_shapes=[
            pltpu.VMEM((3, SLAB, count, wide), jnp.bfloat16),
            pltpu.VMEM((3, kinds, wide, width), jnp.bfloat16),
            pltpu.SemaphoreType.DMA((3, SLAB)),
            pltpu.SemaphoreType.DMA((3,)),
            pltpu.SemaphoreType.DMA((SLAB,)),
        ],
        compiler_params=pltpu.CompilerParams(vmem_limit_bytes=HELD_VMEM),
        cost_estimate=pl.CostEstimate(
            flops=12 * kinds * SLAB * count * rows * width,
            bytes_accessed=6 * kinds * rows * width + 6 * SLAB * count * rows,
            transcendentals=0,
        ),
        name="early",
    )(place, *xs, own, near, far)


def late_kernel(
    place, x_last, acc, last, q_gain, k_gain, query, keys, values, squares, even, odd, w_all,
):
    z, q = place[0], place[1]
    rows = last.shape[1]
    w_all[:, :rows, :] = last[...]
    blank_tail(w_all, rows)
    count = acc.shape[2]
    for r in range(SLAB):
        rows = pl.ds(pl.multiple_of((q ^ r) * count, count), count)
        for kind in range(3):
            part = acc[r, kind] + jnp.dot(
                x_last[r], w_all[kind], preferred_element_type=jnp.float32
            )
            if kind < 2:
                summed = as_row(jnp.sum(part * part, axis=1, keepdims=True))
                squares[kind:kind + 1, rows] = summed[:1]
                part = part * (q_gain, k_gain)[kind][...]
            out = (query, keys, values)[kind]
            out[rows, :] = part.astype(out.dtype)
    reach = even.shape[1]
    for out, at in ((even, 1 - z % 2), (odd, z % 2)):
        rows = pl.ds(pl.multiple_of(at * reach, reach), reach)
        out[0] = keys[rows, :]
        out[1] = values[rows, :]


def late(place, x_last, acc, last, q_gain, k_gain):
    kinds, rows, width = last.shape
    count, wide = x_last.shape[1:]
    slab = SLAB * count
    f32, bf16 = jnp.float32, jnp.bfloat16
    return pl.pallas_call(
        late_kernel,
        out_shape=(
            jax.ShapeDtypeStruct((slab, width), f32),
            jax.ShapeDtypeStruct((slab, width), bf16),
            jax.ShapeDtypeStruct((slab, width), bf16),
            jax.ShapeDtypeStruct((2, slab), f32),
            jax.ShapeDtypeStruct((2, 2 * count, width), bf16),
            jax.ShapeDtypeStruct((2, 2 * count, width), bf16),
        ),
        in_specs=[SMEM] + [VMEM] * 5,
        out_specs=(VMEM,) * 6,
        scratch_shapes=[
            pltpu.VMEM((kinds, wide, width), bf16),
        ],
        compiler_params=pltpu.CompilerParams(vmem_limit_bytes=HELD_VMEM),
        cost_estimate=pl.CostEstimate(
            flops=2 * kinds * slab * rows * width,
            bytes_accessed=2 * kinds * rows * width + 2 * slab * rows,
            transcendentals=0,
        ),
        name="late",
    )(place, x_last, acc, last, q_gain, k_gain)


def attend_kernel(
    full_width, place, spans, query, keys, values, even, odd, mine, near, mid, seg, o0, o1, o2, o3,
    k_all, v_all, o_all, scale_all,
):
    z, q = place[0], place[1]
    slab = query.shape[0]
    count = slab // SLAB
    half = even.shape[1]
    upper = half + slab
    is_even = z % 2 == 0
    even_at = pl.multiple_of(jnp.where(is_even, upper, 0), half)
    odd_at = pl.multiple_of(jnp.where(is_even, 0, upper), half)
    for k, (whole, out) in enumerate(((keys, k_all), (values, v_all))):
        out[half:upper, :] = whole[...]
        out[pl.ds(even_at, half), :] = even[k]
        out[pl.ds(odd_at, half), :] = odd[k]
    scale = [lax.rsqrt(sums[...] / full_width + eps) for sums in (mine, near, mid)]
    scale_all[:, half:upper] = scale[0]
    scale_all[:, :half] = jnp.where(is_even, scale[2], scale[1])[:, slab - half:]
    scale_all[:, upper:] = jnp.where(is_even, scale[1], scale[2])[:, :half]
    heads = query.shape[1] // HEAD_DIM
    factor = HEAD_DIM ** (-0.5) * math.log2(math.e)

    def block(r, _):
        b = q ^ r
        at_query = pl.multiple_of(b * count + half, count)
        query_seg = as_column(seg[:, pl.ds(at_query, count)])
        q_scale = as_column(scale_all[0:1, pl.ds(at_query, count)])
        for tiles in range(2, 2 * half // count + 2):
            @pl.when(spans[b, 1] == tiles)
            def _():
                width = tiles * count
                begin = pl.multiple_of(spans[b, 0], 128)
                keys_at = pl.ds(begin, width)
                mask = jnp.tile(query_seg, (1, width // 128)) == seg[:, keys_at]
                k_scale = scale_all[1:2, keys_at] * factor
                all_cols = [slice(h * HEAD_DIM, (h + 1) * HEAD_DIM) for h in range(heads)]
                rows = pl.ds(pl.multiple_of(b * count, count), count)
                scores = [
                    lax.dot_general(
                        (query[rows, cols] * q_scale).astype(jnp.bfloat16), k_all[keys_at, cols],
                        (((1,), (1,)), ((), ())), preferred_element_type=jnp.float32,
                    )
                    for cols in all_cols
                ]
                parts = []
                for s in scores:
                    s = jnp.where(mask, s * k_scale, floor_score)
                    weights = jnp.exp2(s - jnp.max(s, axis=1, keepdims=True))
                    total = jnp.sum(weights, axis=1, keepdims=True)
                    parts.append((weights.astype(jnp.bfloat16), total))
                for cols, (probs, total) in zip(all_cols, parts):
                    summed = jnp.dot(
                        probs, v_all[keys_at, cols], preferred_element_type=jnp.float32
                    )
                    o_all[r, cols, :] = jnp.transpose(summed / total).astype(jnp.bfloat16)

        return 0

    lax.fori_loop(0, SLAB, block, 0)
    for r, out in enumerate((o0, o1, o2, o3)):
        out[...] = o_all[r]


def key_spans(seg, slab, count, half):
    ext = seg.shape[0]
    index = jnp.arange(ext, dtype=jnp.int32)
    blocks = seg[half:half + slab].reshape(-1, count)
    first, last = blocks[:, :1], blocks[:, -1:]
    begin = jnp.min(jnp.where(seg == first, index, ext), axis=1) // 128 * 128
    end = jnp.max(jnp.where(seg == last, index, -1), axis=1) + 1
    tiles = jnp.maximum((end - begin + count - 1) // count, 2)
    return jnp.stack([jnp.minimum(begin, ext - tiles * count), tiles], axis=1)


def attend(full_width, place, spans, query, keys, values, even, odd, sums, seg):
    slab, width = query.shape
    half = even.shape[1]
    count = slab // SLAB
    ext = slab + 2 * half
    bf16 = jnp.bfloat16
    window = count + 2 * half
    return pl.pallas_call(
        functools.partial(attend_kernel, full_width),
        out_shape=(jax.ShapeDtypeStruct((width, count), bf16),) * SLAB,
        in_specs=[SMEM] * 2 + [VMEM] * 9,
        out_specs=(VMEM,) * SLAB,
        scratch_shapes=[
            pltpu.VMEM((ext, width), bf16),
            pltpu.VMEM((ext, width), bf16),
            pltpu.VMEM((SLAB, width, count), bf16),
            pltpu.VMEM((2, ext), jnp.float32),
        ],
        compiler_params=pltpu.CompilerParams(vmem_limit_bytes=HELD_VMEM),
        cost_estimate=pl.CostEstimate(
            flops=64 * SLAB * count * window * width,
            bytes_accessed=4 * ext * width + 4 * slab * width,
            transcendentals=SLAB * count * window * width // HEAD_DIM,
        ),
        name="attend",
    )(place, spans, query, keys, values, even, odd, *sums, seg)


def collect_kernel(wa0, wb0, wc0, wd0, wa1, wb1, wc1, wd1, out, sems):
    rows, depth = wa0.shape[1:]
    copies = []
    for i, ws in enumerate(((wa0, wb0, wc0, wd0), (wa1, wb1, wc1, wd1))):
        for r, w in enumerate(ws):
            for j in range(2):
                dst = out.at[pl.ds((2 * r + j) * rows, rows), pl.ds(i * depth, depth)]
                copies.append(pltpu.make_async_copy(w.at[j], dst, sems.at[i, r, j]))
    start(copies)
    wait(copies)


def collect(pieces):
    rows, depth = pieces[0].shape[1:]
    return pl.pallas_call(
        collect_kernel,
        out_shape=jax.ShapeDtypeStruct((2 * SLAB * rows, 2 * depth), jnp.bfloat16),
        in_specs=[HBM] * 8,
        out_specs=VMEM,
        scratch_shapes=[pltpu.SemaphoreType.DMA((2, SLAB, 2))],
        compiler_params=pltpu.CompilerParams(vmem_limit_bytes=HELD_VMEM),
        cost_estimate=pl.CostEstimate(
            flops=0, bytes_accessed=16 * SLAB * rows * depth, transcendentals=0
        ),
        name="collect",
    )(*pieces)


def out_kernel(
    place, c20, c01, c31, c30, c11, c21, c10, c00, w, residual, scale, out, c_all, placed,
):
    z, q = place[0], place[1]
    width = c00.shape[0]
    for i, blocks in enumerate(((c00, c10, c20, c30), (c01, c11, c21, c31))):
        for r, c in enumerate(blocks):
            at = pl.multiple_of((i * SLAB + (q ^ r)) * width, width)
            c_all[pl.ds(at, width), :] = c[...]
    column = as_column(scale[...])[:out.shape[0]]
    column = jnp.tile(column, (1, out.shape[1] // 128))
    rows, kept = w.shape[0] // (2 * SLAB), out.shape[0] // (2 * SLAB)
    for r in range(SLAB):
        for j in range(2):
            at = pl.multiple_of((((z % 2) ^ j) * SLAB + (q ^ r)) * kept, 8)
            begin = (2 * r + j) * rows
            total = jnp.dot(
                w[begin:begin + rows, :], c_all[...], preferred_element_type=jnp.float32
            )
            placed[pl.ds(at, kept), :] = total[:kept]
    out[...] = (residual[...].astype(jnp.float32) + column * placed[...]).astype(jnp.bfloat16)


def output(place, blocks, w, residual, scale):
    count = blocks[0].shape[1]
    rows, depth = w.shape
    share = residual.shape[0]
    return pl.pallas_call(
        out_kernel,
        out_shape=jax.ShapeDtypeStruct((share, count), jnp.bfloat16),
        in_specs=[SMEM] + [VMEM] * 11,
        out_specs=VMEM,
        scratch_shapes=[
            pltpu.VMEM((depth, count), jnp.bfloat16),
            pltpu.VMEM((share, count), jnp.float32),
        ],
        compiler_params=pltpu.CompilerParams(vmem_limit_bytes=HELD_VMEM),
        cost_estimate=pl.CostEstimate(
            flops=2 * share * count * depth,
            bytes_accessed=2 * share * depth,
            transcendentals=0,
        ),
        name="output",
    )(place, *blocks, w, residual, scale)


def rows_of_slab(q, got):
    placed = []
    for b in range(SLAB):
        piece = got[b]
        for other in range(1, SLAB):
            piece = jnp.where(q == other, got[b ^ other], piece)
        placed.append(piece)
    return jnp.concatenate(placed, axis=1)


def slab_plan(tokens, norm_gain, qkv_weight, q_gain, k_gain, out_weight, layer_scale, segment_ids):
    count = tokens.shape[0]
    seq, tp = lax.axis_index("seq"), lax.axis_index("tp")
    slabs = lax.axis_size("seq") // SLAB
    z, q = seq // SLAB, seq % SLAB
    place = jnp.stack([z, q, tp]).astype(jnp.int32)
    width = qkv_weight.shape[2] // SLAB
    full_width = qkv_weight.shape[2] * lax.axis_size("tp")
    slab, half = SLAB * count, 2 * count
    home = z // 2 == tp

    by_kind = jnp.transpose(qkv_weight, (1, 0, 2))
    cut = [lax.dynamic_slice_in_dim(by_kind, (q ^ r) * width, width, 2) for r in range(SLAB)]
    got = [cut[0]] + [in_slab(cut[r], r) for r in range(1, SLAB)]
    x0 = norm(tokens, norm_gain, slabs)
    out_own = jnp.transpose(out_weight)
    own = rows_of_slab(q, got)
    out_near, out_far = even_pair(out_own), half_pair(out_own)
    gains = [lax.dynamic_slice_in_dim(g, q * width, width, 0)[None] for g in (q_gain, k_gain)]

    outside = jnp.full((half,), -1, jnp.int32)
    seg = jnp.concatenate([outside, segment_ids, outside], axis=0)
    seg = lax.dynamic_slice_in_dim(seg, z * slab, slab + 2 * half, 0)
    spans = key_spans(seg, slab, count, half)
    seg = seg.astype(jnp.float32)[None]
    share = layer_scale.shape[0]
    residual = jnp.transpose(lax.dynamic_slice_in_dim(tokens, tp * share, share, 1))
    scale = jnp.pad(layer_scale, (0, -share % 128))[None]
    x0, out_near, out_far, seg, spans, residual, scale, *gains = tied(
        x0, out_near, out_far, seg, spans, residual, scale, *gains
    )
    out_last = even_pair(out_far)
    x2 = in_slab(x0, 2)
    far, near = half_pair(own), even_pair(own)
    close, away = jnp.stack([out_own, out_near]), jnp.stack([out_far, out_last])
    pad = ((0, 0), (0, -close.shape[1] % 16), (0, 0))
    keep = jnp.pad(jnp.where(home, close, away), pad)
    got = across(jnp.pad(jnp.where(home, away, close), pad))
    keep_x = in_slab(keep, 2)
    near, far, x0, x2, got, keep_x = tied(near, far, x0, x2, got, keep_x)
    last = even_pair(far)
    x1, x3 = in_slab(x0, 1), in_slab(x2, 1)
    got_x, got_c, keep_c = in_slab(got, 2), in_slab(got, 1), in_slab(keep, 1)
    keep_xc = in_slab(tied(keep_x, x3)[0], 1)
    xs = (x0, x1, x2, x3)
    acc, x_last = early(place, xs, own, near, far)
    last, acc, x_last = tied(last, acc, x_last)
    query, keys, values, squares, even, odd = late(place, x_last, acc, last, *gains)
    even, odd = even_pair(even), odd_pair(odd)
    squares, got_x, got_c, keep_c, keep_xc = tied(squares, got_x, got_c, keep_c, keep_xc)
    sums = squares
    for r in range(1, SLAB):
        sums = sums + in_slab(squares, r)
    sums = sums + across(sums)
    sums = (sums, even_pair(sums), odd_pair(sums))
    got_xc = in_slab(got_x, 1)

    blocks = attend(full_width, place, spans, query, keys, values, even, odd, sums, seg)
    *blocks, got_xc = tied(*blocks, got_xc)
    pieces = (keep, keep_c, keep_x, keep_xc, got, got_c, got_x, got_xc)
    spread = []
    for r, i in ((2, 0), (0, 1), (3, 1), (3, 0), (1, 1), (2, 1), (1, 0), (0, 0)):
        to = functools.partial(lambda r, i, z, q, y: (z, q ^ r, y ^ i), r, i)
        spread.append(permuted(blocks[r], to) if r or i else blocks[r])

    return jnp.transpose(output(place, spread, collect(pieces), residual, scale))


def solution(mesh):
    def shards(*args):
        heads = args[2].shape[2] // HEAD_DIM
        slab = mesh.shape["seq"] == 16 and mesh.shape["tp"] == 2 and heads % SLAB == 0
        return (slab_plan if slab else row_plan)(*args)

    return jax.shard_map(
        shards,
        mesh=mesh,
        in_specs=(
            P("seq", None),
            P(),
            P("seq", None, "tp"),
            P("tp"),
            P("tp"),
            P("tp", "seq"),
            P("tp"),
            P(),
        ),
        out_specs=P("seq", "tp"),
        check_vma=False,
    )
```
